32 devices in a mesh: rows: 8 (over z, x), sub: 4 (over y, core).
Axes of the slice: x: 2, y: 2, z: 4, core: 2. Of those that a mesh axis runs over, the one named last changes fastest.
Arguments:
- rhs_solved: float32 [32768, 128], P(('rows', 'sub')), may hold values from -41 to 41
- generators: float32 [3, 32768, 256], P(None, ('rows', 'sub')), may hold values from -0.047111148 to 0.047111148
- solved_gens: float32 [3, 32768, 256], P(None, ('rows', 'sub')), may hold values from -0.18844459 to 0.18844459
Outputs:
- solution: float32 [32768, 128], P(('rows', 'sub'))
The draws below stay inside these ranges and needn't reach their ends.
All inputs are finite; a program needn't handle non-finite values.
Results may differ from the reference program's by a relative error of at most 0.0001.
Values sent between devices are 32-bit elements; how exact they have to be, the bound alone decides.
No kernel may reach another device: no remote copies, remote signals or barrier semaphores. Data moves between devices by JAX's collectives and lax.ppermute only.
A program may use at most 64 MiB of HBM per device.

```python
import jax
import jax.numpy as jnp
from jax import lax

RANK = 256
RHS = 128
ORDER = 32768


def leaf_parts(key, low_end, high_end):
    key_gens = jax.random.fold_in(key, 11)
    key_rows = jax.random.fold_in(key, 12)
    raw_normal = jnp.clip(jax.random.normal(key_gens, (3, ORDER, RANK), jnp.float32), -5.0, 5.0)
    children = 2.0 ** (3.0 - jnp.arange(3, dtype=jnp.float32))
    level_scale = jnp.sqrt(0.4 * children / (1.1 * ORDER))
    row_factor = jnp.exp(jax.random.uniform(key_rows, (ORDER,), jnp.float32, jnp.log(low_end), jnp.log(high_end)))
    return (raw_normal, level_scale, row_factor)


def draw_rhs_solved(key, part):
    raw_normal, level_scale, row_factor = leaf_parts(key, 0.5, 2.0)
    key = jax.random.fold_in(key, 3)
    key_noise = jax.random.fold_in(key, 1)
    key_cols = jax.random.fold_in(key, 2)
    key_mix = jax.random.fold_in(key, 3)
    mixed_rhs = jnp.clip(jax.random.normal(key_noise, (ORDER, RHS), jnp.float32), -5.0, 5.0)
    for level_index in range(3):
        picked_cols = jax.random.permutation(jax.random.fold_in(key_cols, level_index), RANK)[:RHS]
        weights = jax.random.uniform(jax.random.fold_in(key_mix, level_index), (RHS,), jnp.float32, -1.0, 1.0)
        chosen = jnp.take(raw_normal[level_index], picked_cols, axis=1)
        mixed_rhs = mixed_rhs + 0.6 * weights[None, :] * chosen * row_factor[:, None]
    return mixed_rhs


def draw_generators(key, part):
    raw_normal, level_scale, row_factor = leaf_parts(key, 0.5, 2.0)
    return raw_normal * level_scale[:, None, None]


def draw_solved_gens(key, part):
    raw_normal, level_scale, row_factor = leaf_parts(key, 0.5, 2.0)
    return raw_normal * level_scale[:, None, None] * row_factor[None, :, None]


def setup_inputs(seed: int = 0) -> dict:
    key_of = jax.random.split(jax.random.key(seed), 4)
    rhs_solved = draw_rhs_solved(jax.random.fold_in(key_of[3], 71), 0)
    generators = draw_generators(jax.random.fold_in(key_of[3], 71), 0)
    solved_gens = draw_solved_gens(jax.random.fold_in(key_of[3], 71), 0)
    return dict(rhs_solved=rhs_solved, generators=generators, solved_gens=solved_gens)


highest = lax.Precision.HIGHEST

def lower_solve(factor, values):
    return lax.linalg.triangular_solve(factor, values, left_side=True, lower=True)

def factor_solve(factor, values):
    middle = lax.linalg.triangular_solve(factor, values, left_side=True, lower=True)
    return lax.linalg.triangular_solve(factor, middle, left_side=True, lower=True, transpose_a=True)

def pair_solve(p_first, p_second, r_first, r_second):
    identity_matrix = jnp.eye(p_first.shape[0], dtype=p_first.dtype)
    lower_factor = jnp.linalg.cholesky(p_first)
    inner_matrix = identity_matrix - jnp.dot(lower_factor.T, jnp.dot(p_second, lower_factor, precision=highest), precision=highest)
    inner_factor = jnp.linalg.cholesky(inner_matrix)
    shifted = r_first - jnp.dot(p_first, r_second, precision=highest)
    partial_solve = lower_solve(lower_factor, shifted)
    partial_solve = factor_solve(inner_factor, partial_solve)
    z_second = jnp.dot(lower_factor, partial_solve, precision=highest)
    z_first = r_second - jnp.dot(p_second, z_second, precision=highest)
    return (z_first, z_second)

def reference(rhs_solved, generators, solved_gens):
    current = rhs_solved
    solved_list = [solved_gens[0], solved_gens[1], solved_gens[2]]
    for level_index in range(3):
        child_count = 2 ** (3 - level_index)
        child_rows = ORDER // child_count
        stacked = jnp.concatenate([current] + solved_list[level_index + 1:], axis=1)
        col_count = stacked.shape[1]
        blocks = stacked.reshape(child_count, child_rows, col_count)
        basis_rows = generators[level_index].reshape(child_count, child_rows, RANK)
        own_solved = solved_list[level_index].reshape(child_count, child_rows, RANK)
        projection = jnp.einsum('cnk,cnm->ckm', basis_rows, blocks, precision=highest)
        capacitance = jnp.einsum('cnk,cnl->ckl', basis_rows, own_solved, precision=highest)
        z_first, z_second = jax.vmap(pair_solve)(capacitance[0::2], capacitance[1::2], projection[0::2], projection[1::2])
        correction = jnp.stack([z_first, z_second], axis=1).reshape(child_count, RANK, col_count)
        blocks = blocks - jnp.einsum('cnk,ckm->cnm', own_solved, correction, precision=highest)
        stacked = blocks.reshape(ORDER, col_count)
        current = stacked[:, :RHS]
        for offset in range(2 - level_index):
            solved_list[level_index + 1 + offset] = stacked[:, RHS + offset * RANK:RHS + (offset + 1) * RANK]
    return current
```

```python
import jax
import jax.numpy as jnp
from jax import lax
from jax.experimental import pallas as pl
from jax.experimental.pallas import tpu as pltpu
from jax.sharding import PartitionSpec as P

RANK = 256
RHS = 128
HALF = RANK // 2
TOLERANCE = 1e-7
DIVERGED = 1e4
VMEM_LIMIT = 40 * 2**20

SMEM = pl.BlockSpec(memory_space=pltpu.SMEM)
VMEM = pl.BlockSpec(memory_space=pltpu.VMEM)


def swap(value, axis, bit):
    mask = 2**bit
    pairs = [(source, source ^ mask) for source in range(lax.axis_size(axis))]
    return lax.ppermute(value, axis, pairs)


def split(value):
    high = value.astype(jnp.bfloat16)
    low = (value - high.astype(jnp.float32)).astype(jnp.bfloat16)
    return high, low


def dot(left, right, contract=((1,), (0,))):
    def part(first, second):
        return lax.dot_general(first, second, (contract, ((), ())), preferred_element_type=jnp.float32)

    left_high, left_low = split(left)
    right_high, right_low = split(right)
    return part(left_high, right_high) + (part(left_high, right_low) + part(left_low, right_high))


def in_order(core, own, other):
    first = core == 0
    return jnp.concatenate([jnp.where(first, own, other), jnp.where(first, other, own)], axis=1)


def product_kernel(core_ref, *refs):
    *gens_refs, solved_ref, rhs_ref, keep_ref, send_ref, total = refs
    step = pl.program_id(0)
    for place, gens_ref in enumerate(gens_refs):
        rows = slice(place * RANK, (place + 1) * RANK)
        left = gens_ref[0].T
        for index in range(4):
            right = rhs_ref[...] if index == 3 else solved_ref[index]
            value = dot(left, right)
            cols = slice(index * RANK, index * RANK + value.shape[1])

            @pl.when(step == 0)
            def _():
                total[rows, cols] = value

            @pl.when(step > 0)
            def _():
                total[rows, cols] += value

    @pl.when(step == pl.num_programs(0) - 1)
    def _():
        first = core_ref[0] == 0
        for index in range(3):
            low = total[:, index * RANK : index * RANK + HALF]
            high = total[:, index * RANK + HALF : (index + 1) * RANK]
            cols = slice(index * HALF, (index + 1) * HALF)
            keep_ref[:, cols] = jnp.where(first, low, high)
            send_ref[:, cols] = jnp.where(first, high, low)
        keep_ref[:, 3 * HALF :] = total[:, 3 * RANK :]
        send_ref[:, 3 * HALF :] = total[:, 3 * RANK :]


def products(core, generators, solved_gens, rhs, wanted):
    rows = rhs.shape[0]
    block = 256
    levels = len(wanted)
    out = jax.ShapeDtypeStruct((levels * RANK, 3 * HALF + RHS), jnp.float32)

    def level_block(level):
        return pl.BlockSpec((1, block, RANK), lambda i: (level, i, 0))

    return pl.pallas_call(
        product_kernel,
        grid=(rows // block,),
        in_specs=[
            SMEM,
            *[level_block(level) for level in wanted],
            pl.BlockSpec((3, block, RANK), lambda i: (0, i, 0)),
            pl.BlockSpec((block, RHS), lambda i: (i, 0)),
        ],
        out_specs=[pl.BlockSpec(out.shape, lambda i: (0, 0))] * 2,
        out_shape=[out, out],
        scratch_shapes=[pltpu.VMEM((levels * RANK, 3 * RANK + RHS), jnp.float32)],
        compiler_params=pltpu.CompilerParams(vmem_limit_bytes=VMEM_LIMIT),
        cost_estimate=pl.CostEstimate(
            flops=6 * rows * levels * RANK * (3 * RANK + RHS),
            bytes_accessed=4 * rows * ((levels + 3) * RANK + RHS),
            transcendentals=0,
        ),
    )(core, *[generators] * levels, solved_gens, rhs)


def square_norm(value):
    return jnp.sum(value * value)


def series(power_ref, sum_ref):
    def proceed(state):
        count, norm, _ = state
        return (count < 60) & (norm > TOLERANCE) & (norm < DIVERGED * DIVERGED)

    def body(state):
        count, _, _ = state
        power = power_ref[...]
        norm = square_norm(power)
        values = sum_ref[...]
        both = dot(power, jnp.concatenate([power, values], axis=1))
        power_ref[...] = both[:, :RANK]
        sum_ref[...] = values + both[:, RANK:]
        return count + 1, norm, norm

    return lax.while_loop(proceed, body, (jnp.int32(0), jnp.float32(1.0), jnp.float32(1.0)))


def pair_solve(p_own, p_sibling, r_own, r_sibling, power_ref, sum_ref):
    both = dot(p_sibling, jnp.concatenate([p_own, r_own], axis=1))
    product = both[:, :RANK]
    shifted = r_sibling - both[:, RANK:]
    power_ref[...] = product
    sum_ref[...] = shifted
    _, norm, _ = series(power_ref, sum_ref)

    @pl.when(jnp.logical_not(norm <= TOLERANCE))
    def _():
        scale = 1.0 / (1.0 + jnp.sqrt(square_norm(product)))
        row = lax.broadcasted_iota(jnp.int32, (RANK, RANK), 0)
        col = lax.broadcasted_iota(jnp.int32, (RANK, RANK), 1)
        power_ref[...] = jnp.where(row == col, 1.0 - scale, 0.0) + scale * product
        sum_ref[...] = scale * shifted
        series(power_ref, sum_ref)

    return sum_ref[...]


def solve_kernel(core_ref, own_ref, sib_ref, other_ref, mixed_ref, mixed_other_ref, z_ref, next_ref, power, total):
    core = core_ref[0]
    p_own = in_order(core, own_ref[:, :HALF], other_ref[:, :HALF])
    p_sib = in_order(core, sib_ref[:, :HALF], other_ref[:, HALF:])
    z = pair_solve(p_own, p_sib, own_ref[:, HALF:], sib_ref[:, HALF:], power, total)
    z_ref[...] = z
    mixed = in_order(core, mixed_ref[:, :HALF], mixed_other_ref[...])
    next_ref[...] = mixed_ref[:, HALF:] - dot(mixed, z)


def solve(core, own, sib, other, mixed, mixed_other):
    width = own.shape[1] - HALF
    out = jax.ShapeDtypeStruct((RANK, width), jnp.float32)
    return pl.pallas_call(
        solve_kernel,
        in_specs=[SMEM] + [VMEM] * 5,
        out_specs=[VMEM] * 2,
        out_shape=[out, out],
        scratch_shapes=[pltpu.VMEM((RANK, RANK), jnp.float32), pltpu.VMEM((RANK, width), jnp.float32)],
        compiler_params=pltpu.CompilerParams(vmem_limit_bytes=VMEM_LIMIT),
        cost_estimate=pl.CostEstimate(flops=6 * 7 * RANK * RANK * 640, bytes_accessed=4 * RANK * 2560, transcendentals=0),
    )(core, own, sib, other, mixed, mixed_other)


def mix_kernel(core_ref, mixed_ref, other_ref, z_ref, next_ref):
    mixed = in_order(core_ref[0], mixed_ref[:, :HALF], other_ref[...])
    next_ref[...] = mixed_ref[:, HALF:] - dot(mixed, z_ref[...])


def mix(core, mixed, other, z):
    out = jax.ShapeDtypeStruct(z.shape, jnp.float32)
    return pl.pallas_call(
        mix_kernel,
        in_specs=[SMEM] + [VMEM] * 3,
        out_specs=VMEM,
        out_shape=out,
        compiler_params=pltpu.CompilerParams(vmem_limit_bytes=VMEM_LIMIT),
        cost_estimate=pl.CostEstimate(flops=6 * RANK * RANK * 384, bytes_accessed=4 * RANK * 1400, transcendentals=0),
    )(core, mixed, other, z)


def final_kernel(core_ref, own_ref, sib_ref, other_ref, z1_ref, z1_other_ref, z0_ref, z0_other_ref, solved_ref, rhs_ref, out_ref, power, total, coef):
    core = core_ref[0]

    @pl.when(pl.program_id(0) == 0)
    def _():
        p_own = in_order(core, own_ref[:, :HALF], other_ref[:, :HALF])
        p_sib = in_order(core, sib_ref[:, :HALF], other_ref[:, HALF:])
        last = pair_solve(p_own, p_sib, own_ref[:, HALF:], sib_ref[:, HALF:], power, total)
        middle = z1_ref[:, HALF:] - dot(in_order(core, z1_ref[:, :HALF], z1_other_ref[...]), last)
        z01 = in_order(core, z0_ref[:, :HALF], z0_other_ref[:, :HALF])
        z02 = in_order(core, z0_ref[:, HALF:RANK], z0_other_ref[:, HALF:])
        first = z0_ref[:, RANK:] - dot(z01, middle) - dot(z02, last)
        coef[0] = first
        coef[1] = middle
        coef[2] = last

    value = rhs_ref[...]
    for level in range(3):
        value = value - dot(solved_ref[level], coef[level])
    out_ref[...] = value


def final(core, own, sib, other, z1, z1_other, z0, z0_other, solved_gens, rhs):
    rows = rhs.shape[0]
    block = 256

    def whole(value):
        return pl.BlockSpec(value.shape, lambda i: (0, 0))

    small = (own, sib, other, z1, z1_other, z0, z0_other)
    return pl.pallas_call(
        final_kernel,
        grid=(rows // block,),
        in_specs=[SMEM]
        + [whole(value) for value in small]
        + [pl.BlockSpec((3, block, RANK), lambda i: (0, i, 0)), pl.BlockSpec((block, RHS), lambda i: (i, 0))],
        out_specs=pl.BlockSpec((block, RHS), lambda i: (i, 0)),
        out_shape=jax.ShapeDtypeStruct(rhs.shape, jnp.float32),
        scratch_shapes=[
            pltpu.VMEM((RANK, RANK), jnp.float32),
            pltpu.VMEM((RANK, RHS), jnp.float32),
            pltpu.VMEM((3, RANK, RHS), jnp.float32),
        ],
        compiler_params=pltpu.CompilerParams(vmem_limit_bytes=VMEM_LIMIT),
        cost_estimate=pl.CostEstimate(
            flops=6 * rows * 3 * RANK * RHS, bytes_accessed=4 * rows * 4 * RANK, transcendentals=0
        ),
    )(core, *small, solved_gens, rhs)


def on_device(rhs, generators, solved_gens):
    groups = lax.axis_size("rows")
    sub_bits = lax.axis_size("sub").bit_length() - 1
    span_bits = (groups // 8).bit_length() - 1
    core = (lax.axis_index("sub") % 2).astype(jnp.int32).reshape(1)

    keep, send = products(core, generators, solved_gens, rhs, (0,))
    low = keep + swap(send, "sub", 0)
    keep, send = products(core, generators, solved_gens, rhs, (1, 2))
    high = keep + swap(send, "sub", 0)
    for bit in range(1, sub_bits):
        low = low + swap(low, "sub", bit)
    for bit in range(span_bits):
        low = low + swap(low, "rows", bit)
    sibling = swap(low, "rows", span_bits)
    other = swap(jnp.concatenate([low[:, :HALF], sibling[:, :HALF]], axis=1), "sub", 0)
    for bit in range(1, sub_bits):
        high = high + swap(high, "sub", bit)
    for bit in range(span_bits):
        high = high + swap(high, "rows", bit)
    high_other = swap(high[:, :HALF], "sub", 0)

    z0, own = solve(core, low, sibling, other, high[:RANK], high_other[:RANK])
    own = own + swap(own, "rows", span_bits)
    sibling = swap(own, "rows", span_bits + 1)
    other = swap(jnp.concatenate([own[:, :HALF], sibling[:, :HALF]], axis=1), "sub", 0)
    third = mix(core, high[RANK:], high_other[RANK:], z0)
    third = third + swap(third, "rows", span_bits)
    third_other = swap(third[:, :HALF], "sub", 0)
    z0_other = swap(z0[:, :RANK], "sub", 0)

    z1, own = solve(core, own, sibling, other, third, third_other)
    own = own + swap(own, "rows", span_bits + 1)
    sibling = swap(own, "rows", span_bits + 2)
    other = swap(jnp.concatenate([own[:, :HALF], sibling[:, :HALF]], axis=1), "sub", 0)
    z1_other = swap(z1[:, :HALF], "sub", 0)
    return final(core, own, sibling, other, z1, z1_other, z0, z0_other, solved_gens, rhs)


def solution(mesh):
    placed = (
        P(("rows", "sub"), None),
        P(None, ("rows", "sub"), None),
        P(None, ("rows", "sub"), None),
    )
    return jax.shard_map(
        on_device, mesh=mesh, in_specs=placed, out_specs=P(("rows", "sub"), None), check_vma=False
    )
```

```python
import functools

import jax
import jax.numpy as jnp
from jax import lax
from jax.experimental import pallas as pl
from jax.experimental.pallas import tpu as pltpu
from jax.sharding import PartitionSpec as P

RANK = 256
RHS = 128
HALF = RANK // 2
QUARTER = HALF // 2
TOLERANCE = 1e-7
DIVERGED = 1e4
VMEM_LIMIT = 40 * 2**20
STREAM_LIMIT = 52 * 2**20

SMEM = pl.BlockSpec(memory_space=pltpu.SMEM)
VMEM = pl.BlockSpec(memory_space=pltpu.VMEM)
HBM = pl.BlockSpec(memory_space=pltpu.HBM)
ANY = pl.BlockSpec(memory_space=pl.ANY)


def swap(value, axis, bit):
    mask = 2**bit
    pairs = [(source, source ^ mask) for source in range(lax.axis_size(axis))]
    return lax.ppermute(value, axis, pairs)


def struct(rows, cols=HALF):
    return jax.ShapeDtypeStruct((rows, cols), jnp.float32)


def cost(flops, floats):
    return pl.CostEstimate(flops=int(flops), bytes_accessed=int(4 * floats), transcendentals=0)


def split(value):
    high = value.astype(jnp.bfloat16)
    low = (value - high.astype(jnp.float32)).astype(jnp.bfloat16)
    return high, low


def dot_parts(left, right):
    def part(first, second):
        return lax.dot_general(first, second, (((1,), (0,)), ((), ())), preferred_element_type=jnp.float32)

    return part(left[0], right[0]) + (part(left[0], right[1]) + part(left[1], right[0]))


def dot(left, right):
    return dot_parts(split(left), split(right))


def in_order(core, own, other):
    first = core == 0
    return jnp.concatenate([jnp.where(first, own, other), jnp.where(first, other, own)], axis=1)


def pack(value):
    whole = value.shape[1] // HALF
    units = [value[:, index * HALF : (index + 1) * HALF] for index in range(whole)]
    if value.shape[1] % HALF:
        tail = value[:, whole * HALF :]
        units.append(jnp.concatenate([tail[:HALF], tail[HALF:]], axis=1))
    return units


def unpack(ref):
    whole = ref.shape[0] // RANK
    parts = [ref[index * RANK : (index + 1) * RANK, :] for index in range(whole)]
    if ref.shape[0] % RANK:
        tail = ref[whole * RANK :, :]
        parts.append(jnp.concatenate([tail[:, :QUARTER], tail[:, QUARTER:]], axis=0))
    return jnp.concatenate(parts, axis=1) if len(parts) > 1 else parts[0]


def store(ref, value):
    start = 0
    for unit in pack(value):
        ref[start : start + unit.shape[0], :] = unit
        start += unit.shape[0]


def product_kernel(lefts, rights, core_ref, gens_ref, solved_ref, rhs_ref, *refs):
    keep_ref, send_ref, gens, solved, rhs, total, sems = refs[-7:]
    chunks = sems.shape[1]
    block = gens.shape[1] // chunks
    copies = []
    for chunk in range(chunks):
        rows = pl.ds(chunk * block, block)
        row = []
        for place, level in enumerate(lefts):
            row.append((gens_ref.at[level, rows], gens.at[place, rows]))
        for place, level in enumerate(rights):
            if level < 3:
                row.append((solved_ref.at[level, rows], solved.at[place, rows]))
            else:
                row.append((rhs_ref.at[rows], rhs.at[rows]))
        row = [pltpu.make_async_copy(*ends, sems.at[index, chunk]) for index, ends in enumerate(row)]
        for copy in row:
            copy.start()
        copies.append(row)
    for chunk in range(chunks):
        rows = pl.ds(chunk * block, block)
        for copy in copies[chunk]:
            copy.wait()
        right = [rhs[rows, :] if level == 3 else solved[place, rows, :] for place, level in enumerate(rights)]
        right = split(jnp.concatenate(right, axis=1) if len(right) > 1 else right[0])
        for place in range(len(lefts)):
            left = [part.T for part in split(gens[place, rows, :])]
            value = dot_parts(left, right)
            if chunk == 0:
                total[place] = value
            else:
                total[place] += value
    first = core_ref[0] == 0
    start = 0
    for place in range(len(lefts)):
        for index, level in enumerate(rights):
            at = index * RANK
            if level < 3:
                low = total[place, :, at : at + HALF]
                high = total[place, :, at + HALF : at + RANK]
            else:
                value = total[place, :, at : at + RHS]
                low = jnp.concatenate([value[:HALF, :QUARTER], value[HALF:, :QUARTER]], axis=1)
                high = jnp.concatenate([value[:HALF, QUARTER:], value[HALF:, QUARTER:]], axis=1)
            rows = slice(start, start + low.shape[0])
            keep_ref[rows, :] = jnp.where(first, low, high)
            send_ref[rows, :] = jnp.where(first, high, low)
            start += low.shape[0]


def products(core, generators, solved_gens, rhs, lefts, rights, after):
    rows = rhs.shape[0]
    chunks = 2
    width = sum(RHS if level == 3 else RANK for level in rights)
    out = struct(len(lefts) * sum(HALF if level == 3 else RANK for level in rights))
    held = sum(level < 3 for level in rights)
    return pl.pallas_call(
        functools.partial(product_kernel, lefts, rights),
        in_specs=[SMEM, HBM, HBM, HBM] + [ANY] * len(after),
        out_specs=[VMEM] * 2,
        out_shape=[out, out],
        scratch_shapes=[
            pltpu.VMEM((len(lefts), rows, RANK), jnp.float32),
            pltpu.VMEM((held, rows, RANK), jnp.float32),
            pltpu.VMEM((rows, RHS), jnp.float32),
            pltpu.VMEM((len(lefts), RANK, width), jnp.float32),
            pltpu.SemaphoreType.DMA((len(lefts) + len(rights), chunks)),
        ],
        compiler_params=pltpu.CompilerParams(vmem_limit_bytes=STREAM_LIMIT),
        cost_estimate=cost(6 * rows * len(lefts) * RANK * width, rows * (len(lefts) * RANK + width)),
    )(core, generators, solved_gens, rhs, *after)


def square_norm(value):
    return jnp.sum(value * value)


def identity():
    row = lax.broadcasted_iota(jnp.int32, (RANK, RANK), 0)
    col = lax.broadcasted_iota(jnp.int32, (RANK, RANK), 1)
    return jnp.where(row == col, 1.0, 0.0)


def series(start, scale, power_ref, sum_ref):
    norm = square_norm(start)
    power_ref[...] = dot(start, start)
    sum_ref[...] = scale * (identity() + start)

    def proceed(state):
        count, bound = state
        return (count < 60) & (bound > TOLERANCE) & (bound < DIVERGED * DIVERGED)

    def body(state):
        count, _ = state
        power = power_ref[...]
        bound = square_norm(power)
        values = sum_ref[...]
        both = dot(power, jnp.concatenate([power, values], axis=1))
        power_ref[...] = both[:, :RANK]
        sum_ref[...] = values + both[:, RANK:]
        return count + 1, bound

    return lax.while_loop(proceed, body, (jnp.int32(0), norm))[1]


def invert(p_own, p_sib, power_ref, sum_ref):
    product = dot(p_sib, p_own)
    bound = series(product, 1.0, power_ref, sum_ref)

    @pl.when(jnp.logical_not(bound <= TOLERANCE))
    def _():
        scale = 1.0 / (1.0 + jnp.sqrt(square_norm(product)))
        series((1.0 - scale) * identity() + scale * product, scale, power_ref, sum_ref)


def invert_kernel(core_ref, own_ref, sib_ref, own_other_ref, sib_other_ref, inverse_ref, p_sib_ref, power):
    core = core_ref[0]
    p_own = in_order(core, own_ref[...], own_other_ref[...])
    p_sib = in_order(core, sib_ref[...], sib_other_ref[...])
    p_sib_ref[...] = p_sib
    invert(p_own, p_sib, power, inverse_ref)


def inverse(core, own, sib, own_other, sib_other):
    return pl.pallas_call(
        invert_kernel,
        in_specs=[SMEM] + [VMEM] * 4,
        out_specs=[VMEM] * 2,
        out_shape=[struct(RANK, RANK)] * 2,
        scratch_shapes=[pltpu.VMEM((RANK, RANK), jnp.float32)],
        compiler_params=pltpu.CompilerParams(vmem_limit_bytes=VMEM_LIMIT),
        cost_estimate=cost(6 * 9 * RANK**3, 4 * RANK * RANK),
    )(core, own, sib, own_other, sib_other)


def apply_kernel(core_ref, inverse_ref, p_sib_ref, own_ref, sib_ref, mixed_ref, mixed_other_ref, next_ref, *refs):
    z_ref, out_ref = refs[-2:]
    shifted = unpack(sib_ref) - dot(p_sib_ref[...], unpack(own_ref))
    z = dot(inverse_ref[...], shifted)
    store(z_ref, z)
    mixed = in_order(core_ref[0], mixed_ref[...], mixed_other_ref[...])
    store(out_ref, unpack(next_ref) - dot(mixed, z))


def apply(core, inverted, p_sib, own, sib, mixed, mixed_other, following, *after):
    return pl.pallas_call(
        apply_kernel,
        in_specs=[SMEM] + [VMEM] * 7 + [ANY] * len(after),
        out_specs=[VMEM] * 2,
        out_shape=[struct(own.shape[0])] * 2,
        compiler_params=pltpu.CompilerParams(vmem_limit_bytes=VMEM_LIMIT),
        cost_estimate=cost(6 * 3 * RANK * RANK * HALF, 12 * RANK * HALF),
    )(core, inverted, p_sib, own, sib, mixed, mixed_other, following, *after)


def mix_kernel(core_ref, mixed_ref, mixed_other_ref, next_ref, first_ref, second_ref, out_ref):
    mixed = in_order(core_ref[0], mixed_ref[...], mixed_other_ref[...])
    z = jnp.concatenate([unpack(first_ref), unpack(second_ref)], axis=1)
    store(out_ref, unpack(next_ref) - dot(mixed, z))


def mix(core, mixed, mixed_other, following, first, second):
    return pl.pallas_call(
        mix_kernel,
        in_specs=[SMEM] + [VMEM] * 5,
        out_specs=VMEM,
        out_shape=struct(following.shape[0]),
        compiler_params=pltpu.CompilerParams(vmem_limit_bytes=VMEM_LIMIT),
        cost_estimate=cost(6 * RANK * RANK * 320, 12 * RANK * HALF),
    )(core, mixed, mixed_other, following, first, second)


def rhs_in_order(core, own, other):
    first = core == 0
    low = jnp.where(first, own, other)
    high = jnp.where(first, other, own)
    top = jnp.concatenate([low[:, :QUARTER], high[:, :QUARTER]], axis=1)
    bottom = jnp.concatenate([low[:, QUARTER:], high[:, QUARTER:]], axis=1)
    return jnp.concatenate([top, bottom], axis=0)


def final_kernel(
    core_ref, own_ref, sib_ref, own_other_ref, sib_other_ref, z1_ref, z1_other_ref, z0_ref, z0_other_ref,
    z01_ref, z01_other_ref, solved_ref, rhs_ref, out_ref, power, inverted, solved, rhs, sems,
):
    core = core_ref[0]
    copies = [
        pltpu.make_async_copy(solved_ref, solved, sems.at[0]),
        pltpu.make_async_copy(rhs_ref, rhs, sems.at[1]),
    ]
    for copy in copies:
        copy.start()

    def matrix(own, other):
        return in_order(core, own[:RANK, :], other[:RANK, :])

    def columns(own, other):
        return rhs_in_order(core, own[RANK:, :], other[RANK:, :])

    p_sib = matrix(sib_ref, sib_other_ref)
    invert(matrix(own_ref, own_other_ref), p_sib, power, inverted)
    shifted = columns(sib_ref, sib_other_ref) - dot(p_sib, columns(own_ref, own_other_ref))
    last = dot(inverted[...], shifted)
    middle = columns(z1_ref, z1_other_ref) - dot(matrix(z1_ref, z1_other_ref), last)
    both = jnp.concatenate([matrix(z01_ref, z01_other_ref), matrix(z0_ref, z0_other_ref)], axis=1)
    first = columns(z0_ref, z0_other_ref) - dot(both, jnp.concatenate([middle, last], axis=0))
    for copy in copies:
        copy.wait()
    value = rhs[...]
    for level, coefs in enumerate((first, middle, last)):
        value = value - dot(solved[level], coefs)
    out_ref[...] = value


def final(core, small, solved_gens, rhs):
    rows = rhs.shape[0]
    return pl.pallas_call(
        final_kernel,
        in_specs=[SMEM] + [VMEM] * len(small) + [HBM, HBM],
        out_specs=VMEM,
        out_shape=struct(rows, RHS),
        scratch_shapes=[
            pltpu.VMEM((RANK, RANK), jnp.float32),
            pltpu.VMEM((RANK, RANK), jnp.float32),
            pltpu.VMEM((3, rows, RANK), jnp.float32),
            pltpu.VMEM((rows, RHS), jnp.float32),
            pltpu.SemaphoreType.DMA((2,)),
        ],
        compiler_params=pltpu.CompilerParams(vmem_limit_bytes=STREAM_LIMIT),
        cost_estimate=cost(6 * rows * 3 * RANK * RHS, rows * 4 * RANK),
    )(core, *small, solved_gens, rhs)


def on_device(rhs, generators, solved_gens):
    groups = lax.axis_size("rows")
    sub_bits = lax.axis_size("sub").bit_length() - 1
    span_bits = (groups // 8).bit_length() - 1
    core = (lax.axis_index("sub") % 2).astype(jnp.int32).reshape(1)

    def partial_products(lefts, rights, *after):
        keep, send = products(core, generators, solved_gens, rhs, lefts, rights, after)
        return keep + swap(send, "sub", 0), send

    def over_child(value):
        for bit in range(1, sub_bits):
            value = value + swap(value, "sub", bit)
        for bit in range(span_bits):
            value = value + swap(value, "rows", bit)
        return value

    head, _ = partial_products((0,), (0, 1))
    tail, sent = partial_products((0,), (2, 3), head)
    second, sent = partial_products((1,), (0, 1, 2, 3), sent)
    p_own = over_child(head[:RANK])
    third, _ = partial_products((2,), (0, 1, 2, 3), sent, p_own)

    p_own_other = swap(p_own, "sub", 0)
    r_own = over_child(head[RANK:])
    p_sib = swap(p_own, "rows", span_bits)
    p_sib_other = swap(p_sib, "sub", 0)
    r_sib = swap(r_own, "rows", span_bits)
    tail = over_child(tail)
    tail_sib = swap(tail, "rows", span_bits)
    near = over_child(second[: 2 * RANK])
    near_other = swap(near[:RANK], "sub", 0)
    far = over_child(second[2 * RANK :])
    third = over_child(third)
    third_other = swap(third[:RANK], "sub", 0)

    inverted, p_sib = inverse(core, p_own, p_sib, p_own_other, p_sib_other)
    z01, p_own = apply(core, inverted, p_sib, r_own, r_sib, near[:RANK], near_other, near[RANK:])
    z0, r_own = apply(core, inverted, p_sib, tail, tail_sib, near[:RANK], near_other, far, p_own)
    third = mix(core, third[:RANK], third_other, third[RANK:], z01, z0)

    p_own = p_own + swap(p_own, "rows", span_bits)
    p_own_other = swap(p_own, "sub", 0)
    p_sib = swap(p_own, "rows", span_bits + 1)
    p_sib_other = swap(p_sib, "sub", 0)
    r_own = r_own + swap(r_own, "rows", span_bits)
    r_sib = swap(r_own, "rows", span_bits + 1)
    third = third + swap(third, "rows", span_bits)
    third_other = swap(third[:RANK], "sub", 0)
    z01_other = swap(z01, "sub", 0)
    z0_other = swap(z0, "sub", 0)
    inverted, p_sib = inverse(core, p_own, p_sib, p_own_other, p_sib_other)
    z1, own = apply(core, inverted, p_sib, r_own, r_sib, third[:RANK], third_other, third[RANK:])

    own = own + swap(own, "rows", span_bits + 1)
    own_other = swap(own, "sub", 0)
    sib = swap(own, "rows", span_bits + 2)
    sib_other = swap(sib, "sub", 0)
    z1_other = swap(z1, "sub", 0)
    small = (own, sib, own_other, sib_other, z1, z1_other, z0, z0_other, z01, z01_other)
    return final(core, small, solved_gens, rhs)


def solution(mesh):
    placed = (
        P(("rows", "sub"), None),
        P(None, ("rows", "sub"), None),
        P(None, ("rows", "sub"), None),
    )
    return jax.shard_map(
        on_device, mesh=mesh, in_specs=placed, out_specs=P(("rows", "sub"), None), check_vma=False
    )
```

```python
import functools

import jax
import jax.numpy as jnp
from jax import lax
from jax.experimental import pallas as pl
from jax.experimental.pallas import tpu as pltpu
from jax.sharding import PartitionSpec as P

RANK = 256
RHS = 128
HALF = RANK // 2
QUARTER = HALF // 2
TOLERANCE = 1e-7
DIVERGED = 1e4
VMEM_LIMIT = 40 * 2**20
STREAM_LIMIT = 52 * 2**20

SMEM = pl.BlockSpec(memory_space=pltpu.SMEM)
VMEM = pl.BlockSpec(memory_space=pltpu.VMEM)
HBM = pl.BlockSpec(memory_space=pltpu.HBM)
ANY = pl.BlockSpec(memory_space=pl.ANY)


def swap(value, axis, bit):
    mask = 2**bit
    pairs = [(source, source ^ mask) for source in range(lax.axis_size(axis))]
    return lax.ppermute(value, axis, pairs)


def struct(rows, cols=HALF):
    return jax.ShapeDtypeStruct((rows, cols), jnp.float32)


def cost(flops, floats):
    return pl.CostEstimate(flops=int(flops), bytes_accessed=int(4 * floats), transcendentals=0)


def split(value):
    high = value.astype(jnp.bfloat16)
    low = (value - high.astype(jnp.float32)).astype(jnp.bfloat16)
    return high, low


def dot_parts(left, right):
    def part(first, second):
        return lax.dot_general(first, second, (((1,), (0,)), ((), ())), preferred_element_type=jnp.float32)

    return part(left[0], right[0]) + (part(left[0], right[1]) + part(left[1], right[0]))


def dot(left, right):
    return dot_parts(split(left), split(right))


def dot_turned(left, right):
    return dot_parts([part.T for part in split(left)], split(right))


def in_order(core, own, other):
    first = core == 0
    return jnp.concatenate([jnp.where(first, own, other), jnp.where(first, other, own)], axis=1)


def pack(value):
    whole = value.shape[1] // HALF
    units = [value[:, index * HALF : (index + 1) * HALF] for index in range(whole)]
    if value.shape[1] % HALF:
        tail = value[:, whole * HALF :]
        units.append(jnp.concatenate([tail[:HALF], tail[HALF:]], axis=1))
    return units


def unpack(ref):
    whole = ref.shape[0] // RANK
    parts = [ref[index * RANK : (index + 1) * RANK, :] for index in range(whole)]
    if ref.shape[0] % RANK:
        tail = ref[whole * RANK :, :]
        parts.append(jnp.concatenate([tail[:, :QUARTER], tail[:, QUARTER:]], axis=0))
    return jnp.concatenate(parts, axis=1) if len(parts) > 1 else parts[0]


def store(ref, value):
    start = 0
    for unit in pack(value):
        ref[start : start + unit.shape[0], :] = unit
        start += unit.shape[0]


def product_kernel(groups, core_ref, gens_ref, solved_ref, rhs_ref, *refs):
    gens, solved, rhs, total, sems = refs[-5:]
    outs = refs[-5 - 2 * len(groups) : -5]
    pairs, lefts, rights = needed(groups)
    chunks = sems.shape[1]
    block = gens.shape[1] // chunks
    copies = []
    for chunk in range(chunks):
        rows = pl.ds(chunk * block, block)
        row = []
        for place, level in enumerate(lefts):
            row.append((gens_ref.at[level, rows], gens.at[place, rows]))
        for place, level in enumerate(rights):
            if level < 3:
                row.append((solved_ref.at[level, rows], solved.at[place, rows]))
            else:
                row.append((rhs_ref.at[rows], rhs.at[rows]))
        row = [pltpu.make_async_copy(*ends, sems.at[index, chunk]) for index, ends in enumerate(row)]
        for copy in row:
            copy.start()
        copies.append(row)
    places = {}
    for chunk in range(chunks):
        rows = pl.ds(chunk * block, block)
        for copy in copies[chunk]:
            copy.wait()
        right = {}
        for place, level in enumerate(rights):
            right[level] = split(rhs[rows, :] if level == 3 else solved[place, rows, :])
        start = 0
        for place, level in enumerate(lefts):
            left = [part.T for part in split(gens[place, rows, :])]
            wanted = [second for first, second in pairs if first == level]
            value = dot_parts(left, [jnp.concatenate([right[second][half] for second in wanted], axis=1) for half in (0, 1)])
            for second in wanted:
                places[level, second] = start
                start += width_of(second)
            cols = slice(start - value.shape[1], start)
            if chunk == 0:
                total[:, cols] = value
            else:
                total[:, cols] += value
    first = core_ref[0] == 0
    for index, group in enumerate(groups):
        keep_ref, send_ref = outs[2 * index : 2 * index + 2]
        start = 0
        for pair in group:
            at = places[pair]
            if pair[1] < 3:
                low = total[:, at : at + HALF]
                high = total[:, at + HALF : at + RANK]
            else:
                value = total[:, at : at + RHS]
                low = jnp.concatenate([value[:HALF, :QUARTER], value[HALF:, :QUARTER]], axis=1)
                high = jnp.concatenate([value[:HALF, QUARTER:], value[HALF:, QUARTER:]], axis=1)
            rows = slice(start, start + low.shape[0])
            keep_ref[rows, :] = jnp.where(first, low, high)
            send_ref[rows, :] = jnp.where(first, high, low)
            start += low.shape[0]


def width_of(level):
    return RHS if level == 3 else RANK


def needed(groups):
    pairs = sorted(pair for group in groups for pair in group)
    return pairs, sorted({left for left, _ in pairs}), sorted({right for _, right in pairs})


def products(core, generators, solved_gens, rhs, groups, after):
    rows = rhs.shape[0]
    chunks = 4
    pairs, lefts, rights = needed(groups)
    width = sum(width_of(right) for _, right in pairs)
    outs = [struct(sum(HALF if right == 3 else RANK for _, right in group)) for group in groups for _ in range(2)]
    return pl.pallas_call(
        functools.partial(product_kernel, groups),
        in_specs=[SMEM, HBM, HBM, HBM] + [ANY] * len(after),
        out_specs=[VMEM] * len(outs),
        out_shape=outs,
        scratch_shapes=[
            pltpu.VMEM((len(lefts), rows, RANK), jnp.float32),
            pltpu.VMEM((sum(level < 3 for level in rights), rows, RANK), jnp.float32),
            pltpu.VMEM((rows, RHS), jnp.float32),
            pltpu.VMEM((RANK, width), jnp.float32),
            pltpu.SemaphoreType.DMA((len(lefts) + len(rights), chunks)),
        ],
        compiler_params=pltpu.CompilerParams(vmem_limit_bytes=STREAM_LIMIT),
        cost_estimate=cost(6 * rows * RANK * width, rows * (len(lefts) + len(rights)) * RANK),
    )(core, generators, solved_gens, rhs, *after)


def square_norm(value):
    return jnp.sum(value * value)


def identity():
    row = lax.broadcasted_iota(jnp.int32, (RANK, RANK), 0)
    col = lax.broadcasted_iota(jnp.int32, (RANK, RANK), 1)
    return jnp.where(row == col, 1.0, 0.0)


def series(start, scale, power_ref, sum_ref):
    norm = square_norm(start)
    power_ref[...] = dot(start, start)
    sum_ref[...] = scale * (identity() + start)

    def proceed(state):
        count, bound = state
        return (count < 60) & (bound > TOLERANCE) & (bound < DIVERGED * DIVERGED)

    def body(state):
        count, _ = state
        power = power_ref[...]
        bound = square_norm(power)
        values = sum_ref[...]
        both = dot(power, jnp.concatenate([power, values], axis=1))
        power_ref[...] = both[:, :RANK]
        sum_ref[...] = values + both[:, RANK:]
        return count + 1, bound

    return lax.while_loop(proceed, body, (jnp.int32(0), norm))[1]


def invert_kernel(core_ref, own_ref, sib_ref, own_other_ref, sib_other_ref, inverse_ref, p_sib_ref, power):
    core = core_ref[0]
    p_own = in_order(core, own_ref[...], own_other_ref[...])
    p_sib = in_order(core, sib_ref[...], sib_other_ref[...])
    p_sib_ref[...] = p_sib
    product = dot(p_sib, p_own)
    bound = series(product, 1.0, power, inverse_ref)

    @pl.when(jnp.logical_not(bound <= TOLERANCE))
    def _():
        scale = 1.0 / (1.0 + jnp.sqrt(square_norm(product)))
        series((1.0 - scale) * identity() + scale * product, scale, power, inverse_ref)


def call(kernel, out_shape, flops, *values, after=()):
    many = isinstance(out_shape, (list, tuple))
    floats = sum(value.size for value in values) + sum(out.size for out in (out_shape if many else [out_shape]))
    return pl.pallas_call(
        kernel,
        in_specs=[SMEM] + [VMEM] * (len(values) - 1) + [ANY] * len(after),
        out_specs=[VMEM] * len(out_shape) if many else VMEM,
        out_shape=out_shape,
        compiler_params=pltpu.CompilerParams(vmem_limit_bytes=VMEM_LIMIT),
        cost_estimate=cost(flops, floats),
    )(*values, *after)


def inverse(core, own, sib, own_other, sib_other):
    return pl.pallas_call(
        invert_kernel,
        in_specs=[SMEM] + [VMEM] * 4,
        out_specs=[VMEM] * 2,
        out_shape=[struct(RANK, RANK)] * 2,
        scratch_shapes=[pltpu.VMEM((RANK, RANK), jnp.float32)],
        compiler_params=pltpu.CompilerParams(vmem_limit_bytes=VMEM_LIMIT),
        cost_estimate=cost(6 * 9 * RANK**3, 4 * RANK * RANK),
    )(core, own, sib, own_other, sib_other)


def head_kernel(core_ref, inverse_ref, p_sib_ref, own_ref, sib_ref, own_other_ref, next_ref, z_ref, out_ref):
    own = own_ref[...]
    z = dot(inverse_ref[...], sib_ref[...] - dot(p_sib_ref[...], own))
    z_ref[...] = z
    out_ref[...] = next_ref[...] - dot_turned(in_order(core_ref[0], own, own_other_ref[...]), z)


def tail_kernel(core_ref, inverse_ref, p_sib_ref, own_ref, sib_ref, head_ref, head_other_ref, next_ref, *refs):
    z_ref, out_ref = refs[-2:]
    z = dot(inverse_ref[...], unpack(sib_ref) - dot(p_sib_ref[...], unpack(own_ref)))
    store(z_ref, z)
    crossed = in_order(core_ref[0], head_ref[...], head_other_ref[...])
    store(out_ref, unpack(next_ref) - dot_turned(crossed, z))


def third_kernel(core_ref, own_ref, own_other_ref, z_ref, next_ref, *refs):
    crossed = in_order(core_ref[0], own_ref[:RANK, :], own_other_ref[...])
    store(refs[-1], unpack(next_ref) - dot_turned(crossed, unpack(z_ref)))


def middle_kernel(core_ref, inverse_ref, p_sib_ref, own_ref, sib_ref, own_other_ref, next_ref, z_ref, out_ref):
    z = dot(inverse_ref[...], unpack(sib_ref) - dot(p_sib_ref[...], unpack(own_ref)))
    store(z_ref, z)
    crossed = in_order(core_ref[0], own_ref[:RANK, :], own_other_ref[...])
    store(out_ref, unpack(next_ref) - dot_turned(crossed, z))


def rhs_in_order(core, own, other):
    first = core == 0
    low = jnp.where(first, own, other)
    high = jnp.where(first, other, own)
    top = jnp.concatenate([low[:, :QUARTER], high[:, :QUARTER]], axis=1)
    bottom = jnp.concatenate([low[:, QUARTER:], high[:, QUARTER:]], axis=1)
    return jnp.concatenate([top, bottom], axis=0)


def reduced_kernel(
    core_ref, z1_ref, z1_other_ref, z0_ref, z0_other_ref, z01_ref, z01_other_ref, solved_ref, rhs_ref,
    high_ref, low_ref, out_ref, solved, rhs, sems,
):
    core = core_ref[0]
    copies = [
        pltpu.make_async_copy(solved_ref, solved, sems.at[0]),
        pltpu.make_async_copy(rhs_ref, rhs, sems.at[1]),
    ]
    for copy in copies:
        copy.start()
    z12 = in_order(core, z1_ref[:RANK, :], z1_other_ref[:RANK, :])
    z1x = rhs_in_order(core, z1_ref[RANK:, :], z1_other_ref[RANK:, :])
    z02 = in_order(core, z0_ref[:RANK, :], z0_other_ref[:RANK, :])
    z0x = rhs_in_order(core, z0_ref[RANK:, :], z0_other_ref[RANK:, :])
    z01 = in_order(core, z01_ref[...], z01_other_ref[...])
    middle = jnp.concatenate([z12, z1x], axis=1)
    first = jnp.concatenate([z02, z0x], axis=1) - dot(z01, middle)
    coefs = split(jnp.concatenate([first, middle], axis=0))
    for copy in copies:
        copy.wait()
    blocks = 4
    block = rhs.shape[0] // blocks
    for index in range(blocks):
        rows = slice(index * block, (index + 1) * block)
        left = split(jnp.concatenate([solved[0, rows, :], solved[1, rows, :]], axis=1))
        value = dot_parts(left, coefs)
        high, low = split(solved[2, rows, :] - value[:, :RANK])
        high_ref[rows, :] = high
        low_ref[rows, :] = low
        out_ref[rows, :] = rhs[rows, :] - value[:, RANK:]


def reduced(core, small, solved_gens, rhs):
    rows = rhs.shape[0]
    part = jax.ShapeDtypeStruct((rows, RANK), jnp.bfloat16)
    return pl.pallas_call(
        reduced_kernel,
        in_specs=[SMEM] + [VMEM] * len(small) + [HBM, HBM],
        out_specs=[VMEM] * 3,
        out_shape=[part, part, struct(rows, RHS)],
        scratch_shapes=[
            pltpu.VMEM((3, rows, RANK), jnp.float32),
            pltpu.VMEM((rows, RHS), jnp.float32),
            pltpu.SemaphoreType.DMA((2,)),
        ],
        compiler_params=pltpu.CompilerParams(vmem_limit_bytes=STREAM_LIMIT),
        cost_estimate=cost(6 * rows * 2 * RANK * (RANK + RHS), rows * 5 * RANK),
    )(core, *small, solved_gens, rhs)


def final_kernel(
    core_ref, inverse_ref, p_sib_ref, own_ref, own_other_ref, sib_ref, sib_other_ref, high_ref, low_ref, rhs_ref, out_ref
):
    core = core_ref[0]
    own = rhs_in_order(core, own_ref[...], own_other_ref[...])
    sib = rhs_in_order(core, sib_ref[...], sib_other_ref[...])
    z = dot(inverse_ref[...], sib - dot(p_sib_ref[...], own))
    out_ref[...] = rhs_ref[...] - dot_parts((high_ref[...], low_ref[...]), split(z))


def on_device(rhs, generators, solved_gens):
    groups = lax.axis_size("rows")
    sub_bits = lax.axis_size("sub").bit_length() - 1
    span_bits = (groups // 8).bit_length() - 1
    core = (lax.axis_index("sub") % 2).astype(jnp.int32).reshape(1)
    flops = 6 * RANK * RANK * HALF

    def partial_products(groups, *after):
        values = products(core, generators, solved_gens, rhs, groups, after)
        return [keep + swap(send, "sub", 0) for keep, send in zip(values[::2], values[1::2])], values[-1]

    def over_child(value):
        for bit in range(1, sub_bits):
            value = value + swap(value, "sub", bit)
        for bit in range(span_bits):
            value = value + swap(value, "rows", bit)
        return value

    (p_own, r_own), sent = partial_products((((0, 0),), ((0, 1),)))
    (tail,), _ = partial_products((((0, 2), (0, 3)),), sent)
    (near, far, third), _ = partial_products((((1, 1),), ((1, 2), (1, 3)), ((2, 2), (2, 3))), tail)
    p_own, r_own, tail, near, far, third = map(over_child, (p_own, r_own, tail, near, far, third))

    p_sib = swap(p_own, "rows", span_bits)
    r_sib = swap(r_own, "rows", span_bits)
    tail_sib = swap(tail, "rows", span_bits)
    p_own_other = swap(p_own, "sub", 0)
    r_own_other = swap(r_own, "sub", 0)
    tail_other = swap(tail[:RANK], "sub", 0)
    p_sib_other = swap(p_sib, "sub", 0)
    inverted, p_sib = inverse(core, p_own, p_sib, p_own_other, p_sib_other)
    z01, p_own = call(
        head_kernel, [struct(RANK)] * 2, 3 * flops, core, inverted, p_sib, r_own, r_sib, r_own_other, near
    )
    z0, r_own = call(
        tail_kernel, [struct(RANK + HALF)] * 2, 5 * flops,
        core, inverted, p_sib, tail, tail_sib, r_own, r_own_other, far, after=(p_own,),
    )
    third = call(third_kernel, struct(RANK + HALF), 2 * flops, core, tail, tail_other, z0, third, after=(r_own,))

    p_own = p_own + swap(p_own, "rows", span_bits)
    r_own = r_own + swap(r_own, "rows", span_bits)
    third = third + swap(third, "rows", span_bits)
    p_sib = swap(p_own, "rows", span_bits + 1)
    r_sib = swap(r_own, "rows", span_bits + 1)
    p_own_other = swap(p_own, "sub", 0)
    r_own_other = swap(r_own[:RANK], "sub", 0)
    p_sib_other = swap(p_sib, "sub", 0)
    inverted, p_sib = inverse(core, p_own, p_sib, p_own_other, p_sib_other)
    z1, own = call(
        middle_kernel, [struct(RANK + HALF)] * 2, 5 * flops,
        core, inverted, p_sib, r_own, r_sib, r_own_other, third,
    )

    p_own, r_own = own[:RANK], own[RANK:]
    p_own = p_own + swap(p_own, "rows", span_bits + 1)
    r_own = r_own + swap(r_own, "rows", span_bits + 1)
    p_sib = swap(p_own, "rows", span_bits + 2)
    r_sib = swap(r_own, "rows", span_bits + 2)
    p_own_other = swap(p_own, "sub", 0)
    r_own_other = swap(r_own, "sub", 0)
    small = (z1, swap(z1, "sub", 0), z0, swap(z0, "sub", 0), z01, swap(z01, "sub", 0))
    high, low, current = reduced(core, small, solved_gens, rhs)
    p_sib_other = swap(p_sib, "sub", 0)
    r_sib_other = swap(r_sib, "sub", 0)
    inverted, p_sib = inverse(core, p_own, p_sib, p_own_other, p_sib_other)
    return call(
        final_kernel, struct(rhs.shape[0], RHS), 6 * rhs.shape[0] * RANK * RHS,
        core, inverted, p_sib, r_own, r_own_other, r_sib, r_sib_other, high, low, current,
    )


def solution(mesh):
    placed = (
        P(("rows", "sub"), None),
        P(None, ("rows", "sub"), None),
        P(None, ("rows", "sub"), None),
    )
    return jax.shard_map(
        on_device, mesh=mesh, in_specs=placed, out_specs=P(("rows", "sub"), None), check_vma=False
    )
```

```python
import functools

import jax
import jax.numpy as jnp
from jax import lax
from jax.experimental import pallas as pl
from jax.experimental.pallas import tpu as pltpu
from jax.sharding import PartitionSpec as P

RANK = 256
RHS = 128
HALF = RANK // 2
QUARTER = HALF // 2
TOLERANCE = 1e-7
DIVERGED = 1e4
VMEM_LIMIT = 40 * 2**20
STREAM_LIMIT = 52 * 2**20

SMEM = pl.BlockSpec(memory_space=pltpu.SMEM)
VMEM = pl.BlockSpec(memory_space=pltpu.VMEM)
HBM = pl.BlockSpec(memory_space=pltpu.HBM)
ANY = pl.BlockSpec(memory_space=pl.ANY)


def swap(value, axis, bit):
    mask = 2**bit
    pairs = [(source, source ^ mask) for source in range(lax.axis_size(axis))]
    return lax.ppermute(value, axis, pairs)


def struct(rows, cols=HALF):
    return jax.ShapeDtypeStruct((rows, cols), jnp.float32)


def cost(flops, floats):
    return pl.CostEstimate(flops=int(flops), bytes_accessed=int(4 * floats), transcendentals=0)


def split(value):
    high = value.astype(jnp.bfloat16)
    low = (value - high.astype(jnp.float32)).astype(jnp.bfloat16)
    return high, low


def dot_parts(left, right):
    first = jnp.concatenate([left[0], left[0], left[1]], axis=1)
    second = jnp.concatenate([right[0], right[1], right[0]], axis=0)
    return lax.dot_general(first, second, (((1,), (0,)), ((), ())), preferred_element_type=jnp.float32)


def dot(left, right):
    return dot_parts(split(left), split(right))


def dot_turned(left, right):
    return dot_parts([part.T for part in split(left)], split(right))


def in_order(core, own, other):
    first = core == 0
    return jnp.concatenate([jnp.where(first, own, other), jnp.where(first, other, own)], axis=1)


def pack(value):
    whole = value.shape[1] // HALF
    units = [value[:, index * HALF : (index + 1) * HALF] for index in range(whole)]
    if value.shape[1] % HALF:
        tail = value[:, whole * HALF :]
        units.append(jnp.concatenate([tail[:HALF], tail[HALF:]], axis=1))
    return units


def unpack(ref):
    whole = ref.shape[0] // RANK
    parts = [ref[index * RANK : (index + 1) * RANK, :] for index in range(whole)]
    if ref.shape[0] % RANK:
        tail = ref[whole * RANK :, :]
        parts.append(jnp.concatenate([tail[:, :QUARTER], tail[:, QUARTER:]], axis=0))
    return jnp.concatenate(parts, axis=1) if len(parts) > 1 else parts[0]


def store(ref, value):
    start = 0
    for unit in pack(value):
        ref[start : start + unit.shape[0], :] = unit
        start += unit.shape[0]


def product_kernel(groups, core_ref, gens_ref, solved_ref, *refs):
    gens, solved, rhs, total, sems = refs[-5:]
    outs = refs[-5 - 2 * len(groups) : -5]
    pairs, lefts, rights = needed(groups)
    rhs_ref = refs[0] if 3 in rights else None
    chunks = sems.shape[1]
    block = gens.shape[1] // chunks
    copies = []
    for chunk in range(chunks):
        rows = pl.ds(chunk * block, block)
        row = []
        for place, level in enumerate(lefts):
            row.append((gens_ref.at[level, rows], gens.at[place, rows]))
        for place, level in enumerate(rights):
            if level < 3:
                row.append((solved_ref.at[level, rows], solved.at[place, rows]))
            else:
                row.append((rhs_ref.at[rows], rhs.at[rows]))
        row = [pltpu.make_async_copy(*ends, sems.at[index, chunk]) for index, ends in enumerate(row)]
        for copy in row:
            copy.start()
        copies.append(row)
    places = {}
    for chunk in range(chunks):
        rows = pl.ds(chunk * block, block)
        for copy in copies[chunk]:
            copy.wait()
        right = {}
        for place, level in enumerate(rights):
            right[level] = split(rhs[rows, :] if level == 3 else solved[place, rows, :])
        start = 0
        for place, level in enumerate(lefts):
            left = [part.T for part in split(gens[place, rows, :])]
            wanted = [second for first, second in pairs if first == level]
            value = dot_parts(left, [jnp.concatenate([right[second][half] for second in wanted], axis=1) for half in (0, 1)])
            for second in wanted:
                places[level, second] = start
                start += width_of(second)
            cols = slice(start - value.shape[1], start)
            if chunk == 0:
                total[:, cols] = value
            else:
                total[:, cols] += value
    first = core_ref[0] == 0
    for index, group in enumerate(groups):
        keep_ref, send_ref = outs[2 * index : 2 * index + 2]
        start = 0
        for pair in group:
            at = places[pair]
            if pair[1] < 3:
                low = total[:, at : at + HALF]
                high = total[:, at + HALF : at + RANK]
            else:
                value = total[:, at : at + RHS]
                low = jnp.concatenate([value[:HALF, :QUARTER], value[HALF:, :QUARTER]], axis=1)
                high = jnp.concatenate([value[:HALF, QUARTER:], value[HALF:, QUARTER:]], axis=1)
            rows = slice(start, start + low.shape[0])
            keep_ref[rows, :] = jnp.where(first, low, high)
            send_ref[rows, :] = jnp.where(first, high, low)
            start += low.shape[0]


def width_of(level):
    return RHS if level == 3 else RANK


def needed(groups):
    pairs = sorted(pair for group in groups for pair in group)
    return pairs, sorted({left for left, _ in pairs}), sorted({right for _, right in pairs})


def products(core, generators, solved_gens, rhs, groups, after):
    rows = rhs.shape[0]
    chunks = 4
    pairs, lefts, rights = needed(groups)
    width = sum(width_of(right) for _, right in pairs)
    outs = [struct(sum(HALF if right == 3 else RANK for _, right in group)) for group in groups for _ in range(2)]
    given = (generators, solved_gens, rhs) if 3 in rights else (generators, solved_gens)
    return pl.pallas_call(
        functools.partial(product_kernel, groups),
        in_specs=[SMEM] + [HBM] * len(given) + [ANY] * len(after),
        out_specs=[VMEM] * len(outs),
        out_shape=outs,
        scratch_shapes=[
            pltpu.VMEM((len(lefts), rows, RANK), jnp.float32),
            pltpu.VMEM((sum(level < 3 for level in rights), rows, RANK), jnp.float32),
            pltpu.VMEM((rows, RHS), jnp.float32),
            pltpu.VMEM((RANK, width), jnp.float32),
            pltpu.SemaphoreType.DMA((len(lefts) + len(rights), chunks)),
        ],
        compiler_params=pltpu.CompilerParams(vmem_limit_bytes=STREAM_LIMIT),
        cost_estimate=cost(6 * rows * RANK * width, rows * (len(lefts) + len(rights)) * RANK),
    )(core, *given, *after)


def square_norm(value):
    return jnp.sum(value * value)


def identity():
    row = lax.broadcasted_iota(jnp.int32, (RANK, RANK), 0)
    col = lax.broadcasted_iota(jnp.int32, (RANK, RANK), 1)
    return jnp.where(row == col, 1.0, 0.0)


def series(start, scale, power_ref, sum_ref):
    norm = square_norm(start)
    power_ref[...] = dot(start, start)
    sum_ref[...] = scale * (identity() + start)

    def proceed(state):
        count, bound = state
        return (count < 60) & (bound > TOLERANCE) & (bound < DIVERGED * DIVERGED)

    def body(state):
        count, _ = state
        power = power_ref[...]
        bound = square_norm(power)
        values = sum_ref[...]
        both = dot(power, jnp.concatenate([power, values], axis=1))
        power_ref[...] = both[:, :RANK]
        sum_ref[...] = values + both[:, RANK:]
        return count + 1, bound

    return lax.while_loop(proceed, body, (jnp.int32(0), norm))[1]


def invert_kernel(core_ref, own_ref, sib_ref, own_other_ref, sib_other_ref, inverse_ref, p_sib_ref, power):
    core = core_ref[0]
    p_own = in_order(core, own_ref[:RANK, :], own_other_ref[:RANK, :])
    p_sib = in_order(core, sib_ref[:RANK, :], sib_other_ref[:RANK, :])
    p_sib_ref[...] = p_sib
    product = dot(p_sib, p_own)
    bound = series(product, 1.0, power, inverse_ref)

    @pl.when(jnp.logical_not(bound <= TOLERANCE))
    def _():
        scale = 1.0 / (1.0 + jnp.sqrt(square_norm(product)))
        series((1.0 - scale) * identity() + scale * product, scale, power, inverse_ref)


def call(kernel, out_shape, flops, *values, after=()):
    many = isinstance(out_shape, (list, tuple))
    floats = sum(value.size for value in values) + sum(out.size for out in (out_shape if many else [out_shape]))
    return pl.pallas_call(
        kernel,
        in_specs=[SMEM] + [VMEM] * (len(values) - 1) + [ANY] * len(after),
        out_specs=[VMEM] * len(out_shape) if many else VMEM,
        out_shape=out_shape,
        compiler_params=pltpu.CompilerParams(vmem_limit_bytes=VMEM_LIMIT),
        cost_estimate=cost(flops, floats),
    )(*values, *after)


def inverse(core, own, sib, own_other, sib_other):
    return pl.pallas_call(
        invert_kernel,
        in_specs=[SMEM] + [VMEM] * 4,
        out_specs=[VMEM] * 2,
        out_shape=[struct(RANK, RANK)] * 2,
        scratch_shapes=[pltpu.VMEM((RANK, RANK), jnp.float32)],
        compiler_params=pltpu.CompilerParams(vmem_limit_bytes=VMEM_LIMIT),
        cost_estimate=cost(6 * 9 * RANK**3, 4 * RANK * RANK),
    )(core, own, sib, own_other, sib_other)


def head_kernel(core_ref, inverse_ref, p_sib_ref, own_ref, sib_ref, own_other_ref, next_ref, z_ref, out_ref):
    own = own_ref[RANK:, :]
    z = dot(inverse_ref[...], sib_ref[RANK:, :] - dot(p_sib_ref[...], own))
    z_ref[...] = z
    out_ref[...] = next_ref[:RANK, :] - dot_turned(in_order(core_ref[0], own, own_other_ref[RANK:, :]), z)


def tail_kernel(core_ref, inverse_ref, p_sib_ref, own_ref, sib_ref, head_ref, head_other_ref, next_ref, *refs):
    z_ref, out_ref = refs[-2:]
    z = dot(inverse_ref[...], unpack(sib_ref) - dot(p_sib_ref[...], unpack(own_ref)))
    store(z_ref, z)
    crossed = in_order(core_ref[0], head_ref[RANK:, :], head_other_ref[RANK:, :])
    store(out_ref, unpack(next_ref.at[RANK:]) - dot_turned(crossed, z))


def third_kernel(core_ref, own_ref, own_other_ref, z_ref, next_ref, *refs):
    crossed = in_order(core_ref[0], own_ref[:RANK, :], own_other_ref[...])
    store(refs[-1], unpack(next_ref) - dot_turned(crossed, unpack(z_ref)))


def middle_kernel(core_ref, inverse_ref, p_sib_ref, own_ref, sib_ref, own_other_ref, next_ref, z_ref, out_ref):
    z = dot(inverse_ref[...], unpack(sib_ref) - dot(p_sib_ref[...], unpack(own_ref)))
    store(z_ref, z)
    crossed = in_order(core_ref[0], own_ref[:RANK, :], own_other_ref[...])
    store(out_ref, unpack(next_ref) - dot_turned(crossed, z))


def rhs_in_order(core, own, other):
    first = core == 0
    low = jnp.where(first, own, other)
    high = jnp.where(first, other, own)
    top = jnp.concatenate([low[:, :QUARTER], high[:, :QUARTER]], axis=1)
    bottom = jnp.concatenate([low[:, QUARTER:], high[:, QUARTER:]], axis=1)
    return jnp.concatenate([top, bottom], axis=0)


def reduced_kernel(
    core_ref, z1_ref, z1_other_ref, z0_ref, z0_other_ref, z01_ref, z01_other_ref, solved_ref, rhs_ref, *refs
):
    high_ref, low_ref, out_ref, solved, rhs, sems = refs[-6:]
    core = core_ref[0]
    copies = [
        pltpu.make_async_copy(solved_ref, solved, sems.at[0]),
        pltpu.make_async_copy(rhs_ref, rhs, sems.at[1]),
    ]
    for copy in copies:
        copy.start()
    z12 = in_order(core, z1_ref[:RANK, :], z1_other_ref[:RANK, :])
    z1x = rhs_in_order(core, z1_ref[RANK:, :], z1_other_ref[RANK:, :])
    z02 = in_order(core, z0_ref[:RANK, :], z0_other_ref[:RANK, :])
    z0x = rhs_in_order(core, z0_ref[RANK:, :], z0_other_ref[RANK:, :])
    z01 = in_order(core, z01_ref[...], z01_other_ref[...])
    middle = jnp.concatenate([z12, z1x], axis=1)
    first = jnp.concatenate([z02, z0x], axis=1) - dot(z01, middle)
    coefs = split(jnp.concatenate([first, middle], axis=0))
    for copy in copies:
        copy.wait()
    blocks = 4
    block = rhs.shape[0] // blocks
    for index in range(blocks):
        rows = slice(index * block, (index + 1) * block)
        left = split(jnp.concatenate([solved[0, rows, :], solved[1, rows, :]], axis=1))
        value = dot_parts(left, coefs)
        high, low = split(solved[2, rows, :] - value[:, :RANK])
        high_ref[rows, :] = high
        low_ref[rows, :] = low
        out_ref[rows, :] = rhs[rows, :] - value[:, RANK:]


def reduced(core, small, solved_gens, rhs, *after):
    rows = rhs.shape[0]
    part = jax.ShapeDtypeStruct((rows, RANK), jnp.bfloat16)
    return pl.pallas_call(
        reduced_kernel,
        in_specs=[SMEM] + [VMEM] * len(small) + [HBM, HBM] + [ANY] * len(after),
        out_specs=[VMEM] * 3,
        out_shape=[part, part, struct(rows, RHS)],
        scratch_shapes=[
            pltpu.VMEM((3, rows, RANK), jnp.float32),
            pltpu.VMEM((rows, RHS), jnp.float32),
            pltpu.SemaphoreType.DMA((2,)),
        ],
        compiler_params=pltpu.CompilerParams(vmem_limit_bytes=STREAM_LIMIT),
        cost_estimate=cost(6 * rows * 2 * RANK * (RANK + RHS), rows * 5 * RANK),
    )(core, *small, solved_gens, rhs, *after)


def keep_kernel(core_ref, value_ref, *refs):
    refs[-1][...] = value_ref[...]


def final_kernel(
    core_ref, inverse_ref, p_sib_ref, own_ref, own_other_ref, sib_ref, sib_other_ref, high_ref, low_ref, rhs_ref, out_ref
):
    core = core_ref[0]
    own = rhs_in_order(core, own_ref[...], own_other_ref[...])
    sib = rhs_in_order(core, sib_ref[...], sib_other_ref[...])
    z = dot(inverse_ref[...], sib - dot(p_sib_ref[...], own))
    out_ref[...] = rhs_ref[...] - dot_parts((high_ref[...], low_ref[...]), split(z))


def on_device(rhs, generators, solved_gens):
    groups = lax.axis_size("rows")
    sub_bits = lax.axis_size("sub").bit_length() - 1
    span_bits = (groups // 8).bit_length() - 1
    core = (lax.axis_index("sub") % 2).astype(jnp.int32).reshape(1)
    flops = 6 * RANK * RANK * HALF

    def partial_products(groups, *after):
        values = products(core, generators, solved_gens, rhs, groups, after)
        return [keep + swap(send, "sub", 0) for keep, send in zip(values[::2], values[1::2])]

    def over_child(value):
        for bit in range(1, sub_bits):
            value = value + swap(value, "sub", bit)
        for bit in range(span_bits):
            value = value + swap(value, "rows", bit)
        return value

    (head,) = partial_products((((0, 0), (0, 1)),))
    (tail,) = partial_products((((0, 2), (0, 3)),), head)
    (near,) = partial_products((((1, 1), (1, 2), (1, 3)),), tail)
    head, tail = over_child(head), over_child(tail)
    (third,) = partial_products((((2, 2), (2, 3)),), tail)
    near, third = over_child(near), over_child(third)

    head_sib = swap(head, "rows", span_bits)
    tail_sib = swap(tail, "rows", span_bits)
    head_other = swap(head, "sub", 0)
    tail_other = swap(tail[:RANK], "sub", 0)
    p_sib_other = swap(head_sib[:RANK], "sub", 0)
    inverted, p_sib = inverse(core, head, head_sib, head_other, p_sib_other)
    z01, p_own = call(
        head_kernel, [struct(RANK)] * 2, 3 * flops, core, inverted, p_sib, head, head_sib, head_other, near
    )
    z0, r_own = call(
        tail_kernel, [struct(RANK + HALF)] * 2, 5 * flops,
        core, inverted, p_sib, tail, tail_sib, head, head_other, near, after=(p_own,),
    )
    third = call(third_kernel, struct(RANK + HALF), 2 * flops, core, tail, tail_other, z0, third, after=(r_own,))

    p_own = p_own + swap(p_own, "rows", span_bits)
    r_own = r_own + swap(r_own, "rows", span_bits)
    third = third + swap(third, "rows", span_bits)
    p_sib = swap(p_own, "rows", span_bits + 1)
    r_sib = swap(r_own, "rows", span_bits + 1)
    p_own_other = swap(p_own, "sub", 0)
    r_own_other = swap(r_own[:RANK], "sub", 0)
    p_sib_other = swap(p_sib, "sub", 0)
    inverted, p_sib = inverse(core, p_own, p_sib, p_own_other, p_sib_other)
    z1, own = call(
        middle_kernel, [struct(RANK + HALF)] * 2, 5 * flops,
        core, inverted, p_sib, r_own, r_sib, r_own_other, third,
    )

    p_own, r_own = own[:RANK], own[RANK:]
    p_own = p_own + swap(p_own, "rows", span_bits + 1)
    p_sib = swap(p_own, "rows", span_bits + 2)
    r_own = r_own + swap(r_own, "rows", span_bits + 1)
    r_sib = swap(r_own, "rows", span_bits + 2)
    small = (z1, swap(z1, "sub", 0), z0, swap(z0, "sub", 0), z01, swap(z01, "sub", 0))
    high, low, current = reduced(core, small, solved_gens, rhs, r_own)
    p_sib = call(keep_kernel, struct(RANK), 0, core, p_sib, after=(high,))
    p_own_other = swap(p_own, "sub", 0)
    r_own_other = swap(r_own, "sub", 0)
    p_sib_other = swap(p_sib, "sub", 0)
    r_sib_other = swap(r_sib, "sub", 0)
    inverted, p_sib = inverse(core, p_own, p_sib, p_own_other, p_sib_other)
    return call(
        final_kernel, struct(rhs.shape[0], RHS), 6 * rhs.shape[0] * RANK * RHS,
        core, inverted, p_sib, r_own, r_own_other, r_sib, r_sib_other, high, low, current,
    )


def solution(mesh):
    placed = (
        P(("rows", "sub"), None),
        P(None, ("rows", "sub"), None),
        P(None, ("rows", "sub"), None),
    )
    return jax.shard_map(
        on_device, mesh=mesh, in_specs=placed, out_specs=P(("rows", "sub"), None), check_vma=False
    )
```

```python
import functools

import jax
import jax.numpy as jnp
from jax import lax
from jax.experimental import pallas as pl
from jax.experimental.pallas import tpu as pltpu
from jax.sharding import PartitionSpec as P

RANK = 256
RHS = 128
HALF = RANK // 2
QUARTER = HALF // 2
TOLERANCE = 1e-7
DIVERGED = 1e4
SHIFT_FLOPS = 6e9
VMEM_LIMIT = 40 * 2**20
STREAM_LIMIT = 52 * 2**20
FIRST_LIMIT = 52 * 2**20

SMEM = pl.BlockSpec(memory_space=pltpu.SMEM)
VMEM = pl.BlockSpec(memory_space=pltpu.VMEM)
HBM = pl.BlockSpec(memory_space=pltpu.HBM)
ANY = pl.BlockSpec(memory_space=pl.ANY)


def swap(value, axis, bit):
    mask = 2**bit
    pairs = [(source, source ^ mask) for source in range(lax.axis_size(axis))]
    return lax.ppermute(value, axis, pairs)


def struct(rows, cols=HALF):
    return jax.ShapeDtypeStruct((rows, cols), jnp.float32)


def cost(flops, floats):
    return pl.CostEstimate(flops=int(flops), bytes_accessed=int(4 * floats), transcendentals=0)


def split(value):
    high = value.astype(jnp.bfloat16)
    low = (value - high.astype(jnp.float32)).astype(jnp.bfloat16)
    return high, low


def dot_parts(left, right):
    first = jnp.concatenate([left[0], left[0], left[1]], axis=1)
    second = jnp.concatenate([right[0], right[1], right[0]], axis=0)
    return lax.dot_general(first, second, (((1,), (0,)), ((), ())), preferred_element_type=jnp.float32)


def dot(left, right):
    return dot_parts(split(left), split(right))


def dot_turned(left, right):
    return dot_parts([part.T for part in split(left)], split(right))


def in_order(core, own, other):
    first = core == 0
    return jnp.concatenate([jnp.where(first, own, other), jnp.where(first, other, own)], axis=1)


def pack(value):
    whole = value.shape[1] // HALF
    units = [value[:, index * HALF : (index + 1) * HALF] for index in range(whole)]
    if value.shape[1] % HALF:
        tail = value[:, whole * HALF :]
        units.append(jnp.concatenate([tail[:HALF], tail[HALF:]], axis=1))
    return units


def unpack(ref):
    whole = ref.shape[0] // RANK
    parts = [ref[index * RANK : (index + 1) * RANK, :] for index in range(whole)]
    if ref.shape[0] % RANK:
        tail = ref[whole * RANK :, :]
        parts.append(jnp.concatenate([tail[:, :QUARTER], tail[:, QUARTER:]], axis=0))
    return jnp.concatenate(parts, axis=1) if len(parts) > 1 else parts[0]


def store(ref, value):
    start = 0
    for unit in pack(value):
        ref[start : start + unit.shape[0], :] = unit
        start += unit.shape[0]


def product_kernel(groups, core_ref, gens_ref, solved_ref, *refs):
    gens, solved, rhs, total, sems = refs[-5:]
    outs = refs[-5 - 2 * len(groups) : -5]
    pairs, lefts, rights = needed(groups)
    rhs_ref = refs[0] if 3 in rights else None
    chunks = sems.shape[1]
    block = gens.shape[1] // chunks
    copies = []
    for chunk in range(chunks):
        rows = pl.ds(chunk * block, block)
        row = []
        for place, level in enumerate(lefts):
            row.append((gens_ref.at[level, rows], gens.at[place, rows]))
        for place, level in enumerate(rights):
            if level < 3:
                row.append((solved_ref.at[level, rows], solved.at[place, rows]))
            else:
                row.append((rhs_ref.at[rows], rhs.at[rows]))
        row = [pltpu.make_async_copy(*ends, sems.at[index, chunk]) for index, ends in enumerate(row)]
        for copy in row:
            copy.start()
        copies.append(row)
    places = {}
    for chunk in range(chunks):
        rows = pl.ds(chunk * block, block)
        for copy in copies[chunk]:
            copy.wait()
        right = {}
        for place, level in enumerate(rights):
            right[level] = split(rhs[rows, :] if level == 3 else solved[place, rows, :])
        start = 0
        for place, level in enumerate(lefts):
            left = [part.T for part in split(gens[place, rows, :])]
            wanted = [second for first, second in pairs if first == level]
            value = dot_parts(left, [jnp.concatenate([right[second][half] for second in wanted], axis=1) for half in (0, 1)])
            for second in wanted:
                places[level, second] = start
                start += width_of(second)
            cols = slice(start - value.shape[1], start)
            if chunk == 0:
                total[:, cols] = value
            else:
                total[:, cols] += value
    first = core_ref[0] == 0
    for index, group in enumerate(groups):
        keep_ref, send_ref = outs[2 * index : 2 * index + 2]
        start = 0
        for pair in group:
            at = places[pair]
            if pair[1] < 3:
                low = total[:, at : at + HALF]
                high = total[:, at + HALF : at + RANK]
            else:
                value = total[:, at : at + RHS]
                low = jnp.concatenate([value[:HALF, :QUARTER], value[HALF:, :QUARTER]], axis=1)
                high = jnp.concatenate([value[:HALF, QUARTER:], value[HALF:, QUARTER:]], axis=1)
            rows = slice(start, start + low.shape[0])
            keep_ref[rows, :] = jnp.where(first, low, high)
            send_ref[rows, :] = jnp.where(first, high, low)
            start += low.shape[0]


def width_of(level):
    return RHS if level == 3 else RANK


def needed(groups):
    pairs = sorted(pair for group in groups for pair in group)
    return pairs, sorted({left for left, _ in pairs}), sorted({right for _, right in pairs})


def products(core, generators, solved_gens, rhs, groups, after, limit):
    rows = rhs.shape[0]
    chunks = 4
    pairs, lefts, rights = needed(groups)
    width = sum(width_of(right) for _, right in pairs)
    outs = [struct(sum(HALF if right == 3 else RANK for _, right in group)) for group in groups for _ in range(2)]
    given = (generators, solved_gens, rhs) if 3 in rights else (generators, solved_gens)
    return pl.pallas_call(
        functools.partial(product_kernel, groups),
        in_specs=[SMEM] + [HBM] * len(given) + [ANY] * len(after),
        out_specs=[VMEM] * len(outs),
        out_shape=outs,
        scratch_shapes=[
            pltpu.VMEM((len(lefts), rows, RANK), jnp.float32),
            pltpu.VMEM((sum(level < 3 for level in rights), rows, RANK), jnp.float32),
            pltpu.VMEM((rows, RHS), jnp.float32),
            pltpu.VMEM((RANK, width), jnp.float32),
            pltpu.SemaphoreType.DMA((len(lefts) + len(rights), chunks)),
        ],
        compiler_params=pltpu.CompilerParams(vmem_limit_bytes=limit),
        cost_estimate=cost(6 * rows * RANK * width, rows * (len(lefts) + len(rights)) * RANK),
    )(core, *given, *after)


def square_norm(value):
    return jnp.sum(value * value)


def identity():
    row = lax.broadcasted_iota(jnp.int32, (RANK, RANK), 0)
    col = lax.broadcasted_iota(jnp.int32, (RANK, RANK), 1)
    return jnp.where(row == col, 1.0, 0.0)


def series(start, scale, power_ref, sum_ref):
    norm = square_norm(start)
    power_ref[...] = dot(start, start)
    sum_ref[...] = scale * (identity() + start)

    def proceed(state):
        count, bound = state
        return (count < 60) & (bound > TOLERANCE) & (bound < DIVERGED * DIVERGED)

    def body(state):
        count, _ = state
        power = power_ref[...]
        bound = square_norm(power)
        values = sum_ref[...]
        both = dot(power, jnp.concatenate([power, values], axis=1))
        power_ref[...] = both[:, :RANK]
        sum_ref[...] = values + both[:, RANK:]
        return count + 1, bound

    return lax.while_loop(proceed, body, (jnp.int32(0), norm))[1]


def invert_kernel(core_ref, own_ref, sib_ref, own_other_ref, sib_other_ref, inverse_ref, p_sib_ref, power):
    core = core_ref[0]
    p_own = in_order(core, own_ref[:RANK, :], own_other_ref[:RANK, :])
    p_sib = in_order(core, sib_ref[:RANK, :], sib_other_ref[:RANK, :])
    p_sib_ref[...] = p_sib
    product = dot(p_sib, p_own)
    bound = series(product, 1.0, power, inverse_ref)

    @pl.when(jnp.logical_not(bound <= TOLERANCE))
    def _():
        scale = 1.0 / (1.0 + jnp.sqrt(square_norm(product)))
        series((1.0 - scale) * identity() + scale * product, scale, power, inverse_ref)


def call(kernel, out_shape, flops, *values, after=()):
    many = isinstance(out_shape, (list, tuple))
    floats = sum(value.size for value in values) + sum(out.size for out in (out_shape if many else [out_shape]))
    return pl.pallas_call(
        kernel,
        in_specs=[SMEM] + [VMEM] * (len(values) - 1) + [ANY] * len(after),
        out_specs=[VMEM] * len(out_shape) if many else VMEM,
        out_shape=out_shape,
        compiler_params=pltpu.CompilerParams(vmem_limit_bytes=VMEM_LIMIT),
        cost_estimate=cost(flops, floats),
    )(*values, *after)


def inverse(core, own, sib, own_other, sib_other):
    return pl.pallas_call(
        invert_kernel,
        in_specs=[SMEM] + [VMEM] * 4,
        out_specs=[VMEM] * 2,
        out_shape=[struct(RANK, RANK)] * 2,
        scratch_shapes=[pltpu.VMEM((RANK, RANK), jnp.float32)],
        compiler_params=pltpu.CompilerParams(vmem_limit_bytes=VMEM_LIMIT),
        cost_estimate=cost(6 * 9 * RANK**3, 4 * RANK * RANK),
    )(core, own, sib, own_other, sib_other)


def head_kernel(core_ref, inverse_ref, p_sib_ref, own_ref, sib_ref, own_other_ref, next_ref, z_ref, out_ref):
    own = own_ref[RANK:, :]
    z = dot(inverse_ref[...], sib_ref[RANK:, :] - dot(p_sib_ref[...], own))
    z_ref[...] = z
    out_ref[...] = next_ref[:RANK, :] - dot_turned(in_order(core_ref[0], own, own_other_ref[RANK:, :]), z)


def tail_kernel(core_ref, inverse_ref, shifted_ref, head_ref, head_other_ref, next_ref, *refs):
    z_ref, out_ref = refs[-2:]
    z = dot(inverse_ref[...], unpack(shifted_ref))
    store(z_ref, z)
    crossed = in_order(core_ref[0], head_ref[RANK:, :], head_other_ref[RANK:, :])
    store(out_ref, unpack(next_ref.at[RANK:]) - dot_turned(crossed, z))


def third_kernel(core_ref, own_ref, own_other_ref, z_ref, next_ref, *refs):
    crossed = in_order(core_ref[0], own_ref[:RANK, :], own_other_ref[...])
    store(refs[-1], unpack(next_ref) - dot_turned(crossed, unpack(z_ref)))


def middle_kernel(core_ref, inverse_ref, p_sib_ref, own_ref, sib_ref, own_other_ref, next_ref, z_ref, out_ref):
    z = dot(inverse_ref[...], unpack(sib_ref) - dot(p_sib_ref[...], unpack(own_ref)))
    store(z_ref, z)
    crossed = in_order(core_ref[0], own_ref[:RANK, :], own_other_ref[...])
    store(out_ref, unpack(next_ref) - dot_turned(crossed, z))


def rhs_in_order(core, own, other):
    first = core == 0
    low = jnp.where(first, own, other)
    high = jnp.where(first, other, own)
    top = jnp.concatenate([low[:, :QUARTER], high[:, :QUARTER]], axis=1)
    bottom = jnp.concatenate([low[:, QUARTER:], high[:, QUARTER:]], axis=1)
    return jnp.concatenate([top, bottom], axis=0)


def combine_kernel(core_ref, z1_ref, z1_other_ref, z0_ref, z0_other_ref, z01_ref, z01_other_ref, factor_ref, base_ref):
    core = core_ref[0]
    z12 = in_order(core, z1_ref[:RANK, :], z1_other_ref[:RANK, :])
    z1x = rhs_in_order(core, z1_ref[RANK:, :], z1_other_ref[RANK:, :])
    z02 = in_order(core, z0_ref[:RANK, :], z0_other_ref[:RANK, :])
    z0x = rhs_in_order(core, z0_ref[RANK:, :], z0_other_ref[RANK:, :])
    z01 = in_order(core, z01_ref[...], z01_other_ref[...])
    middle = jnp.concatenate([z12, z1x], axis=1)
    first = jnp.concatenate([z02, z0x], axis=1) - dot(z01, middle)
    factor_ref[:RANK, :] = first[:, :RANK]
    factor_ref[RANK:, :] = z12
    base_ref[:RANK, :] = first[:, RANK:]
    base_ref[RANK:, :] = z1x


def keep_kernel(core_ref, value_ref, *refs):
    refs[-1][...] = value_ref[...]


def shift_kernel(core_ref, p_sib_ref, own_ref, sib_ref, out_ref):
    store(out_ref, unpack(sib_ref) - dot(p_sib_ref[...], unpack(own_ref)))


def final_kernel(
    core_ref, inverse_ref, p_sib_ref, own_ref, own_other_ref, sib_ref, sib_other_ref, factor_ref, base_ref,
    solved_ref, rhs_ref, out_ref,
):
    core = core_ref[0]
    own = rhs_in_order(core, own_ref[RANK:, :], own_other_ref[RANK:, :])
    sib = rhs_in_order(core, sib_ref[RANK:, :], sib_other_ref[RANK:, :])
    z = dot(inverse_ref[...], sib - dot(p_sib_ref[...], own))
    coefs = jnp.concatenate([base_ref[...] - dot(factor_ref[...], z), z], axis=0)
    solved = jnp.concatenate([solved_ref[level] for level in range(3)], axis=1)
    out_ref[...] = rhs_ref[...] - dot(solved, coefs)


def on_device(rhs, generators, solved_gens):
    groups = lax.axis_size("rows")
    sub_bits = lax.axis_size("sub").bit_length() - 1
    span_bits = (groups // 8).bit_length() - 1
    core = (lax.axis_index("sub") % 2).astype(jnp.int32).reshape(1)
    flops = 6 * RANK * RANK * HALF

    def met(keep, send):
        return keep + swap(send, "sub", 0)

    def over_child(value):
        for bit in range(1, sub_bits):
            value = value + swap(value, "sub", bit)
        for bit in range(span_bits):
            value = value + swap(value, "rows", bit)
        return value

    keep, send, tail_keep, tail_send = products(
        core, generators, solved_gens, rhs, (((0, 0), (0, 1)), ((0, 2), (0, 3))), (), FIRST_LIMIT
    )
    head = met(keep, send)
    tail = met(tail_keep, call(keep_kernel, struct(RANK + HALF), 0, core, tail_send, after=(head,)))
    keep, send, third_keep, third_send = products(
        core, generators, solved_gens, rhs, (((1, 1), (1, 2), (1, 3)), ((2, 2), (2, 3))), (tail,), STREAM_LIMIT
    )
    near, third = met(keep, send), met(third_keep, third_send)
    head, tail, near, third = map(over_child, (head, tail, near, third))

    head_sib = swap(head, "rows", span_bits)
    tail_sib = swap(tail, "rows", span_bits)
    head_other = swap(head, "sub", 0)
    tail_other = swap(tail[:RANK], "sub", 0)
    p_sib_other = swap(head_sib[:RANK], "sub", 0)
    inverted, p_sib = inverse(core, head, head_sib, head_other, p_sib_other)
    z01, p_own = call(
        head_kernel, [struct(RANK)] * 2, 3 * flops, core, inverted, p_sib, head, head_sib, head_other, near
    )
    shifted = call(shift_kernel, struct(RANK + HALF), SHIFT_FLOPS, core, p_sib, tail, tail_sib)
    z0, r_own = call(
        tail_kernel, [struct(RANK + HALF)] * 2, 4 * flops, core, inverted, shifted, head, head_other, near, after=(p_own,)
    )
    third = call(third_kernel, struct(RANK + HALF), 2 * flops, core, tail, tail_other, z0, third, after=(r_own,))

    p_own = p_own + swap(p_own, "rows", span_bits)
    r_own = r_own + swap(r_own, "rows", span_bits)
    third = third + swap(third, "rows", span_bits)
    p_sib = swap(p_own, "rows", span_bits + 1)
    r_sib = swap(r_own, "rows", span_bits + 1)
    p_own_other = swap(p_own, "sub", 0)
    r_own_other = swap(r_own[:RANK], "sub", 0)
    p_sib_other = swap(p_sib, "sub", 0)
    inverted, p_sib = inverse(core, p_own, p_sib, p_own_other, p_sib_other)
    z1, own = call(
        middle_kernel, [struct(RANK + HALF)] * 2, 5 * flops,
        core, inverted, p_sib, r_own, r_sib, r_own_other, third,
    )

    p_own, r_own = own[:RANK], own[RANK:]
    p_own = p_own + swap(p_own, "rows", span_bits + 1)
    r_own = r_own + swap(r_own, "rows", span_bits + 1)
    sib = jnp.concatenate([swap(p_own, "rows", span_bits + 2), swap(r_own, "rows", span_bits + 2)])
    own = jnp.concatenate([p_own, r_own])
    own_other, sib_other = swap(own, "sub", 0), swap(sib, "sub", 0)
    factor, base = call(
        combine_kernel, [struct(2 * RANK, RANK), struct(2 * RANK, RHS)], 3 * flops,
        core, z1, swap(z1, "sub", 0), z0, swap(z0, "sub", 0), z01, swap(z01, "sub", 0),
    )
    inverted, p_sib = inverse(core, own, sib, own_other, sib_other)
    return call(
        final_kernel, struct(rhs.shape[0], RHS), 6 * rhs.shape[0] * 3 * RANK * RHS,
        core, inverted, p_sib, own, own_other, sib, sib_other, factor, base, solved_gens, rhs,
    )


def solution(mesh):
    placed = (
        P(("rows", "sub"), None),
        P(None, ("rows", "sub"), None),
        P(None, ("rows", "sub"), None),
    )
    return jax.shard_map(
        on_device, mesh=mesh, in_specs=placed, out_specs=P(("rows", "sub"), None), check_vma=False
    )
```

```python
import functools

import jax
import jax.numpy as jnp
from jax import lax
from jax.experimental import pallas as pl
from jax.experimental.pallas import tpu as pltpu
from jax.sharding import PartitionSpec as P

RANK = 256
RHS = 128
HALF = RANK // 2
QUARTER = HALF // 2
SYM = HALF + QUARTER
TOLERANCE = 1e-7
DIVERGED = 1e4
SCALE = 1
FIRST_FLOPS = 6e9
VMEM_LIMIT = 40 * 2**20
STREAM_LIMIT = 52 * 2**20

SMEM = pl.BlockSpec(memory_space=pltpu.SMEM)
VMEM = pl.BlockSpec(memory_space=pltpu.VMEM)
HBM = pl.BlockSpec(memory_space=pltpu.HBM)
ANY = pl.BlockSpec(memory_space=pl.ANY)


def swap(value, axis, bit):
    mask = 2**bit
    pairs = [(source, source ^ mask) for source in range(lax.axis_size(axis))]
    return lax.ppermute(value, axis, pairs)


def struct(rows, cols=HALF):
    return jax.ShapeDtypeStruct((rows, cols), jnp.float32)


def cost(flops, floats):
    return pl.CostEstimate(flops=int(flops / SCALE), bytes_accessed=int(4 * floats / SCALE), transcendentals=0)


def split(value):
    high = value.astype(jnp.bfloat16)
    low = (value - high.astype(jnp.float32)).astype(jnp.bfloat16)
    return high, low


def dot_parts(left, right):
    first = jnp.concatenate([left[0], left[0], left[1]], axis=1)
    second = jnp.concatenate([right[0], right[1], right[0]], axis=0)
    return lax.dot_general(first, second, (((1,), (0,)), ((), ())), preferred_element_type=jnp.float32)


def dot(left, right):
    return dot_parts(split(left), split(right))


def dot_turned(left, right):
    return dot_parts([part.T for part in split(left)], split(right))


def in_order(core, own, other):
    first = core == 0
    return jnp.concatenate([jnp.where(first, own, other), jnp.where(first, other, own)], axis=1)


def symmetric(core, own, other):
    first = core == 0
    low = jnp.where(first, own, other)
    high = jnp.where(first, other, own)
    upper = jnp.concatenate([low[HALF:], high[HALF:]], axis=0)
    return jnp.concatenate(
        [jnp.concatenate([low[:HALF], upper], axis=1), jnp.concatenate([upper.T, high[:HALF]], axis=1)], axis=0
    )


def symmetric_half(core, value):
    first = core == 0
    return jnp.concatenate(
        [
            jnp.where(first, value[:HALF], value[HALF:]),
            jnp.where(first, value[HALF:].T[:QUARTER], value[QUARTER:HALF]),
        ],
        axis=0,
    )


def pack(value):
    whole = value.shape[1] // HALF
    units = [value[:, index * HALF : (index + 1) * HALF] for index in range(whole)]
    if value.shape[1] % HALF:
        tail = value[:, whole * HALF :]
        units.append(jnp.concatenate([tail[:HALF], tail[HALF:]], axis=1))
    return units


def unpack(ref):
    whole = ref.shape[0] // RANK
    parts = [ref[index * RANK : (index + 1) * RANK, :] for index in range(whole)]
    if ref.shape[0] % RANK:
        tail = ref[whole * RANK :, :]
        parts.append(jnp.concatenate([tail[:, :QUARTER], tail[:, QUARTER:]], axis=0))
    return jnp.concatenate(parts, axis=1) if len(parts) > 1 else parts[0]


def store(ref, value):
    start = 0
    for unit in pack(value):
        ref[start : start + unit.shape[0], :] = unit
        start += unit.shape[0]


def product_kernel(groups, core_ref, gens_ref, solved_ref, *refs):
    gens, solved, rhs, total, sems = refs[-5:]
    outs = refs[-5 - 2 * len(groups) : -5]
    pairs, lefts, rights = needed(groups)
    rhs_ref = refs[0] if 3 in rights else None
    chunks = sems.shape[1]
    block = gens.shape[1] // chunks
    copies = []
    for chunk in range(chunks):
        rows = pl.ds(chunk * block, block)
        row = []
        for place, level in enumerate(lefts):
            row.append((gens_ref.at[level, rows], gens.at[place, rows]))
        for place, level in enumerate(rights):
            if level < 3:
                row.append((solved_ref.at[level, rows], solved.at[place, rows]))
            else:
                row.append((rhs_ref.at[rows], rhs.at[rows]))
        row = [pltpu.make_async_copy(*ends, sems.at[index, chunk]) for index, ends in enumerate(row)]
        for copy in row:
            copy.start()
        copies.append(row)
    places = {}
    for chunk in range(chunks):
        rows = pl.ds(chunk * block, block)
        for copy in copies[chunk]:
            copy.wait()
        right = {}
        for place, level in enumerate(rights):
            right[level] = split(rhs[rows, :] if level == 3 else solved[place, rows, :])
        start = 0
        for place, level in enumerate(lefts):
            left = [part.T for part in split(gens[place, rows, :])]
            wanted = [second for first, second in pairs if first == level]
            value = dot_parts(left, [jnp.concatenate([right[second][half] for second in wanted], axis=1) for half in (0, 1)])
            for second in wanted:
                places[level, second] = start
                start += width_of(second)
            cols = slice(start - value.shape[1], start)
            if chunk == 0:
                total[:, cols] = value
            else:
                total[:, cols] += value
    first = core_ref[0] == 0
    for index, group in enumerate(groups):
        keep_ref, send_ref = outs[2 * index : 2 * index + 2]
        start = 0
        for pair in group:
            at = places[pair]
            if pair[0] == pair[1]:
                value = total[:, at : at + RANK]
                low = jnp.concatenate([value[:HALF, :HALF], value[:QUARTER, HALF:]], axis=0)
                high = jnp.concatenate([value[HALF:, HALF:], value[QUARTER:HALF, HALF:]], axis=0)
            elif pair[1] < 3:
                low = total[:, at : at + HALF]
                high = total[:, at + HALF : at + RANK]
            else:
                value = total[:, at : at + RHS]
                low = jnp.concatenate([value[:HALF, :QUARTER], value[HALF:, :QUARTER]], axis=1)
                high = jnp.concatenate([value[:HALF, QUARTER:], value[HALF:, QUARTER:]], axis=1)
            rows = slice(start, start + low.shape[0])
            keep_ref[rows, :] = jnp.where(first, low, high)
            send_ref[rows, :] = jnp.where(first, high, low)
            start += low.shape[0]


def rows_of(pair):
    return SYM if pair[0] == pair[1] else HALF if pair[1] == 3 else RANK


def width_of(level):
    return RHS if level == 3 else RANK


def needed(groups):
    pairs = sorted(pair for group in groups for pair in group)
    return pairs, sorted({left for left, _ in pairs}), sorted({right for _, right in pairs})


def products(core, generators, solved_gens, rhs, groups, *after):
    rows = rhs.shape[0]
    chunks = 4
    pairs, lefts, rights = needed(groups)
    width = sum(width_of(right) for _, right in pairs)
    outs = [struct(sum(rows_of(pair) for pair in group)) for group in groups for _ in range(2)]
    given = (generators, solved_gens, rhs) if 3 in rights else (generators, solved_gens)
    return pl.pallas_call(
        functools.partial(product_kernel, groups),
        in_specs=[SMEM] + [HBM] * len(given) + [ANY] * len(after),
        out_specs=[VMEM] * len(outs),
        out_shape=outs,
        scratch_shapes=[
            pltpu.VMEM((len(lefts), rows, RANK), jnp.float32),
            pltpu.VMEM((sum(level < 3 for level in rights), rows, RANK), jnp.float32),
            pltpu.VMEM((rows, RHS), jnp.float32),
            pltpu.VMEM((RANK, width), jnp.float32),
            pltpu.SemaphoreType.DMA((len(lefts) + len(rights), chunks)),
        ],
        compiler_params=pltpu.CompilerParams(vmem_limit_bytes=STREAM_LIMIT),
        cost_estimate=cost(6 * rows * RANK * width, rows * (len(lefts) + len(rights)) * RANK),
    )(core, *given, *after)


def square_norm(value):
    return jnp.sum(value * value)


def identity():
    row = lax.broadcasted_iota(jnp.int32, (RANK, RANK), 0)
    col = lax.broadcasted_iota(jnp.int32, (RANK, RANK), 1)
    return jnp.where(row == col, 1.0, 0.0)


def series(start, scale, power_ref, sum_ref):
    norm = square_norm(start)
    power_ref[...] = dot(start, start)
    sum_ref[...] = scale * (identity() + start)

    def proceed(state):
        count, bound = state
        return (count < 60) & (bound > TOLERANCE) & (bound < DIVERGED * DIVERGED)

    def body(state):
        count, _ = state
        power = power_ref[...]
        bound = square_norm(power)
        values = sum_ref[...]
        both = dot(power, jnp.concatenate([power, values], axis=1))
        power_ref[...] = both[:, :RANK]
        sum_ref[...] = values + both[:, RANK:]
        return count + 1, bound

    return lax.while_loop(proceed, body, (jnp.int32(0), norm))[1]


def invert_kernel(core_ref, own_ref, sib_ref, own_other_ref, sib_other_ref, inverse_ref, p_sib_ref, power):
    core = core_ref[0]
    p_own = symmetric(core, own_ref[:SYM, :], own_other_ref[:SYM, :])
    p_sib = symmetric(core, sib_ref[:SYM, :], sib_other_ref[:SYM, :])
    p_sib_ref[...] = p_sib
    product = dot(p_sib, p_own)
    bound = series(product, 1.0, power, inverse_ref)

    @pl.when(jnp.logical_not(bound <= TOLERANCE))
    def _():
        scale = 1.0 / (1.0 + jnp.sqrt(square_norm(product)))
        series((1.0 - scale) * identity() + scale * product, scale, power, inverse_ref)


def call(kernel, out_shape, flops, *values, after=()):
    many = isinstance(out_shape, (list, tuple))
    floats = sum(value.size for value in values) + sum(out.size for out in (out_shape if many else [out_shape]))
    return pl.pallas_call(
        kernel,
        in_specs=[SMEM] + [VMEM] * (len(values) - 1) + [ANY] * len(after),
        out_specs=[VMEM] * len(out_shape) if many else VMEM,
        out_shape=out_shape,
        compiler_params=pltpu.CompilerParams(vmem_limit_bytes=VMEM_LIMIT),
        cost_estimate=cost(flops, floats),
    )(*values, *after)


def inverse(core, own, sib, own_other, sib_other):
    return pl.pallas_call(
        invert_kernel,
        in_specs=[SMEM] + [VMEM] * 4,
        out_specs=[VMEM] * 2,
        out_shape=[struct(RANK, RANK)] * 2,
        scratch_shapes=[pltpu.VMEM((RANK, RANK), jnp.float32)],
        compiler_params=pltpu.CompilerParams(vmem_limit_bytes=VMEM_LIMIT),
        cost_estimate=cost(6 * 9 * RANK**3, 4 * RANK * RANK),
    )(core, own, sib, own_other, sib_other)


def first_kernel(core_ref, inverse_ref, p_sib_ref, head_ref, head_sib_ref, head_other_ref, tail_ref, tail_sib_ref, z_ref, out_ref):
    core = core_ref[0]
    own = jnp.concatenate([head_ref[SYM:, :], unpack(tail_ref)], axis=1)
    sib = jnp.concatenate([head_sib_ref[SYM:, :], unpack(tail_sib_ref)], axis=1)
    z = dot(inverse_ref[...], sib - dot(p_sib_ref[...], own))
    store(z_ref, z)
    value = dot_turned(in_order(core, head_ref[SYM:, :], head_other_ref[SYM:, :]), z)
    out_ref[:SYM, :] = symmetric_half(core, value[:, :HALF])
    store(out_ref.at[SYM:], value[:, HALF:])


def last_parts(core, crossed, z, next_ref, out_ref):
    value = dot_turned(crossed, z)
    out_ref[:SYM, :] = next_ref[:SYM, :] - symmetric_half(core, value[:, :HALF])
    store(out_ref.at[SYM:], unpack(next_ref.at[SYM:]) - value[:, HALF:])


def third_kernel(core_ref, own_ref, own_other_ref, z_ref, next_ref, *refs):
    core = core_ref[0]
    last_parts(core, in_order(core, own_ref[:RANK, :], own_other_ref[...]), unpack(z_ref.at[RANK:]), next_ref, refs[-1])


def middle_kernel(core_ref, inverse_ref, p_sib_ref, own_ref, sib_ref, own_other_ref, next_ref, z_ref, out_ref):
    core = core_ref[0]
    z = dot(inverse_ref[...], unpack(sib_ref) - dot(p_sib_ref[...], unpack(own_ref)))
    store(z_ref, z)
    last_parts(core, in_order(core, own_ref[:RANK, :], own_other_ref[...]), z, next_ref, out_ref)


def rhs_in_order(core, own, other):
    first = core == 0
    low = jnp.where(first, own, other)
    high = jnp.where(first, other, own)
    top = jnp.concatenate([low[:, :QUARTER], high[:, :QUARTER]], axis=1)
    bottom = jnp.concatenate([low[:, QUARTER:], high[:, QUARTER:]], axis=1)
    return jnp.concatenate([top, bottom], axis=0)


def reduced_kernel(
    core_ref, z1_ref, z1_other_ref, z0_ref, z0_other_ref, solved_ref, rhs_ref, *refs
):
    high_ref, low_ref, out_ref, solved, rhs, sems = refs[-6:]
    core = core_ref[0]
    copies = [
        pltpu.make_async_copy(solved_ref.at[0], solved.at[0], sems.at[0]),
        pltpu.make_async_copy(solved_ref.at[1], solved.at[1], sems.at[1]),
        pltpu.make_async_copy(solved_ref.at[2], solved.at[2], sems.at[2]),
        pltpu.make_async_copy(rhs_ref, rhs, sems.at[3]),
    ]
    for copy in copies:
        copy.start()
    z12 = in_order(core, z1_ref[:RANK, :], z1_other_ref[:RANK, :])
    z1x = rhs_in_order(core, z1_ref[RANK:, :], z1_other_ref[RANK:, :])
    z01 = in_order(core, z0_ref[:RANK, :], z0_other_ref[:RANK, :])
    z02 = in_order(core, z0_ref[RANK : 2 * RANK, :], z0_other_ref[RANK : 2 * RANK, :])
    z0x = rhs_in_order(core, z0_ref[2 * RANK :, :], z0_other_ref[2 * RANK :, :])
    middle = jnp.concatenate([z12, z1x], axis=1)
    first = jnp.concatenate([z02, z0x], axis=1) - dot(z01, middle)
    coefs = jnp.concatenate([first, middle], axis=0)
    for copy in copies:
        copy.wait()
    value = dot(jnp.concatenate([solved[0], solved[1]], axis=1), coefs)
    high, low = split(solved[2] - value[:, :RANK])
    high_ref[...] = high
    low_ref[...] = low
    out_ref[...] = rhs[...] - value[:, RANK:]


def reduced(core, small, solved_gens, rhs, *after):
    rows = rhs.shape[0]
    part = jax.ShapeDtypeStruct((rows, RANK), jnp.bfloat16)
    return pl.pallas_call(
        reduced_kernel,
        in_specs=[SMEM] + [VMEM] * len(small) + [HBM, HBM] + [ANY] * len(after),
        out_specs=[VMEM] * 3,
        out_shape=[part, part, struct(rows, RHS)],
        scratch_shapes=[
            pltpu.VMEM((3, rows, RANK), jnp.float32),
            pltpu.VMEM((rows, RHS), jnp.float32),
            pltpu.SemaphoreType.DMA((4,)),
        ],
        compiler_params=pltpu.CompilerParams(vmem_limit_bytes=STREAM_LIMIT),
        cost_estimate=cost(6 * rows * 2 * RANK * (RANK + RHS), rows * 5 * RANK),
    )(core, *small, solved_gens, rhs, *after)


def keep_kernel(core_ref, value_ref, *refs):
    refs[-1][...] = value_ref[...]


def add_kernel(core_ref, first_ref, second_ref, *refs):
    refs[-1][...] = first_ref[...] + second_ref[...]


def final_kernel(
    core_ref, inverse_ref, p_sib_ref, own_ref, own_other_ref, sib_ref, sib_other_ref, high_ref, low_ref, rhs_ref, out_ref
):
    core = core_ref[0]
    own = rhs_in_order(core, own_ref[SYM:, :], own_other_ref[SYM:, :])
    sib = rhs_in_order(core, sib_ref[SYM:, :], sib_other_ref[SYM:, :])
    z = dot(inverse_ref[...], sib - dot(p_sib_ref[...], own))
    out_ref[...] = rhs_ref[...] - dot_parts((high_ref[...], low_ref[...]), split(z))


def on_device(rhs, generators, solved_gens):
    groups = lax.axis_size("rows")
    sub_bits = lax.axis_size("sub").bit_length() - 1
    span_bits = (groups // 8).bit_length() - 1
    core = (lax.axis_index("sub") % 2).astype(jnp.int32).reshape(1)
    flops = 6 * RANK * RANK * HALF
    last = SYM + HALF

    def over_child(value):
        for bit in range(1, sub_bits):
            value = value + swap(value, "sub", bit)
        for bit in range(span_bits):
            value = value + swap(value, "rows", bit)
        return value

    keep, send = products(core, generators, solved_gens, rhs, (((0, 0), (0, 1)),))
    head = keep + swap(send, "sub", 0)
    token = swap(call(keep_kernel, struct(8), 0, core, send[:8], after=(head,)), "sub", 0)
    groups = (((0, 2), (0, 3)), ((1, 1), (1, 2), (1, 3)), ((2, 2), (2, 3)))
    parts = products(core, generators, solved_gens, rhs, groups, token)
    parts = [(keep, swap(send, "sub", 0)) for keep, send in zip(parts[::2], parts[1::2])]
    head = over_child(head)
    tail = over_child(parts[0][0] + parts[0][1])
    near = over_child(call(add_kernel, struct(SYM + RANK + HALF), 0, core, *parts[1], after=(tail,)))
    third = over_child(call(add_kernel, struct(last), 0, core, *parts[2], after=(near,)))

    head_sib = swap(head, "rows", span_bits)
    tail_sib = swap(tail, "rows", span_bits)
    head_other = swap(head, "sub", 0)
    tail_other = swap(tail[:RANK], "sub", 0)
    p_sib_other = swap(head_sib[:SYM], "sub", 0)
    inverted, p_sib = inverse(core, head, head_sib, head_other, p_sib_other)
    z0, crossed = call(
        first_kernel, [struct(2 * RANK + HALF), struct(SYM + RANK + HALF)], FIRST_FLOPS,
        core, inverted, p_sib, head, head_sib, head_other, tail, tail_sib,
    )
    near = near - crossed
    third = call(third_kernel, struct(last), 2 * flops, core, tail, tail_other, z0, third, after=(near,))

    near = near + swap(near, "rows", span_bits)
    p_own, r_own = near[:SYM], near[SYM:]
    third = third + swap(third, "rows", span_bits)
    p_sib = swap(p_own, "rows", span_bits + 1)
    r_sib = swap(r_own, "rows", span_bits + 1)
    p_own_other = swap(p_own, "sub", 0)
    r_own_other = swap(r_own[:RANK], "sub", 0)
    p_sib_other = swap(p_sib, "sub", 0)
    inverted, p_sib = inverse(core, p_own, p_sib, p_own_other, p_sib_other)
    z1, own = call(
        middle_kernel, [struct(RANK + HALF), struct(last)], 5 * flops,
        core, inverted, p_sib, r_own, r_sib, r_own_other, third,
    )

    own = own + swap(own, "rows", span_bits + 1)
    sib = swap(own, "rows", span_bits + 2)
    small = (z1, swap(z1, "sub", 0), z0, swap(z0, "sub", 0))
    high, low, current = reduced(core, small, solved_gens, rhs, own)
    sib = call(keep_kernel, struct(last), 0, core, sib, after=(high,))
    own_other, sib_other = swap(own, "sub", 0), swap(sib, "sub", 0)
    inverted, p_sib = inverse(core, own, sib, own_other, sib_other)
    return call(
        final_kernel, struct(rhs.shape[0], RHS), 6 * rhs.shape[0] * RANK * RHS,
        core, inverted, p_sib, own, own_other, sib, sib_other, high, low, current,
    )


def solution(mesh):
    placed = (
        P(("rows", "sub"), None),
        P(None, ("rows", "sub"), None),
        P(None, ("rows", "sub"), None),
    )
    return jax.shard_map(
        on_device, mesh=mesh, in_specs=placed, out_specs=P(("rows", "sub"), None), check_vma=False
    )
```

```python
import functools

import jax
import jax.numpy as jnp
from jax import lax
from jax.experimental import pallas as pl
from jax.experimental.pallas import tpu as pltpu
from jax.sharding import PartitionSpec as P

RANK = 256
RHS = 128
HALF = RANK // 2
QUARTER = HALF // 2
SYM = HALF + QUARTER
TOLERANCE = 1e-7
DIVERGED = 1e4
FIRST_FLOPS = 6.5e8
THIRD_FLOPS = 3e9
VMEM_LIMIT = 40 * 2**20
STREAM_LIMIT = 52 * 2**20

SMEM = pl.BlockSpec(memory_space=pltpu.SMEM)
VMEM = pl.BlockSpec(memory_space=pltpu.VMEM)
HBM = pl.BlockSpec(memory_space=pltpu.HBM)
ANY = pl.BlockSpec(memory_space=pl.ANY)


def swap(value, axis, bit):
    mask = 2**bit
    pairs = [(source, source ^ mask) for source in range(lax.axis_size(axis))]
    return lax.ppermute(value, axis, pairs)


def struct(rows, cols=HALF):
    return jax.ShapeDtypeStruct((rows, cols), jnp.float32)


def cost(flops, floats):
    return pl.CostEstimate(flops=int(flops), bytes_accessed=int(4 * floats), transcendentals=0)


def split(value):
    high = value.astype(jnp.bfloat16)
    low = (value - high.astype(jnp.float32)).astype(jnp.bfloat16)
    return high, low


def dot_parts(left, right):
    first = jnp.concatenate([left[0], left[0], left[1]], axis=1)
    second = jnp.concatenate([right[0], right[1], right[0]], axis=0)
    return lax.dot_general(first, second, (((1,), (0,)), ((), ())), preferred_element_type=jnp.float32)


def dot(left, right):
    return dot_parts(split(left), split(right))


def dot_turned(left, right):
    return dot_parts([part.T for part in split(left)], split(right))


def in_order(core, own, other):
    first = core == 0
    return jnp.concatenate([jnp.where(first, own, other), jnp.where(first, other, own)], axis=1)


def symmetric(core, own, other):
    first = core == 0
    low = jnp.where(first, own, other)
    high = jnp.where(first, other, own)
    upper = jnp.concatenate([low[HALF:], high[HALF:]], axis=0)
    return jnp.concatenate(
        [jnp.concatenate([low[:HALF], upper], axis=1), jnp.concatenate([upper.T, high[:HALF]], axis=1)], axis=0
    )


def symmetric_half(core, value):
    first = core == 0
    return jnp.concatenate(
        [
            jnp.where(first, value[:HALF], value[HALF:]),
            jnp.where(first, value[HALF:].T[:QUARTER], value[QUARTER:HALF]),
        ],
        axis=0,
    )


def pack(value):
    whole = value.shape[1] // HALF
    units = [value[:, index * HALF : (index + 1) * HALF] for index in range(whole)]
    if value.shape[1] % HALF:
        tail = value[:, whole * HALF :]
        units.append(jnp.concatenate([tail[:HALF], tail[HALF:]], axis=1))
    return units


def unpack(ref):
    whole = ref.shape[0] // RANK
    parts = [ref[index * RANK : (index + 1) * RANK, :] for index in range(whole)]
    if ref.shape[0] % RANK:
        tail = ref[whole * RANK :, :]
        parts.append(jnp.concatenate([tail[:, :QUARTER], tail[:, QUARTER:]], axis=0))
    return jnp.concatenate(parts, axis=1) if len(parts) > 1 else parts[0]


def store(ref, value):
    start = 0
    for unit in pack(value):
        ref[start : start + unit.shape[0], :] = unit
        start += unit.shape[0]


def product_kernel(groups, core_ref, gens_ref, solved_ref, *refs):
    gens, solved, total, sems = refs[-4:]
    outs = refs[-4 - 2 * len(groups) : -4]
    blocks, lefts, rights = needed(groups)
    rhs_ref = refs[0] if 3 in rights else None
    chunks = sems.shape[1]
    block = gens.shape[1] // chunks
    copies = []
    for chunk in range(chunks):
        rows = pl.ds(chunk * block, block)
        row = [(gens_ref.at[level, rows], gens.at[place, rows]) for place, level in enumerate(lefts)]
        row += [(solved_ref.at[level, rows], solved.at[place, rows]) for place, level in enumerate(rights) if level < 3]
        row = [pltpu.make_async_copy(*ends, sems.at[index, chunk]) for index, ends in enumerate(row)]
        for copy in row:
            copy.start()
        copies.append(row)
    places = {}
    for chunk in range(chunks):
        rows = pl.ds(chunk * block, block)
        for copy in copies[chunk]:
            copy.wait()
        right = {}
        for place, level in enumerate(rights):
            right[level] = split(rhs_ref[rows, :] if level == 3 else solved[place, rows, :])
        left = [[part.T for part in split(gens[place, rows, :])] for place in range(len(lefts))]
        start = 0
        for firsts, seconds in blocks:
            value = dot_parts(
                [jnp.concatenate([left[lefts.index(level)][half] for level in firsts], axis=0) for half in (0, 1)],
                [jnp.concatenate([right[level][half] for level in seconds], axis=1) for half in (0, 1)],
            )
            cols = slice(start, start + value.shape[1])
            if chunk == 0:
                total[: value.shape[0], cols] = value
            else:
                total[: value.shape[0], cols] += value
            for level in seconds:
                for place, first in enumerate(firsts):
                    places[first, level] = (place * RANK, start)
                start += width_of(level)
    first = core_ref[0] == 0
    for index, group in enumerate(groups):
        keep_ref, send_ref = outs[2 * index : 2 * index + 2]
        start = 0
        for pair in group:
            row, at = places[pair]
            value = total[row : row + RANK, at : at + width_of(pair[1])]
            if pair[0] == pair[1]:
                low = jnp.concatenate([value[:HALF, :HALF], value[:QUARTER, HALF:]], axis=0)
                high = jnp.concatenate([value[HALF:, HALF:], value[QUARTER:HALF, HALF:]], axis=0)
            elif pair[1] < 3:
                low = value[:, :HALF]
                high = value[:, HALF:]
            else:
                low = jnp.concatenate([value[:HALF, :QUARTER], value[HALF:, :QUARTER]], axis=1)
                high = jnp.concatenate([value[:HALF, QUARTER:], value[HALF:, QUARTER:]], axis=1)
            rows = slice(start, start + low.shape[0])
            keep_ref[rows, :] = jnp.where(first, low, high)
            send_ref[rows, :] = jnp.where(first, high, low)
            start += low.shape[0]


def rows_of(pair):
    return SYM if pair[0] == pair[1] else HALF if pair[1] == 3 else RANK


def width_of(level):
    return RHS if level == 3 else RANK


def needed(groups):
    pairs = sorted(pair for group in groups for pair in group)
    rights = sorted({right for _, right in pairs})
    blocks = {}
    for right in rights:
        blocks.setdefault(tuple(left for left, other in pairs if other == right), []).append(right)
    return list(blocks.items()), sorted({left for left, _ in pairs}), rights


def products(core, generators, solved_gens, rhs, groups, *after):
    rows = rhs.shape[0]
    chunks = 4
    blocks, lefts, rights = needed(groups)
    width = sum(width_of(right) for right in rights)
    height = max(len(firsts) for firsts, _ in blocks) * RANK
    flops = sum(len(firsts) * width_of(right) for firsts, seconds in blocks for right in seconds) * 6 * rows * RANK
    outs = [struct(sum(rows_of(pair) for pair in group)) for group in groups for _ in range(2)]
    held = sum(level < 3 for level in rights)
    given, specs = [generators, solved_gens], [HBM, HBM]
    if 3 in rights:
        given, specs = given + [rhs], specs + [VMEM]
    return pl.pallas_call(
        functools.partial(product_kernel, groups),
        in_specs=[SMEM] + specs + [ANY] * len(after),
        out_specs=[VMEM] * len(outs),
        out_shape=outs,
        scratch_shapes=[
            pltpu.VMEM((len(lefts), rows, RANK), jnp.float32),
            pltpu.VMEM((held, rows, RANK), jnp.float32),
            pltpu.VMEM((height, width), jnp.float32),
            pltpu.SemaphoreType.DMA((len(lefts) + held, chunks)),
        ],
        compiler_params=pltpu.CompilerParams(vmem_limit_bytes=STREAM_LIMIT),
        cost_estimate=cost(flops, rows * (len(lefts) * RANK + width)),
    )(core, *given, *after)


def square_norm(value):
    return jnp.sum(value * value)


def identity():
    row = lax.broadcasted_iota(jnp.int32, (RANK, RANK), 0)
    col = lax.broadcasted_iota(jnp.int32, (RANK, RANK), 1)
    return jnp.where(row == col, 1.0, 0.0)


def series(start, values, power_ref, sum_ref):
    norm = square_norm(start)
    if values is None:
        power_ref[...] = dot(start, start)
        sum_ref[...] = identity() + start
    else:
        both = dot(start, jnp.concatenate([start, values], axis=1))
        power_ref[...] = both[:, :RANK]
        sum_ref[...] = values + both[:, RANK:]

    def proceed(state):
        count, bound = state
        return (count < 60) & (bound > TOLERANCE) & (bound < DIVERGED * DIVERGED)

    def body(state):
        count, _ = state
        power = power_ref[...]
        bound = square_norm(power)
        values = sum_ref[...]
        both = dot(power, jnp.concatenate([power, values], axis=1))
        power_ref[...] = both[:, :RANK]
        sum_ref[...] = values + both[:, RANK:]
        return count + 1, bound

    return lax.while_loop(proceed, body, (jnp.int32(0), norm))[1]


def solve_series(product, values, power_ref, sum_ref):
    bound = series(product, values, power_ref, sum_ref)

    @pl.when(jnp.logical_not(bound <= TOLERANCE))
    def _():
        scale = 1.0 / (1.0 + jnp.sqrt(square_norm(product)))
        series((1.0 - scale) * identity() + scale * product, values, power_ref, sum_ref)
        sum_ref[...] = scale * sum_ref[...]


def invert_kernel(core_ref, own_ref, sib_ref, own_other_ref, sib_other_ref, inverse_ref, p_sib_ref, power):
    core = core_ref[0]
    p_own = symmetric(core, own_ref[:SYM, :], own_other_ref[:SYM, :])
    p_sib = symmetric(core, sib_ref[:SYM, :], sib_other_ref[:SYM, :])
    p_sib_ref[...] = p_sib
    solve_series(dot(p_sib, p_own), None, power, inverse_ref)


def call(kernel, out_shape, flops, *values, after=(), scratch=()):
    many = isinstance(out_shape, (list, tuple))
    floats = sum(value.size for value in values) + sum(out.size for out in (out_shape if many else [out_shape]))
    return pl.pallas_call(
        kernel,
        in_specs=[SMEM] + [VMEM] * (len(values) - 1) + [ANY] * len(after),
        out_specs=[VMEM] * len(out_shape) if many else VMEM,
        out_shape=out_shape,
        scratch_shapes=[pltpu.VMEM(shape, jnp.float32) for shape in scratch],
        compiler_params=pltpu.CompilerParams(vmem_limit_bytes=VMEM_LIMIT),
        cost_estimate=cost(flops, floats),
    )(*values, *after)


def inverse(core, own, sib, own_other, sib_other):
    return pl.pallas_call(
        invert_kernel,
        in_specs=[SMEM] + [VMEM] * 4,
        out_specs=[VMEM] * 2,
        out_shape=[struct(RANK, RANK)] * 2,
        scratch_shapes=[pltpu.VMEM((RANK, RANK), jnp.float32)],
        compiler_params=pltpu.CompilerParams(vmem_limit_bytes=VMEM_LIMIT),
        cost_estimate=cost(6 * 9 * RANK**3, 4 * RANK * RANK),
    )(core, own, sib, own_other, sib_other)


def first_kernel(core_ref, inverse_ref, p_sib_ref, head_ref, head_sib_ref, head_other_ref, tail_ref, tail_sib_ref, z_ref, out_ref):
    core = core_ref[0]
    own = jnp.concatenate([head_ref[SYM:, :], unpack(tail_ref)], axis=1)
    sib = jnp.concatenate([head_sib_ref[SYM:, :], unpack(tail_sib_ref)], axis=1)
    z = dot(inverse_ref[...], sib - dot(p_sib_ref[...], own))
    store(z_ref, z)
    value = dot_turned(in_order(core, head_ref[SYM:, :], head_other_ref[SYM:, :]), z)
    out_ref[:SYM, :] = symmetric_half(core, value[:, :HALF])
    store(out_ref.at[SYM:], value[:, HALF:])


def last_parts(core, crossed, z, out_ref):
    value = dot_turned(crossed, z)
    out_ref[:SYM, :] = symmetric_half(core, value[:, :HALF])
    store(out_ref.at[SYM:], value[:, HALF:])


def third_kernel(core_ref, own_ref, own_other_ref, z_ref, *refs):
    core = core_ref[0]
    last_parts(core, in_order(core, own_ref[:RANK, :], own_other_ref[...]), unpack(z_ref.at[RANK:]), refs[-1])


def middle_kernel(core_ref, inverse_ref, p_sib_ref, own_ref, sib_ref, own_other_ref, z_ref, out_ref):
    core = core_ref[0]
    z = dot(inverse_ref[...], unpack(sib_ref) - dot(p_sib_ref[...], unpack(own_ref)))
    store(z_ref, z)
    last_parts(core, in_order(core, own_ref[:RANK, :], own_other_ref[...]), z, out_ref)


def rhs_in_order(core, own, other):
    first = core == 0
    low = jnp.where(first, own, other)
    high = jnp.where(first, other, own)
    top = jnp.concatenate([low[:, :QUARTER], high[:, :QUARTER]], axis=1)
    bottom = jnp.concatenate([low[:, QUARTER:], high[:, QUARTER:]], axis=1)
    return jnp.concatenate([top, bottom], axis=0)


def reduced_kernel(
    core_ref, z1_ref, z1_other_ref, z0_ref, z0_other_ref, solved_ref, rhs_ref, high_ref, low_ref, out_ref
):
    core = core_ref[0]
    z12 = in_order(core, z1_ref[:RANK, :], z1_other_ref[:RANK, :])
    z1x = rhs_in_order(core, z1_ref[RANK:, :], z1_other_ref[RANK:, :])
    z01 = in_order(core, z0_ref[:RANK, :], z0_other_ref[:RANK, :])
    z02 = in_order(core, z0_ref[RANK : 2 * RANK, :], z0_other_ref[RANK : 2 * RANK, :])
    z0x = rhs_in_order(core, z0_ref[2 * RANK :, :], z0_other_ref[2 * RANK :, :])
    middle = jnp.concatenate([z12, z1x], axis=1)
    first = jnp.concatenate([z02, z0x], axis=1) - dot(z01, middle)
    coefs = jnp.concatenate([first, middle], axis=0)
    value = dot(jnp.concatenate([solved_ref[0], solved_ref[1]], axis=1), coefs)
    high, low = split(solved_ref[2] - value[:, :RANK])
    high_ref[...] = high
    low_ref[...] = low
    out_ref[...] = rhs_ref[...] - value[:, RANK:]


def keep_kernel(core_ref, value_ref, *refs):
    refs[-1][...] = value_ref[...]


def add_kernel(core_ref, first_ref, second_ref, *refs):
    refs[-1][...] = first_ref[...] + second_ref[...]


def subtract_kernel(core_ref, first_ref, second_ref, *refs):
    refs[-1][...] = first_ref[...] - second_ref[...]


def final_kernel(
    core_ref, own_ref, own_other_ref, sib_ref, sib_other_ref, high_ref, low_ref, rhs_ref, out_ref, power, total
):
    core = core_ref[0]
    p_own = symmetric(core, own_ref[:SYM, :], own_other_ref[:SYM, :])
    p_sib = symmetric(core, sib_ref[:SYM, :], sib_other_ref[:SYM, :])
    own = rhs_in_order(core, own_ref[SYM:, :], own_other_ref[SYM:, :])
    sib = rhs_in_order(core, sib_ref[SYM:, :], sib_other_ref[SYM:, :])
    both = dot(p_sib, jnp.concatenate([p_own, own], axis=1))
    solve_series(both[:, :RANK], sib - both[:, RANK:], power, total)
    out_ref[...] = rhs_ref[...] - dot_parts((high_ref[...], low_ref[...]), split(total[...]))


def on_device(rhs, generators, solved_gens):
    groups = lax.axis_size("rows")
    sub_bits = lax.axis_size("sub").bit_length() - 1
    span_bits = (groups // 8).bit_length() - 1
    core = (lax.axis_index("sub") % 2).astype(jnp.int32).reshape(1)
    flops = 6 * RANK * RANK * HALF
    last = SYM + HALF

    def over_child(value):
        for bit in range(1, sub_bits):
            value = value + swap(value, "sub", bit)
        for bit in range(span_bits):
            value = value + swap(value, "rows", bit)
        return value

    keep, send = products(core, generators, solved_gens, rhs, (((0, 0), (0, 1)),))
    head = keep + swap(send, "sub", 0)
    token = swap(call(keep_kernel, struct(8), 0, core, send[:8], after=(head,)), "sub", 0)
    groups = (((0, 2), (0, 3)), ((1, 1), (1, 2), (1, 3)), ((2, 2), (2, 3)))
    parts = products(core, generators, solved_gens, rhs, groups, token)
    parts = [(keep, swap(send, "sub", 0)) for keep, send in zip(parts[::2], parts[1::2])]
    head = over_child(head)
    tail = over_child(parts[0][0] + parts[0][1])
    near = call(add_kernel, struct(SYM + RANK + HALF), 0, core, *parts[1], after=(tail,))
    near = over_child(near)
    third = over_child(call(add_kernel, struct(last), 0, core, *parts[2], after=(near,)))

    head_sib = swap(head, "rows", span_bits)
    tail_sib = swap(tail, "rows", span_bits)
    head_other = swap(head, "sub", 0)
    tail_other = swap(tail[:RANK], "sub", 0)
    p_sib_other = swap(head_sib[:SYM], "sub", 0)
    inverted, p_sib = inverse(core, head, head_sib, head_other, p_sib_other)
    z0, crossed = call(
        first_kernel, [struct(2 * RANK + HALF), struct(SYM + RANK + HALF)], FIRST_FLOPS,
        core, inverted, p_sib, head, head_sib, head_other, tail, tail_sib,
    )
    p_own = call(subtract_kernel, struct(SYM), 0, core, near[:SYM], crossed[:SYM])
    r_own = call(subtract_kernel, struct(RANK + HALF), 0, core, near[SYM:], crossed[SYM:], after=(p_own,))
    third = third - call(third_kernel, struct(last), THIRD_FLOPS, core, tail, tail_other, z0, after=(r_own,))

    p_own = p_own + swap(p_own, "rows", span_bits)
    r_own = r_own + swap(r_own, "rows", span_bits)
    third = third + swap(third, "rows", span_bits)
    p_sib = swap(p_own, "rows", span_bits + 1)
    r_sib = swap(r_own, "rows", span_bits + 1)
    p_own_other = swap(p_own, "sub", 0)
    r_own_other = swap(r_own[:RANK], "sub", 0)
    p_sib_other = swap(p_sib, "sub", 0)
    inverted, p_sib = inverse(core, p_own, p_sib, p_own_other, p_sib_other)
    z1, crossed = call(
        middle_kernel, [struct(RANK + HALF), struct(last)], 5 * flops,
        core, inverted, p_sib, r_own, r_sib, r_own_other,
    )

    own = third - crossed
    own = own + swap(own, "rows", span_bits + 1)
    sib = swap(own, "rows", span_bits + 2)
    z1_other = swap(call(keep_kernel, struct(RANK + HALF), 0, core, z1, after=(own,)), "sub", 0)
    part = jax.ShapeDtypeStruct((rhs.shape[0], RANK), jnp.bfloat16)
    high, low, current = call(
        reduced_kernel, [part, part, struct(rhs.shape[0], RHS)], 6 * rhs.shape[0] * 2 * RANK * (RANK + RHS),
        core, z1, z1_other, z0, swap(z0, "sub", 0), solved_gens, rhs,
    )
    sib = call(keep_kernel, struct(last), 0, core, sib, after=(high,))
    own_other, sib_other = swap(own, "sub", 0), swap(sib, "sub", 0)
    return call(
        final_kernel, struct(rhs.shape[0], RHS), 6 * rhs.shape[0] * RANK * RHS + 6 * 9 * RANK**3,
        core, own, own_other, sib, sib_other, high, low, current, scratch=((RANK, RANK), (RANK, RHS)),
    )


def solution(mesh):
    placed = (
        P(("rows", "sub"), None),
        P(None, ("rows", "sub"), None),
        P(None, ("rows", "sub"), None),
    )
    return jax.shard_map(
        on_device, mesh=mesh, in_specs=placed, out_specs=P(("rows", "sub"), None), check_vma=False
    )
```

```python
import functools

import jax
import jax.numpy as jnp
from jax import lax
from jax.experimental import pallas as pl
from jax.experimental.pallas import tpu as pltpu
from jax.sharding import PartitionSpec as P

RANK = 256
RHS = 128
HALF = RANK // 2
QUARTER = HALF // 2
SYM = HALF + QUARTER
TOLERANCE = 1e-7
DIVERGED = 1e4
FIRST_FLOPS = 6.5e8
THIRD_FLOPS = 3e9
VMEM_LIMIT = 40 * 2**20
STREAM_LIMIT = 52 * 2**20

SMEM = pl.BlockSpec(memory_space=pltpu.SMEM)
VMEM = pl.BlockSpec(memory_space=pltpu.VMEM)
HBM = pl.BlockSpec(memory_space=pltpu.HBM)
ANY = pl.BlockSpec(memory_space=pl.ANY)


def swap(value, axis, bit):
    mask = 2**bit
    pairs = [(source, source ^ mask) for source in range(lax.axis_size(axis))]
    return lax.ppermute(value, axis, pairs)


def struct(rows, cols=HALF):
    return jax.ShapeDtypeStruct((rows, cols), jnp.float32)


def cost(flops, floats):
    return pl.CostEstimate(flops=int(flops), bytes_accessed=int(4 * floats), transcendentals=0)


def split(value):
    high = value.astype(jnp.bfloat16)
    low = (value - high.astype(jnp.float32)).astype(jnp.bfloat16)
    return high, low


def dot_parts(left, right):
    first = jnp.concatenate([left[0], left[0], left[1]], axis=1)
    second = jnp.concatenate([right[0], right[1], right[0]], axis=0)
    return lax.dot_general(first, second, (((1,), (0,)), ((), ())), preferred_element_type=jnp.float32)


def dot(left, right):
    return dot_parts(split(left), split(right))


def dot_turned(left, right):
    return dot_parts([part.T for part in split(left)], split(right))


def in_order(core, own, other):
    first = core == 0
    return jnp.concatenate([jnp.where(first, own, other), jnp.where(first, other, own)], axis=1)


def symmetric(core, own, other):
    first = core == 0
    low = jnp.where(first, own, other)
    high = jnp.where(first, other, own)
    upper = jnp.concatenate([low[HALF:], high[HALF:]], axis=0)
    return jnp.concatenate(
        [jnp.concatenate([low[:HALF], upper], axis=1), jnp.concatenate([upper.T, high[:HALF]], axis=1)], axis=0
    )


def symmetric_half(core, value):
    first = core == 0
    return jnp.concatenate(
        [
            jnp.where(first, value[:HALF], value[HALF:]),
            jnp.where(first, value[HALF:].T[:QUARTER], value[QUARTER:HALF]),
        ],
        axis=0,
    )


def pack(value):
    whole = value.shape[1] // HALF
    units = [value[:, index * HALF : (index + 1) * HALF] for index in range(whole)]
    if value.shape[1] % HALF:
        tail = value[:, whole * HALF :]
        units.append(jnp.concatenate([tail[:HALF], tail[HALF:]], axis=1))
    return units


def unpack(ref):
    whole = ref.shape[0] // RANK
    parts = [ref[index * RANK : (index + 1) * RANK, :] for index in range(whole)]
    if ref.shape[0] % RANK:
        tail = ref[whole * RANK :, :]
        parts.append(jnp.concatenate([tail[:, :QUARTER], tail[:, QUARTER:]], axis=0))
    return jnp.concatenate(parts, axis=1) if len(parts) > 1 else parts[0]


def store(ref, value):
    start = 0
    for unit in pack(value):
        ref[start : start + unit.shape[0], :] = unit
        start += unit.shape[0]


def product_kernel(groups, chunks, core_ref, gens_ref, solved_ref, *refs):
    gens, solved, total, sems = refs[-4:] if chunks > 1 else (None, None, refs[-1], None)
    refs = refs[:-4] if chunks > 1 else refs[:-1]
    outs = refs[-2 * len(groups) :]
    blocks, lefts, rights = needed(groups)
    rhs_ref = refs[0] if 3 in rights else None
    block = gens_ref.shape[1] // chunks
    copies = []
    for chunk in range(chunks if chunks > 1 else 0):
        rows = pl.ds(chunk * block, block)
        row = [(gens_ref.at[level, rows], gens.at[place, rows]) for place, level in enumerate(lefts)]
        row += [(solved_ref.at[level, rows], solved.at[place, rows]) for place, level in enumerate(rights) if level < 3]
        row = [pltpu.make_async_copy(*ends, sems.at[index, chunk]) for index, ends in enumerate(row)]
        for copy in row:
            copy.start()
        copies.append(row)
    places = {}
    for chunk in range(chunks):
        rows = pl.ds(chunk * block, block)
        for copy in copies[chunk] if chunks > 1 else ():
            copy.wait()
        right = {}
        for place, level in enumerate(rights):
            if level == 3:
                right[level] = split(rhs_ref[rows, :])
            else:
                right[level] = split(solved[place, rows, :] if chunks > 1 else solved_ref[level])
        left = []
        for place, level in enumerate(lefts):
            left.append([part.T for part in split(gens[place, rows, :] if chunks > 1 else gens_ref[level])])
        start = 0
        for firsts, seconds in blocks:
            value = dot_parts(
                [jnp.concatenate([left[lefts.index(level)][half] for level in firsts], axis=0) for half in (0, 1)],
                [jnp.concatenate([right[level][half] for level in seconds], axis=1) for half in (0, 1)],
            )
            cols = slice(start, start + value.shape[1])
            if chunk == 0:
                total[: value.shape[0], cols] = value
            else:
                total[: value.shape[0], cols] += value
            for level in seconds:
                for place, first in enumerate(firsts):
                    places[first, level] = (place * RANK, start)
                start += width_of(level)
    first = core_ref[0] == 0
    for index, group in enumerate(groups):
        keep_ref, send_ref = outs[2 * index : 2 * index + 2]
        start = 0
        for pair in group:
            row, at = places[pair]
            value = total[row : row + RANK, at : at + width_of(pair[1])]
            if pair[0] == pair[1]:
                low = jnp.concatenate([value[:HALF, :HALF], value[:QUARTER, HALF:]], axis=0)
                high = jnp.concatenate([value[HALF:, HALF:], value[QUARTER:HALF, HALF:]], axis=0)
            elif pair[1] < 3:
                low = value[:, :HALF]
                high = value[:, HALF:]
            else:
                low = jnp.concatenate([value[:HALF, :QUARTER], value[HALF:, :QUARTER]], axis=1)
                high = jnp.concatenate([value[:HALF, QUARTER:], value[HALF:, QUARTER:]], axis=1)
            rows = slice(start, start + low.shape[0])
            keep_ref[rows, :] = jnp.where(first, low, high)
            send_ref[rows, :] = jnp.where(first, high, low)
            start += low.shape[0]


def rows_of(pair):
    return SYM if pair[0] == pair[1] else HALF if pair[1] == 3 else RANK


def width_of(level):
    return RHS if level == 3 else RANK


def needed(groups):
    pairs = sorted(pair for group in groups for pair in group)
    rights = sorted({right for _, right in pairs})
    blocks = {}
    for right in rights:
        blocks.setdefault(tuple(left for left, other in pairs if other == right), []).append(right)
    return list(blocks.items()), sorted({left for left, _ in pairs}), rights


def products(core, generators, solved_gens, rhs, groups, chunks, *after):
    rows = rhs.shape[0]
    blocks, lefts, rights = needed(groups)
    width = sum(width_of(right) for right in rights)
    height = max(len(firsts) for firsts, _ in blocks) * RANK
    flops = sum(len(firsts) * width_of(right) for firsts, seconds in blocks for right in seconds) * 6 * rows * RANK
    outs = [struct(sum(rows_of(pair) for pair in group)) for group in groups for _ in range(2)]
    held = sum(level < 3 for level in rights)
    scratch = [pltpu.VMEM((height, width), jnp.float32)]
    if chunks > 1:
        scratch = [
            pltpu.VMEM((len(lefts), rows, RANK), jnp.float32),
            pltpu.VMEM((held, rows, RANK), jnp.float32),
            *scratch,
            pltpu.SemaphoreType.DMA((len(lefts) + held, chunks)),
        ]
    given, specs = [generators, solved_gens], [HBM if chunks > 1 else VMEM] * 2
    if 3 in rights:
        given, specs = given + [rhs], specs + [VMEM]
    return pl.pallas_call(
        functools.partial(product_kernel, groups, chunks),
        in_specs=[SMEM] + specs + [ANY] * len(after),
        out_specs=[VMEM] * len(outs),
        out_shape=outs,
        scratch_shapes=scratch,
        compiler_params=pltpu.CompilerParams(vmem_limit_bytes=STREAM_LIMIT if chunks > 1 else VMEM_LIMIT),
        cost_estimate=cost(flops, rows * (len(lefts) * RANK + width)),
    )(core, *given, *after)


def square_norm(value):
    return jnp.sum(value * value)


def identity():
    row = lax.broadcasted_iota(jnp.int32, (RANK, RANK), 0)
    col = lax.broadcasted_iota(jnp.int32, (RANK, RANK), 1)
    return jnp.where(row == col, 1.0, 0.0)


def series(start, values, power_ref, sum_ref):
    norm = square_norm(start)
    if values is None:
        power_ref[...] = dot(start, start)
        sum_ref[...] = identity() + start
    else:
        both = dot(start, jnp.concatenate([start, values], axis=1))
        power_ref[...] = both[:, :RANK]
        sum_ref[...] = values + both[:, RANK:]

    def proceed(state):
        count, bound = state
        return (count < 60) & (bound > TOLERANCE) & (bound < DIVERGED * DIVERGED)

    def body(state):
        count, _ = state
        power = power_ref[...]
        bound = square_norm(power)
        values = sum_ref[...]
        both = dot(power, jnp.concatenate([power, values], axis=1))
        power_ref[...] = both[:, :RANK]
        sum_ref[...] = values + both[:, RANK:]
        return count + 1, bound

    return lax.while_loop(proceed, body, (jnp.int32(0), norm))[1]


def solve_series(product, values, power_ref, sum_ref):
    bound = series(product, values, power_ref, sum_ref)

    @pl.when(jnp.logical_not(bound <= TOLERANCE))
    def _():
        scale = 1.0 / (1.0 + jnp.sqrt(square_norm(product)))
        series((1.0 - scale) * identity() + scale * product, values, power_ref, sum_ref)
        sum_ref[...] = scale * sum_ref[...]


def invert_kernel(core_ref, own_ref, sib_ref, own_other_ref, sib_other_ref, inverse_ref, p_sib_ref, power):
    core = core_ref[0]
    p_own = symmetric(core, own_ref[:SYM, :], own_other_ref[:SYM, :])
    p_sib = symmetric(core, sib_ref[:SYM, :], sib_other_ref[:SYM, :])
    p_sib_ref[...] = p_sib
    solve_series(dot(p_sib, p_own), None, power, inverse_ref)


def call(kernel, out_shape, flops, *values, after=(), scratch=()):
    many = isinstance(out_shape, (list, tuple))
    floats = sum(value.size for value in values) + sum(out.size for out in (out_shape if many else [out_shape]))
    return pl.pallas_call(
        kernel,
        in_specs=[SMEM] + [VMEM] * (len(values) - 1) + [ANY] * len(after),
        out_specs=[VMEM] * len(out_shape) if many else VMEM,
        out_shape=out_shape,
        scratch_shapes=[pltpu.VMEM(shape, jnp.float32) for shape in scratch],
        compiler_params=pltpu.CompilerParams(vmem_limit_bytes=VMEM_LIMIT),
        cost_estimate=cost(flops, floats),
    )(*values, *after)


def inverse(core, own, sib, own_other, sib_other):
    return pl.pallas_call(
        invert_kernel,
        in_specs=[SMEM] + [VMEM] * 4,
        out_specs=[VMEM] * 2,
        out_shape=[struct(RANK, RANK)] * 2,
        scratch_shapes=[pltpu.VMEM((RANK, RANK), jnp.float32)],
        compiler_params=pltpu.CompilerParams(vmem_limit_bytes=VMEM_LIMIT),
        cost_estimate=cost(6 * 9 * RANK**3, 4 * RANK * RANK),
    )(core, own, sib, own_other, sib_other)


def first_kernel(core_ref, inverse_ref, p_sib_ref, head_ref, head_sib_ref, head_other_ref, tail_ref, tail_sib_ref, z_ref, out_ref):
    core = core_ref[0]
    own = jnp.concatenate([head_ref[SYM:, :], unpack(tail_ref)], axis=1)
    sib = jnp.concatenate([head_sib_ref[SYM:, :], unpack(tail_sib_ref)], axis=1)
    z = dot(inverse_ref[...], sib - dot(p_sib_ref[...], own))
    store(z_ref, z)
    value = dot_turned(in_order(core, head_ref[SYM:, :], head_other_ref[SYM:, :]), z)
    out_ref[:SYM, :] = symmetric_half(core, value[:, :HALF])
    store(out_ref.at[SYM:], value[:, HALF:])


def last_parts(core, crossed, z, out_ref):
    value = dot_turned(crossed, z)
    out_ref[:SYM, :] = symmetric_half(core, value[:, :HALF])
    store(out_ref.at[SYM:], value[:, HALF:])


def third_kernel(core_ref, own_ref, own_other_ref, z_ref, *refs):
    core = core_ref[0]
    last_parts(core, in_order(core, own_ref[:RANK, :], own_other_ref[...]), unpack(z_ref.at[RANK:]), refs[-1])


def middle_kernel(core_ref, inverse_ref, p_sib_ref, own_ref, sib_ref, own_other_ref, z_ref, out_ref):
    core = core_ref[0]
    z = dot(inverse_ref[...], unpack(sib_ref) - dot(p_sib_ref[...], unpack(own_ref)))
    store(z_ref, z)
    last_parts(core, in_order(core, own_ref[:RANK, :], own_other_ref[...]), z, out_ref)


def rhs_in_order(core, own, other):
    first = core == 0
    low = jnp.where(first, own, other)
    high = jnp.where(first, other, own)
    top = jnp.concatenate([low[:, :QUARTER], high[:, :QUARTER]], axis=1)
    bottom = jnp.concatenate([low[:, QUARTER:], high[:, QUARTER:]], axis=1)
    return jnp.concatenate([top, bottom], axis=0)


def reduced_kernel(
    core_ref, z1_ref, z1_other_ref, z0_ref, z0_other_ref, solved_ref, rhs_ref, high_ref, low_ref, out_ref
):
    core = core_ref[0]
    z12 = in_order(core, z1_ref[:RANK, :], z1_other_ref[:RANK, :])
    z1x = rhs_in_order(core, z1_ref[RANK:, :], z1_other_ref[RANK:, :])
    z01 = in_order(core, z0_ref[:RANK, :], z0_other_ref[:RANK, :])
    z02 = in_order(core, z0_ref[RANK : 2 * RANK, :], z0_other_ref[RANK : 2 * RANK, :])
    z0x = rhs_in_order(core, z0_ref[2 * RANK :, :], z0_other_ref[2 * RANK :, :])
    middle = jnp.concatenate([z12, z1x], axis=1)
    first = jnp.concatenate([z02, z0x], axis=1) - dot(z01, middle)
    coefs = jnp.concatenate([first, middle], axis=0)
    value = dot(jnp.concatenate([solved_ref[0], solved_ref[1]], axis=1), coefs)
    high, low = split(solved_ref[2] - value[:, :RANK])
    high_ref[...] = high
    low_ref[...] = low
    out_ref[...] = rhs_ref[...] - value[:, RANK:]


def keep_kernel(core_ref, value_ref, *refs):
    refs[-1][...] = value_ref[...]


def add_kernel(core_ref, first_ref, second_ref, *refs):
    refs[-1][...] = first_ref[...] + second_ref[...]


def subtract_kernel(core_ref, first_ref, second_ref, *refs):
    refs[-1][...] = first_ref[...] - second_ref[...]


def final_kernel(
    core_ref, own_ref, own_other_ref, sib_ref, sib_other_ref, high_ref, low_ref, rhs_ref, out_ref, power, total
):
    core = core_ref[0]
    p_own = symmetric(core, own_ref[:SYM, :], own_other_ref[:SYM, :])
    p_sib = symmetric(core, sib_ref[:SYM, :], sib_other_ref[:SYM, :])
    own = rhs_in_order(core, own_ref[SYM:, :], own_other_ref[SYM:, :])
    sib = rhs_in_order(core, sib_ref[SYM:, :], sib_other_ref[SYM:, :])
    both = dot(p_sib, jnp.concatenate([p_own, own], axis=1))
    solve_series(both[:, :RANK], sib - both[:, RANK:], power, total)
    out_ref[...] = rhs_ref[...] - dot_parts((high_ref[...], low_ref[...]), split(total[...]))


def on_device(rhs, generators, solved_gens):
    groups = lax.axis_size("rows")
    sub_bits = lax.axis_size("sub").bit_length() - 1
    span_bits = (groups // 8).bit_length() - 1
    core = (lax.axis_index("sub") % 2).astype(jnp.int32).reshape(1)
    flops = 6 * RANK * RANK * HALF
    last = SYM + HALF

    def over_child(value):
        for bit in range(1, sub_bits):
            value = value + swap(value, "sub", bit)
        for bit in range(span_bits):
            value = value + swap(value, "rows", bit)
        return value

    keep, send = products(core, generators, solved_gens, rhs, (((0, 0), (0, 1)),), 4)
    head = keep + swap(send, "sub", 0)
    token = swap(call(keep_kernel, struct(8), 0, core, send[:8], after=(head,)), "sub", 0)
    groups = (((0, 2), (0, 3)), ((1, 1), (1, 2), (1, 3)), ((2, 2), (2, 3)))
    parts = products(core, generators, solved_gens, rhs, groups, 1, token)
    parts = [(keep, swap(send, "sub", 0)) for keep, send in zip(parts[::2], parts[1::2])]
    head = over_child(head)
    tail = over_child(parts[0][0] + parts[0][1])
    near = call(add_kernel, struct(SYM + RANK + HALF), 0, core, *parts[1], after=(tail,))
    near = over_child(near)
    third = over_child(call(add_kernel, struct(last), 0, core, *parts[2], after=(near,)))

    head_sib = swap(head, "rows", span_bits)
    tail_sib = swap(tail, "rows", span_bits)
    head_other = swap(head, "sub", 0)
    tail_other = swap(tail[:RANK], "sub", 0)
    p_sib_other = swap(head_sib[:SYM], "sub", 0)
    inverted, p_sib = inverse(core, head, head_sib, head_other, p_sib_other)
    z0, crossed = call(
        first_kernel, [struct(2 * RANK + HALF), struct(SYM + RANK + HALF)], FIRST_FLOPS,
        core, inverted, p_sib, head, head_sib, head_other, tail, tail_sib,
    )
    p_own = call(subtract_kernel, struct(SYM), 0, core, near[:SYM], crossed[:SYM])
    r_own = call(subtract_kernel, struct(RANK + HALF), 0, core, near[SYM:], crossed[SYM:], after=(p_own,))
    third = third - call(third_kernel, struct(last), THIRD_FLOPS, core, tail, tail_other, z0, after=(r_own,))

    p_own = p_own + swap(p_own, "rows", span_bits)
    r_own = r_own + swap(r_own, "rows", span_bits)
    third = third + swap(third, "rows", span_bits)
    p_sib = swap(p_own, "rows", span_bits + 1)
    r_sib = swap(r_own, "rows", span_bits + 1)
    p_own_other = swap(p_own, "sub", 0)
    r_own_other = swap(r_own[:RANK], "sub", 0)
    p_sib_other = swap(p_sib, "sub", 0)
    inverted, p_sib = inverse(core, p_own, p_sib, p_own_other, p_sib_other)
    z1, crossed = call(
        middle_kernel, [struct(RANK + HALF), struct(last)], 5 * flops,
        core, inverted, p_sib, r_own, r_sib, r_own_other,
    )

    own = third - crossed
    own = own + swap(own, "rows", span_bits + 1)
    sib = swap(own, "rows", span_bits + 2)
    z1_other = swap(call(keep_kernel, struct(RANK + HALF), 0, core, z1, after=(own,)), "sub", 0)
    part = jax.ShapeDtypeStruct((rhs.shape[0], RANK), jnp.bfloat16)
    high, low, current = call(
        reduced_kernel, [part, part, struct(rhs.shape[0], RHS)], 6 * rhs.shape[0] * 2 * RANK * (RANK + RHS),
        core, z1, z1_other, z0, swap(z0, "sub", 0), solved_gens, rhs,
    )
    sib = call(keep_kernel, struct(last), 0, core, sib, after=(high,))
    own_other, sib_other = swap(own, "sub", 0), swap(sib, "sub", 0)
    return call(
        final_kernel, struct(rhs.shape[0], RHS), 6 * rhs.shape[0] * RANK * RHS + 6 * 9 * RANK**3,
        core, own, own_other, sib, sib_other, high, low, current, scratch=((RANK, RANK), (RANK, RHS)),
    )


def solution(mesh):
    placed = (
        P(("rows", "sub"), None),
        P(None, ("rows", "sub"), None),
        P(None, ("rows", "sub"), None),
    )
    return jax.shard_map(
        on_device, mesh=mesh, in_specs=placed, out_specs=P(("rows", "sub"), None), check_vma=False
    )
```

```python
import functools

import jax
import jax.numpy as jnp
from jax import lax
from jax.experimental import pallas as pl
from jax.experimental.pallas import tpu as pltpu
from jax.sharding import PartitionSpec as P

RANK = 256
RHS = 128
HALF = RANK // 2
QUARTER = HALF // 2
SYM = HALF + QUARTER
TOLERANCE = 1e-7
DIVERGED = 1e4
FIRST_FLOPS = 6.5e8
INVERT_FLOPS = 9e8
THIRD_FLOPS = 3e9
VMEM_LIMIT = 40 * 2**20
STREAM_LIMIT = 52 * 2**20

SMEM = pl.BlockSpec(memory_space=pltpu.SMEM)
VMEM = pl.BlockSpec(memory_space=pltpu.VMEM)
HBM = pl.BlockSpec(memory_space=pltpu.HBM)
ANY = pl.BlockSpec(memory_space=pl.ANY)


def swap(value, axis, bit):
    mask = 2**bit
    pairs = [(source, source ^ mask) for source in range(lax.axis_size(axis))]
    return lax.ppermute(value, axis, pairs)


def struct(rows, cols=HALF):
    return jax.ShapeDtypeStruct((rows, cols), jnp.float32)


def cost(flops, floats):
    return pl.CostEstimate(flops=int(flops), bytes_accessed=int(4 * floats), transcendentals=0)


def split(value):
    high = value.astype(jnp.bfloat16)
    low = (value - high.astype(jnp.float32)).astype(jnp.bfloat16)
    return high, low


def dot_parts(left, right):
    first = jnp.concatenate([left[0], left[0], left[1]], axis=1)
    second = jnp.concatenate([right[0], right[1], right[0]], axis=0)
    return lax.dot_general(first, second, (((1,), (0,)), ((), ())), preferred_element_type=jnp.float32)


def dot(left, right):
    return dot_parts(split(left), split(right))


def dot_turned(left, right):
    return dot_parts([part.T for part in split(left)], split(right))


def in_order(core, own, other):
    first = core == 0
    return jnp.concatenate([jnp.where(first, own, other), jnp.where(first, other, own)], axis=1)


def symmetric(core, own, other):
    first = core == 0
    low = jnp.where(first, own, other)
    high = jnp.where(first, other, own)
    upper = jnp.concatenate([low[HALF:], high[HALF:]], axis=0)
    return jnp.concatenate(
        [jnp.concatenate([low[:HALF], upper], axis=1), jnp.concatenate([upper.T, high[:HALF]], axis=1)], axis=0
    )


def symmetric_half(core, value):
    first = core == 0
    return jnp.concatenate(
        [
            jnp.where(first, value[:HALF], value[HALF:]),
            jnp.where(first, value[HALF:].T[:QUARTER], value[QUARTER:HALF]),
        ],
        axis=0,
    )


def pack(value):
    whole = value.shape[1] // HALF
    units = [value[:, index * HALF : (index + 1) * HALF] for index in range(whole)]
    if value.shape[1] % HALF:
        tail = value[:, whole * HALF :]
        units.append(jnp.concatenate([tail[:HALF], tail[HALF:]], axis=1))
    return units


def unpack(ref):
    whole = ref.shape[0] // RANK
    parts = [ref[index * RANK : (index + 1) * RANK, :] for index in range(whole)]
    if ref.shape[0] % RANK:
        tail = ref[whole * RANK :, :]
        parts.append(jnp.concatenate([tail[:, :QUARTER], tail[:, QUARTER:]], axis=0))
    return jnp.concatenate(parts, axis=1) if len(parts) > 1 else parts[0]


def store(ref, value):
    start = 0
    for unit in pack(value):
        ref[start : start + unit.shape[0], :] = unit
        start += unit.shape[0]


def product_kernel(groups, chunks, core_ref, gens_ref, solved_ref, *refs):
    gens, solved, total, sems = refs[-4:] if chunks > 1 else (None, None, refs[-1], None)
    refs = refs[:-4] if chunks > 1 else refs[:-1]
    outs = refs[-2 * len(groups) :]
    blocks, lefts, rights = needed(groups)
    rhs_ref = refs[0] if 3 in rights else None
    block = gens_ref.shape[1] // chunks
    copies = []
    for chunk in range(chunks if chunks > 1 else 0):
        rows = pl.ds(chunk * block, block)
        row = [(gens_ref.at[level, rows], gens.at[place, rows]) for place, level in enumerate(lefts)]
        row += [(solved_ref.at[level, rows], solved.at[place, rows]) for place, level in enumerate(rights) if level < 3]
        row = [pltpu.make_async_copy(*ends, sems.at[index, chunk]) for index, ends in enumerate(row)]
        for copy in row:
            copy.start()
        copies.append(row)
    places = {}
    for chunk in range(chunks):
        rows = pl.ds(chunk * block, block)
        for copy in copies[chunk] if chunks > 1 else ():
            copy.wait()
        right = {}
        for place, level in enumerate(rights):
            if level == 3:
                right[level] = split(rhs_ref[rows, :])
            else:
                right[level] = split(solved[place, rows, :] if chunks > 1 else solved_ref[level])
        left = []
        for place, level in enumerate(lefts):
            left.append([part.T for part in split(gens[place, rows, :] if chunks > 1 else gens_ref[level])])
        start = 0
        for firsts, seconds in blocks:
            value = dot_parts(
                [jnp.concatenate([left[lefts.index(level)][half] for level in firsts], axis=0) for half in (0, 1)],
                [jnp.concatenate([right[level][half] for level in seconds], axis=1) for half in (0, 1)],
            )
            cols = slice(start, start + value.shape[1])
            if chunk == 0:
                total[: value.shape[0], cols] = value
            else:
                total[: value.shape[0], cols] += value
            for level in seconds:
                for place, first in enumerate(firsts):
                    places[first, level] = (place * RANK, start)
                start += width_of(level)
    first = core_ref[0] == 0
    for index, group in enumerate(groups):
        keep_ref, send_ref = outs[2 * index : 2 * index + 2]
        start = 0
        for pair in group:
            row, at = places[pair]
            value = total[row : row + RANK, at : at + width_of(pair[1])]
            if pair[0] == pair[1]:
                low = jnp.concatenate([value[:HALF, :HALF], value[:QUARTER, HALF:]], axis=0)
                high = jnp.concatenate([value[HALF:, HALF:], value[QUARTER:HALF, HALF:]], axis=0)
            elif pair[1] < 3:
                low = value[:, :HALF]
                high = value[:, HALF:]
            else:
                low = jnp.concatenate([value[:HALF, :QUARTER], value[HALF:, :QUARTER]], axis=1)
                high = jnp.concatenate([value[:HALF, QUARTER:], value[HALF:, QUARTER:]], axis=1)
            rows = slice(start, start + low.shape[0])
            keep_ref[rows, :] = jnp.where(first, low, high)
            send_ref[rows, :] = jnp.where(first, high, low)
            start += low.shape[0]


def rows_of(pair):
    return SYM if pair[0] == pair[1] else HALF if pair[1] == 3 else RANK


def width_of(level):
    return RHS if level == 3 else RANK


def needed(groups):
    pairs = sorted(pair for group in groups for pair in group)
    rights = sorted({right for _, right in pairs})
    blocks = {}
    for right in rights:
        blocks.setdefault(tuple(left for left, other in pairs if other == right), []).append(right)
    return list(blocks.items()), sorted({left for left, _ in pairs}), rights


def products(core, generators, solved_gens, rhs, groups, chunks, *after):
    rows = rhs.shape[0]
    blocks, lefts, rights = needed(groups)
    width = sum(width_of(right) for right in rights)
    height = max(len(firsts) for firsts, _ in blocks) * RANK
    flops = sum(len(firsts) * width_of(right) for firsts, seconds in blocks for right in seconds) * 6 * rows * RANK
    outs = [struct(sum(rows_of(pair) for pair in group)) for group in groups for _ in range(2)]
    held = sum(level < 3 for level in rights)
    scratch = [pltpu.VMEM((height, width), jnp.float32)]
    if chunks > 1:
        scratch = [
            pltpu.VMEM((len(lefts), rows, RANK), jnp.float32),
            pltpu.VMEM((held, rows, RANK), jnp.float32),
            *scratch,
            pltpu.SemaphoreType.DMA((len(lefts) + held, chunks)),
        ]
    given, specs = [generators, solved_gens], [HBM if chunks > 1 else VMEM] * 2
    if 3 in rights:
        given, specs = given + [rhs], specs + [VMEM]
    return pl.pallas_call(
        functools.partial(product_kernel, groups, chunks),
        in_specs=[SMEM] + specs + [ANY] * len(after),
        out_specs=[VMEM] * len(outs),
        out_shape=outs,
        scratch_shapes=scratch,
        compiler_params=pltpu.CompilerParams(vmem_limit_bytes=STREAM_LIMIT if chunks > 1 else VMEM_LIMIT),
        cost_estimate=cost(flops, rows * (len(lefts) * RANK + width)),
    )(core, *given, *after)


def square_norm(value):
    return jnp.sum(value * value)


def identity():
    row = lax.broadcasted_iota(jnp.int32, (RANK, RANK), 0)
    col = lax.broadcasted_iota(jnp.int32, (RANK, RANK), 1)
    return jnp.where(row == col, 1.0, 0.0)


def series(start, values, power_ref, sum_ref):
    norm = square_norm(start)
    if values is None:
        power_ref[...] = dot(start, start)
        sum_ref[...] = identity() + start
    else:
        both = dot(start, jnp.concatenate([start, values], axis=1))
        power_ref[...] = both[:, :RANK]
        sum_ref[...] = values + both[:, RANK:]

    def proceed(state):
        count, bound = state
        return (count < 60) & (bound > TOLERANCE) & (bound < DIVERGED * DIVERGED)

    def body(state):
        count, _ = state
        power = power_ref[...]
        bound = square_norm(power)
        values = sum_ref[...]
        both = dot(power, jnp.concatenate([power, values], axis=1))
        power_ref[...] = both[:, :RANK]
        sum_ref[...] = values + both[:, RANK:]
        return count + 1, bound

    return lax.while_loop(proceed, body, (jnp.int32(0), norm))[1]


def solve_series(product, values, power_ref, sum_ref):
    bound = series(product, values, power_ref, sum_ref)

    @pl.when(jnp.logical_not(bound <= TOLERANCE))
    def _():
        scale = 1.0 / (1.0 + jnp.sqrt(square_norm(product)))
        series((1.0 - scale) * identity() + scale * product, values, power_ref, sum_ref)
        sum_ref[...] = scale * sum_ref[...]


def invert_kernel(core_ref, own_ref, sib_ref, own_other_ref, sib_other_ref, inverse_ref, p_sib_ref, power):
    core = core_ref[0]
    p_own = symmetric(core, own_ref[:SYM, :], own_other_ref[:SYM, :])
    p_sib = symmetric(core, sib_ref[:SYM, :], sib_other_ref[:SYM, :])
    p_sib_ref[...] = p_sib
    solve_series(dot(p_sib, p_own), None, power, inverse_ref)


def call(kernel, out_shape, flops, *values, after=(), scratch=()):
    many = isinstance(out_shape, (list, tuple))
    floats = sum(value.size for value in values) + sum(out.size for out in (out_shape if many else [out_shape]))
    return pl.pallas_call(
        kernel,
        in_specs=[SMEM] + [VMEM] * (len(values) - 1) + [ANY] * len(after),
        out_specs=[VMEM] * len(out_shape) if many else VMEM,
        out_shape=out_shape,
        scratch_shapes=[pltpu.VMEM(shape, jnp.float32) for shape in scratch],
        compiler_params=pltpu.CompilerParams(vmem_limit_bytes=VMEM_LIMIT),
        cost_estimate=cost(flops, floats),
    )(*values, *after)


def inverse(core, own, sib, own_other, sib_other):
    return pl.pallas_call(
        invert_kernel,
        in_specs=[SMEM] + [VMEM] * 4,
        out_specs=[VMEM] * 2,
        out_shape=[struct(RANK, RANK)] * 2,
        scratch_shapes=[pltpu.VMEM((RANK, RANK), jnp.float32)],
        compiler_params=pltpu.CompilerParams(vmem_limit_bytes=VMEM_LIMIT),
        cost_estimate=cost(INVERT_FLOPS, 0),
    )(core, own, sib, own_other, sib_other)


def first_kernel(core_ref, inverse_ref, p_sib_ref, head_ref, head_sib_ref, head_other_ref, tail_ref, tail_sib_ref, z_ref, out_ref):
    core = core_ref[0]
    own = jnp.concatenate([head_ref[SYM:, :], unpack(tail_ref)], axis=1)
    sib = jnp.concatenate([head_sib_ref[SYM:, :], unpack(tail_sib_ref)], axis=1)
    z = dot(inverse_ref[...], sib - dot(p_sib_ref[...], own))
    store(z_ref, z)
    value = dot_turned(in_order(core, head_ref[SYM:, :], head_other_ref[SYM:, :]), z)
    out_ref[:SYM, :] = symmetric_half(core, value[:, :HALF])
    store(out_ref.at[SYM:], value[:, HALF:])


def last_parts(core, crossed, z):
    value = dot_turned(crossed, z)
    return jnp.concatenate([symmetric_half(core, value[:, :HALF]), *pack(value[:, HALF:])], axis=0)


def third_kernel(share, core_ref, own_ref, own_other_ref, z_ref, third_ref, *refs):
    core = core_ref[0]
    crossed = in_order(core, own_ref[:RANK, :], own_other_ref[...])
    refs[-1][...] = third_ref[...] - share * last_parts(core, crossed, unpack(z_ref.at[RANK:]))


def middle_kernel(
    core_ref, inverse_ref, p_sib_ref, own_ref, sib_ref, own_other_ref, p_own_ref, p_own_other_ref, z_ref, z_sib_ref, out_ref,
    crossed_ref,
):
    core = core_ref[0]
    crossed_ref[...] = sib_ref[:RANK, :]
    own = unpack(own_ref)
    z = dot(inverse_ref[...], unpack(sib_ref) - dot(p_sib_ref[...], own))
    store(z_ref, z)
    store(z_sib_ref, own - dot(symmetric(core, p_own_ref[...], p_own_other_ref[...]), z))
    out_ref[...] = last_parts(core, in_order(core, own_ref[:RANK, :], own_other_ref[...]), z)


def cross_kernel(core_ref, sib_ref, sib_other_ref, z_sib_ref, crossed_ref, out_ref):
    core = core_ref[0]
    crossed = in_order(core, sib_ref[...], sib_other_ref[...])
    out_ref[...] = crossed_ref[...] + last_parts(core, crossed, unpack(z_sib_ref))


def rhs_in_order(core, own, other):
    first = core == 0
    low = jnp.where(first, own, other)
    high = jnp.where(first, other, own)
    top = jnp.concatenate([low[:, :QUARTER], high[:, :QUARTER]], axis=1)
    bottom = jnp.concatenate([low[:, QUARTER:], high[:, QUARTER:]], axis=1)
    return jnp.concatenate([top, bottom], axis=0)


def reduced_kernel(
    core_ref, z1_ref, z1_other_ref, z0_ref, z0_other_ref, solved_ref, rhs_ref, high_ref, low_ref, out_ref
):
    core = core_ref[0]
    z12 = in_order(core, z1_ref[:RANK, :], z1_other_ref[:RANK, :])
    z1x = rhs_in_order(core, z1_ref[RANK:, :], z1_other_ref[RANK:, :])
    z01 = in_order(core, z0_ref[:RANK, :], z0_other_ref[:RANK, :])
    z02 = in_order(core, z0_ref[RANK : 2 * RANK, :], z0_other_ref[RANK : 2 * RANK, :])
    z0x = rhs_in_order(core, z0_ref[2 * RANK :, :], z0_other_ref[2 * RANK :, :])
    middle = jnp.concatenate([z12, z1x], axis=1)
    first = jnp.concatenate([z02, z0x], axis=1) - dot(z01, middle)
    coefs = jnp.concatenate([first, middle], axis=0)
    value = dot(jnp.concatenate([solved_ref[0], solved_ref[1]], axis=1), coefs)
    high, low = split(solved_ref[2] - value[:, :RANK])
    high_ref[...] = high
    low_ref[...] = low
    out_ref[...] = rhs_ref[...] - value[:, RANK:]


def keep_kernel(core_ref, value_ref, *refs):
    refs[-1][...] = value_ref[...]


def add_kernel(core_ref, first_ref, second_ref, *refs):
    refs[-1][...] = first_ref[...] + second_ref[...]


def subtract_kernel(core_ref, first_ref, second_ref, *refs):
    refs[-1][...] = first_ref[...] - second_ref[...]


def final_kernel(
    core_ref, own_ref, own_other_ref, sib_ref, sib_other_ref, high_ref, low_ref, rhs_ref, out_ref, power, total
):
    core = core_ref[0]
    p_own = symmetric(core, own_ref[:SYM, :], own_other_ref[:SYM, :])
    p_sib = symmetric(core, sib_ref[:SYM, :], sib_other_ref[:SYM, :])
    own = rhs_in_order(core, own_ref[SYM:, :], own_other_ref[SYM:, :])
    sib = rhs_in_order(core, sib_ref[SYM:, :], sib_other_ref[SYM:, :])
    both = dot(p_sib, jnp.concatenate([p_own, own], axis=1))
    solve_series(both[:, :RANK], sib - both[:, RANK:], power, total)
    out_ref[...] = rhs_ref[...] - dot_parts((high_ref[...], low_ref[...]), split(total[...]))


def on_device(rhs, generators, solved_gens):
    groups = lax.axis_size("rows")
    sub_bits = lax.axis_size("sub").bit_length() - 1
    span_bits = (groups // 8).bit_length() - 1
    core = (lax.axis_index("sub") % 2).astype(jnp.int32).reshape(1)
    flops = 6 * RANK * RANK * HALF
    last = SYM + HALF

    def over_child(value):
        for bit in range(1, sub_bits):
            value = value + swap(value, "sub", bit)
        for bit in range(span_bits):
            value = value + swap(value, "rows", bit)
        return value

    keep, send = products(core, generators, solved_gens, rhs, (((0, 0), (0, 1)),), 4)
    head = keep + swap(send, "sub", 0)
    token = swap(call(keep_kernel, struct(8), 0, core, send[:8], after=(head,)), "sub", 0)
    rest = (((0, 2), (0, 3)), ((1, 1), (1, 2), (1, 3)), ((2, 2), (2, 3)))
    parts = products(core, generators, solved_gens, rhs, rest, 1, token)
    parts = [(keep, swap(send, "sub", 0)) for keep, send in zip(parts[::2], parts[1::2])]
    head = over_child(head)
    tail = over_child(parts[0][0] + parts[0][1])
    near = over_child(call(add_kernel, struct(SYM + RANK + HALF), 0, core, *parts[1], after=(tail,)))
    third = parts[2][0] + parts[2][1]

    head_sib = swap(head, "rows", span_bits)
    tail_sib = swap(tail, "rows", span_bits)
    head_other = swap(head, "sub", 0)
    tail_other = swap(tail[:RANK], "sub", 0)
    p_sib_other = swap(head_sib[:SYM], "sub", 0)
    inverted, p_sib = inverse(core, head, head_sib, head_other, p_sib_other)
    z0, crossed = call(
        first_kernel, [struct(2 * RANK + HALF), struct(SYM + RANK + HALF)], FIRST_FLOPS,
        core, inverted, p_sib, head, head_sib, head_other, tail, tail_sib,
    )
    p_own = call(subtract_kernel, struct(SYM), 0, core, near[:SYM], crossed[:SYM])
    r_own = call(subtract_kernel, struct(RANK + HALF), 0, core, near[SYM:], crossed[SYM:], after=(p_own,))
    share = 1.0 / (lax.axis_size("sub") // 2 * (groups // 8))
    third = call(
        functools.partial(third_kernel, share), struct(last), THIRD_FLOPS,
        core, tail, tail_other, z0, third, after=(r_own,),
    )
    third = third + swap(third, "rows", span_bits + 1)
    third = over_child(third)
    third = third + swap(third, "rows", span_bits)

    p_own = p_own + swap(p_own, "rows", span_bits)
    r_own = r_own + swap(r_own, "rows", span_bits)
    p_sib = swap(p_own, "rows", span_bits + 1)
    r_sib = swap(r_own, "rows", span_bits + 1)
    p_own_other = swap(p_own, "sub", 0)
    r_own_other = swap(r_own[:RANK], "sub", 0)
    p_sib_other = swap(p_sib, "sub", 0)
    inverted, p_sib = inverse(core, p_own, p_sib, p_own_other, p_sib_other)
    z1, z_sib, crossed, r_sib = call(
        middle_kernel, [struct(RANK + HALF), struct(RANK + HALF), struct(last), struct(RANK)], 6 * flops,
        core, inverted, p_sib, r_own, r_sib, r_own_other, p_own, p_own_other,
    )
    crossed = call(cross_kernel, struct(last), 2 * flops, core, r_sib, swap(r_sib, "sub", 0), z_sib, crossed)

    own = third - crossed
    sib = swap(own, "rows", span_bits + 2)
    z1_other = swap(call(keep_kernel, struct(RANK + HALF), 0, core, z1, after=(own,)), "sub", 0)
    part = jax.ShapeDtypeStruct((rhs.shape[0], RANK), jnp.bfloat16)
    high, low, current = call(
        reduced_kernel, [part, part, struct(rhs.shape[0], RHS)], 6 * rhs.shape[0] * 2 * RANK * (RANK + RHS),
        core, z1, z1_other, z0, swap(z0, "sub", 0), solved_gens, rhs,
    )
    sib = call(keep_kernel, struct(last), 0, core, sib, after=(high,))
    own_other, sib_other = swap(own, "sub", 0), swap(sib, "sub", 0)
    return call(
        final_kernel, struct(rhs.shape[0], RHS), 6 * rhs.shape[0] * RANK * RHS + 6 * 9 * RANK**3,
        core, own, own_other, sib, sib_other, high, low, current, scratch=((RANK, RANK), (RANK, RHS)),
    )


def solution(mesh):
    placed = (
        P(("rows", "sub"), None),
        P(None, ("rows", "sub"), None),
        P(None, ("rows", "sub"), None),
    )
    return jax.shard_map(
        on_device, mesh=mesh, in_specs=placed, out_specs=P(("rows", "sub"), None), check_vma=False
    )
```

```python
import functools

import jax
import jax.numpy as jnp
from jax import lax
from jax.experimental import pallas as pl
from jax.experimental.pallas import tpu as pltpu
from jax.sharding import PartitionSpec as P

RANK = 256
RHS = 128
HALF = RANK // 2
QUARTER = HALF // 2
SYM = HALF + QUARTER
TOLERANCE = 1e-7
DIVERGED = 1e4
FIRST_FLOPS = 6.5e8
INVERT_FLOPS = 9e8
INVERT_SECOND = 9e8
MIDDLE_FLOPS = 0
CROSS_FLOPS = 0
THIRD_FLOPS = 1e9
VMEM_LIMIT = 40 * 2**20
STREAM_LIMIT = 52 * 2**20

SMEM = pl.BlockSpec(memory_space=pltpu.SMEM)
VMEM = pl.BlockSpec(memory_space=pltpu.VMEM)
HBM = pl.BlockSpec(memory_space=pltpu.HBM)
ANY = pl.BlockSpec(memory_space=pl.ANY)


def swap(value, axis, bit):
    mask = 2**bit
    pairs = [(source, source ^ mask) for source in range(lax.axis_size(axis))]
    return lax.ppermute(value, axis, pairs)


def struct(rows, cols=HALF):
    return jax.ShapeDtypeStruct((rows, cols), jnp.float32)


def cost(flops, floats):
    return pl.CostEstimate(flops=int(flops), bytes_accessed=int(4 * floats), transcendentals=0)


def split(value):
    high = value.astype(jnp.bfloat16)
    low = (value - high.astype(jnp.float32)).astype(jnp.bfloat16)
    return high, low


def dot_parts(left, right):
    first = jnp.concatenate([left[0], left[0], left[1]], axis=1)
    second = jnp.concatenate([right[0], right[1], right[0]], axis=0)
    return lax.dot_general(first, second, (((1,), (0,)), ((), ())), preferred_element_type=jnp.float32)


def dot(left, right):
    return dot_parts(split(left), split(right))


def dot_turned(left, right):
    return dot_parts([part.T for part in split(left)], split(right))


def in_order(core, own, other):
    first = core == 0
    return jnp.concatenate([jnp.where(first, own, other), jnp.where(first, other, own)], axis=1)


def symmetric(core, own, other):
    first = core == 0
    low = jnp.where(first, own, other)
    high = jnp.where(first, other, own)
    upper = jnp.concatenate([low[HALF:], high[HALF:]], axis=0)
    return jnp.concatenate(
        [jnp.concatenate([low[:HALF], upper], axis=1), jnp.concatenate([upper.T, high[:HALF]], axis=1)], axis=0
    )


def symmetric_half(core, value):
    first = core == 0
    return jnp.concatenate(
        [
            jnp.where(first, value[:HALF], value[HALF:]),
            jnp.where(first, value[HALF:].T[:QUARTER], value[QUARTER:HALF]),
        ],
        axis=0,
    )


def pack(value):
    whole = value.shape[1] // HALF
    units = [value[:, index * HALF : (index + 1) * HALF] for index in range(whole)]
    if value.shape[1] % HALF:
        tail = value[:, whole * HALF :]
        units.append(jnp.concatenate([tail[:HALF], tail[HALF:]], axis=1))
    return units


def unpack(ref):
    whole = ref.shape[0] // RANK
    parts = [ref[index * RANK : (index + 1) * RANK, :] for index in range(whole)]
    if ref.shape[0] % RANK:
        tail = ref[whole * RANK :, :]
        parts.append(jnp.concatenate([tail[:, :QUARTER], tail[:, QUARTER:]], axis=0))
    return jnp.concatenate(parts, axis=1) if len(parts) > 1 else parts[0]


def store(ref, value):
    start = 0
    for unit in pack(value):
        ref[start : start + unit.shape[0], :] = unit
        start += unit.shape[0]


def product_kernel(groups, chunks, core_ref, gens_ref, solved_ref, *refs):
    gens, solved, total, sems = refs[-4:] if chunks > 1 else (None, None, refs[-1], None)
    refs = refs[:-4] if chunks > 1 else refs[:-1]
    outs = refs[-2 * len(groups) :]
    blocks, lefts, rights = needed(groups)
    rhs_ref = refs[0] if 3 in rights else None
    block = gens_ref.shape[1] // chunks
    copies = []
    for chunk in range(chunks if chunks > 1 else 0):
        rows = pl.ds(chunk * block, block)
        row = [(gens_ref.at[level, rows], gens.at[place, rows]) for place, level in enumerate(lefts)]
        row += [(solved_ref.at[level, rows], solved.at[place, rows]) for place, level in enumerate(rights) if level < 3]
        row = [pltpu.make_async_copy(*ends, sems.at[index, chunk]) for index, ends in enumerate(row)]
        for copy in row:
            copy.start()
        copies.append(row)
    places = {}
    for chunk in range(chunks):
        rows = pl.ds(chunk * block, block)
        for copy in copies[chunk] if chunks > 1 else ():
            copy.wait()
        right = {}
        for place, level in enumerate(rights):
            if level == 3:
                right[level] = split(rhs_ref[rows, :])
            else:
                right[level] = split(solved[place, rows, :] if chunks > 1 else solved_ref[level])
        left = []
        for place, level in enumerate(lefts):
            left.append([part.T for part in split(gens[place, rows, :] if chunks > 1 else gens_ref[level])])
        start = 0
        for firsts, seconds in blocks:
            value = dot_parts(
                [jnp.concatenate([left[lefts.index(level)][half] for level in firsts], axis=0) for half in (0, 1)],
                [jnp.concatenate([right[level][half] for level in seconds], axis=1) for half in (0, 1)],
            )
            cols = slice(start, start + value.shape[1])
            if chunk == 0:
                total[: value.shape[0], cols] = value
            else:
                total[: value.shape[0], cols] += value
            for level in seconds:
                for place, first in enumerate(firsts):
                    places[first, level] = (place * RANK, start)
                start += width_of(level)
    first = core_ref[0] == 0
    for index, group in enumerate(groups):
        keep_ref, send_ref = outs[2 * index : 2 * index + 2]
        start = 0
        for pair in group:
            row, at = places[pair]
            value = total[row : row + RANK, at : at + width_of(pair[1])]
            if pair[0] == pair[1]:
                low = jnp.concatenate([value[:HALF, :HALF], value[:QUARTER, HALF:]], axis=0)
                high = jnp.concatenate([value[HALF:, HALF:], value[QUARTER:HALF, HALF:]], axis=0)
            elif pair[1] < 3:
                low = value[:, :HALF]
                high = value[:, HALF:]
            else:
                low = jnp.concatenate([value[:HALF, :QUARTER], value[HALF:, :QUARTER]], axis=1)
                high = jnp.concatenate([value[:HALF, QUARTER:], value[HALF:, QUARTER:]], axis=1)
            rows = slice(start, start + low.shape[0])
            keep_ref[rows, :] = jnp.where(first, low, high)
            send_ref[rows, :] = jnp.where(first, high, low)
            start += low.shape[0]


def rows_of(pair):
    return SYM if pair[0] == pair[1] else HALF if pair[1] == 3 else RANK


def width_of(level):
    return RHS if level == 3 else RANK


def needed(groups):
    pairs = sorted(pair for group in groups for pair in group)
    rights = sorted({right for _, right in pairs})
    blocks = {}
    for right in rights:
        blocks.setdefault(tuple(left for left, other in pairs if other == right), []).append(right)
    return list(blocks.items()), sorted({left for left, _ in pairs}), rights


def products(core, generators, solved_gens, rhs, groups, chunks, *after):
    rows = rhs.shape[0]
    blocks, lefts, rights = needed(groups)
    width = sum(width_of(right) for right in rights)
    height = max(len(firsts) for firsts, _ in blocks) * RANK
    flops = sum(len(firsts) * width_of(right) for firsts, seconds in blocks for right in seconds) * 6 * rows * RANK
    outs = [struct(sum(rows_of(pair) for pair in group)) for group in groups for _ in range(2)]
    held = sum(level < 3 for level in rights)
    scratch = [pltpu.VMEM((height, width), jnp.float32)]
    if chunks > 1:
        scratch = [
            pltpu.VMEM((len(lefts), rows, RANK), jnp.float32),
            pltpu.VMEM((held, rows, RANK), jnp.float32),
            *scratch,
            pltpu.SemaphoreType.DMA((len(lefts) + held, chunks)),
        ]
    given, specs = [generators, solved_gens], [HBM if chunks > 1 else VMEM] * 2
    if 3 in rights:
        given, specs = given + [rhs], specs + [VMEM]
    return pl.pallas_call(
        functools.partial(product_kernel, groups, chunks),
        in_specs=[SMEM] + specs + [ANY] * len(after),
        out_specs=[VMEM] * len(outs),
        out_shape=outs,
        scratch_shapes=scratch,
        compiler_params=pltpu.CompilerParams(vmem_limit_bytes=STREAM_LIMIT if chunks > 1 else VMEM_LIMIT),
        cost_estimate=cost(flops, rows * (len(lefts) * RANK + width)),
    )(core, *given, *after)


def square_norm(value):
    return jnp.sum(value * value)


def identity():
    row = lax.broadcasted_iota(jnp.int32, (RANK, RANK), 0)
    col = lax.broadcasted_iota(jnp.int32, (RANK, RANK), 1)
    return jnp.where(row == col, 1.0, 0.0)


def series(start, values, power_ref, sum_ref):
    norm = square_norm(start)
    if values is None:
        power_ref[...] = dot(start, start)
        sum_ref[...] = identity() + start
    else:
        both = dot(start, jnp.concatenate([start, values], axis=1))
        power_ref[...] = both[:, :RANK]
        sum_ref[...] = values + both[:, RANK:]

    def proceed(state):
        count, bound = state
        return (count < 60) & (bound > TOLERANCE) & (bound < DIVERGED * DIVERGED)

    def body(state):
        count, _ = state
        power = power_ref[...]
        bound = square_norm(power)
        values = sum_ref[...]
        both = dot(power, jnp.concatenate([power, values], axis=1))
        power_ref[...] = both[:, :RANK]
        sum_ref[...] = values + both[:, RANK:]
        return count + 1, bound

    return lax.while_loop(proceed, body, (jnp.int32(0), norm))[1]


def solve_series(product, values, power_ref, sum_ref):
    bound = series(product, values, power_ref, sum_ref)

    @pl.when(jnp.logical_not(bound <= TOLERANCE))
    def _():
        scale = 1.0 / (1.0 + jnp.sqrt(square_norm(product)))
        series((1.0 - scale) * identity() + scale * product, values, power_ref, sum_ref)
        sum_ref[...] = scale * sum_ref[...]


def invert_kernel(core_ref, own_ref, sib_ref, own_other_ref, sib_other_ref, inverse_ref, p_sib_ref, power):
    core = core_ref[0]
    p_own = symmetric(core, own_ref[:SYM, :], own_other_ref[:SYM, :])
    p_sib = symmetric(core, sib_ref[:SYM, :], sib_other_ref[:SYM, :])
    p_sib_ref[...] = p_sib
    solve_series(dot(p_sib, p_own), None, power, inverse_ref)


def call(kernel, out_shape, flops, *values, after=(), scratch=()):
    many = isinstance(out_shape, (list, tuple))
    floats = sum(value.size for value in values) + sum(out.size for out in (out_shape if many else [out_shape]))
    return pl.pallas_call(
        kernel,
        in_specs=[SMEM] + [VMEM] * (len(values) - 1) + [ANY] * len(after),
        out_specs=[VMEM] * len(out_shape) if many else VMEM,
        out_shape=out_shape,
        scratch_shapes=[pltpu.VMEM(shape, jnp.float32) for shape in scratch],
        compiler_params=pltpu.CompilerParams(vmem_limit_bytes=VMEM_LIMIT),
        cost_estimate=cost(flops, floats),
    )(*values, *after)


def inverse(flops, core, own, sib, own_other, sib_other):
    return pl.pallas_call(
        invert_kernel,
        in_specs=[SMEM] + [VMEM] * 4,
        out_specs=[VMEM] * 2,
        out_shape=[struct(RANK, RANK)] * 2,
        scratch_shapes=[pltpu.VMEM((RANK, RANK), jnp.float32)],
        compiler_params=pltpu.CompilerParams(vmem_limit_bytes=VMEM_LIMIT),
        cost_estimate=cost(flops, 0),
    )(core, own, sib, own_other, sib_other)


def first_kernel(core_ref, inverse_ref, p_sib_ref, head_ref, head_sib_ref, head_other_ref, tail_ref, tail_sib_ref, z_ref, out_ref):
    core = core_ref[0]
    own = jnp.concatenate([head_ref[SYM:, :], unpack(tail_ref)], axis=1)
    sib = jnp.concatenate([head_sib_ref[SYM:, :], unpack(tail_sib_ref)], axis=1)
    z = dot(inverse_ref[...], sib - dot(p_sib_ref[...], own))
    store(z_ref, z)
    value = dot_turned(in_order(core, head_ref[SYM:, :], head_other_ref[SYM:, :]), z)
    out_ref[:SYM, :] = symmetric_half(core, value[:, :HALF])
    store(out_ref.at[SYM:], value[:, HALF:])


def last_parts(core, crossed, z):
    value = dot_turned(crossed, z)
    return jnp.concatenate([symmetric_half(core, value[:, :HALF]), *pack(value[:, HALF:])], axis=0)


def third_kernel(core_ref, own_ref, own_other_ref, z_ref, *refs):
    core = core_ref[0]
    crossed = in_order(core, own_ref[:RANK, :], own_other_ref[...])
    refs[-1][...] = last_parts(core, crossed, unpack(z_ref.at[RANK:]))


def middle_kernel(
    core_ref, inverse_ref, p_sib_ref, own_ref, sib_ref, own_other_ref, p_own_ref, p_own_other_ref, z_ref, z_sib_ref, out_ref,
    crossed_ref,
):
    core = core_ref[0]
    crossed_ref[...] = sib_ref[:RANK, :]
    own = unpack(own_ref)
    z = dot(inverse_ref[...], unpack(sib_ref) - dot(p_sib_ref[...], own))
    store(z_ref, z)
    store(z_sib_ref, own - dot(symmetric(core, p_own_ref[...], p_own_other_ref[...]), z))
    out_ref[...] = last_parts(core, in_order(core, own_ref[:RANK, :], own_other_ref[...]), z)


def cross_kernel(core_ref, sib_ref, sib_other_ref, z_sib_ref, crossed_ref, out_ref):
    core = core_ref[0]
    crossed = in_order(core, sib_ref[...], sib_other_ref[...])
    out_ref[...] = crossed_ref[...] + last_parts(core, crossed, unpack(z_sib_ref))


def rhs_in_order(core, own, other):
    first = core == 0
    low = jnp.where(first, own, other)
    high = jnp.where(first, other, own)
    top = jnp.concatenate([low[:, :QUARTER], high[:, :QUARTER]], axis=1)
    bottom = jnp.concatenate([low[:, QUARTER:], high[:, QUARTER:]], axis=1)
    return jnp.concatenate([top, bottom], axis=0)


def reduced_kernel(
    core_ref, z1_ref, z1_other_ref, z0_ref, z0_other_ref, solved_ref, rhs_ref, high_ref, low_ref, out_ref
):
    core = core_ref[0]
    z12 = in_order(core, z1_ref[:RANK, :], z1_other_ref[:RANK, :])
    z1x = rhs_in_order(core, z1_ref[RANK:, :], z1_other_ref[RANK:, :])
    z01 = in_order(core, z0_ref[:RANK, :], z0_other_ref[:RANK, :])
    z02 = in_order(core, z0_ref[RANK : 2 * RANK, :], z0_other_ref[RANK : 2 * RANK, :])
    z0x = rhs_in_order(core, z0_ref[2 * RANK :, :], z0_other_ref[2 * RANK :, :])
    middle = jnp.concatenate([z12, z1x], axis=1)
    first = jnp.concatenate([z02, z0x], axis=1) - dot(z01, middle)
    coefs = jnp.concatenate([first, middle], axis=0)
    value = dot(jnp.concatenate([solved_ref[0], solved_ref[1]], axis=1), coefs)
    high, low = split(solved_ref[2] - value[:, :RANK])
    high_ref[...] = high
    low_ref[...] = low
    out_ref[...] = rhs_ref[...] - value[:, RANK:]


def keep_kernel(core_ref, value_ref, *refs):
    refs[-1][...] = value_ref[...]


def add_kernel(core_ref, first_ref, second_ref, *refs):
    refs[-1][...] = first_ref[...] + second_ref[...]


def subtract_kernel(core_ref, first_ref, second_ref, *refs):
    refs[-1][...] = first_ref[...] - second_ref[...]


def final_kernel(
    core_ref, own_ref, own_other_ref, sib_ref, sib_other_ref, high_ref, low_ref, rhs_ref, out_ref, power, total
):
    core = core_ref[0]
    p_own = symmetric(core, own_ref[:SYM, :], own_other_ref[:SYM, :])
    p_sib = symmetric(core, sib_ref[:SYM, :], sib_other_ref[:SYM, :])
    own = rhs_in_order(core, own_ref[SYM:, :], own_other_ref[SYM:, :])
    sib = rhs_in_order(core, sib_ref[SYM:, :], sib_other_ref[SYM:, :])
    both = dot(p_sib, jnp.concatenate([p_own, own], axis=1))
    solve_series(both[:, :RANK], sib - both[:, RANK:], power, total)
    out_ref[...] = rhs_ref[...] - dot_parts((high_ref[...], low_ref[...]), split(total[...]))


def on_device(rhs, generators, solved_gens):
    groups = lax.axis_size("rows")
    sub_bits = lax.axis_size("sub").bit_length() - 1
    span_bits = (groups // 8).bit_length() - 1
    core = (lax.axis_index("sub") % 2).astype(jnp.int32).reshape(1)
    flops = 6 * RANK * RANK * HALF
    last = SYM + HALF

    def over_child(value):
        for bit in range(1, sub_bits):
            value = value + swap(value, "sub", bit)
        for bit in range(span_bits):
            value = value + swap(value, "rows", bit)
        return value

    keep, send = products(core, generators, solved_gens, rhs, (((0, 0), (0, 1)),), 4)
    head = keep + swap(send, "sub", 0)
    token = swap(call(keep_kernel, struct(8), 0, core, send[:8], after=(head,)), "sub", 0)
    rest = (((0, 2), (0, 3)), ((1, 1), (1, 2), (1, 3)), ((2, 2), (2, 3)))
    parts = products(core, generators, solved_gens, rhs, rest, 1, token)
    parts = [(keep, swap(send, "sub", 0)) for keep, send in zip(parts[::2], parts[1::2])]
    head = over_child(head)
    tail = over_child(parts[0][0] + parts[0][1])
    near = over_child(call(add_kernel, struct(SYM + RANK + HALF), 0, core, *parts[1], after=(tail,)))
    third = parts[2][0] + parts[2][1]
    third = over_child(
        call(add_kernel, struct(last), 0, core, third, swap(third, "rows", span_bits + 1), after=(near,))
    )

    head_sib = swap(head, "rows", span_bits)
    tail_sib = swap(tail, "rows", span_bits)
    head_other = swap(head, "sub", 0)
    tail_other = swap(tail[:RANK], "sub", 0)
    p_sib_other = swap(head_sib[:SYM], "sub", 0)
    inverted, p_sib = inverse(INVERT_FLOPS, core, head, head_sib, head_other, p_sib_other)
    z0, crossed = call(
        first_kernel, [struct(2 * RANK + HALF), struct(SYM + RANK + HALF)], FIRST_FLOPS,
        core, inverted, p_sib, head, head_sib, head_other, tail, tail_sib,
    )
    p_own = call(subtract_kernel, struct(SYM), 0, core, near[:SYM], crossed[:SYM])
    r_own = call(subtract_kernel, struct(RANK + HALF), 0, core, near[SYM:], crossed[SYM:], after=(p_own,))
    crossed = call(third_kernel, struct(last), THIRD_FLOPS, core, tail, tail_other, z0, after=(r_own,))
    third = third - (crossed + swap(crossed, "rows", span_bits + 1))
    third = third + swap(third, "rows", span_bits)

    p_own = p_own + swap(p_own, "rows", span_bits)
    r_own = r_own + swap(r_own, "rows", span_bits)
    p_sib = swap(p_own, "rows", span_bits + 1)
    r_sib = swap(r_own, "rows", span_bits + 1)
    p_own_other = swap(p_own, "sub", 0)
    r_own_other = swap(r_own[:RANK], "sub", 0)
    p_sib_other = swap(p_sib, "sub", 0)
    inverted, p_sib = inverse(INVERT_SECOND, core, p_own, p_sib, p_own_other, p_sib_other)
    z1, z_sib, crossed, r_sib = call(
        middle_kernel, [struct(RANK + HALF), struct(RANK + HALF), struct(last), struct(RANK)], MIDDLE_FLOPS,
        core, inverted, p_sib, r_own, r_sib, r_own_other, p_own, p_own_other,
    )
    crossed = call(cross_kernel, struct(last), CROSS_FLOPS, core, r_sib, swap(r_sib, "sub", 0), z_sib, crossed)

    own = third - crossed
    sib = swap(own, "rows", span_bits + 2)
    z1_other = swap(call(keep_kernel, struct(RANK + HALF), 0, core, z1, after=(own,)), "sub", 0)
    part = jax.ShapeDtypeStruct((rhs.shape[0], RANK), jnp.bfloat16)
    high, low, current = call(
        reduced_kernel, [part, part, struct(rhs.shape[0], RHS)], 6 * rhs.shape[0] * 2 * RANK * (RANK + RHS),
        core, z1, z1_other, z0, swap(z0, "sub", 0), solved_gens, rhs,
    )
    sib = call(keep_kernel, struct(last), 0, core, sib, after=(high,))
    own_other, sib_other = swap(own, "sub", 0), swap(sib, "sub", 0)
    return call(
        final_kernel, struct(rhs.shape[0], RHS), 6 * rhs.shape[0] * RANK * RHS + 6 * 9 * RANK**3,
        core, own, own_other, sib, sib_other, high, low, current, scratch=((RANK, RANK), (RANK, RHS)),
    )


def solution(mesh):
    placed = (
        P(("rows", "sub"), None),
        P(None, ("rows", "sub"), None),
        P(None, ("rows", "sub"), None),
    )
    return jax.shard_map(
        on_device, mesh=mesh, in_specs=placed, out_specs=P(("rows", "sub"), None), check_vma=False
    )
```

```python
import functools

import jax
import jax.numpy as jnp
from jax import lax
from jax.experimental import pallas as pl
from jax.experimental.pallas import tpu as pltpu
from jax.sharding import PartitionSpec as P

RANK = 256
RHS = 128
HALF = RANK // 2
QUARTER = HALF // 2
SYM = HALF + QUARTER
TOLERANCE = 1e-7
DIVERGED = 1e4
FIRST_FLOPS = 6.5e8
INVERT_FLOPS = 9e8
INVERT_SECOND = 9e8
MIDDLE_FLOPS = 0
CROSS_FLOPS = 0
THIRD_FLOPS = 1e9
VMEM_LIMIT = 40 * 2**20
STREAM_LIMIT = 52 * 2**20

SMEM = pl.BlockSpec(memory_space=pltpu.SMEM)
VMEM = pl.BlockSpec(memory_space=pltpu.VMEM)
HBM = pl.BlockSpec(memory_space=pltpu.HBM)
ANY = pl.BlockSpec(memory_space=pl.ANY)


def swap(value, axis, bit):
    mask = 2**bit
    pairs = [(source, source ^ mask) for source in range(lax.axis_size(axis))]
    return lax.ppermute(value, axis, pairs)


def struct(rows, cols=HALF):
    return jax.ShapeDtypeStruct((rows, cols), jnp.float32)


def cost(flops, floats):
    return pl.CostEstimate(flops=int(flops), bytes_accessed=int(4 * floats), transcendentals=0)


def split(value):
    high = value.astype(jnp.bfloat16)
    low = (value - high.astype(jnp.float32)).astype(jnp.bfloat16)
    return high, low


def dot_parts(left, right):
    first = jnp.concatenate([left[0], left[0], left[1]], axis=1)
    second = jnp.concatenate([right[0], right[1], right[0]], axis=0)
    return lax.dot_general(first, second, (((1,), (0,)), ((), ())), preferred_element_type=jnp.float32)


def dot(left, right):
    return dot_parts(split(left), split(right))


def dot_turned(left, right):
    return dot_parts([part.T for part in split(left)], split(right))


def in_order(core, own, other):
    first = core == 0
    return jnp.concatenate([jnp.where(first, own, other), jnp.where(first, other, own)], axis=1)


def symmetric(core, own, other):
    first = core == 0
    low = jnp.where(first, own, other)
    high = jnp.where(first, other, own)
    upper = jnp.concatenate([low[HALF:], high[HALF:]], axis=0)
    return jnp.concatenate(
        [jnp.concatenate([low[:HALF], upper], axis=1), jnp.concatenate([upper.T, high[:HALF]], axis=1)], axis=0
    )


def symmetric_half(core, value):
    first = core == 0
    return jnp.concatenate(
        [
            jnp.where(first, value[:HALF], value[HALF:]),
            jnp.where(first, value[HALF:].T[:QUARTER], value[QUARTER:HALF]),
        ],
        axis=0,
    )


def pack(value):
    whole = value.shape[1] // HALF
    units = [value[:, index * HALF : (index + 1) * HALF] for index in range(whole)]
    if value.shape[1] % HALF:
        tail = value[:, whole * HALF :]
        units.append(jnp.concatenate([tail[:HALF], tail[HALF:]], axis=1))
    return units


def unpack(ref):
    whole = ref.shape[0] // RANK
    parts = [ref[index * RANK : (index + 1) * RANK, :] for index in range(whole)]
    if ref.shape[0] % RANK:
        tail = ref[whole * RANK :, :]
        parts.append(jnp.concatenate([tail[:, :QUARTER], tail[:, QUARTER:]], axis=0))
    return jnp.concatenate(parts, axis=1) if len(parts) > 1 else parts[0]


def store(ref, value):
    start = 0
    for unit in pack(value):
        ref[start : start + unit.shape[0], :] = unit
        start += unit.shape[0]


def product_kernel(groups, chunks, core_ref, gens_ref, solved_ref, *refs):
    gens, solved, total, sems = refs[-4:] if chunks > 1 else (None, None, refs[-1], None)
    refs = refs[:-4] if chunks > 1 else refs[:-1]
    outs = refs[-2 * len(groups) :]
    blocks, lefts, rights = needed(groups)
    rhs_ref = refs[0] if 3 in rights else None
    block = gens_ref.shape[1] // chunks
    copies = []
    for chunk in range(chunks if chunks > 1 else 0):
        rows = pl.ds(chunk * block, block)
        row = [(gens_ref.at[level, rows], gens.at[place, rows]) for place, level in enumerate(lefts)]
        row += [(solved_ref.at[level, rows], solved.at[place, rows]) for place, level in enumerate(rights) if level < 3]
        row = [pltpu.make_async_copy(*ends, sems.at[index, chunk]) for index, ends in enumerate(row)]
        for copy in row:
            copy.start()
        copies.append(row)
    places = {}
    for chunk in range(chunks):
        rows = pl.ds(chunk * block, block)
        for copy in copies[chunk] if chunks > 1 else ():
            copy.wait()
        right = {}
        for place, level in enumerate(rights):
            if level == 3:
                right[level] = split(rhs_ref[rows, :])
            else:
                right[level] = split(solved[place, rows, :] if chunks > 1 else solved_ref[level])
        left = []
        for place, level in enumerate(lefts):
            left.append([part.T for part in split(gens[place, rows, :] if chunks > 1 else gens_ref[level])])
        start = 0
        for firsts, seconds in blocks:
            value = dot_parts(
                [jnp.concatenate([left[lefts.index(level)][half] for level in firsts], axis=0) for half in (0, 1)],
                [jnp.concatenate([right[level][half] for level in seconds], axis=1) for half in (0, 1)],
            )
            cols = slice(start, start + value.shape[1])
            if chunk == 0:
                total[: value.shape[0], cols] = value
            else:
                total[: value.shape[0], cols] += value
            for level in seconds:
                for place, first in enumerate(firsts):
                    places[first, level] = (place * RANK, start)
                start += width_of(level)
    first = core_ref[0] == 0
    for index, group in enumerate(groups):
        keep_ref, send_ref = outs[2 * index : 2 * index + 2]
        start = 0
        for pair in group:
            row, at = places[pair]
            value = total[row : row + RANK, at : at + width_of(pair[1])]
            if pair[0] == pair[1]:
                low = jnp.concatenate([value[:HALF, :HALF], value[:QUARTER, HALF:]], axis=0)
                high = jnp.concatenate([value[HALF:, HALF:], value[QUARTER:HALF, HALF:]], axis=0)
            elif pair[1] < 3:
                low = value[:, :HALF]
                high = value[:, HALF:]
            else:
                low = jnp.concatenate([value[:HALF, :QUARTER], value[HALF:, :QUARTER]], axis=1)
                high = jnp.concatenate([value[:HALF, QUARTER:], value[HALF:, QUARTER:]], axis=1)
            rows = slice(start, start + low.shape[0])
            keep_ref[rows, :] = jnp.where(first, low, high)
            send_ref[rows, :] = jnp.where(first, high, low)
            start += low.shape[0]


def rows_of(pair):
    return SYM if pair[0] == pair[1] else HALF if pair[1] == 3 else RANK


def width_of(level):
    return RHS if level == 3 else RANK


def needed(groups):
    pairs = sorted(pair for group in groups for pair in group)
    rights = sorted({right for _, right in pairs})
    blocks = {}
    for right in rights:
        blocks.setdefault(tuple(left for left, other in pairs if other == right), []).append(right)
    return list(blocks.items()), sorted({left for left, _ in pairs}), rights


def products(core, generators, solved_gens, rhs, groups, chunks, *after):
    rows = rhs.shape[0]
    blocks, lefts, rights = needed(groups)
    width = sum(width_of(right) for right in rights)
    height = max(len(firsts) for firsts, _ in blocks) * RANK
    flops = sum(len(firsts) * width_of(right) for firsts, seconds in blocks for right in seconds) * 6 * rows * RANK
    outs = [struct(sum(rows_of(pair) for pair in group)) for group in groups for _ in range(2)]
    held = sum(level < 3 for level in rights)
    scratch = [pltpu.VMEM((height, width), jnp.float32)]
    if chunks > 1:
        scratch = [
            pltpu.VMEM((len(lefts), rows, RANK), jnp.float32),
            pltpu.VMEM((held, rows, RANK), jnp.float32),
            *scratch,
            pltpu.SemaphoreType.DMA((len(lefts) + held, chunks)),
        ]
    given, specs = [generators, solved_gens], [HBM if chunks > 1 else VMEM] * 2
    if 3 in rights:
        given, specs = given + [rhs], specs + [VMEM]
    return pl.pallas_call(
        functools.partial(product_kernel, groups, chunks),
        in_specs=[SMEM] + specs + [ANY] * len(after),
        out_specs=[VMEM] * len(outs),
        out_shape=outs,
        scratch_shapes=scratch,
        compiler_params=pltpu.CompilerParams(vmem_limit_bytes=STREAM_LIMIT if chunks > 1 else VMEM_LIMIT),
        cost_estimate=cost(flops, rows * (len(lefts) * RANK + width)),
    )(core, *given, *after)


def square_norm(value):
    return jnp.sum(value * value)


def identity():
    row = lax.broadcasted_iota(jnp.int32, (RANK, RANK), 0)
    col = lax.broadcasted_iota(jnp.int32, (RANK, RANK), 1)
    return jnp.where(row == col, 1.0, 0.0)


def series(start, values, power_ref, sum_ref):
    norm = square_norm(start)
    if values is None:
        power_ref[...] = dot(start, start)
        sum_ref[...] = identity() + start
    else:
        both = dot(start, jnp.concatenate([start, values], axis=1))
        power_ref[...] = both[:, :RANK]
        sum_ref[...] = values + both[:, RANK:]

    def proceed(state):
        count, bound = state
        return (count < 60) & (bound > TOLERANCE) & (bound < DIVERGED * DIVERGED)

    def body(state):
        count, _ = state
        power = power_ref[...]
        bound = square_norm(power)
        values = sum_ref[...]
        both = dot(power, jnp.concatenate([power, values], axis=1))
        power_ref[...] = both[:, :RANK]
        sum_ref[...] = values + both[:, RANK:]
        return count + 1, bound

    return lax.while_loop(proceed, body, (jnp.int32(0), norm))[1]


def solve_series(product, values, power_ref, sum_ref):
    bound = series(product, values, power_ref, sum_ref)

    @pl.when(jnp.logical_not(bound <= TOLERANCE))
    def _():
        scale = 1.0 / (1.0 + jnp.sqrt(square_norm(product)))
        series((1.0 - scale) * identity() + scale * product, values, power_ref, sum_ref)
        sum_ref[...] = scale * sum_ref[...]


def invert_kernel(core_ref, own_ref, sib_ref, own_other_ref, sib_other_ref, inverse_ref, p_sib_ref, power):
    core = core_ref[0]
    p_own = symmetric(core, own_ref[:SYM, :], own_other_ref[:SYM, :])
    p_sib = symmetric(core, sib_ref[:SYM, :], sib_other_ref[:SYM, :])
    p_sib_ref[...] = p_sib
    solve_series(dot(p_sib, p_own), None, power, inverse_ref)


def call(kernel, out_shape, flops, *values, after=(), scratch=()):
    many = isinstance(out_shape, (list, tuple))
    floats = sum(value.size for value in values) + sum(out.size for out in (out_shape if many else [out_shape]))
    return pl.pallas_call(
        kernel,
        in_specs=[SMEM] + [VMEM] * (len(values) - 1) + [ANY] * len(after),
        out_specs=[VMEM] * len(out_shape) if many else VMEM,
        out_shape=out_shape,
        scratch_shapes=[pltpu.VMEM(shape, jnp.float32) for shape in scratch],
        compiler_params=pltpu.CompilerParams(vmem_limit_bytes=VMEM_LIMIT),
        cost_estimate=cost(flops, floats),
    )(*values, *after)


def inverse(flops, core, own, sib, own_other, sib_other):
    return pl.pallas_call(
        invert_kernel,
        in_specs=[SMEM] + [VMEM] * 4,
        out_specs=[VMEM] * 2,
        out_shape=[struct(RANK, RANK)] * 2,
        scratch_shapes=[pltpu.VMEM((RANK, RANK), jnp.float32)],
        compiler_params=pltpu.CompilerParams(vmem_limit_bytes=VMEM_LIMIT),
        cost_estimate=cost(flops, 0),
    )(core, own, sib, own_other, sib_other)


def first_kernel(core_ref, inverse_ref, p_sib_ref, head_ref, head_sib_ref, head_other_ref, tail_ref, tail_sib_ref, z_ref, out_ref):
    core = core_ref[0]
    own = jnp.concatenate([head_ref[SYM:, :], unpack(tail_ref)], axis=1)
    sib = jnp.concatenate([head_sib_ref[SYM:, :], unpack(tail_sib_ref)], axis=1)
    z = dot(inverse_ref[...], sib - dot(p_sib_ref[...], own))
    store(z_ref, z)
    value = dot_turned(in_order(core, head_ref[SYM:, :], head_other_ref[SYM:, :]), z)
    out_ref[:SYM, :] = symmetric_half(core, value[:, :HALF])
    store(out_ref.at[SYM:], value[:, HALF:])


def last_parts(core, crossed, z):
    value = dot_turned(crossed, z)
    return jnp.concatenate([symmetric_half(core, value[:, :HALF]), *pack(value[:, HALF:])], axis=0)


def third_kernel(core_ref, own_ref, own_other_ref, z_ref, *refs):
    core = core_ref[0]
    crossed = in_order(core, own_ref[:RANK, :], own_other_ref[...])
    refs[-1][...] = last_parts(core, crossed, unpack(z_ref.at[RANK:]))


def middle_kernel(
    core_ref, inverse_ref, p_sib_ref, own_ref, sib_ref, own_other_ref, p_own_ref, p_own_other_ref, z_ref, z_sib_ref, out_ref,
    crossed_ref,
):
    core = core_ref[0]
    crossed_ref[...] = sib_ref[:RANK, :]
    own = unpack(own_ref)
    z = dot(inverse_ref[...], unpack(sib_ref) - dot(p_sib_ref[...], own))
    store(z_ref, z)
    store(z_sib_ref, own - dot(symmetric(core, p_own_ref[...], p_own_other_ref[...]), z))
    out_ref[...] = last_parts(core, in_order(core, own_ref[:RANK, :], own_other_ref[...]), z)


def cross_kernel(core_ref, sib_ref, sib_other_ref, z_sib_ref, crossed_ref, out_ref):
    core = core_ref[0]
    crossed = in_order(core, sib_ref[...], sib_other_ref[...])
    out_ref[...] = crossed_ref[...] + last_parts(core, crossed, unpack(z_sib_ref))


def rhs_in_order(core, own, other):
    first = core == 0
    low = jnp.where(first, own, other)
    high = jnp.where(first, other, own)
    top = jnp.concatenate([low[:, :QUARTER], high[:, :QUARTER]], axis=1)
    bottom = jnp.concatenate([low[:, QUARTER:], high[:, QUARTER:]], axis=1)
    return jnp.concatenate([top, bottom], axis=0)


def reduced_kernel(
    core_ref, z1_ref, z1_other_ref, z0_ref, z0_other_ref, solved_ref, rhs_ref, high_ref, low_ref, out_ref
):
    core = core_ref[0]
    z12 = in_order(core, z1_ref[:RANK, :], z1_other_ref[:RANK, :])
    z1x = rhs_in_order(core, z1_ref[RANK:, :], z1_other_ref[RANK:, :])
    z01 = in_order(core, z0_ref[:RANK, :], z0_other_ref[:RANK, :])
    z02 = in_order(core, z0_ref[RANK : 2 * RANK, :], z0_other_ref[RANK : 2 * RANK, :])
    z0x = rhs_in_order(core, z0_ref[2 * RANK :, :], z0_other_ref[2 * RANK :, :])
    middle = jnp.concatenate([z12, z1x], axis=1)
    first = jnp.concatenate([z02, z0x], axis=1) - dot(z01, middle)
    coefs = jnp.concatenate([first, middle], axis=0)
    value = dot(jnp.concatenate([solved_ref[0], solved_ref[1]], axis=1), coefs)
    high, low = split(solved_ref[2] - value[:, :RANK])
    high_ref[...] = high
    low_ref[...] = low
    out_ref[...] = rhs_ref[...] - value[:, RANK:]


def keep_kernel(core_ref, value_ref, *refs):
    refs[-1][...] = value_ref[...]


def add_kernel(core_ref, first_ref, second_ref, *refs):
    refs[-1][...] = first_ref[...] + second_ref[...]


def subtract_kernel(core_ref, first_ref, second_ref, *refs):
    refs[-1][...] = first_ref[...] - second_ref[...]


def final_kernel(
    core_ref, own_ref, own_other_ref, sib_ref, sib_other_ref, high_ref, low_ref, rhs_ref, out_ref, power, total
):
    core = core_ref[0]
    p_own = symmetric(core, own_ref[:SYM, :], own_other_ref[:SYM, :])
    p_sib = symmetric(core, sib_ref[:SYM, :], sib_other_ref[:SYM, :])
    own = rhs_in_order(core, own_ref[SYM:, :], own_other_ref[SYM:, :])
    sib = rhs_in_order(core, sib_ref[SYM:, :], sib_other_ref[SYM:, :])
    both = dot(p_sib, jnp.concatenate([p_own, own], axis=1))
    solve_series(both[:, :RANK], sib - both[:, RANK:], power, total)
    out_ref[...] = rhs_ref[...] - dot_parts((high_ref[...], low_ref[...]), split(total[...]))


def on_device(rhs, generators, solved_gens):
    groups = lax.axis_size("rows")
    sub_bits = lax.axis_size("sub").bit_length() - 1
    span_bits = (groups // 8).bit_length() - 1
    core = (lax.axis_index("sub") % 2).astype(jnp.int32).reshape(1)
    flops = 6 * RANK * RANK * HALF
    last = SYM + HALF

    def over_child(value):
        for bit in range(1, sub_bits):
            value = value + swap(value, "sub", bit)
        for bit in range(span_bits):
            value = value + swap(value, "rows", bit)
        return value

    keep, send = products(core, generators, solved_gens, rhs, (((0, 0), (0, 1)),), 2)
    head = keep + swap(send, "sub", 0)
    token = swap(call(keep_kernel, struct(8), 0, core, send[:8], after=(head,)), "sub", 0)
    parts = products(core, generators, solved_gens, rhs, (((0, 2), (0, 3)),), 1, token)
    rest = (((1, 1), (1, 2), (1, 3)), ((2, 2), (2, 3)))
    parts += products(core, generators, solved_gens, rhs, rest, 1, parts[1])
    parts = [(keep, swap(send, "sub", 0)) for keep, send in zip(parts[::2], parts[1::2])]
    head = over_child(head)
    tail = over_child(parts[0][0] + parts[0][1])
    near = over_child(call(add_kernel, struct(SYM + RANK + HALF), 0, core, *parts[1], after=(tail,)))
    third = parts[2][0] + parts[2][1]

    head_sib = swap(head, "rows", span_bits)
    tail_sib = swap(tail, "rows", span_bits)
    head_other = swap(head, "sub", 0)
    tail_other = swap(tail[:RANK], "sub", 0)
    p_sib_other = swap(head_sib[:SYM], "sub", 0)
    inverted, p_sib = inverse(INVERT_FLOPS, core, head, head_sib, head_other, p_sib_other)
    z0, crossed = call(
        first_kernel, [struct(2 * RANK + HALF), struct(SYM + RANK + HALF)], FIRST_FLOPS,
        core, inverted, p_sib, head, head_sib, head_other, tail, tail_sib,
    )
    p_own = call(subtract_kernel, struct(SYM), 0, core, near[:SYM], crossed[:SYM])
    r_own = call(subtract_kernel, struct(RANK + HALF), 0, core, near[SYM:], crossed[SYM:], after=(p_own,))
    third = over_child(
        call(add_kernel, struct(last), 0, core, third, swap(third, "rows", span_bits + 1), after=(r_own,))
    )
    crossed = call(third_kernel, struct(last), THIRD_FLOPS, core, tail, tail_other, z0, after=(r_own,))
    third = third - (crossed + swap(crossed, "rows", span_bits + 1))
    third = third + swap(third, "rows", span_bits)

    p_own = p_own + swap(p_own, "rows", span_bits)
    r_own = r_own + swap(r_own, "rows", span_bits)
    p_sib = swap(p_own, "rows", span_bits + 1)
    r_sib = swap(r_own, "rows", span_bits + 1)
    p_own_other = swap(p_own, "sub", 0)
    r_own_other = swap(r_own[:RANK], "sub", 0)
    p_sib_other = swap(p_sib, "sub", 0)
    inverted, p_sib = inverse(INVERT_SECOND, core, p_own, p_sib, p_own_other, p_sib_other)
    z1, z_sib, crossed, r_sib = call(
        middle_kernel, [struct(RANK + HALF), struct(RANK + HALF), struct(last), struct(RANK)], MIDDLE_FLOPS,
        core, inverted, p_sib, r_own, r_sib, r_own_other, p_own, p_own_other,
    )
    crossed = call(cross_kernel, struct(last), CROSS_FLOPS, core, r_sib, swap(r_sib, "sub", 0), z_sib, crossed)

    own = third - crossed
    sib = swap(own, "rows", span_bits + 2)
    z1_other = swap(call(keep_kernel, struct(RANK + HALF), 0, core, z1, after=(own,)), "sub", 0)
    part = jax.ShapeDtypeStruct((rhs.shape[0], RANK), jnp.bfloat16)
    high, low, current = call(
        reduced_kernel, [part, part, struct(rhs.shape[0], RHS)], 6 * rhs.shape[0] * 2 * RANK * (RANK + RHS),
        core, z1, z1_other, z0, swap(z0, "sub", 0), solved_gens, rhs,
    )
    sib = call(keep_kernel, struct(last), 0, core, sib, after=(high,))
    own_other, sib_other = swap(own, "sub", 0), swap(sib, "sub", 0)
    return call(
        final_kernel, struct(rhs.shape[0], RHS), 6 * rhs.shape[0] * RANK * RHS + 6 * 9 * RANK**3,
        core, own, own_other, sib, sib_other, high, low, current, scratch=((RANK, RANK), (RANK, RHS)),
    )


def solution(mesh):
    placed = (
        P(("rows", "sub"), None),
        P(None, ("rows", "sub"), None),
        P(None, ("rows", "sub"), None),
    )
    return jax.shard_map(
        on_device, mesh=mesh, in_specs=placed, out_specs=P(("rows", "sub"), None), check_vma=False
    )
```

```python
import functools

import jax
import jax.numpy as jnp
from jax import lax
from jax.experimental import pallas as pl
from jax.experimental.pallas import tpu as pltpu
from jax.sharding import PartitionSpec as P

RANK = 256
RHS = 128
HALF = RANK // 2
QUARTER = HALF // 2
SYM = HALF + QUARTER
TOLERANCE = 1e-7
DIVERGED = 1e4
FIRST_FLOPS = 6.5e8
INVERT_FLOPS = 9e8
INVERT_SECOND = 9e8
MIDDLE_FLOPS = 0
CROSS_FLOPS = 0
THIRD_FLOPS = 1e9
VMEM_LIMIT = 40 * 2**20
STREAM_LIMIT = 52 * 2**20

SMEM = pl.BlockSpec(memory_space=pltpu.SMEM)
VMEM = pl.BlockSpec(memory_space=pltpu.VMEM)
HBM = pl.BlockSpec(memory_space=pltpu.HBM)
ANY = pl.BlockSpec(memory_space=pl.ANY)


def swap(value, axis, bit):
    mask = 2**bit
    pairs = [(source, source ^ mask) for source in range(lax.axis_size(axis))]
    return lax.ppermute(value, axis, pairs)


def struct(rows, cols=HALF):
    return jax.ShapeDtypeStruct((rows, cols), jnp.float32)


def cost(flops, floats):
    return pl.CostEstimate(flops=int(flops), bytes_accessed=int(4 * floats), transcendentals=0)


def split(value):
    high = value.astype(jnp.bfloat16)
    low = (value - high.astype(jnp.float32)).astype(jnp.bfloat16)
    return high, low


def dot_parts(left, right):
    first = jnp.concatenate([left[0], left[0], left[1]], axis=1)
    second = jnp.concatenate([right[0], right[1], right[0]], axis=0)
    return lax.dot_general(first, second, (((1,), (0,)), ((), ())), preferred_element_type=jnp.float32)


def dot(left, right):
    return dot_parts(split(left), split(right))


def dot_turned(left, right):
    return dot_parts([part.T for part in split(left)], split(right))


def in_order(core, own, other):
    first = core == 0
    return jnp.concatenate([jnp.where(first, own, other), jnp.where(first, other, own)], axis=1)


def symmetric(core, own, other):
    first = core == 0
    low = jnp.where(first, own, other)
    high = jnp.where(first, other, own)
    upper = jnp.concatenate([low[HALF:], high[HALF:]], axis=0)
    return jnp.concatenate(
        [jnp.concatenate([low[:HALF], upper], axis=1), jnp.concatenate([upper.T, high[:HALF]], axis=1)], axis=0
    )


def symmetric_half(core, value):
    first = core == 0
    return jnp.concatenate(
        [
            jnp.where(first, value[:HALF], value[HALF:]),
            jnp.where(first, value[HALF:].T[:QUARTER], value[QUARTER:HALF]),
        ],
        axis=0,
    )


def pack(value):
    whole = value.shape[1] // HALF
    units = [value[:, index * HALF : (index + 1) * HALF] for index in range(whole)]
    if value.shape[1] % HALF:
        tail = value[:, whole * HALF :]
        units.append(jnp.concatenate([tail[:HALF], tail[HALF:]], axis=1))
    return units


def unpack(ref):
    whole = ref.shape[0] // RANK
    parts = [ref[index * RANK : (index + 1) * RANK, :] for index in range(whole)]
    if ref.shape[0] % RANK:
        tail = ref[whole * RANK :, :]
        parts.append(jnp.concatenate([tail[:, :QUARTER], tail[:, QUARTER:]], axis=0))
    return jnp.concatenate(parts, axis=1) if len(parts) > 1 else parts[0]


def store(ref, value):
    start = 0
    for unit in pack(value):
        ref[start : start + unit.shape[0], :] = unit
        start += unit.shape[0]


def product_kernel(groups, chunks, core_ref, gens_ref, solved_ref, *refs):
    gens, solved, total, sems = refs[-4:] if chunks > 1 else (None, None, refs[-1], None)
    refs = refs[:-4] if chunks > 1 else refs[:-1]
    outs = refs[-2 * len(groups) :]
    blocks, lefts, rights = needed(groups)
    rhs_ref = refs[0] if 3 in rights else None
    block = gens_ref.shape[1] // chunks
    copies = []
    for chunk in range(chunks if chunks > 1 else 0):
        rows = pl.ds(chunk * block, block)
        row = [(gens_ref.at[level, rows], gens.at[place, rows]) for place, level in enumerate(lefts)]
        row += [(solved_ref.at[level, rows], solved.at[place, rows]) for place, level in enumerate(rights) if level < 3]
        row = [pltpu.make_async_copy(*ends, sems.at[index, chunk]) for index, ends in enumerate(row)]
        for copy in row:
            copy.start()
        copies.append(row)
    places = {}
    for chunk in range(chunks):
        rows = pl.ds(chunk * block, block)
        for copy in copies[chunk] if chunks > 1 else ():
            copy.wait()
        right = {}
        for place, level in enumerate(rights):
            if level == 3:
                right[level] = split(rhs_ref[rows, :])
            else:
                right[level] = split(solved[place, rows, :] if chunks > 1 else solved_ref[level])
        left = []
        for place, level in enumerate(lefts):
            left.append([part.T for part in split(gens[place, rows, :] if chunks > 1 else gens_ref[level])])
        start = 0
        for firsts, seconds in blocks:
            value = dot_parts(
                [jnp.concatenate([left[lefts.index(level)][half] for level in firsts], axis=0) for half in (0, 1)],
                [jnp.concatenate([right[level][half] for level in seconds], axis=1) for half in (0, 1)],
            )
            cols = slice(start, start + value.shape[1])
            if chunk == 0:
                total[: value.shape[0], cols] = value
            else:
                total[: value.shape[0], cols] += value
            for level in seconds:
                for place, first in enumerate(firsts):
                    places[first, level] = (place * RANK, start)
                start += width_of(level)
    first = core_ref[0] == 0
    for index, group in enumerate(groups):
        keep_ref, send_ref = outs[2 * index : 2 * index + 2]
        start = 0
        for pair in group:
            row, at = places[pair]
            value = total[row : row + RANK, at : at + width_of(pair[1])]
            if pair[0] == pair[1]:
                low = jnp.concatenate([value[:HALF, :HALF], value[:QUARTER, HALF:]], axis=0)
                high = jnp.concatenate([value[HALF:, HALF:], value[QUARTER:HALF, HALF:]], axis=0)
            elif pair[1] < 3:
                low = value[:, :HALF]
                high = value[:, HALF:]
            else:
                low = jnp.concatenate([value[:HALF, :QUARTER], value[HALF:, :QUARTER]], axis=1)
                high = jnp.concatenate([value[:HALF, QUARTER:], value[HALF:, QUARTER:]], axis=1)
            rows = slice(start, start + low.shape[0])
            keep_ref[rows, :] = jnp.where(first, low, high)
            send_ref[rows, :] = jnp.where(first, high, low)
            start += low.shape[0]


def rows_of(pair):
    return SYM if pair[0] == pair[1] else HALF if pair[1] == 3 else RANK


def width_of(level):
    return RHS if level == 3 else RANK


def needed(groups):
    pairs = sorted(pair for group in groups for pair in group)
    rights = sorted({right for _, right in pairs})
    blocks = {}
    for right in rights:
        blocks.setdefault(tuple(left for left, other in pairs if other == right), []).append(right)
    return list(blocks.items()), sorted({left for left, _ in pairs}), rights


def products(core, generators, solved_gens, rhs, groups, chunks, *after):
    rows = rhs.shape[0]
    blocks, lefts, rights = needed(groups)
    width = sum(width_of(right) for right in rights)
    height = max(len(firsts) for firsts, _ in blocks) * RANK
    flops = sum(len(firsts) * width_of(right) for firsts, seconds in blocks for right in seconds) * 6 * rows * RANK
    outs = [struct(sum(rows_of(pair) for pair in group)) for group in groups for _ in range(2)]
    held = sum(level < 3 for level in rights)
    scratch = [pltpu.VMEM((height, width), jnp.float32)]
    if chunks > 1:
        scratch = [
            pltpu.VMEM((len(lefts), rows, RANK), jnp.float32),
            pltpu.VMEM((held, rows, RANK), jnp.float32),
            *scratch,
            pltpu.SemaphoreType.DMA((len(lefts) + held, chunks)),
        ]
    given, specs = [generators, solved_gens], [HBM if chunks > 1 else VMEM] * 2
    if 3 in rights:
        given, specs = given + [rhs], specs + [VMEM]
    return pl.pallas_call(
        functools.partial(product_kernel, groups, chunks),
        in_specs=[SMEM] + specs + [ANY] * len(after),
        out_specs=[VMEM] * len(outs),
        out_shape=outs,
        scratch_shapes=scratch,
        compiler_params=pltpu.CompilerParams(vmem_limit_bytes=STREAM_LIMIT if chunks > 1 else VMEM_LIMIT),
        cost_estimate=cost(flops, rows * (len(lefts) * RANK + width)),
    )(core, *given, *after)


def square_norm(value):
    return jnp.sum(value * value)


def identity():
    row = lax.broadcasted_iota(jnp.int32, (RANK, RANK), 0)
    col = lax.broadcasted_iota(jnp.int32, (RANK, RANK), 1)
    return jnp.where(row == col, 1.0, 0.0)


def doubled(power, values):
    both = dot(power, jnp.concatenate([power, values], axis=1))
    return both[:, :RANK], values + both[:, RANK:]


def series(start, values, power_ref, sum_ref):
    if values is None:
        power, values = dot(start, start), identity() + start
    else:
        power, values = doubled(start, values)
    for _ in range(2):
        power, values = doubled(power, values)
    norm = square_norm(power)
    power_ref[...], sum_ref[...] = doubled(power, values)

    def proceed(state):
        count, bound = state
        return (count < 60) & (bound > TOLERANCE) & (bound < DIVERGED * DIVERGED)

    def body(state):
        count, _ = state
        bound = square_norm(power_ref[...])
        power_ref[...], sum_ref[...] = doubled(power_ref[...], sum_ref[...])
        return count + 1, bound

    return lax.while_loop(proceed, body, (jnp.int32(0), norm))[1]


def solve_series(product, values, power_ref, sum_ref):
    bound = series(product, values, power_ref, sum_ref)

    @pl.when(jnp.logical_not(bound <= TOLERANCE))
    def _():
        scale = 1.0 / (1.0 + jnp.sqrt(square_norm(product)))
        series((1.0 - scale) * identity() + scale * product, values, power_ref, sum_ref)
        sum_ref[...] = scale * sum_ref[...]


def invert_kernel(core_ref, own_ref, sib_ref, own_other_ref, sib_other_ref, inverse_ref, p_sib_ref, power):
    core = core_ref[0]
    p_own = symmetric(core, own_ref[:SYM, :], own_other_ref[:SYM, :])
    p_sib = symmetric(core, sib_ref[:SYM, :], sib_other_ref[:SYM, :])
    p_sib_ref[...] = p_sib
    solve_series(dot(p_sib, p_own), None, power, inverse_ref)


def call(kernel, out_shape, flops, *values, after=(), scratch=()):
    many = isinstance(out_shape, (list, tuple))
    floats = sum(value.size for value in values) + sum(out.size for out in (out_shape if many else [out_shape]))
    return pl.pallas_call(
        kernel,
        in_specs=[SMEM] + [VMEM] * (len(values) - 1) + [ANY] * len(after),
        out_specs=[VMEM] * len(out_shape) if many else VMEM,
        out_shape=out_shape,
        scratch_shapes=[pltpu.VMEM(shape, jnp.float32) for shape in scratch],
        compiler_params=pltpu.CompilerParams(vmem_limit_bytes=VMEM_LIMIT),
        cost_estimate=cost(flops, floats),
    )(*values, *after)


def inverse(flops, core, own, sib, own_other, sib_other):
    return pl.pallas_call(
        invert_kernel,
        in_specs=[SMEM] + [VMEM] * 4,
        out_specs=[VMEM] * 2,
        out_shape=[struct(RANK, RANK)] * 2,
        scratch_shapes=[pltpu.VMEM((RANK, RANK), jnp.float32)],
        compiler_params=pltpu.CompilerParams(vmem_limit_bytes=VMEM_LIMIT),
        cost_estimate=cost(flops, 0),
    )(core, own, sib, own_other, sib_other)


def first_kernel(core_ref, inverse_ref, p_sib_ref, head_ref, head_sib_ref, head_other_ref, tail_ref, tail_sib_ref, z_ref, out_ref):
    core = core_ref[0]
    own = jnp.concatenate([head_ref[SYM:, :], unpack(tail_ref)], axis=1)
    sib = jnp.concatenate([head_sib_ref[SYM:, :], unpack(tail_sib_ref)], axis=1)
    z = dot(inverse_ref[...], sib - dot(p_sib_ref[...], own))
    store(z_ref, z)
    value = dot_turned(in_order(core, head_ref[SYM:, :], head_other_ref[SYM:, :]), z)
    out_ref[:SYM, :] = symmetric_half(core, value[:, :HALF])
    store(out_ref.at[SYM:], value[:, HALF:])


def last_parts(core, crossed, z):
    value = dot_turned(crossed, z)
    return jnp.concatenate([symmetric_half(core, value[:, :HALF]), *pack(value[:, HALF:])], axis=0)


def third_kernel(core_ref, own_ref, own_other_ref, z_ref, *refs):
    core = core_ref[0]
    crossed = in_order(core, own_ref[:RANK, :], own_other_ref[...])
    refs[-1][...] = last_parts(core, crossed, unpack(z_ref.at[RANK:]))


def middle_kernel(
    core_ref, inverse_ref, p_sib_ref, own_ref, sib_ref, own_other_ref, p_own_ref, p_own_other_ref, z_ref, z_sib_ref, out_ref
):
    core = core_ref[0]
    own = unpack(own_ref)
    z = dot(inverse_ref[...], unpack(sib_ref) - dot(p_sib_ref[...], own))
    store(z_ref, z)
    store(z_sib_ref, own - dot(symmetric(core, p_own_ref[...], p_own_other_ref[...]), z))
    out_ref[...] = last_parts(core, in_order(core, own_ref[:RANK, :], own_other_ref[...]), z)


def cross_kernel(core_ref, sib_ref, sib_other_ref, z_sib_ref, crossed_ref, out_ref):
    core = core_ref[0]
    crossed = in_order(core, sib_ref[...], sib_other_ref[...])
    out_ref[...] = crossed_ref[...] + last_parts(core, crossed, unpack(z_sib_ref))


def rhs_in_order(core, own, other):
    first = core == 0
    low = jnp.where(first, own, other)
    high = jnp.where(first, other, own)
    top = jnp.concatenate([low[:, :QUARTER], high[:, :QUARTER]], axis=1)
    bottom = jnp.concatenate([low[:, QUARTER:], high[:, QUARTER:]], axis=1)
    return jnp.concatenate([top, bottom], axis=0)


def reduced_kernel(
    core_ref, z1_ref, z1_other_ref, z0_ref, z0_other_ref, solved_ref, rhs_ref, high_ref, low_ref, out_ref
):
    core = core_ref[0]
    z12 = in_order(core, z1_ref[:RANK, :], z1_other_ref[:RANK, :])
    z1x = rhs_in_order(core, z1_ref[RANK:, :], z1_other_ref[RANK:, :])
    z01 = in_order(core, z0_ref[:RANK, :], z0_other_ref[:RANK, :])
    z02 = in_order(core, z0_ref[RANK : 2 * RANK, :], z0_other_ref[RANK : 2 * RANK, :])
    z0x = rhs_in_order(core, z0_ref[2 * RANK :, :], z0_other_ref[2 * RANK :, :])
    middle = jnp.concatenate([z12, z1x], axis=1)
    first = jnp.concatenate([z02, z0x], axis=1) - dot(z01, middle)
    coefs = jnp.concatenate([first, middle], axis=0)
    value = dot(jnp.concatenate([solved_ref[0], solved_ref[1]], axis=1), coefs)
    high, low = split(solved_ref[2] - value[:, :RANK])
    high_ref[...] = high
    low_ref[...] = low
    out_ref[...] = rhs_ref[...] - value[:, RANK:]


def keep_kernel(core_ref, value_ref, *refs):
    refs[-1][...] = value_ref[...]


def add_kernel(core_ref, first_ref, second_ref, *refs):
    refs[-1][...] = first_ref[...] + second_ref[...]


def subtract_kernel(core_ref, first_ref, second_ref, *refs):
    refs[-1][...] = first_ref[...] - second_ref[...]


def final_kernel(
    core_ref, own_ref, own_other_ref, sib_ref, sib_other_ref, high_ref, low_ref, rhs_ref, out_ref, power, total
):
    core = core_ref[0]
    p_own = symmetric(core, own_ref[:SYM, :], own_other_ref[:SYM, :])
    p_sib = symmetric(core, sib_ref[:SYM, :], sib_other_ref[:SYM, :])
    own = rhs_in_order(core, own_ref[SYM:, :], own_other_ref[SYM:, :])
    sib = rhs_in_order(core, sib_ref[SYM:, :], sib_other_ref[SYM:, :])
    both = dot(p_sib, jnp.concatenate([p_own, own], axis=1))
    solve_series(both[:, :RANK], sib - both[:, RANK:], power, total)
    out_ref[...] = rhs_ref[...] - dot_parts((high_ref[...], low_ref[...]), split(total[...]))


def on_device(rhs, generators, solved_gens):
    groups = lax.axis_size("rows")
    sub_bits = lax.axis_size("sub").bit_length() - 1
    span_bits = (groups // 8).bit_length() - 1
    core = (lax.axis_index("sub") % 2).astype(jnp.int32).reshape(1)
    flops = 6 * RANK * RANK * HALF
    last = SYM + HALF

    def over_child(value):
        for bit in range(1, sub_bits):
            value = value + swap(value, "sub", bit)
        for bit in range(span_bits):
            value = value + swap(value, "rows", bit)
        return value

    keep, send = products(core, generators, solved_gens, rhs, (((0, 0), (0, 1)),), 2)
    head = keep + swap(send, "sub", 0)
    token = swap(call(keep_kernel, struct(8), 0, core, send[:8], after=(head,)), "sub", 0)
    parts = products(core, generators, solved_gens, rhs, (((0, 2), (0, 3)),), 1, token)
    rest = (((1, 1), (1, 2), (1, 3)), ((2, 2), (2, 3)))
    parts += products(core, generators, solved_gens, rhs, rest, 1, parts[1])
    parts = [(keep, swap(send, "sub", 0)) for keep, send in zip(parts[::2], parts[1::2])]
    head = over_child(head)
    tail = over_child(parts[0][0] + parts[0][1])
    near = over_child(call(add_kernel, struct(SYM + RANK + HALF), 0, core, *parts[1], after=(tail,)))
    third = parts[2][0] + parts[2][1]

    head_sib = swap(head, "rows", span_bits)
    tail_sib = swap(tail, "rows", span_bits)
    head_other = swap(head, "sub", 0)
    tail_other = swap(tail[:RANK], "sub", 0)
    p_sib_other = swap(head_sib[:SYM], "sub", 0)
    inverted, p_sib = inverse(INVERT_FLOPS, core, head, head_sib, head_other, p_sib_other)
    z0, crossed = call(
        first_kernel, [struct(2 * RANK + HALF), struct(SYM + RANK + HALF)], FIRST_FLOPS,
        core, inverted, p_sib, head, head_sib, head_other, tail, tail_sib,
    )
    p_own = call(subtract_kernel, struct(SYM), 0, core, near[:SYM], crossed[:SYM])
    r_own = call(subtract_kernel, struct(RANK + HALF), 0, core, near[SYM:], crossed[SYM:], after=(p_own,))
    third = over_child(
        call(add_kernel, struct(last), 0, core, third, swap(third, "rows", span_bits + 1), after=(r_own,))
    )
    crossed = call(third_kernel, struct(last), THIRD_FLOPS, core, tail, tail_other, z0, after=(r_own,))
    third = third - (crossed + swap(crossed, "rows", span_bits + 1))
    third = third + swap(third, "rows", span_bits)

    p_own = p_own + swap(p_own, "rows", span_bits)
    r_own = r_own + swap(r_own, "rows", span_bits)
    p_sib = swap(p_own, "rows", span_bits + 1)
    r_sib = swap(r_own, "rows", span_bits + 1)
    p_own_other = swap(p_own, "sub", 0)
    r_own_other = swap(r_own[:RANK], "sub", 0)
    p_sib_other = swap(p_sib, "sub", 0)
    inverted, p_sib = inverse(INVERT_SECOND, core, p_own, p_sib, p_own_other, p_sib_other)
    cross_sib = call(keep_kernel, struct(RANK), 0, core, r_sib[:RANK], after=(inverted,))
    z1, z_sib, crossed = call(
        middle_kernel, [struct(RANK + HALF), struct(RANK + HALF), struct(last)], MIDDLE_FLOPS,
        core, inverted, p_sib, r_own, r_sib, r_own_other, p_own, p_own_other,
    )
    crossed = call(cross_kernel, struct(last), CROSS_FLOPS, core, cross_sib, swap(cross_sib, "sub", 0), z_sib, crossed)

    own = third - crossed
    sib = swap(own, "rows", span_bits + 2)
    z1_other = swap(call(keep_kernel, struct(RANK + HALF), 0, core, z1, after=(own,)), "sub", 0)
    part = jax.ShapeDtypeStruct((rhs.shape[0], RANK), jnp.bfloat16)
    high, low, current = call(
        reduced_kernel, [part, part, struct(rhs.shape[0], RHS)], 6 * rhs.shape[0] * 2 * RANK * (RANK + RHS),
        core, z1, z1_other, z0, swap(z0, "sub", 0), solved_gens, rhs,
    )
    sib = call(keep_kernel, struct(last), 0, core, sib, after=(high,))
    own_other, sib_other = swap(own, "sub", 0), swap(sib, "sub", 0)
    return call(
        final_kernel, struct(rhs.shape[0], RHS), 6 * rhs.shape[0] * RANK * RHS + 6 * 9 * RANK**3,
        core, own, own_other, sib, sib_other, high, low, current, scratch=((RANK, RANK), (RANK, RHS)),
    )


def solution(mesh):
    placed = (
        P(("rows", "sub"), None),
        P(None, ("rows", "sub"), None),
        P(None, ("rows", "sub"), None),
    )
    return jax.shard_map(
        on_device, mesh=mesh, in_specs=placed, out_specs=P(("rows", "sub"), None), check_vma=False
    )
```

```python
import functools

import jax
import jax.numpy as jnp
from jax import lax
from jax.experimental import pallas as pl
from jax.experimental.pallas import tpu as pltpu
from jax.sharding import PartitionSpec as P

RANK = 256
RHS = 128
HALF = RANK // 2
QUARTER = HALF // 2
SYM = HALF + QUARTER
TOLERANCE = 1e-7
DIVERGED = 1e4
FIRST_FLOPS = 6.5e8
INVERT_FLOPS = 9e8
INVERT_SECOND = 9e8
MIDDLE_FLOPS = 0
CROSS_FLOPS = 0
THIRD_FLOPS = 1e9
VMEM_LIMIT = 40 * 2**20
STREAM_LIMIT = 52 * 2**20

SMEM = pl.BlockSpec(memory_space=pltpu.SMEM)
VMEM = pl.BlockSpec(memory_space=pltpu.VMEM)
HBM = pl.BlockSpec(memory_space=pltpu.HBM)
ANY = pl.BlockSpec(memory_space=pl.ANY)


def swap(value, axis, bit):
    mask = 2**bit
    pairs = [(source, source ^ mask) for source in range(lax.axis_size(axis))]
    return lax.ppermute(value, axis, pairs)


def struct(rows, cols=HALF):
    return jax.ShapeDtypeStruct((rows, cols), jnp.float32)


def cost(flops, floats):
    return pl.CostEstimate(flops=int(flops), bytes_accessed=int(4 * floats), transcendentals=0)


def split(value):
    high = value.astype(jnp.bfloat16)
    low = (value - high.astype(jnp.float32)).astype(jnp.bfloat16)
    return high, low


def dot_parts(left, right):
    first = jnp.concatenate([left[0], left[0], left[1]], axis=1)
    second = jnp.concatenate([right[0], right[1], right[0]], axis=0)
    return lax.dot_general(first, second, (((1,), (0,)), ((), ())), preferred_element_type=jnp.float32)


def dot(left, right):
    return dot_parts(split(left), split(right))


def dot_turned(left, right):
    return dot_parts([part.T for part in split(left)], split(right))


def in_order(core, own, other):
    first = core == 0
    return jnp.concatenate([jnp.where(first, own, other), jnp.where(first, other, own)], axis=1)


def symmetric(core, own, other):
    first = core == 0
    low = jnp.where(first, own, other)
    high = jnp.where(first, other, own)
    upper = jnp.concatenate([low[HALF:], high[HALF:]], axis=0)
    return jnp.concatenate(
        [jnp.concatenate([low[:HALF], upper], axis=1), jnp.concatenate([upper.T, high[:HALF]], axis=1)], axis=0
    )


def symmetric_half(core, value):
    first = core == 0
    return jnp.concatenate(
        [
            jnp.where(first, value[:HALF], value[HALF:]),
            jnp.where(first, value[HALF:].T[:QUARTER], value[QUARTER:HALF]),
        ],
        axis=0,
    )


def pack(value):
    whole = value.shape[1] // HALF
    units = [value[:, index * HALF : (index + 1) * HALF] for index in range(whole)]
    if value.shape[1] % HALF:
        tail = value[:, whole * HALF :]
        units.append(jnp.concatenate([tail[:HALF], tail[HALF:]], axis=1))
    return units


def unpack(ref):
    whole = ref.shape[0] // RANK
    parts = [ref[index * RANK : (index + 1) * RANK, :] for index in range(whole)]
    if ref.shape[0] % RANK:
        tail = ref[whole * RANK :, :]
        parts.append(jnp.concatenate([tail[:, :QUARTER], tail[:, QUARTER:]], axis=0))
    return jnp.concatenate(parts, axis=1) if len(parts) > 1 else parts[0]


def store(ref, value):
    start = 0
    for unit in pack(value):
        ref[start : start + unit.shape[0], :] = unit
        start += unit.shape[0]


def product_kernel(groups, chunks, core_ref, gens_ref, solved_ref, *refs):
    gens, solved, total, sems = refs[-4:] if chunks > 1 else (None, None, refs[-1], None)
    refs = refs[:-4] if chunks > 1 else refs[:-1]
    outs = refs[-2 * len(groups) :]
    blocks, lefts, rights = needed(groups)
    rhs_ref = refs[0] if 3 in rights else None
    block = gens_ref.shape[1] // chunks
    copies = []
    for chunk in range(chunks if chunks > 1 else 0):
        rows = pl.ds(chunk * block, block)
        row = [(gens_ref.at[level, rows], gens.at[place, rows]) for place, level in enumerate(lefts)]
        row += [(solved_ref.at[level, rows], solved.at[place, rows]) for place, level in enumerate(rights) if level < 3]
        row = [pltpu.make_async_copy(*ends, sems.at[index, chunk]) for index, ends in enumerate(row)]
        for copy in row:
            copy.start()
        copies.append(row)
    places = {}
    for chunk in range(chunks):
        rows = pl.ds(chunk * block, block)
        for copy in copies[chunk] if chunks > 1 else ():
            copy.wait()
        right = {}
        for place, level in enumerate(rights):
            if level == 3:
                right[level] = split(rhs_ref[rows, :])
            else:
                right[level] = split(solved[place, rows, :] if chunks > 1 else solved_ref[level])
        left = []
        for place, level in enumerate(lefts):
            left.append([part.T for part in split(gens[place, rows, :] if chunks > 1 else gens_ref[level])])
        start = 0
        for firsts, seconds in blocks:
            value = dot_parts(
                [jnp.concatenate([left[lefts.index(level)][half] for level in firsts], axis=0) for half in (0, 1)],
                [jnp.concatenate([right[level][half] for level in seconds], axis=1) for half in (0, 1)],
            )
            cols = slice(start, start + value.shape[1])
            if chunk == 0:
                total[: value.shape[0], cols] = value
            else:
                total[: value.shape[0], cols] += value
            for level in seconds:
                for place, first in enumerate(firsts):
                    places[first, level] = (place * RANK, start)
                start += width_of(level)
    first = core_ref[0] == 0
    for index, group in enumerate(groups):
        keep_ref, send_ref = outs[2 * index : 2 * index + 2]
        start = 0
        for pair in group:
            row, at = places[pair]
            value = total[row : row + RANK, at : at + width_of(pair[1])]
            if pair[0] == pair[1]:
                low = jnp.concatenate([value[:HALF, :HALF], value[:QUARTER, HALF:]], axis=0)
                high = jnp.concatenate([value[HALF:, HALF:], value[QUARTER:HALF, HALF:]], axis=0)
            elif pair[1] < 3:
                low = value[:, :HALF]
                high = value[:, HALF:]
            else:
                low = jnp.concatenate([value[:HALF, :QUARTER], value[HALF:, :QUARTER]], axis=1)
                high = jnp.concatenate([value[:HALF, QUARTER:], value[HALF:, QUARTER:]], axis=1)
            rows = slice(start, start + low.shape[0])
            keep_ref[rows, :] = jnp.where(first, low, high)
            send_ref[rows, :] = jnp.where(first, high, low)
            start += low.shape[0]


def rows_of(pair):
    return SYM if pair[0] == pair[1] else HALF if pair[1] == 3 else RANK


def width_of(level):
    return RHS if level == 3 else RANK


def needed(groups):
    pairs = sorted(pair for group in groups for pair in group)
    rights = sorted({right for _, right in pairs})
    blocks = {}
    for right in rights:
        blocks.setdefault(tuple(left for left, other in pairs if other == right), []).append(right)
    return list(blocks.items()), sorted({left for left, _ in pairs}), rights


def products(core, generators, solved_gens, rhs, groups, chunks, *after):
    rows = rhs.shape[0]
    blocks, lefts, rights = needed(groups)
    width = sum(width_of(right) for right in rights)
    height = max(len(firsts) for firsts, _ in blocks) * RANK
    flops = sum(len(firsts) * width_of(right) for firsts, seconds in blocks for right in seconds) * 6 * rows * RANK
    outs = [struct(sum(rows_of(pair) for pair in group)) for group in groups for _ in range(2)]
    held = sum(level < 3 for level in rights)
    scratch = [pltpu.VMEM((height, width), jnp.float32)]
    if chunks > 1:
        scratch = [
            pltpu.VMEM((len(lefts), rows, RANK), jnp.float32),
            pltpu.VMEM((held, rows, RANK), jnp.float32),
            *scratch,
            pltpu.SemaphoreType.DMA((len(lefts) + held, chunks)),
        ]
    given, specs = [generators, solved_gens], [HBM if chunks > 1 else VMEM] * 2
    if 3 in rights:
        given, specs = given + [rhs], specs + [VMEM]
    return pl.pallas_call(
        functools.partial(product_kernel, groups, chunks),
        in_specs=[SMEM] + specs + [ANY] * len(after),
        out_specs=[VMEM] * len(outs),
        out_shape=outs,
        scratch_shapes=scratch,
        compiler_params=pltpu.CompilerParams(vmem_limit_bytes=STREAM_LIMIT if chunks > 1 else VMEM_LIMIT),
        cost_estimate=cost(flops, rows * (len(lefts) * RANK + width)),
    )(core, *given, *after)


def square_norm(value):
    return jnp.sum(value * value)


def identity():
    row = lax.broadcasted_iota(jnp.int32, (RANK, RANK), 0)
    col = lax.broadcasted_iota(jnp.int32, (RANK, RANK), 1)
    return jnp.where(row == col, 1.0, 0.0)


def doubled(power, values):
    both = dot(power, jnp.concatenate([power, values], axis=1))
    return both[:, :RANK], values + both[:, RANK:]


def series(start, values, power_ref, sum_ref):
    if values is None:
        power, values = dot(start, start), identity() + start
    else:
        power, values = doubled(start, values)
    for _ in range(2):
        power, values = doubled(power, values)
    norm = square_norm(power)
    power_ref[...], sum_ref[...] = doubled(power, values)

    def proceed(state):
        count, bound = state
        return (count < 60) & (bound > TOLERANCE) & (bound < DIVERGED * DIVERGED)

    def body(state):
        count, _ = state
        bound = square_norm(power_ref[...])
        power_ref[...], sum_ref[...] = doubled(power_ref[...], sum_ref[...])
        return count + 1, bound

    return lax.while_loop(proceed, body, (jnp.int32(0), norm))[1]


def solve_series(product, values, power_ref, sum_ref):
    bound = series(product, values, power_ref, sum_ref)

    @pl.when(jnp.logical_not(bound <= TOLERANCE))
    def _():
        scale = 1.0 / (1.0 + jnp.sqrt(square_norm(product)))
        series((1.0 - scale) * identity() + scale * product, values, power_ref, sum_ref)
        sum_ref[...] = scale * sum_ref[...]


def invert_kernel(core_ref, own_ref, sib_ref, own_other_ref, sib_other_ref, inverse_ref, p_sib_ref, power):
    core = core_ref[0]
    p_own = symmetric(core, own_ref[:SYM, :], own_other_ref[:SYM, :])
    p_sib = symmetric(core, sib_ref[:SYM, :], sib_other_ref[:SYM, :])
    p_sib_ref[...] = p_sib
    solve_series(dot(p_sib, p_own), None, power, inverse_ref)


def invert_second_kernel(
    core_ref, own_ref, sib_ref, own_other_ref, sib_other_ref, r_own_ref, r_own_other_ref,
    inverse_ref, product_ref, turned_ref, power,
):
    core = core_ref[0]
    p_own = symmetric(core, own_ref[...], own_other_ref[...])
    p_sib = symmetric(core, sib_ref[...], sib_other_ref[...])
    both = dot(p_sib, jnp.concatenate([p_own, unpack(r_own_ref)], axis=1))
    product_ref[...] = both[:, RANK:]
    turned_ref[:RANK, :] = p_own
    turned_ref[RANK:, :] = in_order(core, r_own_ref[:RANK, :], r_own_other_ref[...]).T
    solve_series(both[:, :RANK], None, power, inverse_ref)


def call(kernel, out_shape, flops, *values, after=(), scratch=()):
    many = isinstance(out_shape, (list, tuple))
    floats = sum(value.size for value in values) + sum(out.size for out in (out_shape if many else [out_shape]))
    return pl.pallas_call(
        kernel,
        in_specs=[SMEM] + [VMEM] * (len(values) - 1) + [ANY] * len(after),
        out_specs=[VMEM] * len(out_shape) if many else VMEM,
        out_shape=out_shape,
        scratch_shapes=[pltpu.VMEM(shape, jnp.float32) for shape in scratch],
        compiler_params=pltpu.CompilerParams(vmem_limit_bytes=VMEM_LIMIT),
        cost_estimate=cost(flops, floats),
    )(*values, *after)


def inverse(flops, core, own, sib, own_other, sib_other):
    return pl.pallas_call(
        invert_kernel,
        in_specs=[SMEM] + [VMEM] * 4,
        out_specs=[VMEM] * 2,
        out_shape=[struct(RANK, RANK)] * 2,
        scratch_shapes=[pltpu.VMEM((RANK, RANK), jnp.float32)],
        compiler_params=pltpu.CompilerParams(vmem_limit_bytes=VMEM_LIMIT),
        cost_estimate=cost(flops, 0),
    )(core, own, sib, own_other, sib_other)


def first_kernel(core_ref, inverse_ref, p_sib_ref, head_ref, head_sib_ref, head_other_ref, tail_ref, tail_sib_ref, z_ref, out_ref):
    core = core_ref[0]
    own = jnp.concatenate([head_ref[SYM:, :], unpack(tail_ref)], axis=1)
    sib = jnp.concatenate([head_sib_ref[SYM:, :], unpack(tail_sib_ref)], axis=1)
    z = dot(inverse_ref[...], sib - dot(p_sib_ref[...], own))
    store(z_ref, z)
    value = dot_turned(in_order(core, head_ref[SYM:, :], head_other_ref[SYM:, :]), z)
    out_ref[:SYM, :] = symmetric_half(core, value[:, :HALF])
    store(out_ref.at[SYM:], value[:, HALF:])


def last_parts(core, crossed, z):
    return lost_parts(core, dot_turned(crossed, z))


def lost_parts(core, value):
    return jnp.concatenate([symmetric_half(core, value[:, :HALF]), *pack(value[:, HALF:])], axis=0)


def third_kernel(core_ref, own_ref, own_other_ref, z_ref, *refs):
    core = core_ref[0]
    crossed = in_order(core, own_ref[:RANK, :], own_other_ref[...])
    refs[-1][...] = last_parts(core, crossed, unpack(z_ref.at[RANK:]))


def middle_kernel(core_ref, inverse_ref, product_ref, turned_ref, own_ref, sib_ref, z_ref, z_sib_ref, out_ref):
    core = core_ref[0]
    z = dot(inverse_ref[...], unpack(sib_ref) - product_ref[...])
    store(z_ref, z)
    value = dot(turned_ref[...], z)
    store(z_sib_ref, unpack(own_ref) - value[:RANK])
    out_ref[...] = lost_parts(core, value[RANK:])


def cross_kernel(core_ref, sib_ref, sib_other_ref, z_sib_ref, crossed_ref, out_ref):
    core = core_ref[0]
    crossed = in_order(core, sib_ref[...], sib_other_ref[...])
    out_ref[...] = crossed_ref[...] + last_parts(core, crossed, unpack(z_sib_ref))


def rhs_in_order(core, own, other):
    first = core == 0
    low = jnp.where(first, own, other)
    high = jnp.where(first, other, own)
    top = jnp.concatenate([low[:, :QUARTER], high[:, :QUARTER]], axis=1)
    bottom = jnp.concatenate([low[:, QUARTER:], high[:, QUARTER:]], axis=1)
    return jnp.concatenate([top, bottom], axis=0)


def reduced_kernel(
    core_ref, z1_ref, z1_other_ref, z0_ref, z0_other_ref, solved_ref, rhs_ref, high_ref, low_ref, out_ref
):
    core = core_ref[0]
    z12 = in_order(core, z1_ref[:RANK, :], z1_other_ref[:RANK, :])
    z1x = rhs_in_order(core, z1_ref[RANK:, :], z1_other_ref[RANK:, :])
    z01 = in_order(core, z0_ref[:RANK, :], z0_other_ref[:RANK, :])
    z02 = in_order(core, z0_ref[RANK : 2 * RANK, :], z0_other_ref[RANK : 2 * RANK, :])
    z0x = rhs_in_order(core, z0_ref[2 * RANK :, :], z0_other_ref[2 * RANK :, :])
    middle = jnp.concatenate([z12, z1x], axis=1)
    first = jnp.concatenate([z02, z0x], axis=1) - dot(z01, middle)
    coefs = jnp.concatenate([first, middle], axis=0)
    value = dot(jnp.concatenate([solved_ref[0], solved_ref[1]], axis=1), coefs)
    high, low = split(solved_ref[2] - value[:, :RANK])
    high_ref[...] = high
    low_ref[...] = low
    out_ref[...] = rhs_ref[...] - value[:, RANK:]


def keep_kernel(core_ref, value_ref, *refs):
    refs[-1][...] = value_ref[...]


def add_kernel(core_ref, first_ref, second_ref, *refs):
    refs[-1][...] = first_ref[...] + second_ref[...]


def subtract_kernel(core_ref, first_ref, second_ref, *refs):
    refs[-1][...] = first_ref[...] - second_ref[...]


def final_kernel(
    core_ref, own_ref, own_other_ref, sib_ref, sib_other_ref, high_ref, low_ref, rhs_ref, out_ref, power, total, out, sems
):
    core = core_ref[0]
    p_own = symmetric(core, own_ref[:SYM, :], own_other_ref[:SYM, :])
    p_sib = symmetric(core, sib_ref[:SYM, :], sib_other_ref[:SYM, :])
    own = rhs_in_order(core, own_ref[SYM:, :], own_other_ref[SYM:, :])
    sib = rhs_in_order(core, sib_ref[SYM:, :], sib_other_ref[SYM:, :])
    both = dot(p_sib, jnp.concatenate([p_own, own], axis=1))
    solve_series(both[:, :RANK], sib - both[:, RANK:], power, total)
    z = split(total[...])
    blocks = sems.shape[0]
    block = out.shape[0] // blocks
    copies = []
    for index in range(blocks):
        rows = pl.ds(index * block, block)
        out[rows, :] = rhs_ref[rows, :] - dot_parts((high_ref[rows, :], low_ref[rows, :]), z)
        copies.append(pltpu.make_async_copy(out.at[rows], out_ref.at[rows], sems.at[index]))
        copies[-1].start()
    for copy in copies:
        copy.wait()


def on_device(rhs, generators, solved_gens):
    groups = lax.axis_size("rows")
    sub_bits = lax.axis_size("sub").bit_length() - 1
    span_bits = (groups // 8).bit_length() - 1
    core = (lax.axis_index("sub") % 2).astype(jnp.int32).reshape(1)
    flops = 6 * RANK * RANK * HALF
    last = SYM + HALF

    def over_child(value):
        for bit in range(1, sub_bits):
            value = value + swap(value, "sub", bit)
        for bit in range(span_bits):
            value = value + swap(value, "rows", bit)
        return value

    keep, send = products(core, generators, solved_gens, rhs, (((0, 0), (0, 1)),), 2)
    head = keep + swap(send, "sub", 0)
    token = swap(call(keep_kernel, struct(8), 0, core, send[:8], after=(head,)), "sub", 0)
    parts = products(core, generators, solved_gens, rhs, (((0, 2), (0, 3)),), 1, token)
    rest = (((1, 1), (1, 2), (1, 3)), ((2, 2), (2, 3)))
    parts += products(core, generators, solved_gens, rhs, rest, 1, parts[1])
    parts = [(keep, swap(send, "sub", 0)) for keep, send in zip(parts[::2], parts[1::2])]
    head = over_child(head)
    tail = over_child(parts[0][0] + parts[0][1])
    near = over_child(call(add_kernel, struct(SYM + RANK + HALF), 0, core, *parts[1], after=(tail,)))
    third = parts[2][0] + parts[2][1]

    head_sib = swap(head, "rows", span_bits)
    tail_sib = swap(tail, "rows", span_bits)
    head_other = swap(head, "sub", 0)
    tail_other = swap(tail[:RANK], "sub", 0)
    p_sib_other = swap(head_sib[:SYM], "sub", 0)
    inverted, p_sib = inverse(INVERT_FLOPS, core, head, head_sib, head_other, p_sib_other)
    z0, crossed = call(
        first_kernel, [struct(2 * RANK + HALF), struct(SYM + RANK + HALF)], FIRST_FLOPS,
        core, inverted, p_sib, head, head_sib, head_other, tail, tail_sib,
    )
    p_own = call(subtract_kernel, struct(SYM), 0, core, near[:SYM], crossed[:SYM])
    r_own = call(subtract_kernel, struct(RANK + HALF), 0, core, near[SYM:], crossed[SYM:], after=(p_own,))
    third = over_child(
        call(add_kernel, struct(last), 0, core, third, swap(third, "rows", span_bits + 1), after=(r_own,))
    )
    crossed = call(third_kernel, struct(last), THIRD_FLOPS, core, tail, tail_other, z0, after=(r_own,))
    third = third - (crossed + swap(crossed, "rows", span_bits + 1))
    third = third + swap(third, "rows", span_bits)

    p_own = p_own + swap(p_own, "rows", span_bits)
    r_own = r_own + swap(r_own, "rows", span_bits)
    p_sib = swap(p_own, "rows", span_bits + 1)
    r_sib = swap(r_own, "rows", span_bits + 1)
    p_own_other = swap(p_own, "sub", 0)
    r_own_other = swap(r_own[:RANK], "sub", 0)
    p_sib_other = swap(p_sib, "sub", 0)
    width = HALF + QUARTER
    inverted, product, turned = call(
        invert_second_kernel, [struct(RANK, RANK), struct(RANK, width), struct(2 * RANK, RANK)], INVERT_SECOND,
        core, p_own, p_sib, p_own_other, p_sib_other, r_own, r_own_other, scratch=((RANK, RANK),),
    )
    cross_sib = call(keep_kernel, struct(RANK), 0, core, r_sib[:RANK], after=(inverted,))
    z1, z_sib, crossed = call(
        middle_kernel, [struct(RANK + HALF), struct(RANK + HALF), struct(last)], MIDDLE_FLOPS,
        core, inverted, product, turned, r_own, r_sib,
    )
    crossed = call(cross_kernel, struct(last), CROSS_FLOPS, core, cross_sib, swap(cross_sib, "sub", 0), z_sib, crossed)

    own = third - crossed
    sib = swap(own, "rows", span_bits + 2)
    z1_other = swap(call(keep_kernel, struct(RANK + HALF), 0, core, z1, after=(own,)), "sub", 0)
    part = jax.ShapeDtypeStruct((rhs.shape[0], RANK), jnp.bfloat16)
    high, low, current = call(
        reduced_kernel, [part, part, struct(rhs.shape[0], RHS)], 6 * rhs.shape[0] * 2 * RANK * (RANK + RHS),
        core, z1, z1_other, z0, swap(z0, "sub", 0), solved_gens, rhs,
    )
    sib = call(keep_kernel, struct(last), 0, core, sib, after=(high,))
    own_other, sib_other = swap(own, "sub", 0), swap(sib, "sub", 0)
    rows = rhs.shape[0]
    small = (own, own_other, sib, sib_other, high, low, current)
    return pl.pallas_call(
        final_kernel,
        in_specs=[SMEM] + [VMEM] * len(small),
        out_specs=HBM,
        out_shape=struct(rows, RHS),
        scratch_shapes=[
            pltpu.VMEM((RANK, RANK), jnp.float32),
            pltpu.VMEM((RANK, RHS), jnp.float32),
            pltpu.VMEM((rows, RHS), jnp.float32),
            pltpu.SemaphoreType.DMA((2,)),
        ],
        compiler_params=pltpu.CompilerParams(vmem_limit_bytes=VMEM_LIMIT),
        cost_estimate=cost(6 * rows * RANK * RHS + 6 * 9 * RANK**3, 3 * rows * RANK),
    )(core, *small)


def solution(mesh):
    placed = (
        P(("rows", "sub"), None),
        P(None, ("rows", "sub"), None),
        P(None, ("rows", "sub"), None),
    )
    return jax.shard_map(
        on_device, mesh=mesh, in_specs=placed, out_specs=P(("rows", "sub"), None), check_vma=False
    )
```

```python
import functools

import jax
import jax.numpy as jnp
from jax import lax
from jax.experimental import pallas as pl
from jax.experimental.pallas import tpu as pltpu
from jax.sharding import PartitionSpec as P

RANK = 256
RHS = 128
HALF = RANK // 2
QUARTER = HALF // 2
SYM = HALF + QUARTER
TOLERANCE = 1e-7
DIVERGED = 1e4
FIRST_FLOPS = 6.5e8
INVERT_FLOPS = 9e8
INVERT_SECOND = 9e8
MIDDLE_FLOPS = 0
CROSS_FLOPS = 0
THIRD_FLOPS = 1e9
VMEM_LIMIT = 40 * 2**20
STREAM_LIMIT = 52 * 2**20

SMEM = pl.BlockSpec(memory_space=pltpu.SMEM)
VMEM = pl.BlockSpec(memory_space=pltpu.VMEM)
HBM = pl.BlockSpec(memory_space=pltpu.HBM)
ANY = pl.BlockSpec(memory_space=pl.ANY)


def swap(value, axis, bit):
    mask = 2**bit
    pairs = [(source, source ^ mask) for source in range(lax.axis_size(axis))]
    return lax.ppermute(value, axis, pairs)


def struct(rows, cols=HALF):
    return jax.ShapeDtypeStruct((rows, cols), jnp.float32)


def cost(flops, floats):
    return pl.CostEstimate(flops=int(flops), bytes_accessed=int(4 * floats), transcendentals=0)


def split(value):
    high = value.astype(jnp.bfloat16)
    low = (value - high.astype(jnp.float32)).astype(jnp.bfloat16)
    return high, low


def dot_parts(left, right):
    first = jnp.concatenate([left[0], left[0], left[1]], axis=1)
    second = jnp.concatenate([right[0], right[1], right[0]], axis=0)
    return lax.dot_general(first, second, (((1,), (0,)), ((), ())), preferred_element_type=jnp.float32)


def dot(left, right):
    return dot_parts(split(left), split(right))


def dot_turned(left, right):
    return dot_parts([part.T for part in split(left)], split(right))


def in_order(core, own, other):
    first = core == 0
    return jnp.concatenate([jnp.where(first, own, other), jnp.where(first, other, own)], axis=1)


def symmetric(core, own, other):
    first = core == 0
    low = jnp.where(first, own, other)
    high = jnp.where(first, other, own)
    upper = jnp.concatenate([low[HALF:], high[HALF:]], axis=0)
    return jnp.concatenate(
        [jnp.concatenate([low[:HALF], upper], axis=1), jnp.concatenate([upper.T, high[:HALF]], axis=1)], axis=0
    )


def symmetric_half(core, value):
    first = core == 0
    return jnp.concatenate(
        [
            jnp.where(first, value[:HALF], value[HALF:]),
            jnp.where(first, value[HALF:].T[:QUARTER], value[QUARTER:HALF]),
        ],
        axis=0,
    )


def pack(value):
    whole = value.shape[1] // HALF
    units = [value[:, index * HALF : (index + 1) * HALF] for index in range(whole)]
    if value.shape[1] % HALF:
        tail = value[:, whole * HALF :]
        units.append(jnp.concatenate([tail[:HALF], tail[HALF:]], axis=1))
    return units


def unpack(ref):
    whole = ref.shape[0] // RANK
    parts = [ref[index * RANK : (index + 1) * RANK, :] for index in range(whole)]
    if ref.shape[0] % RANK:
        tail = ref[whole * RANK :, :]
        parts.append(jnp.concatenate([tail[:, :QUARTER], tail[:, QUARTER:]], axis=0))
    return jnp.concatenate(parts, axis=1) if len(parts) > 1 else parts[0]


def store(ref, value):
    start = 0
    for unit in pack(value):
        ref[start : start + unit.shape[0], :] = unit
        start += unit.shape[0]


def product_kernel(groups, chunks, core_ref, gens_ref, solved_ref, *refs):
    gens, solved, total, sems = refs[-4:] if chunks > 1 else (None, None, refs[-1], None)
    refs = refs[:-4] if chunks > 1 else refs[:-1]
    outs = refs[-2 * len(groups) :]
    blocks, lefts, rights = needed(groups)
    rhs_ref = refs[0] if 3 in rights else None
    block = gens_ref.shape[1] // chunks
    copies = []
    for chunk in range(chunks if chunks > 1 else 0):
        rows = pl.ds(chunk * block, block)
        row = [(gens_ref.at[level, rows], gens.at[place, rows]) for place, level in enumerate(lefts)]
        row += [(solved_ref.at[level, rows], solved.at[place, rows]) for place, level in enumerate(rights) if level < 3]
        row = [pltpu.make_async_copy(*ends, sems.at[index, chunk]) for index, ends in enumerate(row)]
        for copy in row:
            copy.start()
        copies.append(row)
    places = {}
    for chunk in range(chunks):
        rows = pl.ds(chunk * block, block)
        for copy in copies[chunk] if chunks > 1 else ():
            copy.wait()
        right = {}
        for place, level in enumerate(rights):
            if level == 3:
                right[level] = split(rhs_ref[rows, :])
            else:
                right[level] = split(solved[place, rows, :] if chunks > 1 else solved_ref[level])
        left = []
        for place, level in enumerate(lefts):
            left.append([part.T for part in split(gens[place, rows, :] if chunks > 1 else gens_ref[level])])
        start = 0
        for firsts, seconds in blocks:
            value = dot_parts(
                [jnp.concatenate([left[lefts.index(level)][half] for level in firsts], axis=0) for half in (0, 1)],
                [jnp.concatenate([right[level][half] for level in seconds], axis=1) for half in (0, 1)],
            )
            cols = slice(start, start + value.shape[1])
            if chunk == 0:
                total[: value.shape[0], cols] = value
            else:
                total[: value.shape[0], cols] += value
            for level in seconds:
                for place, first in enumerate(firsts):
                    places[first, level] = (place * RANK, start)
                start += width_of(level)
    first = core_ref[0] == 0
    for index, group in enumerate(groups):
        keep_ref, send_ref = outs[2 * index : 2 * index + 2]
        start = 0
        for pair in group:
            row, at = places[pair]
            value = total[row : row + RANK, at : at + width_of(pair[1])]
            if pair[0] == pair[1]:
                low = jnp.concatenate([value[:HALF, :HALF], value[:QUARTER, HALF:]], axis=0)
                high = jnp.concatenate([value[HALF:, HALF:], value[QUARTER:HALF, HALF:]], axis=0)
            elif pair[1] < 3:
                low = value[:, :HALF]
                high = value[:, HALF:]
            else:
                low = jnp.concatenate([value[:HALF, :QUARTER], value[HALF:, :QUARTER]], axis=1)
                high = jnp.concatenate([value[:HALF, QUARTER:], value[HALF:, QUARTER:]], axis=1)
            rows = slice(start, start + low.shape[0])
            keep_ref[rows, :] = jnp.where(first, low, high)
            send_ref[rows, :] = jnp.where(first, high, low)
            start += low.shape[0]


def rows_of(pair):
    return SYM if pair[0] == pair[1] else HALF if pair[1] == 3 else RANK


def width_of(level):
    return RHS if level == 3 else RANK


def needed(groups):
    pairs = sorted(pair for group in groups for pair in group)
    rights = sorted({right for _, right in pairs})
    blocks = {}
    for right in rights:
        blocks.setdefault(tuple(left for left, other in pairs if other == right), []).append(right)
    return list(blocks.items()), sorted({left for left, _ in pairs}), rights


def products(core, generators, solved_gens, rhs, groups, chunks, *after):
    rows = rhs.shape[0]
    blocks, lefts, rights = needed(groups)
    width = sum(width_of(right) for right in rights)
    height = max(len(firsts) for firsts, _ in blocks) * RANK
    flops = sum(len(firsts) * width_of(right) for firsts, seconds in blocks for right in seconds) * 6 * rows * RANK
    outs = [struct(sum(rows_of(pair) for pair in group)) for group in groups for _ in range(2)]
    held = sum(level < 3 for level in rights)
    scratch = [pltpu.VMEM((height, width), jnp.float32)]
    if chunks > 1:
        scratch = [
            pltpu.VMEM((len(lefts), rows, RANK), jnp.float32),
            pltpu.VMEM((held, rows, RANK), jnp.float32),
            *scratch,
            pltpu.SemaphoreType.DMA((len(lefts) + held, chunks)),
        ]
    given, specs = [generators, solved_gens], [HBM if chunks > 1 else VMEM] * 2
    if 3 in rights:
        given, specs = given + [rhs], specs + [VMEM]
    return pl.pallas_call(
        functools.partial(product_kernel, groups, chunks),
        in_specs=[SMEM] + specs + [ANY] * len(after),
        out_specs=[VMEM] * len(outs),
        out_shape=outs,
        scratch_shapes=scratch,
        compiler_params=pltpu.CompilerParams(vmem_limit_bytes=STREAM_LIMIT if chunks > 1 else VMEM_LIMIT),
        cost_estimate=cost(flops, rows * (len(lefts) * RANK + width)),
    )(core, *given, *after)


def square_norm(value):
    return jnp.sum(value * value)


def identity():
    row = lax.broadcasted_iota(jnp.int32, (RANK, RANK), 0)
    col = lax.broadcasted_iota(jnp.int32, (RANK, RANK), 1)
    return jnp.where(row == col, 1.0, 0.0)


def doubled(power, values):
    power = split(power)
    right = [jnp.concatenate(parts, axis=1) for parts in zip(power, split(values))]
    both = dot_parts(power, right)
    return both[:, :RANK], values + both[:, RANK:]


def series(start, values, power_ref, sum_ref):
    if values is None:
        power, values = dot(start, start), identity() + start
    else:
        power, values = doubled(start, values)
    for _ in range(2):
        power, values = doubled(power, values)
    norm = square_norm(power)
    power_ref[...] = power
    sum_ref[...] = values + dot(power, values)

    def proceed(state):
        count, bound = state
        return (count < 60) & (bound > TOLERANCE) & (bound < DIVERGED * DIVERGED)

    def body(state):
        count, _ = state
        power = dot(power_ref[...], power_ref[...])
        power_ref[...] = power
        sum_ref[...] = sum_ref[...] + dot(power, sum_ref[...])
        return count + 1, square_norm(power)

    return lax.while_loop(proceed, body, (jnp.int32(0), norm))[1]


def solve_series(product, values, power_ref, sum_ref):
    bound = series(product, values, power_ref, sum_ref)

    @pl.when(jnp.logical_not(bound <= TOLERANCE))
    def _():
        scale = 1.0 / (1.0 + jnp.sqrt(square_norm(product)))
        series((1.0 - scale) * identity() + scale * product, values, power_ref, sum_ref)
        sum_ref[...] = scale * sum_ref[...]


def invert_kernel(core_ref, own_ref, sib_ref, own_other_ref, sib_other_ref, inverse_ref, p_sib_ref, power):
    core = core_ref[0]
    p_own = symmetric(core, own_ref[:SYM, :], own_other_ref[:SYM, :])
    p_sib = symmetric(core, sib_ref[:SYM, :], sib_other_ref[:SYM, :])
    p_sib_ref[...] = p_sib
    solve_series(dot(p_sib, p_own), None, power, inverse_ref)


def invert_second_kernel(
    core_ref, own_ref, sib_ref, own_other_ref, sib_other_ref, r_own_ref, r_own_other_ref,
    inverse_ref, product_ref, turned_ref, power,
):
    core = core_ref[0]
    p_own = symmetric(core, own_ref[...], own_other_ref[...])
    p_sib = symmetric(core, sib_ref[...], sib_other_ref[...])
    both = dot(p_sib, jnp.concatenate([p_own, unpack(r_own_ref)], axis=1))
    product_ref[...] = both[:, RANK:]
    turned_ref[:RANK, :] = p_own
    turned_ref[RANK:, :] = in_order(core, r_own_ref[:RANK, :], r_own_other_ref[...]).T
    solve_series(both[:, :RANK], None, power, inverse_ref)


def call(kernel, out_shape, flops, *values, after=(), scratch=()):
    many = isinstance(out_shape, (list, tuple))
    floats = sum(value.size for value in values) + sum(out.size for out in (out_shape if many else [out_shape]))
    return pl.pallas_call(
        kernel,
        in_specs=[SMEM] + [VMEM] * (len(values) - 1) + [ANY] * len(after),
        out_specs=[VMEM] * len(out_shape) if many else VMEM,
        out_shape=out_shape,
        scratch_shapes=[pltpu.VMEM(shape, jnp.float32) for shape in scratch],
        compiler_params=pltpu.CompilerParams(vmem_limit_bytes=VMEM_LIMIT),
        cost_estimate=cost(flops, floats),
    )(*values, *after)


def inverse(flops, core, own, sib, own_other, sib_other):
    return pl.pallas_call(
        invert_kernel,
        in_specs=[SMEM] + [VMEM] * 4,
        out_specs=[VMEM] * 2,
        out_shape=[struct(RANK, RANK)] * 2,
        scratch_shapes=[pltpu.VMEM((RANK, RANK), jnp.float32)],
        compiler_params=pltpu.CompilerParams(vmem_limit_bytes=VMEM_LIMIT),
        cost_estimate=cost(flops, 0),
    )(core, own, sib, own_other, sib_other)


def first_kernel(core_ref, inverse_ref, p_sib_ref, head_ref, head_sib_ref, head_other_ref, tail_ref, tail_sib_ref, z_ref, out_ref):
    core = core_ref[0]
    own = jnp.concatenate([head_ref[SYM:, :], unpack(tail_ref)], axis=1)
    sib = jnp.concatenate([head_sib_ref[SYM:, :], unpack(tail_sib_ref)], axis=1)
    z = dot(inverse_ref[...], sib - dot(p_sib_ref[...], own))
    store(z_ref, z)
    value = dot_turned(in_order(core, head_ref[SYM:, :], head_other_ref[SYM:, :]), z)
    out_ref[:SYM, :] = symmetric_half(core, value[:, :HALF])
    store(out_ref.at[SYM:], value[:, HALF:])


def last_parts(core, crossed, z):
    return lost_parts(core, dot_turned(crossed, z))


def lost_parts(core, value):
    return jnp.concatenate([symmetric_half(core, value[:, :HALF]), *pack(value[:, HALF:])], axis=0)


def third_kernel(core_ref, own_ref, own_other_ref, z_ref, *refs):
    core = core_ref[0]
    crossed = in_order(core, own_ref[:RANK, :], own_other_ref[...])
    refs[-1][...] = last_parts(core, crossed, unpack(z_ref.at[RANK:]))


def middle_kernel(core_ref, inverse_ref, product_ref, turned_ref, own_ref, sib_ref, z_ref, z_sib_ref, out_ref):
    core = core_ref[0]
    z = dot(inverse_ref[...], unpack(sib_ref) - product_ref[...])
    store(z_ref, z)
    value = dot(turned_ref[...], z)
    store(z_sib_ref, unpack(own_ref) - value[:RANK])
    out_ref[...] = lost_parts(core, value[RANK:])


def cross_kernel(core_ref, sib_ref, sib_other_ref, z_sib_ref, crossed_ref, out_ref):
    core = core_ref[0]
    crossed = in_order(core, sib_ref[...], sib_other_ref[...])
    out_ref[...] = crossed_ref[...] + last_parts(core, crossed, unpack(z_sib_ref))


def rhs_in_order(core, own, other):
    first = core == 0
    low = jnp.where(first, own, other)
    high = jnp.where(first, other, own)
    top = jnp.concatenate([low[:, :QUARTER], high[:, :QUARTER]], axis=1)
    bottom = jnp.concatenate([low[:, QUARTER:], high[:, QUARTER:]], axis=1)
    return jnp.concatenate([top, bottom], axis=0)


def reduced_kernel(
    core_ref, z1_ref, z1_other_ref, z0_ref, z0_other_ref, solved_ref, rhs_ref, high_ref, low_ref, out_ref
):
    core = core_ref[0]
    z12 = in_order(core, z1_ref[:RANK, :], z1_other_ref[:RANK, :])
    z1x = rhs_in_order(core, z1_ref[RANK:, :], z1_other_ref[RANK:, :])
    z01 = in_order(core, z0_ref[:RANK, :], z0_other_ref[:RANK, :])
    z02 = in_order(core, z0_ref[RANK : 2 * RANK, :], z0_other_ref[RANK : 2 * RANK, :])
    z0x = rhs_in_order(core, z0_ref[2 * RANK :, :], z0_other_ref[2 * RANK :, :])
    middle = jnp.concatenate([z12, z1x], axis=1)
    first = jnp.concatenate([z02, z0x], axis=1) - dot(z01, middle)
    coefs = jnp.concatenate([first, middle], axis=0)
    value = dot(jnp.concatenate([solved_ref[0], solved_ref[1]], axis=1), coefs)
    high, low = split(solved_ref[2] - value[:, :RANK])
    high_ref[...] = high
    low_ref[...] = low
    out_ref[...] = rhs_ref[...] - value[:, RANK:]


def keep_kernel(core_ref, value_ref, *refs):
    refs[-1][...] = value_ref[...]


def add_kernel(core_ref, first_ref, second_ref, *refs):
    refs[-1][...] = first_ref[...] + second_ref[...]


def subtract_kernel(core_ref, first_ref, second_ref, *refs):
    refs[-1][...] = first_ref[...] - second_ref[...]


def final_kernel(
    core_ref, own_ref, own_other_ref, sib_ref, sib_other_ref, high_ref, low_ref, rhs_ref, out_ref, power, total, out, sems
):
    core = core_ref[0]
    p_own = symmetric(core, own_ref[:SYM, :], own_other_ref[:SYM, :])
    p_sib = symmetric(core, sib_ref[:SYM, :], sib_other_ref[:SYM, :])
    own = rhs_in_order(core, own_ref[SYM:, :], own_other_ref[SYM:, :])
    sib = rhs_in_order(core, sib_ref[SYM:, :], sib_other_ref[SYM:, :])
    both = dot(p_sib, jnp.concatenate([p_own, own], axis=1))
    solve_series(both[:, :RANK], sib - both[:, RANK:], power, total)
    z = split(total[...])
    blocks = sems.shape[0]
    block = out.shape[0] // blocks
    copies = []
    for index in range(blocks):
        rows = pl.ds(index * block, block)
        out[rows, :] = rhs_ref[rows, :] - dot_parts((high_ref[rows, :], low_ref[rows, :]), z)
        copies.append(pltpu.make_async_copy(out.at[rows], out_ref.at[rows], sems.at[index]))
        copies[-1].start()
    for copy in copies:
        copy.wait()


def on_device(rhs, generators, solved_gens):
    groups = lax.axis_size("rows")
    sub_bits = lax.axis_size("sub").bit_length() - 1
    span_bits = (groups // 8).bit_length() - 1
    core = (lax.axis_index("sub") % 2).astype(jnp.int32).reshape(1)
    flops = 6 * RANK * RANK * HALF
    last = SYM + HALF

    def over_child(value):
        for bit in range(1, sub_bits):
            value = value + swap(value, "sub", bit)
        for bit in range(span_bits):
            value = value + swap(value, "rows", bit)
        return value

    keep, send = products(core, generators, solved_gens, rhs, (((0, 0), (0, 1)),), 8)
    head = keep + swap(send, "sub", 0)
    token = swap(call(keep_kernel, struct(8), 0, core, send[:8], after=(head,)), "sub", 0)
    parts = products(core, generators, solved_gens, rhs, (((0, 2), (0, 3)),), 1, token)
    rest = (((1, 1), (1, 2), (1, 3)), ((2, 2), (2, 3)))
    parts += products(core, generators, solved_gens, rhs, rest, 1, parts[1])
    parts = [(keep, swap(send, "sub", 0)) for keep, send in zip(parts[::2], parts[1::2])]
    head = over_child(head)
    tail = over_child(parts[0][0] + parts[0][1])
    near = over_child(call(add_kernel, struct(SYM + RANK + HALF), 0, core, *parts[1], after=(tail,)))
    third = parts[2][0] + parts[2][1]

    head_sib = swap(head, "rows", span_bits)
    tail_sib = swap(tail, "rows", span_bits)
    head_other = swap(head, "sub", 0)
    tail_other = swap(tail[:RANK], "sub", 0)
    p_sib_other = swap(head_sib[:SYM], "sub", 0)
    inverted, p_sib = inverse(INVERT_FLOPS, core, head, head_sib, head_other, p_sib_other)
    z0, crossed = call(
        first_kernel, [struct(2 * RANK + HALF), struct(SYM + RANK + HALF)], FIRST_FLOPS,
        core, inverted, p_sib, head, head_sib, head_other, tail, tail_sib,
    )
    p_own = call(subtract_kernel, struct(SYM), 0, core, near[:SYM], crossed[:SYM])
    r_own = call(subtract_kernel, struct(RANK + HALF), 0, core, near[SYM:], crossed[SYM:], after=(p_own,))
    third = over_child(
        call(add_kernel, struct(last), 0, core, third, swap(third, "rows", span_bits + 1), after=(r_own,))
    )
    crossed = call(third_kernel, struct(last), THIRD_FLOPS, core, tail, tail_other, z0, after=(r_own,))
    third = third - (crossed + swap(crossed, "rows", span_bits + 1))
    third = third + swap(third, "rows", span_bits)

    p_own = p_own + swap(p_own, "rows", span_bits)
    r_own = r_own + swap(r_own, "rows", span_bits)
    p_sib = swap(p_own, "rows", span_bits + 1)
    r_sib = swap(r_own, "rows", span_bits + 1)
    p_own_other = swap(p_own, "sub", 0)
    r_own_other = swap(r_own[:RANK], "sub", 0)
    p_sib_other = swap(p_sib, "sub", 0)
    width = HALF + QUARTER
    inverted, product, turned = call(
        invert_second_kernel, [struct(RANK, RANK), struct(RANK, width), struct(2 * RANK, RANK)], INVERT_SECOND,
        core, p_own, p_sib, p_own_other, p_sib_other, r_own, r_own_other, scratch=((RANK, RANK),),
    )
    cross_sib = call(keep_kernel, struct(RANK), 0, core, r_sib[:RANK], after=(inverted,))
    z1, z_sib, crossed = call(
        middle_kernel, [struct(RANK + HALF), struct(RANK + HALF), struct(last)], MIDDLE_FLOPS,
        core, inverted, product, turned, r_own, r_sib,
    )
    crossed = call(cross_kernel, struct(last), CROSS_FLOPS, core, cross_sib, swap(cross_sib, "sub", 0), z_sib, crossed)

    own = third - crossed
    sib = swap(own, "rows", span_bits + 2)
    z1_other = swap(call(keep_kernel, struct(RANK + HALF), 0, core, z1, after=(own,)), "sub", 0)
    part = jax.ShapeDtypeStruct((rhs.shape[0], RANK), jnp.bfloat16)
    high, low, current = call(
        reduced_kernel, [part, part, struct(rhs.shape[0], RHS)], 6 * rhs.shape[0] * 2 * RANK * (RANK + RHS),
        core, z1, z1_other, z0, swap(z0, "sub", 0), solved_gens, rhs,
    )
    sib = call(keep_kernel, struct(last), 0, core, sib, after=(high,))
    own_other, sib_other = swap(own, "sub", 0), swap(sib, "sub", 0)
    rows = rhs.shape[0]
    small = (own, own_other, sib, sib_other, high, low, current)
    return pl.pallas_call(
        final_kernel,
        in_specs=[SMEM] + [VMEM] * len(small),
        out_specs=HBM,
        out_shape=struct(rows, RHS),
        scratch_shapes=[
            pltpu.VMEM((RANK, RANK), jnp.float32),
            pltpu.VMEM((RANK, RHS), jnp.float32),
            pltpu.VMEM((rows, RHS), jnp.float32),
            pltpu.SemaphoreType.DMA((2,)),
        ],
        compiler_params=pltpu.CompilerParams(vmem_limit_bytes=VMEM_LIMIT),
        cost_estimate=cost(6 * rows * RANK * RHS + 6 * 9 * RANK**3, 3 * rows * RANK),
    )(core, *small)


def solution(mesh):
    placed = (
        P(("rows", "sub"), None),
        P(None, ("rows", "sub"), None),
        P(None, ("rows", "sub"), None),
    )
    return jax.shard_map(
        on_device, mesh=mesh, in_specs=placed, out_specs=P(("rows", "sub"), None), check_vma=False
    )
```

```python
import functools

import jax
import jax.numpy as jnp
from jax import lax
from jax.experimental import pallas as pl
from jax.experimental.pallas import tpu as pltpu
from jax.sharding import PartitionSpec as P

RANK = 256
RHS = 128
HALF = RANK // 2
QUARTER = HALF // 2
SYM = HALF + QUARTER
TOLERANCE = 1e-7
DIVERGED = 1e4
FIRST_FLOPS = 6.5e8
INVERT_FLOPS = 9e8
INVERT_SECOND = 9e8
MIDDLE_FLOPS = 0
CROSS_FLOPS = 0
THIRD_FLOPS = 1e9
VMEM_LIMIT = 40 * 2**20
STREAM_LIMIT = 52 * 2**20

SMEM = pl.BlockSpec(memory_space=pltpu.SMEM)
VMEM = pl.BlockSpec(memory_space=pltpu.VMEM)
HBM = pl.BlockSpec(memory_space=pltpu.HBM)
ANY = pl.BlockSpec(memory_space=pl.ANY)


def swap(value, axis, bit):
    mask = 2**bit
    pairs = [(source, source ^ mask) for source in range(lax.axis_size(axis))]
    return lax.ppermute(value, axis, pairs)


def struct(rows, cols=HALF):
    return jax.ShapeDtypeStruct((rows, cols), jnp.float32)


def cost(flops, floats):
    return pl.CostEstimate(flops=int(flops), bytes_accessed=int(4 * floats), transcendentals=0)


def split(value):
    high = value.astype(jnp.bfloat16)
    low = (value - high.astype(jnp.float32)).astype(jnp.bfloat16)
    return high, low


def dot_parts(left, right):
    first = jnp.concatenate([left[0], left[0], left[1]], axis=1)
    second = jnp.concatenate([right[0], right[1], right[0]], axis=0)
    return lax.dot_general(first, second, (((1,), (0,)), ((), ())), preferred_element_type=jnp.float32)


def dot(left, right):
    return dot_parts(split(left), split(right))


def dot_turned(left, right):
    return dot_parts([part.T for part in split(left)], split(right))


def in_order(core, own, other):
    first = core == 0
    return jnp.concatenate([jnp.where(first, own, other), jnp.where(first, other, own)], axis=1)


def symmetric(core, own, other):
    first = core == 0
    low = jnp.where(first, own, other)
    high = jnp.where(first, other, own)
    upper = jnp.concatenate([low[HALF:], high[HALF:]], axis=0)
    return jnp.concatenate(
        [jnp.concatenate([low[:HALF], upper], axis=1), jnp.concatenate([upper.T, high[:HALF]], axis=1)], axis=0
    )


def symmetric_half(core, value):
    first = core == 0
    return jnp.concatenate(
        [
            jnp.where(first, value[:HALF], value[HALF:]),
            jnp.where(first, value[HALF:].T[:QUARTER], value[QUARTER:HALF]),
        ],
        axis=0,
    )


def pack(value):
    whole = value.shape[1] // HALF
    units = [value[:, index * HALF : (index + 1) * HALF] for index in range(whole)]
    if value.shape[1] % HALF:
        tail = value[:, whole * HALF :]
        units.append(jnp.concatenate([tail[:HALF], tail[HALF:]], axis=1))
    return units


def unpack(ref):
    whole = ref.shape[0] // RANK
    parts = [ref[index * RANK : (index + 1) * RANK, :] for index in range(whole)]
    if ref.shape[0] % RANK:
        tail = ref[whole * RANK :, :]
        parts.append(jnp.concatenate([tail[:, :QUARTER], tail[:, QUARTER:]], axis=0))
    return jnp.concatenate(parts, axis=1) if len(parts) > 1 else parts[0]


def store(ref, value):
    start = 0
    for unit in pack(value):
        ref[start : start + unit.shape[0], :] = unit
        start += unit.shape[0]


def product_kernel(groups, chunks, core_ref, gens_ref, solved_ref, *refs):
    gens, solved, total, sems = refs[-4:] if chunks > 1 else (None, None, refs[-1], None)
    refs = refs[:-4] if chunks > 1 else refs[:-1]
    outs = refs[-2 * len(groups) :]
    blocks, lefts, rights = needed(groups)
    rhs_ref = refs[0] if 3 in rights else None
    block = gens_ref.shape[1] // chunks
    copies = []
    for chunk in range(chunks if chunks > 1 else 0):
        rows = pl.ds(chunk * block, block)
        row = [(gens_ref.at[level, rows], gens.at[place, rows]) for place, level in enumerate(lefts)]
        row += [(solved_ref.at[level, rows], solved.at[place, rows]) for place, level in enumerate(rights) if level < 3]
        row = [pltpu.make_async_copy(*ends, sems.at[index, chunk]) for index, ends in enumerate(row)]
        for copy in row:
            copy.start()
        copies.append(row)
    places = {}
    for chunk in range(chunks):
        rows = pl.ds(chunk * block, block)
        for copy in copies[chunk] if chunks > 1 else ():
            copy.wait()
        right = {}
        for place, level in enumerate(rights):
            if level == 3:
                right[level] = split(rhs_ref[rows, :])
            else:
                right[level] = split(solved[place, rows, :] if chunks > 1 else solved_ref[level])
        left = []
        for place, level in enumerate(lefts):
            left.append([part.T for part in split(gens[place, rows, :] if chunks > 1 else gens_ref[level])])
        start = 0
        for firsts, seconds in blocks:
            value = dot_parts(
                [jnp.concatenate([left[lefts.index(level)][half] for level in firsts], axis=0) for half in (0, 1)],
                [jnp.concatenate([right[level][half] for level in seconds], axis=1) for half in (0, 1)],
            )
            cols = slice(start, start + value.shape[1])
            if chunk == 0:
                total[: value.shape[0], cols] = value
            else:
                total[: value.shape[0], cols] += value
            for level in seconds:
                for place, first in enumerate(firsts):
                    places[first, level] = (place * RANK, start)
                start += width_of(level)
    first = core_ref[0] == 0
    for index, group in enumerate(groups):
        keep_ref, send_ref = outs[2 * index : 2 * index + 2]
        start = 0
        for pair in group:
            row, at = places[pair]
            value = total[row : row + RANK, at : at + width_of(pair[1])]
            if pair[0] == pair[1]:
                low = jnp.concatenate([value[:HALF, :HALF], value[:QUARTER, HALF:]], axis=0)
                high = jnp.concatenate([value[HALF:, HALF:], value[QUARTER:HALF, HALF:]], axis=0)
            elif pair[1] < 3:
                low = value[:, :HALF]
                high = value[:, HALF:]
            else:
                low = jnp.concatenate([value[:HALF, :QUARTER], value[HALF:, :QUARTER]], axis=1)
                high = jnp.concatenate([value[:HALF, QUARTER:], value[HALF:, QUARTER:]], axis=1)
            rows = slice(start, start + low.shape[0])
            keep_ref[rows, :] = jnp.where(first, low, high)
            send_ref[rows, :] = jnp.where(first, high, low)
            start += low.shape[0]


def rows_of(pair):
    return SYM if pair[0] == pair[1] else HALF if pair[1] == 3 else RANK


def width_of(level):
    return RHS if level == 3 else RANK


def needed(groups):
    pairs = sorted(pair for group in groups for pair in group)
    rights = sorted({right for _, right in pairs})
    blocks = {}
    for right in rights:
        blocks.setdefault(tuple(left for left, other in pairs if other == right), []).append(right)
    return list(blocks.items()), sorted({left for left, _ in pairs}), rights


def products(core, generators, solved_gens, rhs, groups, chunks, *after):
    rows = rhs.shape[0]
    blocks, lefts, rights = needed(groups)
    width = sum(width_of(right) for right in rights)
    height = max(len(firsts) for firsts, _ in blocks) * RANK
    flops = sum(len(firsts) * width_of(right) for firsts, seconds in blocks for right in seconds) * 6 * rows * RANK
    outs = [struct(sum(rows_of(pair) for pair in group)) for group in groups for _ in range(2)]
    held = sum(level < 3 for level in rights)
    scratch = [pltpu.VMEM((height, width), jnp.float32)]
    if chunks > 1:
        scratch = [
            pltpu.VMEM((len(lefts), rows, RANK), jnp.float32),
            pltpu.VMEM((held, rows, RANK), jnp.float32),
            *scratch,
            pltpu.SemaphoreType.DMA((len(lefts) + held, chunks)),
        ]
    given, specs = [generators, solved_gens], [HBM if chunks > 1 else VMEM] * 2
    if 3 in rights:
        given, specs = given + [rhs], specs + [VMEM]
    return pl.pallas_call(
        functools.partial(product_kernel, groups, chunks),
        in_specs=[SMEM] + specs + [ANY] * len(after),
        out_specs=[VMEM] * len(outs),
        out_shape=outs,
        scratch_shapes=scratch,
        compiler_params=pltpu.CompilerParams(vmem_limit_bytes=STREAM_LIMIT if chunks > 1 else VMEM_LIMIT),
        cost_estimate=cost(flops, rows * (len(lefts) * RANK + width)),
    )(core, *given, *after)


def square_norm(value):
    return jnp.sum(value * value)


def identity():
    row = lax.broadcasted_iota(jnp.int32, (RANK, RANK), 0)
    col = lax.broadcasted_iota(jnp.int32, (RANK, RANK), 1)
    return jnp.where(row == col, 1.0, 0.0)


def doubled(power, values):
    power = split(power)
    right = [jnp.concatenate(parts, axis=1) for parts in zip(power, split(values))]
    both = dot_parts(power, right)
    return both[:, :RANK], values + both[:, RANK:]


def series(start, values, power_ref, sum_ref):
    if values is None:
        power, values = dot(start, start), identity() + start
    else:
        power, values = doubled(start, values)
    for _ in range(2):
        power, values = doubled(power, values)
    norm = square_norm(power)
    power_ref[...] = power
    sum_ref[...] = values + dot(power, values)

    def proceed(state):
        count, bound = state
        return (count < 60) & (bound > TOLERANCE) & (bound < DIVERGED * DIVERGED)

    def body(state):
        count, _ = state
        power = dot(power_ref[...], power_ref[...])
        power_ref[...] = power
        sum_ref[...] = sum_ref[...] + dot(power, sum_ref[...])
        return count + 1, square_norm(power)

    return lax.while_loop(proceed, body, (jnp.int32(0), norm))[1]


def solve_series(product, values, power_ref, sum_ref):
    bound = series(product, values, power_ref, sum_ref)

    @pl.when(jnp.logical_not(bound <= TOLERANCE))
    def _():
        scale = 1.0 / (1.0 + jnp.sqrt(square_norm(product)))
        series((1.0 - scale) * identity() + scale * product, values, power_ref, sum_ref)
        sum_ref[...] = scale * sum_ref[...]


def invert_kernel(core_ref, own_ref, sib_ref, own_other_ref, sib_other_ref, tail_ref, inverse_ref, product_ref, power):
    core = core_ref[0]
    p_own = symmetric(core, own_ref[:SYM, :], own_other_ref[:SYM, :])
    p_sib = symmetric(core, sib_ref[:SYM, :], sib_other_ref[...])
    both = dot(p_sib, jnp.concatenate([p_own, own_ref[SYM:, :], unpack(tail_ref)], axis=1))
    product_ref[...] = both[:, RANK:]
    solve_series(both[:, :RANK], None, power, inverse_ref)


def invert_second_kernel(
    core_ref, own_ref, sib_ref, own_other_ref, sib_other_ref, r_own_ref, r_own_other_ref,
    inverse_ref, product_ref, turned_ref, power,
):
    core = core_ref[0]
    p_own = symmetric(core, own_ref[...], own_other_ref[...])
    p_sib = symmetric(core, sib_ref[...], sib_other_ref[...])
    both = dot(p_sib, jnp.concatenate([p_own, unpack(r_own_ref)], axis=1))
    product_ref[...] = both[:, RANK:]
    turned_ref[:RANK, :] = p_own
    turned_ref[RANK:, :] = in_order(core, r_own_ref[:RANK, :], r_own_other_ref[...]).T
    solve_series(both[:, :RANK], None, power, inverse_ref)


def call(kernel, out_shape, flops, *values, after=(), scratch=()):
    many = isinstance(out_shape, (list, tuple))
    floats = sum(value.size for value in values) + sum(out.size for out in (out_shape if many else [out_shape]))
    return pl.pallas_call(
        kernel,
        in_specs=[SMEM] + [VMEM] * (len(values) - 1) + [ANY] * len(after),
        out_specs=[VMEM] * len(out_shape) if many else VMEM,
        out_shape=out_shape,
        scratch_shapes=[pltpu.VMEM(shape, jnp.float32) for shape in scratch],
        compiler_params=pltpu.CompilerParams(vmem_limit_bytes=VMEM_LIMIT),
        cost_estimate=cost(flops, floats),
    )(*values, *after)


def first_kernel(core_ref, inverse_ref, product_ref, head_ref, head_sib_ref, head_other_ref, tail_sib_ref, z_ref, out_ref):
    core = core_ref[0]
    sib = jnp.concatenate([head_sib_ref[SYM:, :], unpack(tail_sib_ref)], axis=1)
    z = dot(inverse_ref[...], sib - product_ref[...])
    store(z_ref, z)
    value = dot_turned(in_order(core, head_ref[SYM:, :], head_other_ref[SYM:, :]), z)
    out_ref[:SYM, :] = symmetric_half(core, value[:, :HALF])
    store(out_ref.at[SYM:], value[:, HALF:])


def last_parts(core, crossed, z):
    return lost_parts(core, dot_turned(crossed, z))


def lost_parts(core, value):
    return jnp.concatenate([symmetric_half(core, value[:, :HALF]), *pack(value[:, HALF:])], axis=0)


def third_kernel(core_ref, own_ref, own_other_ref, z_ref, *refs):
    core = core_ref[0]
    crossed = in_order(core, own_ref[:RANK, :], own_other_ref[...])
    refs[-1][...] = last_parts(core, crossed, unpack(z_ref.at[RANK:]))


def middle_kernel(core_ref, inverse_ref, product_ref, turned_ref, own_ref, sib_ref, z_ref, z_sib_ref, out_ref):
    core = core_ref[0]
    z = dot(inverse_ref[...], unpack(sib_ref) - product_ref[...])
    store(z_ref, z)
    value = dot(turned_ref[...], z)
    store(z_sib_ref, unpack(own_ref) - value[:RANK])
    out_ref[...] = lost_parts(core, value[RANK:])


def cross_kernel(core_ref, sib_ref, sib_other_ref, z_sib_ref, crossed_ref, out_ref):
    core = core_ref[0]
    crossed = in_order(core, sib_ref[...], sib_other_ref[...])
    out_ref[...] = crossed_ref[...] + last_parts(core, crossed, unpack(z_sib_ref))


def rhs_in_order(core, own, other):
    first = core == 0
    low = jnp.where(first, own, other)
    high = jnp.where(first, other, own)
    top = jnp.concatenate([low[:, :QUARTER], high[:, :QUARTER]], axis=1)
    bottom = jnp.concatenate([low[:, QUARTER:], high[:, QUARTER:]], axis=1)
    return jnp.concatenate([top, bottom], axis=0)


def reduced_kernel(
    core_ref, z1_ref, z1_other_ref, z0_ref, z0_other_ref, solved_ref, rhs_ref, high_ref, low_ref, out_ref
):
    core = core_ref[0]
    z12 = in_order(core, z1_ref[:RANK, :], z1_other_ref[:RANK, :])
    z1x = rhs_in_order(core, z1_ref[RANK:, :], z1_other_ref[RANK:, :])
    z01 = in_order(core, z0_ref[:RANK, :], z0_other_ref[:RANK, :])
    z02 = in_order(core, z0_ref[RANK : 2 * RANK, :], z0_other_ref[RANK : 2 * RANK, :])
    z0x = rhs_in_order(core, z0_ref[2 * RANK :, :], z0_other_ref[2 * RANK :, :])
    middle = jnp.concatenate([z12, z1x], axis=1)
    first = jnp.concatenate([z02, z0x], axis=1) - dot(z01, middle)
    coefs = jnp.concatenate([first, middle], axis=0)
    value = dot(jnp.concatenate([solved_ref[0], solved_ref[1]], axis=1), coefs)
    high, low = split(solved_ref[2] - value[:, :RANK])
    high_ref[...] = high
    low_ref[...] = low
    out_ref[...] = rhs_ref[...] - value[:, RANK:]


def keep_kernel(core_ref, value_ref, *refs):
    refs[-1][...] = value_ref[...]


def add_kernel(core_ref, first_ref, second_ref, *refs):
    refs[-1][...] = first_ref[...] + second_ref[...]


def subtract_kernel(core_ref, first_ref, second_ref, *refs):
    refs[-1][...] = first_ref[...] - second_ref[...]


def final_kernel(
    core_ref, own_ref, own_other_ref, sib_ref, sib_other_ref, high_ref, low_ref, rhs_ref, out_ref, power, total, out, sems
):
    core = core_ref[0]
    p_own = symmetric(core, own_ref[:SYM, :], own_other_ref[:SYM, :])
    p_sib = symmetric(core, sib_ref[:SYM, :], sib_other_ref[:SYM, :])
    own = rhs_in_order(core, own_ref[SYM:, :], own_other_ref[SYM:, :])
    sib = rhs_in_order(core, sib_ref[SYM:, :], sib_other_ref[SYM:, :])
    both = dot(p_sib, jnp.concatenate([p_own, own], axis=1))
    solve_series(both[:, :RANK], sib - both[:, RANK:], power, total)
    z = split(total[...])
    blocks = sems.shape[0]
    block = out.shape[0] // blocks
    copies = []
    for index in range(blocks):
        rows = pl.ds(index * block, block)
        out[rows, :] = rhs_ref[rows, :] - dot_parts((high_ref[rows, :], low_ref[rows, :]), z)
        copies.append(pltpu.make_async_copy(out.at[rows], out_ref.at[rows], sems.at[index]))
        copies[-1].start()
    for copy in copies:
        copy.wait()


def on_device(rhs, generators, solved_gens):
    groups = lax.axis_size("rows")
    sub_bits = lax.axis_size("sub").bit_length() - 1
    span_bits = (groups // 8).bit_length() - 1
    core = (lax.axis_index("sub") % 2).astype(jnp.int32).reshape(1)
    flops = 6 * RANK * RANK * HALF
    last = SYM + HALF

    def over_child(value):
        for bit in range(1, sub_bits):
            value = value + swap(value, "sub", bit)
        for bit in range(span_bits):
            value = value + swap(value, "rows", bit)
        return value

    keep, send = products(core, generators, solved_gens, rhs, (((0, 0), (0, 1)),), 4)
    head = keep + swap(send, "sub", 0)
    token = swap(call(keep_kernel, struct(8), 0, core, send[:8], after=(head,)), "sub", 0)
    parts = products(core, generators, solved_gens, rhs, (((0, 2), (0, 3)),), 1, token)
    rest = (((1, 1), (1, 2), (1, 3)), ((2, 2), (2, 3)))
    parts += products(core, generators, solved_gens, rhs, rest, 1, parts[1])
    parts = [(keep, swap(send, "sub", 0)) for keep, send in zip(parts[::2], parts[1::2])]
    head = over_child(head)
    tail = over_child(parts[0][0] + parts[0][1])
    near = over_child(call(add_kernel, struct(SYM + RANK + HALF), 0, core, *parts[1], after=(tail,)))
    third = parts[2][0] + parts[2][1]

    head_sib = swap(head, "rows", span_bits)
    tail_sib = swap(tail, "rows", span_bits)
    head_other = swap(head, "sub", 0)
    tail_other = swap(tail[:RANK], "sub", 0)
    p_sib_other = swap(head_sib[:SYM], "sub", 0)
    inverted, product = call(
        invert_kernel, [struct(RANK, RANK), struct(RANK, 2 * HALF + QUARTER)], INVERT_FLOPS,
        core, head, head_sib, head_other, p_sib_other, tail, scratch=((RANK, RANK),),
    )
    z0, crossed = call(
        first_kernel, [struct(2 * RANK + HALF), struct(SYM + RANK + HALF)], FIRST_FLOPS,
        core, inverted, product, head, head_sib, head_other, tail_sib,
    )
    p_own = call(subtract_kernel, struct(SYM), 0, core, near[:SYM], crossed[:SYM])
    r_own = call(subtract_kernel, struct(RANK + HALF), 0, core, near[SYM:], crossed[SYM:], after=(p_own,))
    third = over_child(
        call(add_kernel, struct(last), 0, core, third, swap(third, "rows", span_bits + 1), after=(r_own,))
    )
    crossed = call(third_kernel, struct(last), THIRD_FLOPS, core, tail, tail_other, z0, after=(r_own,))
    third = third - (crossed + swap(crossed, "rows", span_bits + 1))
    third = third + swap(third, "rows", span_bits)

    p_own = p_own + swap(p_own, "rows", span_bits)
    r_own = r_own + swap(r_own, "rows", span_bits)
    p_sib = swap(p_own, "rows", span_bits + 1)
    r_sib = swap(r_own, "rows", span_bits + 1)
    p_own_other = swap(p_own, "sub", 0)
    r_own_other = swap(r_own[:RANK], "sub", 0)
    p_sib_other = swap(p_sib, "sub", 0)
    width = HALF + QUARTER
    inverted, product, turned = call(
        invert_second_kernel, [struct(RANK, RANK), struct(RANK, width), struct(2 * RANK, RANK)], INVERT_SECOND,
        core, p_own, p_sib, p_own_other, p_sib_other, r_own, r_own_other, scratch=((RANK, RANK),),
    )
    cross_sib = call(keep_kernel, struct(RANK), 0, core, r_sib[:RANK], after=(inverted,))
    z1, z_sib, crossed = call(
        middle_kernel, [struct(RANK + HALF), struct(RANK + HALF), struct(last)], MIDDLE_FLOPS,
        core, inverted, product, turned, r_own, r_sib,
    )
    crossed = call(cross_kernel, struct(last), CROSS_FLOPS, core, cross_sib, swap(cross_sib, "sub", 0), z_sib, crossed)

    own = third - crossed
    sib = swap(own, "rows", span_bits + 2)
    z1_other = swap(call(keep_kernel, struct(RANK + HALF), 0, core, z1, after=(own,)), "sub", 0)
    part = jax.ShapeDtypeStruct((rhs.shape[0], RANK), jnp.bfloat16)
    high, low, current = call(
        reduced_kernel, [part, part, struct(rhs.shape[0], RHS)], 6 * rhs.shape[0] * 2 * RANK * (RANK + RHS),
        core, z1, z1_other, z0, swap(z0, "sub", 0), solved_gens, rhs,
    )
    sib = call(keep_kernel, struct(last), 0, core, sib, after=(high,))
    own_other, sib_other = swap(own, "sub", 0), swap(sib, "sub", 0)
    rows = rhs.shape[0]
    small = (own, own_other, sib, sib_other, high, low, current)
    return pl.pallas_call(
        final_kernel,
        in_specs=[SMEM] + [VMEM] * len(small),
        out_specs=HBM,
        out_shape=struct(rows, RHS),
        scratch_shapes=[
            pltpu.VMEM((RANK, RANK), jnp.float32),
            pltpu.VMEM((RANK, RHS), jnp.float32),
            pltpu.VMEM((rows, RHS), jnp.float32),
            pltpu.SemaphoreType.DMA((2,)),
        ],
        compiler_params=pltpu.CompilerParams(vmem_limit_bytes=VMEM_LIMIT),
        cost_estimate=cost(6 * rows * RANK * RHS + 6 * 9 * RANK**3, 3 * rows * RANK),
    )(core, *small)


def solution(mesh):
    placed = (
        P(("rows", "sub"), None),
        P(None, ("rows", "sub"), None),
        P(None, ("rows", "sub"), None),
    )
    return jax.shard_map(
        on_device, mesh=mesh, in_specs=placed, out_specs=P(("rows", "sub"), None), check_vma=False
    )
```

```python
import functools

import jax
import jax.numpy as jnp
from jax import lax
from jax.experimental import pallas as pl
from jax.experimental.pallas import tpu as pltpu
from jax.sharding import PartitionSpec as P

RANK = 256
RHS = 128
HALF = RANK // 2
QUARTER = HALF // 2
SYM = HALF + QUARTER
TOLERANCE = 1e-7
DIVERGED = 1e4
FIRST_FLOPS = 6.5e8
INVERT_FLOPS = 5e8
INVERT_SECOND = 9e8
MIDDLE_FLOPS = 0
CROSS_FLOPS = 0
THIRD_FLOPS = 1e9
VMEM_LIMIT = 40 * 2**20
STREAM_LIMIT = 52 * 2**20

SMEM = pl.BlockSpec(memory_space=pltpu.SMEM)
VMEM = pl.BlockSpec(memory_space=pltpu.VMEM)
HBM = pl.BlockSpec(memory_space=pltpu.HBM)
ANY = pl.BlockSpec(memory_space=pl.ANY)


def swap(value, axis, bit):
    mask = 2**bit
    pairs = [(source, source ^ mask) for source in range(lax.axis_size(axis))]
    return lax.ppermute(value, axis, pairs)


def struct(rows, cols=HALF):
    return jax.ShapeDtypeStruct((rows, cols), jnp.float32)


def cost(flops, floats):
    return pl.CostEstimate(flops=int(flops), bytes_accessed=int(4 * floats), transcendentals=0)


def split(value):
    high = value.astype(jnp.bfloat16)
    low = (value - high.astype(jnp.float32)).astype(jnp.bfloat16)
    return high, low


def dot_parts(left, right):
    first = jnp.concatenate([left[0], left[0], left[1]], axis=1)
    second = jnp.concatenate([right[0], right[1], right[0]], axis=0)
    return lax.dot_general(first, second, (((1,), (0,)), ((), ())), preferred_element_type=jnp.float32)


def dot(left, right):
    return dot_parts(split(left), split(right))


def dot_turned(left, right):
    return dot_parts([part.T for part in split(left)], split(right))


def in_order(core, own, other):
    first = core == 0
    return jnp.concatenate([jnp.where(first, own, other), jnp.where(first, other, own)], axis=1)


def symmetric(core, own, other):
    first = core == 0
    low = jnp.where(first, own, other)
    high = jnp.where(first, other, own)
    upper = jnp.concatenate([low[HALF:], high[HALF:]], axis=0)
    return jnp.concatenate(
        [jnp.concatenate([low[:HALF], upper], axis=1), jnp.concatenate([upper.T, high[:HALF]], axis=1)], axis=0
    )


def symmetric_half(core, value):
    first = core == 0
    return jnp.concatenate(
        [
            jnp.where(first, value[:HALF], value[HALF:]),
            jnp.where(first, value[HALF:].T[:QUARTER], value[QUARTER:HALF]),
        ],
        axis=0,
    )


def pack(value):
    whole = value.shape[1] // HALF
    units = [value[:, index * HALF : (index + 1) * HALF] for index in range(whole)]
    if value.shape[1] % HALF:
        tail = value[:, whole * HALF :]
        units.append(jnp.concatenate([tail[:HALF], tail[HALF:]], axis=1))
    return units


def unpack(ref):
    whole = ref.shape[0] // RANK
    parts = [ref[index * RANK : (index + 1) * RANK, :] for index in range(whole)]
    if ref.shape[0] % RANK:
        tail = ref[whole * RANK :, :]
        parts.append(jnp.concatenate([tail[:, :QUARTER], tail[:, QUARTER:]], axis=0))
    return jnp.concatenate(parts, axis=1) if len(parts) > 1 else parts[0]


def store(ref, value):
    start = 0
    for unit in pack(value):
        ref[start : start + unit.shape[0], :] = unit
        start += unit.shape[0]


def product_kernel(groups, chunks, core_ref, gens_ref, solved_ref, *refs):
    gens, solved, total, sems = refs[-4:] if chunks > 1 else (None, None, refs[-1], None)
    refs = refs[:-4] if chunks > 1 else refs[:-1]
    outs = refs[-2 * len(groups) :]
    blocks, lefts, rights = needed(groups)
    rhs_ref = refs[0] if 3 in rights else None
    block = gens_ref.shape[1] // chunks
    copies = []
    for chunk in range(chunks if chunks > 1 else 0):
        rows = pl.ds(chunk * block, block)
        row = [(gens_ref.at[level, rows], gens.at[place, rows]) for place, level in enumerate(lefts)]
        row += [(solved_ref.at[level, rows], solved.at[place, rows]) for place, level in enumerate(rights) if level < 3]
        row = [pltpu.make_async_copy(*ends, sems.at[index, chunk]) for index, ends in enumerate(row)]
        for copy in row:
            copy.start()
        copies.append(row)
    places = {}
    for chunk in range(chunks):
        rows = pl.ds(chunk * block, block)
        for copy in copies[chunk] if chunks > 1 else ():
            copy.wait()
        right = {}
        for place, level in enumerate(rights):
            if level == 3:
                right[level] = split(rhs_ref[rows, :])
            else:
                right[level] = split(solved[place, rows, :] if chunks > 1 else solved_ref[level])
        left = []
        for place, level in enumerate(lefts):
            left.append([part.T for part in split(gens[place, rows, :] if chunks > 1 else gens_ref[level])])
        start = 0
        for firsts, seconds in blocks:
            value = dot_parts(
                [jnp.concatenate([left[lefts.index(level)][half] for level in firsts], axis=0) for half in (0, 1)],
                [jnp.concatenate([right[level][half] for level in seconds], axis=1) for half in (0, 1)],
            )
            cols = slice(start, start + value.shape[1])
            if chunk == 0:
                total[: value.shape[0], cols] = value
            else:
                total[: value.shape[0], cols] += value
            for level in seconds:
                for place, first in enumerate(firsts):
                    places[first, level] = (place * RANK, start)
                start += width_of(level)
    first = core_ref[0] == 0
    for index, group in enumerate(groups):
        keep_ref, send_ref = outs[2 * index : 2 * index + 2]
        start = 0
        for pair in group:
            row, at = places[pair]
            value = total[row : row + RANK, at : at + width_of(pair[1])]
            if pair[0] == pair[1]:
                low = jnp.concatenate([value[:HALF, :HALF], value[:QUARTER, HALF:]], axis=0)
                high = jnp.concatenate([value[HALF:, HALF:], value[QUARTER:HALF, HALF:]], axis=0)
            elif pair[1] < 3:
                low = value[:, :HALF]
                high = value[:, HALF:]
            else:
                low = jnp.concatenate([value[:HALF, :QUARTER], value[HALF:, :QUARTER]], axis=1)
                high = jnp.concatenate([value[:HALF, QUARTER:], value[HALF:, QUARTER:]], axis=1)
            rows = slice(start, start + low.shape[0])
            keep_ref[rows, :] = jnp.where(first, low, high)
            send_ref[rows, :] = jnp.where(first, high, low)
            start += low.shape[0]


def rows_of(pair):
    return SYM if pair[0] == pair[1] else HALF if pair[1] == 3 else RANK


def width_of(level):
    return RHS if level == 3 else RANK


def needed(groups):
    pairs = sorted(pair for group in groups for pair in group)
    rights = sorted({right for _, right in pairs})
    blocks = {}
    for right in rights:
        blocks.setdefault(tuple(left for left, other in pairs if other == right), []).append(right)
    return list(blocks.items()), sorted({left for left, _ in pairs}), rights


def products(core, generators, solved_gens, rhs, groups, chunks, *after):
    rows = rhs.shape[0]
    blocks, lefts, rights = needed(groups)
    width = sum(width_of(right) for right in rights)
    height = max(len(firsts) for firsts, _ in blocks) * RANK
    flops = sum(len(firsts) * width_of(right) for firsts, seconds in blocks for right in seconds) * 6 * rows * RANK
    outs = [struct(sum(rows_of(pair) for pair in group)) for group in groups for _ in range(2)]
    held = sum(level < 3 for level in rights)
    scratch = [pltpu.VMEM((height, width), jnp.float32)]
    if chunks > 1:
        scratch = [
            pltpu.VMEM((len(lefts), rows, RANK), jnp.float32),
            pltpu.VMEM((held, rows, RANK), jnp.float32),
            *scratch,
            pltpu.SemaphoreType.DMA((len(lefts) + held, chunks)),
        ]
    given, specs = [generators, solved_gens], [HBM if chunks > 1 else VMEM] * 2
    if 3 in rights:
        given, specs = given + [rhs], specs + [VMEM]
    return pl.pallas_call(
        functools.partial(product_kernel, groups, chunks),
        in_specs=[SMEM] + specs + [ANY] * len(after),
        out_specs=[VMEM] * len(outs),
        out_shape=outs,
        scratch_shapes=scratch,
        compiler_params=pltpu.CompilerParams(vmem_limit_bytes=STREAM_LIMIT if chunks > 1 else VMEM_LIMIT),
        cost_estimate=cost(flops, rows * (len(lefts) * RANK + width)),
    )(core, *given, *after)


def square_norm(value):
    return jnp.sum(value * value)


def identity():
    row = lax.broadcasted_iota(jnp.int32, (RANK, RANK), 0)
    col = lax.broadcasted_iota(jnp.int32, (RANK, RANK), 1)
    return jnp.where(row == col, 1.0, 0.0)


def doubled(power, values):
    power = split(power)
    right = [jnp.concatenate(parts, axis=1) for parts in zip(power, split(values))]
    both = dot_parts(power, right)
    return both[:, :RANK], values + both[:, RANK:]


def series(start, values, power_ref, sum_ref):
    if values is None:
        power, values = dot(start, start), identity() + start
    else:
        power, values = doubled(start, values)
    for _ in range(2):
        power, values = doubled(power, values)
    norm = square_norm(power)
    power_ref[...] = power
    sum_ref[...] = values + dot(power, values)

    def proceed(state):
        count, bound = state
        return (count < 60) & (bound > TOLERANCE) & (bound < DIVERGED * DIVERGED)

    def body(state):
        count, _ = state
        power = dot(power_ref[...], power_ref[...])
        power_ref[...] = power
        sum_ref[...] = sum_ref[...] + dot(power, sum_ref[...])
        return count + 1, square_norm(power)

    return lax.while_loop(proceed, body, (jnp.int32(0), norm))[1]


def solve_series(product, values, power_ref, sum_ref):
    bound = series(product, values, power_ref, sum_ref)

    @pl.when(jnp.logical_not(bound <= TOLERANCE))
    def _():
        scale = 1.0 / (1.0 + jnp.sqrt(square_norm(product)))
        series((1.0 - scale) * identity() + scale * product, values, power_ref, sum_ref)
        sum_ref[...] = scale * sum_ref[...]


def invert_kernel(core_ref, own_ref, sib_ref, own_other_ref, sib_other_ref, tail_ref, inverse_ref, product_ref, power):
    core = core_ref[0]
    p_own = symmetric(core, own_ref[:SYM, :], own_other_ref[:SYM, :])
    p_sib = symmetric(core, sib_ref[:SYM, :], sib_other_ref[...])
    both = dot(p_sib, jnp.concatenate([p_own, own_ref[SYM:, :], unpack(tail_ref)], axis=1))
    product_ref[...] = both[:, RANK:]
    solve_series(both[:, :RANK], None, power, inverse_ref)


def invert_second_kernel(
    core_ref, own_ref, sib_ref, own_other_ref, sib_other_ref, r_own_ref, r_own_other_ref,
    inverse_ref, product_ref, turned_ref, power,
):
    core = core_ref[0]
    p_own = symmetric(core, own_ref[...], own_other_ref[...])
    p_sib = symmetric(core, sib_ref[...], sib_other_ref[...])
    both = dot(p_sib, jnp.concatenate([p_own, unpack(r_own_ref)], axis=1))
    product_ref[...] = both[:, RANK:]
    turned_ref[:RANK, :] = p_own
    turned_ref[RANK:, :] = in_order(core, r_own_ref[:RANK, :], r_own_other_ref[...]).T
    solve_series(both[:, :RANK], None, power, inverse_ref)


def call(kernel, out_shape, flops, *values, after=(), scratch=()):
    many = isinstance(out_shape, (list, tuple))
    floats = sum(value.size for value in values) + sum(out.size for out in (out_shape if many else [out_shape]))
    return pl.pallas_call(
        kernel,
        in_specs=[SMEM] + [VMEM] * (len(values) - 1) + [ANY] * len(after),
        out_specs=[VMEM] * len(out_shape) if many else VMEM,
        out_shape=out_shape,
        scratch_shapes=[pltpu.VMEM(shape, jnp.float32) for shape in scratch],
        compiler_params=pltpu.CompilerParams(vmem_limit_bytes=VMEM_LIMIT),
        cost_estimate=cost(flops, floats),
    )(*values, *after)


def first_kernel(core_ref, inverse_ref, product_ref, head_ref, head_sib_ref, head_other_ref, tail_sib_ref, z_ref, out_ref):
    core = core_ref[0]
    sib = jnp.concatenate([head_sib_ref[SYM:, :], unpack(tail_sib_ref)], axis=1)
    z = dot(inverse_ref[...], sib - product_ref[...])
    store(z_ref, z)
    value = dot_turned(in_order(core, head_ref[SYM:, :], head_other_ref[SYM:, :]), z)
    out_ref[:SYM, :] = symmetric_half(core, value[:, :HALF])
    store(out_ref.at[SYM:], value[:, HALF:])


def last_parts(core, crossed, z):
    return lost_parts(core, dot_turned(crossed, z))


def lost_parts(core, value):
    return jnp.concatenate([symmetric_half(core, value[:, :HALF]), *pack(value[:, HALF:])], axis=0)


def third_kernel(core_ref, own_ref, own_other_ref, z_ref, *refs):
    core = core_ref[0]
    crossed = in_order(core, own_ref[:RANK, :], own_other_ref[...])
    refs[-1][...] = last_parts(core, crossed, unpack(z_ref.at[RANK:]))


def middle_kernel(core_ref, inverse_ref, product_ref, turned_ref, own_ref, sib_ref, z_ref, z_sib_ref, out_ref):
    core = core_ref[0]
    z = dot(inverse_ref[...], unpack(sib_ref) - product_ref[...])
    store(z_ref, z)
    value = dot(turned_ref[...], z)
    store(z_sib_ref, unpack(own_ref) - value[:RANK])
    out_ref[...] = lost_parts(core, value[RANK:])


def cross_kernel(core_ref, sib_ref, sib_other_ref, z_sib_ref, crossed_ref, out_ref):
    core = core_ref[0]
    crossed = in_order(core, sib_ref[...], sib_other_ref[...])
    out_ref[...] = crossed_ref[...] + last_parts(core, crossed, unpack(z_sib_ref))


def rhs_in_order(core, own, other):
    first = core == 0
    low = jnp.where(first, own, other)
    high = jnp.where(first, other, own)
    top = jnp.concatenate([low[:, :QUARTER], high[:, :QUARTER]], axis=1)
    bottom = jnp.concatenate([low[:, QUARTER:], high[:, QUARTER:]], axis=1)
    return jnp.concatenate([top, bottom], axis=0)


def reduced_kernel(
    core_ref, z1_ref, z1_other_ref, z0_ref, z0_other_ref, solved_ref, rhs_ref, high_ref, low_ref, out_ref
):
    core = core_ref[0]
    z12 = in_order(core, z1_ref[:RANK, :], z1_other_ref[:RANK, :])
    z1x = rhs_in_order(core, z1_ref[RANK:, :], z1_other_ref[RANK:, :])
    z01 = in_order(core, z0_ref[:RANK, :], z0_other_ref[:RANK, :])
    z02 = in_order(core, z0_ref[RANK : 2 * RANK, :], z0_other_ref[RANK : 2 * RANK, :])
    z0x = rhs_in_order(core, z0_ref[2 * RANK :, :], z0_other_ref[2 * RANK :, :])
    middle = jnp.concatenate([z12, z1x], axis=1)
    first = jnp.concatenate([z02, z0x], axis=1) - dot(z01, middle)
    coefs = jnp.concatenate([first, middle], axis=0)
    value = dot(jnp.concatenate([solved_ref[0], solved_ref[1]], axis=1), coefs)
    high, low = split(solved_ref[2] - value[:, :RANK])
    high_ref[...] = high
    low_ref[...] = low
    out_ref[...] = rhs_ref[...] - value[:, RANK:]


def keep_kernel(core_ref, value_ref, *refs):
    refs[-1][...] = value_ref[...]


def add_kernel(core_ref, first_ref, second_ref, *refs):
    refs[-1][...] = first_ref[...] + second_ref[...]


def subtract_kernel(core_ref, first_ref, second_ref, *refs):
    refs[-1][...] = first_ref[...] - second_ref[...]


def final_kernel(
    core_ref, own_ref, own_other_ref, sib_ref, sib_other_ref, high_ref, low_ref, rhs_ref, out_ref, power, total, out, sems
):
    core = core_ref[0]
    p_own = symmetric(core, own_ref[:SYM, :], own_other_ref[:SYM, :])
    p_sib = symmetric(core, sib_ref[:SYM, :], sib_other_ref[:SYM, :])
    own = rhs_in_order(core, own_ref[SYM:, :], own_other_ref[SYM:, :])
    sib = rhs_in_order(core, sib_ref[SYM:, :], sib_other_ref[SYM:, :])
    both = dot(p_sib, jnp.concatenate([p_own, own], axis=1))
    solve_series(both[:, :RANK], sib - both[:, RANK:], power, total)
    z = split(total[...])
    blocks = sems.shape[0]
    block = out.shape[0] // blocks
    copies = []
    for index in range(blocks):
        rows = pl.ds(index * block, block)
        out[rows, :] = rhs_ref[rows, :] - dot_parts((high_ref[rows, :], low_ref[rows, :]), z)
        copies.append(pltpu.make_async_copy(out.at[rows], out_ref.at[rows], sems.at[index]))
        copies[-1].start()
    for copy in copies:
        copy.wait()


def on_device(rhs, generators, solved_gens):
    groups = lax.axis_size("rows")
    sub_bits = lax.axis_size("sub").bit_length() - 1
    span_bits = (groups // 8).bit_length() - 1
    core = (lax.axis_index("sub") % 2).astype(jnp.int32).reshape(1)
    flops = 6 * RANK * RANK * HALF
    last = SYM + HALF

    def over_child(value):
        for bit in range(1, sub_bits):
            value = value + swap(value, "sub", bit)
        for bit in range(span_bits):
            value = value + swap(value, "rows", bit)
        return value

    keep, send = products(core, generators, solved_gens, rhs, (((0, 0), (0, 1)),), 4)
    head = keep + swap(send, "sub", 0)
    token = swap(call(keep_kernel, struct(8), 0, core, send[:8], after=(head,)), "sub", 0)
    parts = products(core, generators, solved_gens, rhs, (((0, 2), (0, 3)),), 1, token)
    rest = (((1, 1), (1, 2), (1, 3)), ((2, 2), (2, 3)))
    parts += products(core, generators, solved_gens, rhs, rest, 1, parts[1])
    parts = [(keep, swap(send, "sub", 0)) for keep, send in zip(parts[::2], parts[1::2])]
    head = over_child(head)
    tail = over_child(parts[0][0] + parts[0][1])
    third = parts[2][0] + parts[2][1]
    near = over_child(call(add_kernel, struct(SYM + RANK + HALF), 0, core, *parts[1], after=(third,)))

    head_sib = swap(head, "rows", span_bits)
    tail_sib = swap(tail, "rows", span_bits)
    head_other = swap(head, "sub", 0)
    tail_other = swap(tail[:RANK], "sub", 0)
    p_sib_other = swap(head_sib[:SYM], "sub", 0)
    inverted, product = call(
        invert_kernel, [struct(RANK, RANK), struct(RANK, 2 * HALF + QUARTER)], INVERT_FLOPS,
        core, head, head_sib, head_other, p_sib_other, tail, scratch=((RANK, RANK),),
    )
    z0, crossed = call(
        first_kernel, [struct(2 * RANK + HALF), struct(SYM + RANK + HALF)], FIRST_FLOPS,
        core, inverted, product, head, head_sib, head_other, tail_sib,
    )
    p_own = call(subtract_kernel, struct(SYM), 0, core, near[:SYM], crossed[:SYM])
    r_own = call(subtract_kernel, struct(RANK + HALF), 0, core, near[SYM:], crossed[SYM:], after=(p_own,))
    third = over_child(
        call(add_kernel, struct(last), 0, core, third, swap(third, "rows", span_bits + 1), after=(r_own,))
    )
    crossed = call(third_kernel, struct(last), THIRD_FLOPS, core, tail, tail_other, z0, after=(r_own,))
    third = third - (crossed + swap(crossed, "rows", span_bits + 1))
    third = third + swap(third, "rows", span_bits)

    p_own = p_own + swap(p_own, "rows", span_bits)
    r_own = r_own + swap(r_own, "rows", span_bits)
    p_sib = swap(p_own, "rows", span_bits + 1)
    r_sib = swap(r_own, "rows", span_bits + 1)
    p_own_other = swap(p_own, "sub", 0)
    r_own_other = swap(r_own[:RANK], "sub", 0)
    p_sib_other = swap(p_sib, "sub", 0)
    width = HALF + QUARTER
    inverted, product, turned = call(
        invert_second_kernel, [struct(RANK, RANK), struct(RANK, width), struct(2 * RANK, RANK)], INVERT_SECOND,
        core, p_own, p_sib, p_own_other, p_sib_other, r_own, r_own_other, scratch=((RANK, RANK),),
    )
    cross_sib = call(keep_kernel, struct(RANK), 0, core, r_sib[:RANK], after=(inverted,))
    z1, z_sib, crossed = call(
        middle_kernel, [struct(RANK + HALF), struct(RANK + HALF), struct(last)], MIDDLE_FLOPS,
        core, inverted, product, turned, r_own, r_sib,
    )
    crossed = call(cross_kernel, struct(last), CROSS_FLOPS, core, cross_sib, swap(cross_sib, "sub", 0), z_sib, crossed)

    own = third - crossed
    sib = swap(own, "rows", span_bits + 2)
    z1_other = swap(call(keep_kernel, struct(RANK + HALF), 0, core, z1, after=(own,)), "sub", 0)
    part = jax.ShapeDtypeStruct((rhs.shape[0], RANK), jnp.bfloat16)
    high, low, current = call(
        reduced_kernel, [part, part, struct(rhs.shape[0], RHS)], 6 * rhs.shape[0] * 2 * RANK * (RANK + RHS),
        core, z1, z1_other, z0, swap(z0, "sub", 0), solved_gens, rhs,
    )
    sib = call(keep_kernel, struct(last), 0, core, sib, after=(high,))
    own_other, sib_other = swap(own, "sub", 0), swap(sib, "sub", 0)
    rows = rhs.shape[0]
    small = (own, own_other, sib, sib_other, high, low, current)
    return pl.pallas_call(
        final_kernel,
        in_specs=[SMEM] + [VMEM] * len(small),
        out_specs=HBM,
        out_shape=struct(rows, RHS),
        scratch_shapes=[
            pltpu.VMEM((RANK, RANK), jnp.float32),
            pltpu.VMEM((RANK, RHS), jnp.float32),
            pltpu.VMEM((rows, RHS), jnp.float32),
            pltpu.SemaphoreType.DMA((2,)),
        ],
        compiler_params=pltpu.CompilerParams(vmem_limit_bytes=VMEM_LIMIT),
        cost_estimate=cost(6 * rows * RANK * RHS + 6 * 9 * RANK**3, 3 * rows * RANK),
    )(core, *small)


def solution(mesh):
    placed = (
        P(("rows", "sub"), None),
        P(None, ("rows", "sub"), None),
        P(None, ("rows", "sub"), None),
    )
    return jax.shard_map(
        on_device, mesh=mesh, in_specs=placed, out_specs=P(("rows", "sub"), None), check_vma=False
    )
```

```python
import functools

import jax
import jax.numpy as jnp
from jax import lax
from jax.experimental import pallas as pl
from jax.experimental.pallas import tpu as pltpu
from jax.sharding import PartitionSpec as P

RANK = 256
RHS = 128
HALF = RANK // 2
QUARTER = HALF // 2
SYM = HALF + QUARTER
TOLERANCE = 1e-7
DIVERGED = 1e4
FIRST_FLOPS = 8e8
INVERT_FLOPS = 5e8
INVERT_SECOND = 9e8
MIDDLE_FLOPS = 0
CROSS_FLOPS = 0
THIRD_FLOPS = 1e9
VMEM_LIMIT = 40 * 2**20
STREAM_LIMIT = 52 * 2**20

SMEM = pl.BlockSpec(memory_space=pltpu.SMEM)
VMEM = pl.BlockSpec(memory_space=pltpu.VMEM)
HBM = pl.BlockSpec(memory_space=pltpu.HBM)
ANY = pl.BlockSpec(memory_space=pl.ANY)


def swap(value, axis, bit):
    mask = 2**bit
    pairs = [(source, source ^ mask) for source in range(lax.axis_size(axis))]
    return lax.ppermute(value, axis, pairs)


def struct(rows, cols=HALF):
    return jax.ShapeDtypeStruct((rows, cols), jnp.float32)


def cost(flops, floats):
    return pl.CostEstimate(flops=int(flops), bytes_accessed=int(4 * floats), transcendentals=0)


def split(value):
    high = value.astype(jnp.bfloat16)
    low = (value - high.astype(jnp.float32)).astype(jnp.bfloat16)
    return high, low


def dot_parts(left, right):
    first = jnp.concatenate([left[0], left[0], left[1]], axis=1)
    second = jnp.concatenate([right[0], right[1], right[0]], axis=0)
    return lax.dot_general(first, second, (((1,), (0,)), ((), ())), preferred_element_type=jnp.float32)


def dot(left, right):
    return dot_parts(split(left), split(right))


def dot_turned(left, right):
    return dot_parts([part.T for part in split(left)], split(right))


def in_order(core, own, other):
    first = core == 0
    return jnp.concatenate([jnp.where(first, own, other), jnp.where(first, other, own)], axis=1)


def symmetric(core, own, other):
    first = core == 0
    low = jnp.where(first, own, other)
    high = jnp.where(first, other, own)
    upper = jnp.concatenate([low[HALF:], high[HALF:]], axis=0)
    return jnp.concatenate(
        [jnp.concatenate([low[:HALF], upper], axis=1), jnp.concatenate([upper.T, high[:HALF]], axis=1)], axis=0
    )


def symmetric_half(core, value):
    first = core == 0
    return jnp.concatenate(
        [
            jnp.where(first, value[:HALF], value[HALF:]),
            jnp.where(first, value[HALF:].T[:QUARTER], value[QUARTER:HALF]),
        ],
        axis=0,
    )


def pack(value):
    whole = value.shape[1] // HALF
    units = [value[:, index * HALF : (index + 1) * HALF] for index in range(whole)]
    if value.shape[1] % HALF:
        tail = value[:, whole * HALF :]
        units.append(jnp.concatenate([tail[:HALF], tail[HALF:]], axis=1))
    return units


def unpack(ref):
    whole = ref.shape[0] // RANK
    parts = [ref[index * RANK : (index + 1) * RANK, :] for index in range(whole)]
    if ref.shape[0] % RANK:
        tail = ref[whole * RANK :, :]
        parts.append(jnp.concatenate([tail[:, :QUARTER], tail[:, QUARTER:]], axis=0))
    return jnp.concatenate(parts, axis=1) if len(parts) > 1 else parts[0]


def store(ref, value):
    start = 0
    for unit in pack(value):
        ref[start : start + unit.shape[0], :] = unit
        start += unit.shape[0]


def product_kernel(groups, chunks, core_ref, gens_ref, solved_ref, *refs):
    gens, solved, total, sems = refs[-4:] if chunks > 1 else (None, None, refs[-1], None)
    refs = refs[:-4] if chunks > 1 else refs[:-1]
    outs = refs[-2 * len(groups) :]
    blocks, lefts, rights = needed(groups)
    rhs_ref = refs[0] if 3 in rights else None
    block = gens_ref.shape[1] // chunks
    copies = []
    for chunk in range(chunks if chunks > 1 else 0):
        rows = pl.ds(chunk * block, block)
        row = [(gens_ref.at[level, rows], gens.at[place, rows]) for place, level in enumerate(lefts)]
        row += [(solved_ref.at[level, rows], solved.at[place, rows]) for place, level in enumerate(rights) if level < 3]
        row = [pltpu.make_async_copy(*ends, sems.at[index, chunk]) for index, ends in enumerate(row)]
        for copy in row:
            copy.start()
        copies.append(row)
    places = {}
    for chunk in range(chunks):
        rows = pl.ds(chunk * block, block)
        for copy in copies[chunk] if chunks > 1 else ():
            copy.wait()
        right = {}
        for place, level in enumerate(rights):
            if level == 3:
                right[level] = split(rhs_ref[rows, :])
            else:
                right[level] = split(solved[place, rows, :] if chunks > 1 else solved_ref[level])
        left = []
        for place, level in enumerate(lefts):
            left.append([part.T for part in split(gens[place, rows, :] if chunks > 1 else gens_ref[level])])
        start = 0
        for firsts, seconds in blocks:
            value = dot_parts(
                [jnp.concatenate([left[lefts.index(level)][half] for level in firsts], axis=0) for half in (0, 1)],
                [jnp.concatenate([right[level][half] for level in seconds], axis=1) for half in (0, 1)],
            )
            cols = slice(start, start + value.shape[1])
            if chunk == 0:
                total[: value.shape[0], cols] = value
            else:
                total[: value.shape[0], cols] += value
            for level in seconds:
                for place, first in enumerate(firsts):
                    places[first, level] = (place * RANK, start)
                start += width_of(level)
    first = core_ref[0] == 0
    for index, group in enumerate(groups):
        keep_ref, send_ref = outs[2 * index : 2 * index + 2]
        start = 0
        for pair in group:
            row, at = places[pair]
            value = total[row : row + RANK, at : at + width_of(pair[1])]
            if pair[0] == pair[1]:
                low = jnp.concatenate([value[:HALF, :HALF], value[:QUARTER, HALF:]], axis=0)
                high = jnp.concatenate([value[HALF:, HALF:], value[QUARTER:HALF, HALF:]], axis=0)
            elif pair[1] < 3:
                low = value[:, :HALF]
                high = value[:, HALF:]
            else:
                low = jnp.concatenate([value[:HALF, :QUARTER], value[HALF:, :QUARTER]], axis=1)
                high = jnp.concatenate([value[:HALF, QUARTER:], value[HALF:, QUARTER:]], axis=1)
            rows = slice(start, start + low.shape[0])
            keep_ref[rows, :] = jnp.where(first, low, high)
            send_ref[rows, :] = jnp.where(first, high, low)
            start += low.shape[0]


def rows_of(pair):
    return SYM if pair[0] == pair[1] else HALF if pair[1] == 3 else RANK


def width_of(level):
    return RHS if level == 3 else RANK


def needed(groups):
    pairs = sorted(pair for group in groups for pair in group)
    rights = sorted({right for _, right in pairs})
    blocks = {}
    for right in rights:
        blocks.setdefault(tuple(left for left, other in pairs if other == right), []).append(right)
    return list(blocks.items()), sorted({left for left, _ in pairs}), rights


def products(core, generators, solved_gens, rhs, groups, chunks, *after):
    rows = rhs.shape[0]
    blocks, lefts, rights = needed(groups)
    width = sum(width_of(right) for right in rights)
    height = max(len(firsts) for firsts, _ in blocks) * RANK
    flops = sum(len(firsts) * width_of(right) for firsts, seconds in blocks for right in seconds) * 6 * rows * RANK
    outs = [struct(sum(rows_of(pair) for pair in group)) for group in groups for _ in range(2)]
    held = sum(level < 3 for level in rights)
    scratch = [pltpu.VMEM((height, width), jnp.float32)]
    if chunks > 1:
        scratch = [
            pltpu.VMEM((len(lefts), rows, RANK), jnp.float32),
            pltpu.VMEM((held, rows, RANK), jnp.float32),
            *scratch,
            pltpu.SemaphoreType.DMA((len(lefts) + held, chunks)),
        ]
    given, specs = [generators, solved_gens], [HBM if chunks > 1 else VMEM] * 2
    if 3 in rights:
        given, specs = given + [rhs], specs + [VMEM]
    return pl.pallas_call(
        functools.partial(product_kernel, groups, chunks),
        in_specs=[SMEM] + specs + [ANY] * len(after),
        out_specs=[VMEM] * len(outs),
        out_shape=outs,
        scratch_shapes=scratch,
        compiler_params=pltpu.CompilerParams(vmem_limit_bytes=STREAM_LIMIT if chunks > 1 else VMEM_LIMIT),
        cost_estimate=cost(flops, rows * (len(lefts) * RANK + width)),
    )(core, *given, *after)


def square_norm(value):
    return jnp.sum(value * value)


def identity():
    row = lax.broadcasted_iota(jnp.int32, (RANK, RANK), 0)
    col = lax.broadcasted_iota(jnp.int32, (RANK, RANK), 1)
    return jnp.where(row == col, 1.0, 0.0)


def doubled(power, values):
    power = split(power)
    right = [jnp.concatenate(parts, axis=1) for parts in zip(power, split(values))]
    both = dot_parts(power, right)
    return both[:, :RANK], values + both[:, RANK:]


def series(start, values, power_ref, sum_ref):
    if values is None:
        power, values = dot(start, start), identity() + start
    else:
        power, values = doubled(start, values)
    for _ in range(2):
        power, values = doubled(power, values)
    norm = square_norm(power)
    power_ref[...] = power
    sum_ref[...] = values + dot(power, values)

    def proceed(state):
        count, bound = state
        return (count < 60) & (bound > TOLERANCE) & (bound < DIVERGED * DIVERGED)

    def body(state):
        count, _ = state
        power = dot(power_ref[...], power_ref[...])
        power_ref[...] = power
        sum_ref[...] = sum_ref[...] + dot(power, sum_ref[...])
        return count + 1, square_norm(power)

    return lax.while_loop(proceed, body, (jnp.int32(0), norm))[1]


def solve_series(product, values, power_ref, sum_ref):
    bound = series(product, values, power_ref, sum_ref)

    @pl.when(jnp.logical_not(bound <= TOLERANCE))
    def _():
        scale = 1.0 / (1.0 + jnp.sqrt(square_norm(product)))
        series((1.0 - scale) * identity() + scale * product, values, power_ref, sum_ref)
        sum_ref[...] = scale * sum_ref[...]


def invert_kernel(core_ref, own_ref, sib_ref, own_other_ref, sib_other_ref, tail_ref, inverse_ref, product_ref, power):
    core = core_ref[0]
    p_own = symmetric(core, own_ref[:SYM, :], own_other_ref[:SYM, :])
    p_sib = symmetric(core, sib_ref[:SYM, :], sib_other_ref[...])
    both = dot(p_sib, jnp.concatenate([p_own, own_ref[SYM:, :], unpack(tail_ref)], axis=1))
    product_ref[...] = both[:, RANK:]
    solve_series(both[:, :RANK], None, power, inverse_ref)


def invert_second_kernel(
    core_ref, own_ref, sib_ref, own_other_ref, sib_other_ref, r_own_ref, r_own_other_ref,
    inverse_ref, product_ref, turned_ref, power,
):
    core = core_ref[0]
    p_own = symmetric(core, own_ref[...], own_other_ref[...])
    p_sib = symmetric(core, sib_ref[...], sib_other_ref[...])
    both = dot(p_sib, jnp.concatenate([p_own, unpack(r_own_ref)], axis=1))
    product_ref[...] = both[:, RANK:]
    turned_ref[:RANK, :] = p_own
    turned_ref[RANK:, :] = in_order(core, r_own_ref[:RANK, :], r_own_other_ref[...]).T
    solve_series(both[:, :RANK], None, power, inverse_ref)


def call(kernel, out_shape, flops, *values, after=(), scratch=()):
    many = isinstance(out_shape, (list, tuple))
    floats = sum(value.size for value in values) + sum(out.size for out in (out_shape if many else [out_shape]))
    return pl.pallas_call(
        kernel,
        in_specs=[SMEM] + [VMEM] * (len(values) - 1) + [ANY] * len(after),
        out_specs=[VMEM] * len(out_shape) if many else VMEM,
        out_shape=out_shape,
        scratch_shapes=[pltpu.VMEM(shape, jnp.float32) for shape in scratch],
        compiler_params=pltpu.CompilerParams(vmem_limit_bytes=VMEM_LIMIT),
        cost_estimate=cost(flops, floats),
    )(*values, *after)


def first_kernel(core_ref, inverse_ref, product_ref, head_ref, head_sib_ref, head_other_ref, tail_sib_ref, z_ref, out_ref):
    core = core_ref[0]
    sib = jnp.concatenate([head_sib_ref[SYM:, :], unpack(tail_sib_ref)], axis=1)
    z = dot(inverse_ref[...], sib - product_ref[...])
    store(z_ref, z)
    value = dot_turned(in_order(core, head_ref[SYM:, :], head_other_ref[SYM:, :]), z)
    out_ref[:SYM, :] = symmetric_half(core, value[:, :HALF])
    store(out_ref.at[SYM:], value[:, HALF:])


def last_parts(core, crossed, z):
    return lost_parts(core, dot_turned(crossed, z))


def lost_parts(core, value):
    return jnp.concatenate([symmetric_half(core, value[:, :HALF]), *pack(value[:, HALF:])], axis=0)


def third_kernel(core_ref, own_ref, own_other_ref, z_ref, *refs):
    core = core_ref[0]
    crossed = in_order(core, own_ref[:RANK, :], own_other_ref[...])
    refs[-1][...] = last_parts(core, crossed, unpack(z_ref.at[RANK:]))


def middle_kernel(core_ref, inverse_ref, product_ref, turned_ref, own_ref, sib_ref, z_ref, z_sib_ref, out_ref):
    core = core_ref[0]
    z = dot(inverse_ref[...], unpack(sib_ref) - product_ref[...])
    store(z_ref, z)
    value = dot(turned_ref[...], z)
    store(z_sib_ref, unpack(own_ref) - value[:RANK])
    out_ref[...] = lost_parts(core, value[RANK:])


def cross_kernel(core_ref, sib_ref, sib_other_ref, z_sib_ref, crossed_ref, out_ref):
    core = core_ref[0]
    crossed = in_order(core, sib_ref[...], sib_other_ref[...])
    out_ref[...] = crossed_ref[...] + last_parts(core, crossed, unpack(z_sib_ref))


def rhs_in_order(core, own, other):
    first = core == 0
    low = jnp.where(first, own, other)
    high = jnp.where(first, other, own)
    top = jnp.concatenate([low[:, :QUARTER], high[:, :QUARTER]], axis=1)
    bottom = jnp.concatenate([low[:, QUARTER:], high[:, QUARTER:]], axis=1)
    return jnp.concatenate([top, bottom], axis=0)


def reduced_kernel(
    core_ref, z1_ref, z1_other_ref, z0_ref, z0_other_ref, solved_ref, rhs_ref, high_ref, low_ref, out_ref
):
    core = core_ref[0]
    z12 = in_order(core, z1_ref[:RANK, :], z1_other_ref[:RANK, :])
    z1x = rhs_in_order(core, z1_ref[RANK:, :], z1_other_ref[RANK:, :])
    z01 = in_order(core, z0_ref[:RANK, :], z0_other_ref[:RANK, :])
    z02 = in_order(core, z0_ref[RANK : 2 * RANK, :], z0_other_ref[RANK : 2 * RANK, :])
    z0x = rhs_in_order(core, z0_ref[2 * RANK :, :], z0_other_ref[2 * RANK :, :])
    middle = jnp.concatenate([z12, z1x], axis=1)
    first = jnp.concatenate([z02, z0x], axis=1) - dot(z01, middle)
    coefs = jnp.concatenate([first, middle], axis=0)
    value = dot(jnp.concatenate([solved_ref[0], solved_ref[1]], axis=1), coefs)
    high, low = split(solved_ref[2] - value[:, :RANK])
    high_ref[...] = high
    low_ref[...] = low
    out_ref[...] = rhs_ref[...] - value[:, RANK:]


def keep_kernel(core_ref, value_ref, *refs):
    refs[-1][...] = value_ref[...]


def add_kernel(core_ref, first_ref, second_ref, *refs):
    refs[-1][...] = first_ref[...] + second_ref[...]


def subtract_kernel(core_ref, first_ref, second_ref, *refs):
    refs[-1][...] = first_ref[...] - second_ref[...]


def final_kernel(
    core_ref, own_ref, own_other_ref, sib_ref, sib_other_ref, high_ref, low_ref, rhs_ref, out_ref, power, total, out, sems
):
    core = core_ref[0]
    p_own = symmetric(core, own_ref[:SYM, :], own_other_ref[:SYM, :])
    p_sib = symmetric(core, sib_ref[:SYM, :], sib_other_ref[:SYM, :])
    own = rhs_in_order(core, own_ref[SYM:, :], own_other_ref[SYM:, :])
    sib = rhs_in_order(core, sib_ref[SYM:, :], sib_other_ref[SYM:, :])
    both = dot(p_sib, jnp.concatenate([p_own, own], axis=1))
    solve_series(both[:, :RANK], sib - both[:, RANK:], power, total)
    z = split(total[...])
    blocks = sems.shape[0]
    block = out.shape[0] // blocks
    copies = []
    for index in range(blocks):
        rows = pl.ds(index * block, block)
        out[rows, :] = rhs_ref[rows, :] - dot_parts((high_ref[rows, :], low_ref[rows, :]), z)
        copies.append(pltpu.make_async_copy(out.at[rows], out_ref.at[rows], sems.at[index]))
        copies[-1].start()
    for copy in copies:
        copy.wait()


def on_device(rhs, generators, solved_gens):
    groups = lax.axis_size("rows")
    sub_bits = lax.axis_size("sub").bit_length() - 1
    span_bits = (groups // 8).bit_length() - 1
    core = (lax.axis_index("sub") % 2).astype(jnp.int32).reshape(1)
    flops = 6 * RANK * RANK * HALF
    last = SYM + HALF

    def over_child(value):
        for bit in range(1, sub_bits):
            value = value + swap(value, "sub", bit)
        for bit in range(span_bits):
            value = value + swap(value, "rows", bit)
        return value

    keep, send = products(core, generators, solved_gens, rhs, (((0, 0), (0, 1)),), 4)
    head = keep + swap(send, "sub", 0)
    token = swap(call(keep_kernel, struct(8), 0, core, send[:8], after=(head,)), "sub", 0)
    parts = products(core, generators, solved_gens, rhs, (((0, 2), (0, 3)),), 1, token)
    rest = (((1, 1), (1, 2), (1, 3)), ((2, 2), (2, 3)))
    parts += products(core, generators, solved_gens, rhs, rest, 1, parts[1])
    parts = [(keep, swap(send, "sub", 0)) for keep, send in zip(parts[::2], parts[1::2])]
    head = over_child(head)
    tail = over_child(parts[0][0] + parts[0][1])
    third = parts[2][0] + parts[2][1]
    token = swap(call(keep_kernel, struct(8), 0, core, third[:8]), "sub", 0)
    near = over_child(call(add_kernel, struct(SYM + RANK + HALF), 0, core, *parts[1], after=(token,)))

    head_sib = swap(head, "rows", span_bits)
    tail_sib = swap(tail, "rows", span_bits)
    head_other = swap(head, "sub", 0)
    tail_other = swap(tail[:RANK], "sub", 0)
    p_sib_other = swap(head_sib[:SYM], "sub", 0)
    inverted, product = call(
        invert_kernel, [struct(RANK, RANK), struct(RANK, 2 * HALF + QUARTER)], INVERT_FLOPS,
        core, head, head_sib, head_other, p_sib_other, tail, scratch=((RANK, RANK),),
    )
    z0, crossed = call(
        first_kernel, [struct(2 * RANK + HALF), struct(SYM + RANK + HALF)], FIRST_FLOPS,
        core, inverted, product, head, head_sib, head_other, tail_sib,
    )
    p_own = call(subtract_kernel, struct(SYM), 0, core, near[:SYM], crossed[:SYM])
    r_own = call(subtract_kernel, struct(RANK + HALF), 0, core, near[SYM:], crossed[SYM:], after=(p_own,))
    third = over_child(
        call(add_kernel, struct(last), 0, core, third, swap(third, "rows", span_bits + 1), after=(r_own,))
    )
    crossed = call(third_kernel, struct(last), THIRD_FLOPS, core, tail, tail_other, z0, after=(r_own,))
    third = third - (crossed + swap(crossed, "rows", span_bits + 1))
    third = third + swap(third, "rows", span_bits)

    p_own = p_own + swap(p_own, "rows", span_bits)
    r_own = r_own + swap(r_own, "rows", span_bits)
    p_sib = swap(p_own, "rows", span_bits + 1)
    r_sib = swap(r_own, "rows", span_bits + 1)
    p_own_other = swap(p_own, "sub", 0)
    r_own_other = swap(r_own[:RANK], "sub", 0)
    p_sib_other = swap(p_sib, "sub", 0)
    width = HALF + QUARTER
    inverted, product, turned = call(
        invert_second_kernel, [struct(RANK, RANK), struct(RANK, width), struct(2 * RANK, RANK)], INVERT_SECOND,
        core, p_own, p_sib, p_own_other, p_sib_other, r_own, r_own_other, scratch=((RANK, RANK),),
    )
    cross_sib = call(keep_kernel, struct(RANK), 0, core, r_sib[:RANK], after=(inverted,))
    z1, z_sib, crossed = call(
        middle_kernel, [struct(RANK + HALF), struct(RANK + HALF), struct(last)], MIDDLE_FLOPS,
        core, inverted, product, turned, r_own, r_sib,
    )
    crossed = call(cross_kernel, struct(last), CROSS_FLOPS, core, cross_sib, swap(cross_sib, "sub", 0), z_sib, crossed)

    own = third - crossed
    sib = swap(own, "rows", span_bits + 2)
    z1_other = swap(call(keep_kernel, struct(RANK + HALF), 0, core, z1, after=(own,)), "sub", 0)
    part = jax.ShapeDtypeStruct((rhs.shape[0], RANK), jnp.bfloat16)
    high, low, current = call(
        reduced_kernel, [part, part, struct(rhs.shape[0], RHS)], 6 * rhs.shape[0] * 2 * RANK * (RANK + RHS),
        core, z1, z1_other, z0, swap(z0, "sub", 0), solved_gens, rhs,
    )
    sib = call(keep_kernel, struct(last), 0, core, sib, after=(high,))
    own_other, sib_other = swap(own, "sub", 0), swap(sib, "sub", 0)
    rows = rhs.shape[0]
    small = (own, own_other, sib, sib_other, high, low, current)
    return pl.pallas_call(
        final_kernel,
        in_specs=[SMEM] + [VMEM] * len(small),
        out_specs=HBM,
        out_shape=struct(rows, RHS),
        scratch_shapes=[
            pltpu.VMEM((RANK, RANK), jnp.float32),
            pltpu.VMEM((RANK, RHS), jnp.float32),
            pltpu.VMEM((rows, RHS), jnp.float32),
            pltpu.SemaphoreType.DMA((2,)),
        ],
        compiler_params=pltpu.CompilerParams(vmem_limit_bytes=VMEM_LIMIT),
        cost_estimate=cost(6 * rows * RANK * RHS + 6 * 9 * RANK**3, 3 * rows * RANK),
    )(core, *small)


def solution(mesh):
    placed = (
        P(("rows", "sub"), None),
        P(None, ("rows", "sub"), None),
        P(None, ("rows", "sub"), None),
    )
    return jax.shard_map(
        on_device, mesh=mesh, in_specs=placed, out_specs=P(("rows", "sub"), None), check_vma=False
    )
```

```python
import functools

import jax
import jax.numpy as jnp
from jax import lax
from jax.experimental import pallas as pl
from jax.experimental.pallas import tpu as pltpu
from jax.sharding import PartitionSpec as P

RANK = 256
RHS = 128
HALF = RANK // 2
QUARTER = HALF // 2
SYM = HALF + QUARTER
TOLERANCE = 1e-7
DIVERGED = 1e4
FIRST_FLOPS = 6.5e8
INVERT_FLOPS = 9e8
INVERT_SECOND = 9e8
MIDDLE_FLOPS = 0
CROSS_FLOPS = 0
THIRD_FLOPS = 1e9
VMEM_LIMIT = 40 * 2**20
STREAM_LIMIT = 52 * 2**20

SMEM = pl.BlockSpec(memory_space=pltpu.SMEM)
VMEM = pl.BlockSpec(memory_space=pltpu.VMEM)
HBM = pl.BlockSpec(memory_space=pltpu.HBM)
ANY = pl.BlockSpec(memory_space=pl.ANY)


def swap(value, axis, bit):
    mask = 2**bit
    pairs = [(source, source ^ mask) for source in range(lax.axis_size(axis))]
    return lax.ppermute(value, axis, pairs)


def struct(rows, cols=HALF):
    return jax.ShapeDtypeStruct((rows, cols), jnp.float32)


def cost(flops, floats):
    return pl.CostEstimate(flops=int(flops), bytes_accessed=int(4 * floats), transcendentals=0)


def split(value):
    high = value.astype(jnp.bfloat16)
    low = (value - high.astype(jnp.float32)).astype(jnp.bfloat16)
    return high, low


def dot_parts(left, right):
    first = jnp.concatenate([left[0], left[0], left[1]], axis=1)
    second = jnp.concatenate([right[0], right[1], right[0]], axis=0)
    return lax.dot_general(first, second, (((1,), (0,)), ((), ())), preferred_element_type=jnp.float32)


def dot(left, right):
    return dot_parts(split(left), split(right))


def dot_turned(left, right):
    return dot_parts([part.T for part in split(left)], split(right))


def in_order(core, own, other):
    first = core == 0
    return jnp.concatenate([jnp.where(first, own, other), jnp.where(first, other, own)], axis=1)


def symmetric(core, own, other):
    first = core == 0
    low = jnp.where(first, own, other)
    high = jnp.where(first, other, own)
    upper = jnp.concatenate([low[HALF:], high[HALF:]], axis=0)
    return jnp.concatenate(
        [jnp.concatenate([low[:HALF], upper], axis=1), jnp.concatenate([upper.T, high[:HALF]], axis=1)], axis=0
    )


def symmetric_half(core, value):
    first = core == 0
    return jnp.concatenate(
        [
            jnp.where(first, value[:HALF], value[HALF:]),
            jnp.where(first, value[HALF:].T[:QUARTER], value[QUARTER:HALF]),
        ],
        axis=0,
    )


def pack(value):
    whole = value.shape[1] // HALF
    units = [value[:, index * HALF : (index + 1) * HALF] for index in range(whole)]
    if value.shape[1] % HALF:
        tail = value[:, whole * HALF :]
        units.append(jnp.concatenate([tail[:HALF], tail[HALF:]], axis=1))
    return units


def unpack(ref):
    whole = ref.shape[0] // RANK
    parts = [ref[index * RANK : (index + 1) * RANK, :] for index in range(whole)]
    if ref.shape[0] % RANK:
        tail = ref[whole * RANK :, :]
        parts.append(jnp.concatenate([tail[:, :QUARTER], tail[:, QUARTER:]], axis=0))
    return jnp.concatenate(parts, axis=1) if len(parts) > 1 else parts[0]


def store(ref, value):
    start = 0
    for unit in pack(value):
        ref[start : start + unit.shape[0], :] = unit
        start += unit.shape[0]


def product_kernel(groups, chunks, core_ref, gens_ref, solved_ref, *refs):
    gens, solved, total, sems = refs[-4:] if chunks > 1 else (None, None, refs[-1], None)
    refs = refs[:-4] if chunks > 1 else refs[:-1]
    outs = refs[-2 * len(groups) :]
    blocks, lefts, rights = needed(groups)
    rhs_ref = refs[0] if 3 in rights else None
    block = gens_ref.shape[1] // chunks
    copies = []
    for chunk in range(chunks if chunks > 1 else 0):
        rows = pl.ds(chunk * block, block)
        row = [(gens_ref.at[level, rows], gens.at[place, rows]) for place, level in enumerate(lefts)]
        row += [(solved_ref.at[level, rows], solved.at[place, rows]) for place, level in enumerate(rights) if level < 3]
        row = [pltpu.make_async_copy(*ends, sems.at[index, chunk]) for index, ends in enumerate(row)]
        for copy in row:
            copy.start()
        copies.append(row)
    places = {}
    for chunk in range(chunks):
        rows = pl.ds(chunk * block, block)
        for copy in copies[chunk] if chunks > 1 else ():
            copy.wait()
        right = {}
        for place, level in enumerate(rights):
            if level == 3:
                right[level] = split(rhs_ref[rows, :])
            else:
                right[level] = split(solved[place, rows, :] if chunks > 1 else solved_ref[level])
        left = []
        for place, level in enumerate(lefts):
            left.append([part.T for part in split(gens[place, rows, :] if chunks > 1 else gens_ref[level])])
        start = 0
        for firsts, seconds in blocks:
            value = dot_parts(
                [jnp.concatenate([left[lefts.index(level)][half] for level in firsts], axis=0) for half in (0, 1)],
                [jnp.concatenate([right[level][half] for level in seconds], axis=1) for half in (0, 1)],
            )
            cols = slice(start, start + value.shape[1])
            if chunk == 0:
                total[: value.shape[0], cols] = value
            else:
                total[: value.shape[0], cols] += value
            for level in seconds:
                for place, first in enumerate(firsts):
                    places[first, level] = (place * RANK, start)
                start += width_of(level)
    first = core_ref[0] == 0
    for index, group in enumerate(groups):
        keep_ref, send_ref = outs[2 * index : 2 * index + 2]
        start = 0
        for pair in group:
            row, at = places[pair]
            value = total[row : row + RANK, at : at + width_of(pair[1])]
            if pair[0] == pair[1]:
                low = jnp.concatenate([value[:HALF, :HALF], value[:QUARTER, HALF:]], axis=0)
                high = jnp.concatenate([value[HALF:, HALF:], value[QUARTER:HALF, HALF:]], axis=0)
            elif pair[1] < 3:
                low = value[:, :HALF]
                high = value[:, HALF:]
            else:
                low = jnp.concatenate([value[:HALF, :QUARTER], value[HALF:, :QUARTER]], axis=1)
                high = jnp.concatenate([value[:HALF, QUARTER:], value[HALF:, QUARTER:]], axis=1)
            rows = slice(start, start + low.shape[0])
            keep_ref[rows, :] = jnp.where(first, low, high)
            send_ref[rows, :] = jnp.where(first, high, low)
            start += low.shape[0]


def rows_of(pair):
    return SYM if pair[0] == pair[1] else HALF if pair[1] == 3 else RANK


def width_of(level):
    return RHS if level == 3 else RANK


def needed(groups):
    pairs = sorted(pair for group in groups for pair in group)
    rights = sorted({right for _, right in pairs})
    blocks = {}
    for right in rights:
        blocks.setdefault(tuple(left for left, other in pairs if other == right), []).append(right)
    return list(blocks.items()), sorted({left for left, _ in pairs}), rights


def products(core, generators, solved_gens, rhs, groups, chunks, *after):
    rows = rhs.shape[0]
    blocks, lefts, rights = needed(groups)
    width = sum(width_of(right) for right in rights)
    height = max(len(firsts) for firsts, _ in blocks) * RANK
    flops = sum(len(firsts) * width_of(right) for firsts, seconds in blocks for right in seconds) * 6 * rows * RANK
    outs = [struct(sum(rows_of(pair) for pair in group)) for group in groups for _ in range(2)]
    held = sum(level < 3 for level in rights)
    scratch = [pltpu.VMEM((height, width), jnp.float32)]
    if chunks > 1:
        scratch = [
            pltpu.VMEM((len(lefts), rows, RANK), jnp.float32),
            pltpu.VMEM((held, rows, RANK), jnp.float32),
            *scratch,
            pltpu.SemaphoreType.DMA((len(lefts) + held, chunks)),
        ]
    given, specs = [generators, solved_gens], [HBM if chunks > 1 else VMEM] * 2
    if 3 in rights:
        given, specs = given + [rhs], specs + [VMEM]
    return pl.pallas_call(
        functools.partial(product_kernel, groups, chunks),
        in_specs=[SMEM] + specs + [ANY] * len(after),
        out_specs=[VMEM] * len(outs),
        out_shape=outs,
        scratch_shapes=scratch,
        compiler_params=pltpu.CompilerParams(vmem_limit_bytes=STREAM_LIMIT if chunks > 1 else VMEM_LIMIT),
        cost_estimate=cost(flops, rows * (len(lefts) * RANK + width)),
    )(core, *given, *after)


def square_norm(value):
    return jnp.sum(value * value)


def identity():
    row = lax.broadcasted_iota(jnp.int32, (RANK, RANK), 0)
    col = lax.broadcasted_iota(jnp.int32, (RANK, RANK), 1)
    return jnp.where(row == col, 1.0, 0.0)


def doubled(power, values):
    power = split(power)
    right = [jnp.concatenate(parts, axis=1) for parts in zip(power, split(values))]
    both = dot_parts(power, right)
    return both[:, :RANK], values + both[:, RANK:]


def series(start, values, power_ref, sum_ref):
    if values is None:
        power, values = dot(start, start), identity() + start
    else:
        power, values = doubled(start, values)
    for _ in range(2):
        power, values = doubled(power, values)
    norm = square_norm(power)
    power_ref[...] = power
    sum_ref[...] = values + dot(power, values)

    def proceed(state):
        count, bound = state
        return (count < 60) & (bound > TOLERANCE) & (bound < DIVERGED * DIVERGED)

    def body(state):
        count, _ = state
        power = dot(power_ref[...], power_ref[...])
        power_ref[...] = power
        sum_ref[...] = sum_ref[...] + dot(power, sum_ref[...])
        return count + 1, square_norm(power)

    return lax.while_loop(proceed, body, (jnp.int32(0), norm))[1]


def solve_series(product, values, power_ref, sum_ref):
    bound = series(product, values, power_ref, sum_ref)

    @pl.when(jnp.logical_not(bound <= TOLERANCE))
    def _():
        scale = 1.0 / (1.0 + jnp.sqrt(square_norm(product)))
        series((1.0 - scale) * identity() + scale * product, values, power_ref, sum_ref)
        sum_ref[...] = scale * sum_ref[...]


def invert_kernel(core_ref, own_ref, sib_ref, own_other_ref, sib_other_ref, tail_ref, inverse_ref, product_ref, power):
    core = core_ref[0]
    p_own = symmetric(core, own_ref[:SYM, :], own_other_ref[:SYM, :])
    p_sib = symmetric(core, sib_ref[:SYM, :], sib_other_ref[...])
    both = dot(p_sib, jnp.concatenate([p_own, own_ref[SYM:, :], unpack(tail_ref)], axis=1))
    product_ref[...] = both[:, RANK:]
    solve_series(both[:, :RANK], None, power, inverse_ref)


def invert_second_kernel(
    core_ref, own_ref, sib_ref, own_other_ref, sib_other_ref, r_own_ref, r_own_other_ref,
    inverse_ref, product_ref, turned_ref, power,
):
    core = core_ref[0]
    p_own = symmetric(core, own_ref[...], own_other_ref[...])
    p_sib = symmetric(core, sib_ref[...], sib_other_ref[...])
    both = dot(p_sib, jnp.concatenate([p_own, unpack(r_own_ref)], axis=1))
    product_ref[...] = both[:, RANK:]
    turned_ref[:RANK, :] = p_own
    turned_ref[RANK:, :] = in_order(core, r_own_ref[:RANK, :], r_own_other_ref[...]).T
    solve_series(both[:, :RANK], None, power, inverse_ref)


def call(kernel, out_shape, flops, *values, after=(), scratch=()):
    many = isinstance(out_shape, (list, tuple))
    floats = sum(value.size for value in values) + sum(out.size for out in (out_shape if many else [out_shape]))
    return pl.pallas_call(
        kernel,
        in_specs=[SMEM] + [VMEM] * (len(values) - 1) + [ANY] * len(after),
        out_specs=[VMEM] * len(out_shape) if many else VMEM,
        out_shape=out_shape,
        scratch_shapes=[pltpu.VMEM(shape, jnp.float32) for shape in scratch],
        compiler_params=pltpu.CompilerParams(vmem_limit_bytes=VMEM_LIMIT),
        cost_estimate=cost(flops, floats),
    )(*values, *after)


def first_kernel(core_ref, inverse_ref, product_ref, head_ref, head_sib_ref, head_other_ref, tail_sib_ref, z_ref, out_ref):
    core = core_ref[0]
    sib = jnp.concatenate([head_sib_ref[SYM:, :], unpack(tail_sib_ref)], axis=1)
    z = dot(inverse_ref[...], sib - product_ref[...])
    store(z_ref, z)
    value = dot_turned(in_order(core, head_ref[SYM:, :], head_other_ref[SYM:, :]), z)
    out_ref[:SYM, :] = symmetric_half(core, value[:, :HALF])
    store(out_ref.at[SYM:], value[:, HALF:])


def last_parts(core, crossed, z):
    return lost_parts(core, dot_turned(crossed, z))


def lost_parts(core, value):
    return jnp.concatenate([symmetric_half(core, value[:, :HALF]), *pack(value[:, HALF:])], axis=0)


def third_kernel(core_ref, own_ref, own_other_ref, z_ref, *refs):
    core = core_ref[0]
    crossed = in_order(core, own_ref[:RANK, :], own_other_ref[...])
    refs[-1][...] = last_parts(core, crossed, unpack(z_ref.at[RANK:]))


def middle_kernel(core_ref, inverse_ref, product_ref, turned_ref, own_ref, sib_ref, z_ref, z_sib_ref, out_ref):
    core = core_ref[0]
    z = dot(inverse_ref[...], unpack(sib_ref) - product_ref[...])
    store(z_ref, z)
    value = dot(turned_ref[...], z)
    store(z_sib_ref, unpack(own_ref) - value[:RANK])
    out_ref[...] = lost_parts(core, value[RANK:])


def cross_kernel(core_ref, sib_ref, sib_other_ref, z_sib_ref, crossed_ref, out_ref):
    core = core_ref[0]
    crossed = in_order(core, sib_ref[...], sib_other_ref[...])
    out_ref[...] = crossed_ref[...] + last_parts(core, crossed, unpack(z_sib_ref))


def rhs_in_order(core, own, other):
    first = core == 0
    low = jnp.where(first, own, other)
    high = jnp.where(first, other, own)
    top = jnp.concatenate([low[:, :QUARTER], high[:, :QUARTER]], axis=1)
    bottom = jnp.concatenate([low[:, QUARTER:], high[:, QUARTER:]], axis=1)
    return jnp.concatenate([top, bottom], axis=0)


def reduced_kernel(
    core_ref, z1_ref, z1_other_ref, z0_ref, z0_other_ref, solved_ref, rhs_ref, high_ref, low_ref, out_ref
):
    core = core_ref[0]
    z12 = in_order(core, z1_ref[:RANK, :], z1_other_ref[:RANK, :])
    z1x = rhs_in_order(core, z1_ref[RANK:, :], z1_other_ref[RANK:, :])
    z01 = in_order(core, z0_ref[:RANK, :], z0_other_ref[:RANK, :])
    z02 = in_order(core, z0_ref[RANK : 2 * RANK, :], z0_other_ref[RANK : 2 * RANK, :])
    z0x = rhs_in_order(core, z0_ref[2 * RANK :, :], z0_other_ref[2 * RANK :, :])
    middle = jnp.concatenate([z12, z1x], axis=1)
    first = jnp.concatenate([z02, z0x], axis=1) - dot(z01, middle)
    coefs = jnp.concatenate([first, middle], axis=0)
    value = dot(jnp.concatenate([solved_ref[0], solved_ref[1]], axis=1), coefs)
    high, low = split(solved_ref[2] - value[:, :RANK])
    high_ref[...] = high
    low_ref[...] = low
    out_ref[...] = rhs_ref[...] - value[:, RANK:]


def keep_kernel(core_ref, value_ref, *refs):
    refs[-1][...] = value_ref[...]


def join_kernel(core_ref, first_ref, second_ref, *refs):
    rows = first_ref.shape[0]
    refs[-1][:rows, :] = first_ref[...]
    refs[-1][rows:, :] = second_ref[...]


def add_kernel(core_ref, first_ref, second_ref, *refs):
    refs[-1][...] = first_ref[...] + second_ref[...]


def subtract_kernel(core_ref, first_ref, second_ref, *refs):
    refs[-1][...] = first_ref[...] - second_ref[...]


def final_kernel(
    core_ref, own_ref, own_other_ref, sib_ref, sib_other_ref, high_ref, low_ref, rhs_ref, out_ref, power, total, out, sems
):
    core = core_ref[0]
    p_own = symmetric(core, own_ref[:SYM, :], own_other_ref[:SYM, :])
    p_sib = symmetric(core, sib_ref[:SYM, :], sib_other_ref[:SYM, :])
    own = rhs_in_order(core, own_ref[SYM:, :], own_other_ref[SYM:, :])
    sib = rhs_in_order(core, sib_ref[SYM:, :], sib_other_ref[SYM:, :])
    both = dot(p_sib, jnp.concatenate([p_own, own], axis=1))
    solve_series(both[:, :RANK], sib - both[:, RANK:], power, total)
    z = split(total[...])
    blocks = sems.shape[0]
    block = out.shape[0] // blocks
    copies = []
    for index in range(blocks):
        rows = pl.ds(index * block, block)
        out[rows, :] = rhs_ref[rows, :] - dot_parts((high_ref[rows, :], low_ref[rows, :]), z)
        copies.append(pltpu.make_async_copy(out.at[rows], out_ref.at[rows], sems.at[index]))
        copies[-1].start()
    for copy in copies:
        copy.wait()


def on_device(rhs, generators, solved_gens):
    groups = lax.axis_size("rows")
    sub_bits = lax.axis_size("sub").bit_length() - 1
    span_bits = (groups // 8).bit_length() - 1
    core = (lax.axis_index("sub") % 2).astype(jnp.int32).reshape(1)
    flops = 6 * RANK * RANK * HALF
    last = SYM + HALF

    def over_child(value):
        for bit in range(1, sub_bits):
            value = value + swap(value, "sub", bit)
        for bit in range(span_bits):
            value = value + swap(value, "rows", bit)
        return value

    keep, send = products(core, generators, solved_gens, rhs, (((0, 0), (0, 1)),), 4)
    head = keep + swap(send, "sub", 0)
    token = swap(call(keep_kernel, struct(8), 0, core, send[:8], after=(head,)), "sub", 0)
    parts = products(core, generators, solved_gens, rhs, (((0, 2), (0, 3)),), 1, token)
    rest = (((1, 1), (1, 2), (1, 3)), ((2, 2), (2, 3)))
    parts += products(core, generators, solved_gens, rhs, rest, 1, parts[1])
    parts = [(keep, swap(send, "sub", 0)) for keep, send in zip(parts[::2], parts[1::2])]
    head = over_child(head)
    tail = over_child(parts[0][0] + parts[0][1])
    near = over_child(call(add_kernel, struct(SYM + RANK + HALF), 0, core, *parts[1], after=(tail,)))
    third = parts[2][0] + parts[2][1]

    head_sib = swap(head, "rows", span_bits)
    tail_sib = swap(tail, "rows", span_bits)
    head_other = swap(head, "sub", 0)
    tail_other = swap(tail[:RANK], "sub", 0)
    p_sib_other = swap(head_sib[:SYM], "sub", 0)
    inverted, product = call(
        invert_kernel, [struct(RANK, RANK), struct(RANK, 2 * HALF + QUARTER)], INVERT_FLOPS,
        core, head, head_sib, head_other, p_sib_other, tail, scratch=((RANK, RANK),),
    )
    z0, crossed = call(
        first_kernel, [struct(2 * RANK + HALF), struct(SYM + RANK + HALF)], FIRST_FLOPS,
        core, inverted, product, head, head_sib, head_other, tail_sib,
    )
    p_own = call(subtract_kernel, struct(SYM), 0, core, near[:SYM], crossed[:SYM])
    r_own = call(subtract_kernel, struct(RANK + HALF), 0, core, near[SYM:], crossed[SYM:], after=(p_own,))
    third = over_child(
        call(add_kernel, struct(last), 0, core, third, swap(third, "rows", span_bits + 1), after=(r_own,))
    )
    crossed = call(third_kernel, struct(last), THIRD_FLOPS, core, tail, tail_other, z0, after=(r_own,))
    third = third - (crossed + swap(crossed, "rows", span_bits + 1))
    third = third + swap(third, "rows", span_bits)

    p_own = p_own + swap(p_own, "rows", span_bits)
    r_own = r_own + swap(r_own, "rows", span_bits)
    p_sib = swap(p_own, "rows", span_bits + 1)
    r_sib = swap(r_own, "rows", span_bits + 1)
    p_own_other = swap(p_own, "sub", 0)
    r_own_other = swap(r_own[:RANK], "sub", 0)
    p_sib_other = swap(p_sib, "sub", 0)
    width = HALF + QUARTER
    inverted, product, turned = call(
        invert_second_kernel, [struct(RANK, RANK), struct(RANK, width), struct(2 * RANK, RANK)], INVERT_SECOND,
        core, p_own, p_sib, p_own_other, p_sib_other, r_own, r_own_other, scratch=((RANK, RANK),),
    )
    cross_sib = call(keep_kernel, struct(RANK), 0, core, r_sib[:RANK], after=(inverted,))
    z1, z_sib, crossed = call(
        middle_kernel, [struct(RANK + HALF), struct(RANK + HALF), struct(last)], MIDDLE_FLOPS,
        core, inverted, product, turned, r_own, r_sib,
    )
    crossed = call(cross_kernel, struct(last), CROSS_FLOPS, core, cross_sib, swap(cross_sib, "sub", 0), z_sib, crossed)

    own = third - crossed
    sib = swap(own, "rows", span_bits + 2)
    solved = swap(call(join_kernel, struct(3 * RANK + 2 * HALF), 0, core, z1, z0, after=(own,)), "sub", 0)
    z1_other, z0_other = solved[: RANK + HALF], solved[RANK + HALF :]
    part = jax.ShapeDtypeStruct((rhs.shape[0], RANK), jnp.bfloat16)
    high, low, current = call(
        reduced_kernel, [part, part, struct(rhs.shape[0], RHS)], 6 * rhs.shape[0] * 2 * RANK * (RANK + RHS),
        core, z1, z1_other, z0, z0_other, solved_gens, rhs,
    )
    sib = call(keep_kernel, struct(last), 0, core, sib, after=(high,))
    own_other, sib_other = swap(own, "sub", 0), swap(sib, "sub", 0)
    rows = rhs.shape[0]
    small = (own, own_other, sib, sib_other, high, low, current)
    return pl.pallas_call(
        final_kernel,
        in_specs=[SMEM] + [VMEM] * len(small),
        out_specs=HBM,
        out_shape=struct(rows, RHS),
        scratch_shapes=[
            pltpu.VMEM((RANK, RANK), jnp.float32),
            pltpu.VMEM((RANK, RHS), jnp.float32),
            pltpu.VMEM((rows, RHS), jnp.float32),
            pltpu.SemaphoreType.DMA((2,)),
        ],
        compiler_params=pltpu.CompilerParams(vmem_limit_bytes=VMEM_LIMIT),
        cost_estimate=cost(6 * rows * RANK * RHS + 6 * 9 * RANK**3, 3 * rows * RANK),
    )(core, *small)


def solution(mesh):
    placed = (
        P(("rows", "sub"), None),
        P(None, ("rows", "sub"), None),
        P(None, ("rows", "sub"), None),
    )
    return jax.shard_map(
        on_device, mesh=mesh, in_specs=placed, out_specs=P(("rows", "sub"), None), check_vma=False
    )
```

```python
import functools

import jax
import jax.numpy as jnp
from jax import lax
from jax.experimental import pallas as pl
from jax.experimental.pallas import tpu as pltpu
from jax.sharding import PartitionSpec as P

RANK = 256
RHS = 128
HALF = RANK // 2
QUARTER = HALF // 2
SYM = HALF + QUARTER
TOLERANCE = 1e-7
DIVERGED = 1e4
FIRST_FLOPS = 6.5e8
INVERT_FLOPS = 9e8
INVERT_SECOND = 9e8
MIDDLE_FLOPS = 0
CROSS_FLOPS = 0
THIRD_FLOPS = 1e9
VMEM_LIMIT = 40 * 2**20
STREAM_LIMIT = 52 * 2**20

SMEM = pl.BlockSpec(memory_space=pltpu.SMEM)
VMEM = pl.BlockSpec(memory_space=pltpu.VMEM)
HBM = pl.BlockSpec(memory_space=pltpu.HBM)
ANY = pl.BlockSpec(memory_space=pl.ANY)


def swap(value, axis, bit):
    mask = 2**bit
    pairs = [(source, source ^ mask) for source in range(lax.axis_size(axis))]
    return lax.ppermute(value, axis, pairs)


def struct(rows, cols=HALF):
    return jax.ShapeDtypeStruct((rows, cols), jnp.float32)


def cost(flops, floats):
    return pl.CostEstimate(flops=int(flops), bytes_accessed=int(4 * floats), transcendentals=0)


def split(value):
    high = value.astype(jnp.bfloat16)
    low = (value - high.astype(jnp.float32)).astype(jnp.bfloat16)
    return high, low


def dot_parts(left, right):
    first = jnp.concatenate([left[0], left[0], left[1]], axis=1)
    second = jnp.concatenate([right[0], right[1], right[0]], axis=0)
    return lax.dot_general(first, second, (((1,), (0,)), ((), ())), preferred_element_type=jnp.float32)


def dot(left, right):
    return dot_parts(split(left), split(right))


def dot_turned(left, right):
    return dot_parts([part.T for part in split(left)], split(right))


def in_order(core, own, other):
    first = core == 0
    return jnp.concatenate([jnp.where(first, own, other), jnp.where(first, other, own)], axis=1)


def symmetric(core, own, other):
    first = core == 0
    low = jnp.where(first, own, other)
    high = jnp.where(first, other, own)
    upper = jnp.concatenate([low[HALF:], high[HALF:]], axis=0)
    return jnp.concatenate(
        [jnp.concatenate([low[:HALF], upper], axis=1), jnp.concatenate([upper.T, high[:HALF]], axis=1)], axis=0
    )


def symmetric_half(core, value):
    first = core == 0
    return jnp.concatenate(
        [
            jnp.where(first, value[:HALF], value[HALF:]),
            jnp.where(first, value[HALF:].T[:QUARTER], value[QUARTER:HALF]),
        ],
        axis=0,
    )


def pack(value):
    whole = value.shape[1] // HALF
    units = [value[:, index * HALF : (index + 1) * HALF] for index in range(whole)]
    if value.shape[1] % HALF:
        tail = value[:, whole * HALF :]
        units.append(jnp.concatenate([tail[:HALF], tail[HALF:]], axis=1))
    return units


def unpack(ref):
    whole = ref.shape[0] // RANK
    parts = [ref[index * RANK : (index + 1) * RANK, :] for index in range(whole)]
    if ref.shape[0] % RANK:
        tail = ref[whole * RANK :, :]
        parts.append(jnp.concatenate([tail[:, :QUARTER], tail[:, QUARTER:]], axis=0))
    return jnp.concatenate(parts, axis=1) if len(parts) > 1 else parts[0]


def store(ref, value):
    start = 0
    for unit in pack(value):
        ref[start : start + unit.shape[0], :] = unit
        start += unit.shape[0]


def product_kernel(groups, chunks, core_ref, gens_ref, solved_ref, *refs):
    gens, solved, total, sems = refs[-4:] if chunks > 1 else (None, None, refs[-1], None)
    refs = refs[:-4] if chunks > 1 else refs[:-1]
    outs = refs[-2 * len(groups) :]
    blocks, lefts, rights = needed(groups)
    rhs_ref = refs[0] if 3 in rights else None
    block = gens_ref.shape[1] // chunks
    copies = []
    for chunk in range(chunks if chunks > 1 else 0):
        rows = pl.ds(chunk * block, block)
        row = [(gens_ref.at[level, rows], gens.at[place, rows]) for place, level in enumerate(lefts)]
        row += [(solved_ref.at[level, rows], solved.at[place, rows]) for place, level in enumerate(rights) if level < 3]
        row = [pltpu.make_async_copy(*ends, sems.at[index, chunk]) for index, ends in enumerate(row)]
        for copy in row:
            copy.start()
        copies.append(row)
    places = {}
    for chunk in range(chunks):
        rows = pl.ds(chunk * block, block)
        for copy in copies[chunk] if chunks > 1 else ():
            copy.wait()
        right = {}
        for place, level in enumerate(rights):
            if level == 3:
                right[level] = split(rhs_ref[rows, :])
            else:
                right[level] = split(solved[place, rows, :] if chunks > 1 else solved_ref[level])
        left = []
        for place, level in enumerate(lefts):
            left.append([part.T for part in split(gens[place, rows, :] if chunks > 1 else gens_ref[level])])
        start = 0
        for firsts, seconds in blocks:
            value = dot_parts(
                [jnp.concatenate([left[lefts.index(level)][half] for level in firsts], axis=0) for half in (0, 1)],
                [jnp.concatenate([right[level][half] for level in seconds], axis=1) for half in (0, 1)],
            )
            cols = slice(start, start + value.shape[1])
            if chunk == 0:
                total[: value.shape[0], cols] = value
            else:
                total[: value.shape[0], cols] += value
            for level in seconds:
                for place, first in enumerate(firsts):
                    places[first, level] = (place * RANK, start)
                start += width_of(level)
    first = core_ref[0] == 0
    for index, group in enumerate(groups):
        keep_ref, send_ref = outs[2 * index : 2 * index + 2]
        start = 0
        for pair in group:
            row, at = places[pair]
            value = total[row : row + RANK, at : at + width_of(pair[1])]
            if pair[0] == pair[1]:
                low = jnp.concatenate([value[:HALF, :HALF], value[:QUARTER, HALF:]], axis=0)
                high = jnp.concatenate([value[HALF:, HALF:], value[QUARTER:HALF, HALF:]], axis=0)
            elif pair[1] < 3:
                low = value[:, :HALF]
                high = value[:, HALF:]
            else:
                low = jnp.concatenate([value[:HALF, :QUARTER], value[HALF:, :QUARTER]], axis=1)
                high = jnp.concatenate([value[:HALF, QUARTER:], value[HALF:, QUARTER:]], axis=1)
            rows = slice(start, start + low.shape[0])
            keep_ref[rows, :] = jnp.where(first, low, high)
            send_ref[rows, :] = jnp.where(first, high, low)
            start += low.shape[0]


def rows_of(pair):
    return SYM if pair[0] == pair[1] else HALF if pair[1] == 3 else RANK


def width_of(level):
    return RHS if level == 3 else RANK


def needed(groups):
    pairs = sorted(pair for group in groups for pair in group)
    rights = sorted({right for _, right in pairs})
    blocks = {}
    for right in rights:
        blocks.setdefault(tuple(left for left, other in pairs if other == right), []).append(right)
    return list(blocks.items()), sorted({left for left, _ in pairs}), rights


def products(core, generators, solved_gens, rhs, groups, chunks, *after):
    rows = rhs.shape[0]
    blocks, lefts, rights = needed(groups)
    width = sum(width_of(right) for right in rights)
    height = max(len(firsts) for firsts, _ in blocks) * RANK
    flops = sum(len(firsts) * width_of(right) for firsts, seconds in blocks for right in seconds) * 6 * rows * RANK
    outs = [struct(sum(rows_of(pair) for pair in group)) for group in groups for _ in range(2)]
    held = sum(level < 3 for level in rights)
    scratch = [pltpu.VMEM((height, width), jnp.float32)]
    if chunks > 1:
        scratch = [
            pltpu.VMEM((len(lefts), rows, RANK), jnp.float32),
            pltpu.VMEM((held, rows, RANK), jnp.float32),
            *scratch,
            pltpu.SemaphoreType.DMA((len(lefts) + held, chunks)),
        ]
    given, specs = [generators, solved_gens], [HBM if chunks > 1 else VMEM] * 2
    if 3 in rights:
        given, specs = given + [rhs], specs + [VMEM]
    return pl.pallas_call(
        functools.partial(product_kernel, groups, chunks),
        in_specs=[SMEM] + specs + [ANY] * len(after),
        out_specs=[VMEM] * len(outs),
        out_shape=outs,
        scratch_shapes=scratch,
        compiler_params=pltpu.CompilerParams(vmem_limit_bytes=STREAM_LIMIT if chunks > 1 else VMEM_LIMIT),
        cost_estimate=cost(flops, rows * (len(lefts) * RANK + width)),
    )(core, *given, *after)


def square_norm(value):
    return jnp.sum(value * value)


def identity():
    row = lax.broadcasted_iota(jnp.int32, (RANK, RANK), 0)
    col = lax.broadcasted_iota(jnp.int32, (RANK, RANK), 1)
    return jnp.where(row == col, 1.0, 0.0)


def doubled(power, values):
    power = split(power)
    right = [jnp.concatenate(parts, axis=1) for parts in zip(power, split(values))]
    both = dot_parts(power, right)
    return both[:, :RANK], values + both[:, RANK:]


def series(start, values, power_ref, sum_ref):
    if values is None:
        power, values = dot(start, start), identity() + start
    else:
        power, values = doubled(start, values)
    for _ in range(2):
        power, values = doubled(power, values)
    norm = square_norm(power)
    power_ref[...] = power
    sum_ref[...] = values + dot(power, values)

    def proceed(state):
        count, bound = state
        return (count < 60) & (bound > TOLERANCE) & (bound < DIVERGED * DIVERGED)

    def body(state):
        count, _ = state
        power = dot(power_ref[...], power_ref[...])
        power_ref[...] = power
        sum_ref[...] = sum_ref[...] + dot(power, sum_ref[...])
        return count + 1, square_norm(power)

    return lax.while_loop(proceed, body, (jnp.int32(0), norm))[1]


def solve_series(product, values, power_ref, sum_ref):
    bound = series(product, values, power_ref, sum_ref)

    @pl.when(jnp.logical_not(bound <= TOLERANCE))
    def _():
        scale = 1.0 / (1.0 + jnp.sqrt(square_norm(product)))
        series((1.0 - scale) * identity() + scale * product, values, power_ref, sum_ref)
        sum_ref[...] = scale * sum_ref[...]


def invert_kernel(core_ref, own_ref, sib_ref, own_other_ref, sib_other_ref, tail_ref, inverse_ref, product_ref, power):
    core = core_ref[0]
    p_own = symmetric(core, own_ref[:SYM, :], own_other_ref[:SYM, :])
    p_sib = symmetric(core, sib_ref[:SYM, :], sib_other_ref[...])
    both = dot(p_sib, jnp.concatenate([p_own, own_ref[SYM:, :], unpack(tail_ref)], axis=1))
    product_ref[...] = both[:, RANK:]
    solve_series(both[:, :RANK], None, power, inverse_ref)


def invert_second_kernel(
    core_ref, own_ref, sib_ref, own_other_ref, sib_other_ref, r_own_ref, r_own_other_ref,
    inverse_ref, product_ref, turned_ref, power,
):
    core = core_ref[0]
    p_own = symmetric(core, own_ref[...], own_other_ref[...])
    p_sib = symmetric(core, sib_ref[...], sib_other_ref[...])
    both = dot(p_sib, jnp.concatenate([p_own, unpack(r_own_ref)], axis=1))
    product_ref[...] = both[:, RANK:]
    turned_ref[:RANK, :] = p_own
    turned_ref[RANK:, :] = in_order(core, r_own_ref[:RANK, :], r_own_other_ref[...]).T
    solve_series(both[:, :RANK], None, power, inverse_ref)


def call(kernel, out_shape, flops, *values, after=(), scratch=()):
    many = isinstance(out_shape, (list, tuple))
    floats = sum(value.size for value in values) + sum(out.size for out in (out_shape if many else [out_shape]))
    return pl.pallas_call(
        kernel,
        in_specs=[SMEM] + [VMEM] * (len(values) - 1) + [ANY] * len(after),
        out_specs=[VMEM] * len(out_shape) if many else VMEM,
        out_shape=out_shape,
        scratch_shapes=[pltpu.VMEM(shape, jnp.float32) for shape in scratch],
        compiler_params=pltpu.CompilerParams(vmem_limit_bytes=VMEM_LIMIT),
        cost_estimate=cost(flops, floats),
    )(*values, *after)


def first_kernel(core_ref, inverse_ref, product_ref, head_ref, head_sib_ref, head_other_ref, tail_ref, tail_other_ref, tail_sib_ref, *refs):
    z_ref, out_ref, last_ref = refs
    core = core_ref[0]
    sib = jnp.concatenate([head_sib_ref[SYM:, :], unpack(tail_sib_ref)], axis=1)
    z = dot(inverse_ref[...], sib - product_ref[...])
    store(z_ref, z)
    value = dot_turned(in_order(core, head_ref[SYM:, :], head_other_ref[SYM:, :]), z)
    out_ref[:SYM, :] = symmetric_half(core, value[:, :HALF])
    store(out_ref.at[SYM:], value[:, HALF:])
    last_ref[...] = last_parts(core, in_order(core, tail_ref[:RANK, :], tail_other_ref[...]), z[:, HALF:])


def last_parts(core, crossed, z):
    return lost_parts(core, dot_turned(crossed, z))


def lost_parts(core, value):
    return jnp.concatenate([symmetric_half(core, value[:, :HALF]), *pack(value[:, HALF:])], axis=0)


def middle_kernel(core_ref, inverse_ref, product_ref, turned_ref, own_ref, sib_ref, z_ref, z_sib_ref, out_ref):
    core = core_ref[0]
    z = dot(inverse_ref[...], unpack(sib_ref) - product_ref[...])
    store(z_ref, z)
    value = dot(turned_ref[...], z)
    store(z_sib_ref, unpack(own_ref) - value[:RANK])
    out_ref[...] = lost_parts(core, value[RANK:])


def cross_kernel(core_ref, sib_ref, sib_other_ref, z_sib_ref, crossed_ref, out_ref):
    core = core_ref[0]
    crossed = in_order(core, sib_ref[...], sib_other_ref[...])
    out_ref[...] = crossed_ref[...] + last_parts(core, crossed, unpack(z_sib_ref))


def rhs_in_order(core, own, other):
    first = core == 0
    low = jnp.where(first, own, other)
    high = jnp.where(first, other, own)
    top = jnp.concatenate([low[:, :QUARTER], high[:, :QUARTER]], axis=1)
    bottom = jnp.concatenate([low[:, QUARTER:], high[:, QUARTER:]], axis=1)
    return jnp.concatenate([top, bottom], axis=0)


def reduced_kernel(
    core_ref, z1_ref, z1_other_ref, z0_ref, z0_other_ref, solved_ref, rhs_ref, high_ref, low_ref, out_ref
):
    core = core_ref[0]
    z12 = in_order(core, z1_ref[:RANK, :], z1_other_ref[:RANK, :])
    z1x = rhs_in_order(core, z1_ref[RANK:, :], z1_other_ref[RANK:, :])
    z01 = in_order(core, z0_ref[:RANK, :], z0_other_ref[:RANK, :])
    z02 = in_order(core, z0_ref[RANK : 2 * RANK, :], z0_other_ref[RANK : 2 * RANK, :])
    z0x = rhs_in_order(core, z0_ref[2 * RANK :, :], z0_other_ref[2 * RANK :, :])
    middle = jnp.concatenate([z12, z1x], axis=1)
    first = jnp.concatenate([z02, z0x], axis=1) - dot(z01, middle)
    coefs = jnp.concatenate([first, middle], axis=0)
    value = dot(jnp.concatenate([solved_ref[0], solved_ref[1]], axis=1), coefs)
    high, low = split(solved_ref[2] - value[:, :RANK])
    high_ref[...] = high
    low_ref[...] = low
    out_ref[...] = rhs_ref[...] - value[:, RANK:]


def keep_kernel(core_ref, value_ref, *refs):
    refs[-1][...] = value_ref[...]


def join_kernel(core_ref, first_ref, second_ref, *refs):
    rows = first_ref.shape[0]
    refs[-1][:rows, :] = first_ref[...]
    refs[-1][rows:, :] = second_ref[...]


def add_kernel(core_ref, first_ref, second_ref, *refs):
    refs[-1][...] = first_ref[...] + second_ref[...]


def subtract_kernel(core_ref, first_ref, second_ref, *refs):
    refs[-1][...] = first_ref[...] - second_ref[...]


def final_kernel(
    core_ref, own_ref, own_other_ref, sib_ref, sib_other_ref, high_ref, low_ref, rhs_ref, out_ref, power, total, out, sems
):
    core = core_ref[0]
    p_own = symmetric(core, own_ref[:SYM, :], own_other_ref[:SYM, :])
    p_sib = symmetric(core, sib_ref[:SYM, :], sib_other_ref[:SYM, :])
    own = rhs_in_order(core, own_ref[SYM:, :], own_other_ref[SYM:, :])
    sib = rhs_in_order(core, sib_ref[SYM:, :], sib_other_ref[SYM:, :])
    both = dot(p_sib, jnp.concatenate([p_own, own], axis=1))
    solve_series(both[:, :RANK], sib - both[:, RANK:], power, total)
    z = split(total[...])
    blocks = sems.shape[0]
    block = out.shape[0] // blocks
    copies = []
    for index in range(blocks):
        rows = pl.ds(index * block, block)
        out[rows, :] = rhs_ref[rows, :] - dot_parts((high_ref[rows, :], low_ref[rows, :]), z)
        copies.append(pltpu.make_async_copy(out.at[rows], out_ref.at[rows], sems.at[index]))
        copies[-1].start()
    for copy in copies:
        copy.wait()


def on_device(rhs, generators, solved_gens):
    groups = lax.axis_size("rows")
    sub_bits = lax.axis_size("sub").bit_length() - 1
    span_bits = (groups // 8).bit_length() - 1
    core = (lax.axis_index("sub") % 2).astype(jnp.int32).reshape(1)
    flops = 6 * RANK * RANK * HALF
    last = SYM + HALF

    def over_child(value):
        for bit in range(1, sub_bits):
            value = value + swap(value, "sub", bit)
        for bit in range(span_bits):
            value = value + swap(value, "rows", bit)
        return value

    keep, send = products(core, generators, solved_gens, rhs, (((0, 0), (0, 1)),), 4)
    head = keep + swap(send, "sub", 0)
    token = swap(call(keep_kernel, struct(8), 0, core, send[:8], after=(head,)), "sub", 0)
    parts = products(core, generators, solved_gens, rhs, (((0, 2), (0, 3)),), 1, token)
    rest = (((1, 1), (1, 2), (1, 3)), ((2, 2), (2, 3)))
    parts += products(core, generators, solved_gens, rhs, rest, 1, parts[1])
    parts = [(keep, swap(send, "sub", 0)) for keep, send in zip(parts[::2], parts[1::2])]
    head = over_child(head)
    tail = over_child(parts[0][0] + parts[0][1])
    near = over_child(call(add_kernel, struct(SYM + RANK + HALF), 0, core, *parts[1], after=(tail,)))
    third = parts[2][0] + parts[2][1]

    head_sib = swap(head, "rows", span_bits)
    tail_sib = swap(tail, "rows", span_bits)
    head_other = swap(head, "sub", 0)
    tail_other = swap(tail[:RANK], "sub", 0)
    p_sib_other = swap(head_sib[:SYM], "sub", 0)
    inverted, product = call(
        invert_kernel, [struct(RANK, RANK), struct(RANK, 2 * HALF + QUARTER)], INVERT_FLOPS,
        core, head, head_sib, head_other, p_sib_other, tail, scratch=((RANK, RANK),),
    )
    z0, crossed, lost = call(
        first_kernel, [struct(2 * RANK + HALF), struct(SYM + RANK + HALF), struct(last)], FIRST_FLOPS,
        core, inverted, product, head, head_sib, head_other, tail, tail_other, tail_sib,
    )
    p_own = call(subtract_kernel, struct(SYM), 0, core, near[:SYM], crossed[:SYM])
    r_own = call(subtract_kernel, struct(RANK + HALF), 0, core, near[SYM:], crossed[SYM:], after=(p_own,))
    third = over_child(
        call(add_kernel, struct(last), 0, core, third, swap(third, "rows", span_bits + 1), after=(r_own,))
    )
    crossed = call(keep_kernel, struct(last), THIRD_FLOPS, core, lost, after=(r_own,))
    third = third - (crossed + swap(crossed, "rows", span_bits + 1))
    third = third + swap(third, "rows", span_bits)

    p_own = p_own + swap(p_own, "rows", span_bits)
    r_own = r_own + swap(r_own, "rows", span_bits)
    p_sib = swap(p_own, "rows", span_bits + 1)
    r_sib = swap(r_own, "rows", span_bits + 1)
    p_own_other = swap(p_own, "sub", 0)
    r_own_other = swap(r_own[:RANK], "sub", 0)
    p_sib_other = swap(p_sib, "sub", 0)
    width = HALF + QUARTER
    inverted, product, turned = call(
        invert_second_kernel, [struct(RANK, RANK), struct(RANK, width), struct(2 * RANK, RANK)], INVERT_SECOND,
        core, p_own, p_sib, p_own_other, p_sib_other, r_own, r_own_other, scratch=((RANK, RANK),),
    )
    cross_sib = call(keep_kernel, struct(RANK), 0, core, r_sib[:RANK], after=(inverted,))
    z1, z_sib, crossed = call(
        middle_kernel, [struct(RANK + HALF), struct(RANK + HALF), struct(last)], MIDDLE_FLOPS,
        core, inverted, product, turned, r_own, r_sib,
    )
    crossed = call(cross_kernel, struct(last), CROSS_FLOPS, core, cross_sib, swap(cross_sib, "sub", 0), z_sib, crossed)

    own = third - crossed
    sib = swap(own, "rows", span_bits + 2)
    solved = swap(call(join_kernel, struct(3 * RANK + 2 * HALF), 0, core, z1, z0, after=(own,)), "sub", 0)
    z1_other, z0_other = solved[: RANK + HALF], solved[RANK + HALF :]
    part = jax.ShapeDtypeStruct((rhs.shape[0], RANK), jnp.bfloat16)
    high, low, current = call(
        reduced_kernel, [part, part, struct(rhs.shape[0], RHS)], 6 * rhs.shape[0] * 2 * RANK * (RANK + RHS),
        core, z1, z1_other, z0, z0_other, solved_gens, rhs,
    )
    sib = call(keep_kernel, struct(last), 0, core, sib, after=(high,))
    own_other, sib_other = swap(own, "sub", 0), swap(sib, "sub", 0)
    rows = rhs.shape[0]
    small = (own, own_other, sib, sib_other, high, low, current)
    return pl.pallas_call(
        final_kernel,
        in_specs=[SMEM] + [VMEM] * len(small),
        out_specs=HBM,
        out_shape=struct(rows, RHS),
        scratch_shapes=[
            pltpu.VMEM((RANK, RANK), jnp.float32),
            pltpu.VMEM((RANK, RHS), jnp.float32),
            pltpu.VMEM((rows, RHS), jnp.float32),
            pltpu.SemaphoreType.DMA((2,)),
        ],
        compiler_params=pltpu.CompilerParams(vmem_limit_bytes=VMEM_LIMIT),
        cost_estimate=cost(6 * rows * RANK * RHS + 6 * 9 * RANK**3, 3 * rows * RANK),
    )(core, *small)


def solution(mesh):
    placed = (
        P(("rows", "sub"), None),
        P(None, ("rows", "sub"), None),
        P(None, ("rows", "sub"), None),
    )
    return jax.shard_map(
        on_device, mesh=mesh, in_specs=placed, out_specs=P(("rows", "sub"), None), check_vma=False
    )
```

```python
import functools

import jax
import jax.numpy as jnp
from jax import lax
from jax.experimental import pallas as pl
from jax.experimental.pallas import tpu as pltpu
from jax.sharding import PartitionSpec as P

RANK = 256
RHS = 128
HALF = RANK // 2
QUARTER = HALF // 2
SYM = HALF + QUARTER
TOLERANCE = 1e-7
DIVERGED = 1e4
FIRST_FLOPS = 6.5e8
INVERT_FLOPS = 5e8
INVERT_SECOND = 9e8
MIDDLE_FLOPS = 0
CROSS_FLOPS = 0
THIRD_FLOPS = 1e9
VMEM_LIMIT = 40 * 2**20
STREAM_LIMIT = 52 * 2**20

SMEM = pl.BlockSpec(memory_space=pltpu.SMEM)
VMEM = pl.BlockSpec(memory_space=pltpu.VMEM)
HBM = pl.BlockSpec(memory_space=pltpu.HBM)
ANY = pl.BlockSpec(memory_space=pl.ANY)


def swap(value, axis, bit):
    mask = 2**bit
    pairs = [(source, source ^ mask) for source in range(lax.axis_size(axis))]
    return lax.ppermute(value, axis, pairs)


def struct(rows, cols=HALF):
    return jax.ShapeDtypeStruct((rows, cols), jnp.float32)


def cost(flops, floats):
    return pl.CostEstimate(flops=int(flops), bytes_accessed=int(4 * floats), transcendentals=0)


def split(value):
    high = value.astype(jnp.bfloat16)
    low = (value - high.astype(jnp.float32)).astype(jnp.bfloat16)
    return high, low


def dot_parts(left, right):
    first = jnp.concatenate([left[0], left[0], left[1]], axis=1)
    second = jnp.concatenate([right[0], right[1], right[0]], axis=0)
    return lax.dot_general(first, second, (((1,), (0,)), ((), ())), preferred_element_type=jnp.float32)


def dot(left, right):
    return dot_parts(split(left), split(right))


def dot_turned(left, right):
    return dot_parts([part.T for part in split(left)], split(right))


def in_order(core, own, other):
    first = core == 0
    return jnp.concatenate([jnp.where(first, own, other), jnp.where(first, other, own)], axis=1)


def symmetric(core, own, other):
    first = core == 0
    low = jnp.where(first, own, other)
    high = jnp.where(first, other, own)
    upper = jnp.concatenate([low[HALF:], high[HALF:]], axis=0)
    return jnp.concatenate(
        [jnp.concatenate([low[:HALF], upper], axis=1), jnp.concatenate([upper.T, high[:HALF]], axis=1)], axis=0
    )


def symmetric_half(core, value):
    first = core == 0
    return jnp.concatenate(
        [
            jnp.where(first, value[:HALF], value[HALF:]),
            jnp.where(first, value[HALF:].T[:QUARTER], value[QUARTER:HALF]),
        ],
        axis=0,
    )


def pack(value):
    whole = value.shape[1] // HALF
    units = [value[:, index * HALF : (index + 1) * HALF] for index in range(whole)]
    if value.shape[1] % HALF:
        tail = value[:, whole * HALF :]
        units.append(jnp.concatenate([tail[:HALF], tail[HALF:]], axis=1))
    return units


def unpack(ref):
    whole = ref.shape[0] // RANK
    parts = [ref[index * RANK : (index + 1) * RANK, :] for index in range(whole)]
    if ref.shape[0] % RANK:
        tail = ref[whole * RANK :, :]
        parts.append(jnp.concatenate([tail[:, :QUARTER], tail[:, QUARTER:]], axis=0))
    return jnp.concatenate(parts, axis=1) if len(parts) > 1 else parts[0]


def store(ref, value):
    start = 0
    for unit in pack(value):
        ref[start : start + unit.shape[0], :] = unit
        start += unit.shape[0]


def product_kernel(groups, chunks, core_ref, gens_ref, solved_ref, *refs):
    gens, solved, total, sems = refs[-4:] if chunks > 1 else (None, None, refs[-1], None)
    refs = refs[:-4] if chunks > 1 else refs[:-1]
    outs = refs[-2 * len(groups) :]
    blocks, lefts, rights = needed(groups)
    rhs_ref = refs[0] if 3 in rights else None
    block = gens_ref.shape[1] // chunks
    copies = []
    for chunk in range(chunks if chunks > 1 else 0):
        rows = pl.ds(chunk * block, block)
        row = [(gens_ref.at[level, rows], gens.at[place, rows]) for place, level in enumerate(lefts)]
        row += [(solved_ref.at[level, rows], solved.at[place, rows]) for place, level in enumerate(rights) if level < 3]
        row = [pltpu.make_async_copy(*ends, sems.at[index, chunk]) for index, ends in enumerate(row)]
        for copy in row:
            copy.start()
        copies.append(row)
    places = {}
    for chunk in range(chunks):
        rows = pl.ds(chunk * block, block)
        for copy in copies[chunk] if chunks > 1 else ():
            copy.wait()
        right = {}
        for place, level in enumerate(rights):
            if level == 3:
                right[level] = split(rhs_ref[rows, :])
            else:
                right[level] = split(solved[place, rows, :] if chunks > 1 else solved_ref[level])
        left = []
        for place, level in enumerate(lefts):
            left.append([part.T for part in split(gens[place, rows, :] if chunks > 1 else gens_ref[level])])
        start = 0
        for firsts, seconds in blocks:
            value = dot_parts(
                [jnp.concatenate([left[lefts.index(level)][half] for level in firsts], axis=0) for half in (0, 1)],
                [jnp.concatenate([right[level][half] for level in seconds], axis=1) for half in (0, 1)],
            )
            cols = slice(start, start + value.shape[1])
            if chunk == 0:
                total[: value.shape[0], cols] = value
            else:
                total[: value.shape[0], cols] += value
            for level in seconds:
                for place, first in enumerate(firsts):
                    places[first, level] = (place * RANK, start)
                start += width_of(level)
    first = core_ref[0] == 0
    for index, group in enumerate(groups):
        keep_ref, send_ref = outs[2 * index : 2 * index + 2]
        start = 0
        for pair in group:
            row, at = places[pair]
            value = total[row : row + RANK, at : at + width_of(pair[1])]
            if pair[0] == pair[1]:
                low = jnp.concatenate([value[:HALF, :HALF], value[:QUARTER, HALF:]], axis=0)
                high = jnp.concatenate([value[HALF:, HALF:], value[QUARTER:HALF, HALF:]], axis=0)
            elif pair[1] < 3:
                low = value[:, :HALF]
                high = value[:, HALF:]
            else:
                low = jnp.concatenate([value[:HALF, :QUARTER], value[HALF:, :QUARTER]], axis=1)
                high = jnp.concatenate([value[:HALF, QUARTER:], value[HALF:, QUARTER:]], axis=1)
            rows = slice(start, start + low.shape[0])
            keep_ref[rows, :] = jnp.where(first, low, high)
            send_ref[rows, :] = jnp.where(first, high, low)
            start += low.shape[0]


def rows_of(pair):
    return SYM if pair[0] == pair[1] else HALF if pair[1] == 3 else RANK


def width_of(level):
    return RHS if level == 3 else RANK


def needed(groups):
    pairs = sorted(pair for group in groups for pair in group)
    rights = sorted({right for _, right in pairs})
    blocks = {}
    for right in rights:
        blocks.setdefault(tuple(left for left, other in pairs if other == right), []).append(right)
    return list(blocks.items()), sorted({left for left, _ in pairs}), rights


def products(core, generators, solved_gens, rhs, groups, chunks, *after):
    rows = rhs.shape[0]
    blocks, lefts, rights = needed(groups)
    width = sum(width_of(right) for right in rights)
    height = max(len(firsts) for firsts, _ in blocks) * RANK
    flops = sum(len(firsts) * width_of(right) for firsts, seconds in blocks for right in seconds) * 6 * rows * RANK
    outs = [struct(sum(rows_of(pair) for pair in group)) for group in groups for _ in range(2)]
    held = sum(level < 3 for level in rights)
    scratch = [pltpu.VMEM((height, width), jnp.float32)]
    if chunks > 1:
        scratch = [
            pltpu.VMEM((len(lefts), rows, RANK), jnp.float32),
            pltpu.VMEM((held, rows, RANK), jnp.float32),
            *scratch,
            pltpu.SemaphoreType.DMA((len(lefts) + held, chunks)),
        ]
    given, specs = [generators, solved_gens], [HBM if chunks > 1 else VMEM] * 2
    if 3 in rights:
        given, specs = given + [rhs], specs + [VMEM]
    return pl.pallas_call(
        functools.partial(product_kernel, groups, chunks),
        in_specs=[SMEM] + specs + [ANY] * len(after),
        out_specs=[VMEM] * len(outs),
        out_shape=outs,
        scratch_shapes=scratch,
        compiler_params=pltpu.CompilerParams(vmem_limit_bytes=STREAM_LIMIT if chunks > 1 else VMEM_LIMIT),
        cost_estimate=cost(flops, rows * (len(lefts) * RANK + width)),
    )(core, *given, *after)


def square_norm(value):
    return jnp.sum(value * value)


def identity():
    row = lax.broadcasted_iota(jnp.int32, (RANK, RANK), 0)
    col = lax.broadcasted_iota(jnp.int32, (RANK, RANK), 1)
    return jnp.where(row == col, 1.0, 0.0)


def doubled(power, values):
    power = split(power)
    right = [jnp.concatenate(parts, axis=1) for parts in zip(power, split(values))]
    both = dot_parts(power, right)
    return both[:, :RANK], values + both[:, RANK:]


def series(start, values, power_ref, sum_ref):
    if values is None:
        power, values = dot(start, start), identity() + start
    else:
        power, values = doubled(start, values)
    for _ in range(2):
        power, values = doubled(power, values)
    norm = square_norm(power)
    power_ref[...] = power
    sum_ref[...] = values + dot(power, values)

    def proceed(state):
        count, bound = state
        return (count < 60) & (bound > TOLERANCE) & (bound < DIVERGED * DIVERGED)

    def body(state):
        count, _ = state
        power = dot(power_ref[...], power_ref[...])
        power_ref[...] = power
        sum_ref[...] = sum_ref[...] + dot(power, sum_ref[...])
        return count + 1, square_norm(power)

    return lax.while_loop(proceed, body, (jnp.int32(0), norm))[1]


def solve_series(product, values, power_ref, sum_ref):
    bound = series(product, values, power_ref, sum_ref)

    @pl.when(jnp.logical_not(bound <= TOLERANCE))
    def _():
        scale = 1.0 / (1.0 + jnp.sqrt(square_norm(product)))
        series((1.0 - scale) * identity() + scale * product, values, power_ref, sum_ref)
        sum_ref[...] = scale * sum_ref[...]


def invert_kernel(core_ref, own_ref, sib_ref, own_other_ref, sib_other_ref, tail_ref, inverse_ref, product_ref, power):
    core = core_ref[0]
    p_own = symmetric(core, own_ref[:SYM, :], own_other_ref[:SYM, :])
    p_sib = symmetric(core, sib_ref[:SYM, :], sib_other_ref[...])
    both = dot(p_sib, jnp.concatenate([p_own, own_ref[SYM:, :], unpack(tail_ref)], axis=1))
    product_ref[...] = both[:, RANK:]
    solve_series(both[:, :RANK], None, power, inverse_ref)


def invert_second_kernel(
    core_ref, own_ref, sib_ref, own_other_ref, sib_other_ref, r_own_ref, r_own_other_ref,
    inverse_ref, product_ref, turned_ref, power,
):
    core = core_ref[0]
    p_own = symmetric(core, own_ref[...], own_other_ref[...])
    p_sib = symmetric(core, sib_ref[...], sib_other_ref[...])
    both = dot(p_sib, jnp.concatenate([p_own, unpack(r_own_ref)], axis=1))
    product_ref[...] = both[:, RANK:]
    turned_ref[:RANK, :] = p_own
    turned_ref[RANK:, :] = in_order(core, r_own_ref[:RANK, :], r_own_other_ref[...]).T
    solve_series(both[:, :RANK], None, power, inverse_ref)


def call(kernel, out_shape, flops, *values, after=(), scratch=()):
    many = isinstance(out_shape, (list, tuple))
    floats = sum(value.size for value in values) + sum(out.size for out in (out_shape if many else [out_shape]))
    return pl.pallas_call(
        kernel,
        in_specs=[SMEM] + [VMEM] * (len(values) - 1) + [ANY] * len(after),
        out_specs=[VMEM] * len(out_shape) if many else VMEM,
        out_shape=out_shape,
        scratch_shapes=[pltpu.VMEM(shape, jnp.float32) for shape in scratch],
        compiler_params=pltpu.CompilerParams(vmem_limit_bytes=VMEM_LIMIT),
        cost_estimate=cost(flops, floats),
    )(*values, *after)


def first_kernel(core_ref, inverse_ref, product_ref, head_ref, head_sib_ref, head_other_ref, tail_ref, tail_other_ref, tail_sib_ref, *refs):
    z_ref, out_ref, last_ref = refs
    core = core_ref[0]
    sib = jnp.concatenate([head_sib_ref[SYM:, :], unpack(tail_sib_ref)], axis=1)
    z = dot(inverse_ref[...], sib - product_ref[...])
    store(z_ref, z)
    value = dot_turned(in_order(core, head_ref[SYM:, :], head_other_ref[SYM:, :]), z)
    out_ref[:SYM, :] = symmetric_half(core, value[:, :HALF])
    store(out_ref.at[SYM:], value[:, HALF:])
    last_ref[...] = last_parts(core, in_order(core, tail_ref[:RANK, :], tail_other_ref[...]), z[:, HALF:])


def last_parts(core, crossed, z):
    return lost_parts(core, dot_turned(crossed, z))


def lost_parts(core, value):
    return jnp.concatenate([symmetric_half(core, value[:, :HALF]), *pack(value[:, HALF:])], axis=0)


def middle_kernel(core_ref, inverse_ref, product_ref, turned_ref, own_ref, sib_ref, z_ref, z_sib_ref, out_ref):
    core = core_ref[0]
    z = dot(inverse_ref[...], unpack(sib_ref) - product_ref[...])
    store(z_ref, z)
    value = dot(turned_ref[...], z)
    store(z_sib_ref, unpack(own_ref) - value[:RANK])
    out_ref[...] = lost_parts(core, value[RANK:])


def cross_kernel(core_ref, sib_ref, sib_other_ref, z_sib_ref, crossed_ref, out_ref):
    core = core_ref[0]
    crossed = in_order(core, sib_ref[...], sib_other_ref[...])
    out_ref[...] = crossed_ref[...] + last_parts(core, crossed, unpack(z_sib_ref))


def rhs_in_order(core, own, other):
    first = core == 0
    low = jnp.where(first, own, other)
    high = jnp.where(first, other, own)
    top = jnp.concatenate([low[:, :QUARTER], high[:, :QUARTER]], axis=1)
    bottom = jnp.concatenate([low[:, QUARTER:], high[:, QUARTER:]], axis=1)
    return jnp.concatenate([top, bottom], axis=0)


def reduced_kernel(
    core_ref, z1_ref, z1_other_ref, z0_ref, z0_other_ref, solved_ref, rhs_ref, high_ref, low_ref, out_ref
):
    core = core_ref[0]
    z12 = in_order(core, z1_ref[:RANK, :], z1_other_ref[:RANK, :])
    z1x = rhs_in_order(core, z1_ref[RANK:, :], z1_other_ref[RANK:, :])
    z01 = in_order(core, z0_ref[:RANK, :], z0_other_ref[:RANK, :])
    z02 = in_order(core, z0_ref[RANK : 2 * RANK, :], z0_other_ref[RANK : 2 * RANK, :])
    z0x = rhs_in_order(core, z0_ref[2 * RANK :, :], z0_other_ref[2 * RANK :, :])
    middle = jnp.concatenate([z12, z1x], axis=1)
    first = jnp.concatenate([z02, z0x], axis=1) - dot(z01, middle)
    coefs = jnp.concatenate([first, middle], axis=0)
    value = dot(jnp.concatenate([solved_ref[0], solved_ref[1]], axis=1), coefs)
    high, low = split(solved_ref[2] - value[:, :RANK])
    high_ref[...] = high
    low_ref[...] = low
    out_ref[...] = rhs_ref[...] - value[:, RANK:]


def keep_kernel(core_ref, value_ref, *refs):
    refs[-1][...] = value_ref[...]


def join_kernel(core_ref, first_ref, second_ref, *refs):
    rows = first_ref.shape[0]
    refs[-1][:rows, :] = first_ref[...]
    refs[-1][rows:, :] = second_ref[...]


def add_kernel(core_ref, first_ref, second_ref, *refs):
    refs[-1][...] = first_ref[...] + second_ref[...]


def subtract_kernel(core_ref, first_ref, second_ref, *refs):
    refs[-1][...] = first_ref[...] - second_ref[...]


def final_kernel(
    core_ref, own_ref, own_other_ref, sib_ref, sib_other_ref, high_ref, low_ref, rhs_ref, out_ref, power, total, out, sems
):
    core = core_ref[0]
    p_own = symmetric(core, own_ref[:SYM, :], own_other_ref[:SYM, :])
    p_sib = symmetric(core, sib_ref[:SYM, :], sib_other_ref[:SYM, :])
    own = rhs_in_order(core, own_ref[SYM:, :], own_other_ref[SYM:, :])
    sib = rhs_in_order(core, sib_ref[SYM:, :], sib_other_ref[SYM:, :])
    both = dot(p_sib, jnp.concatenate([p_own, own], axis=1))
    solve_series(both[:, :RANK], sib - both[:, RANK:], power, total)
    z = split(total[...])
    blocks = sems.shape[0]
    block = out.shape[0] // blocks
    copies = []
    for index in range(blocks):
        rows = pl.ds(index * block, block)
        out[rows, :] = rhs_ref[rows, :] - dot_parts((high_ref[rows, :], low_ref[rows, :]), z)
        copies.append(pltpu.make_async_copy(out.at[rows], out_ref.at[rows], sems.at[index]))
        copies[-1].start()
    for copy in copies:
        copy.wait()


def on_device(rhs, generators, solved_gens):
    groups = lax.axis_size("rows")
    sub_bits = lax.axis_size("sub").bit_length() - 1
    span_bits = (groups // 8).bit_length() - 1
    core = (lax.axis_index("sub") % 2).astype(jnp.int32).reshape(1)
    flops = 6 * RANK * RANK * HALF
    last = SYM + HALF

    def over_child(value):
        for bit in range(1, sub_bits):
            value = value + swap(value, "sub", bit)
        for bit in range(span_bits):
            value = value + swap(value, "rows", bit)
        return value

    keep, send = products(core, generators, solved_gens, rhs, (((0, 0), (0, 1)),), 4)
    head = keep + swap(send, "sub", 0)
    token = swap(call(keep_kernel, struct(8), 0, core, send[:8], after=(head,)), "sub", 0)
    parts = products(core, generators, solved_gens, rhs, (((0, 2), (0, 3)),), 1, token)
    rest = (((1, 1), (1, 2), (1, 3)), ((2, 2), (2, 3)))
    parts += products(core, generators, solved_gens, rhs, rest, 1, parts[1])
    parts = [(keep, swap(send, "sub", 0)) for keep, send in zip(parts[::2], parts[1::2])]
    head = over_child(head)
    tail = over_child(parts[0][0] + parts[0][1])
    third = parts[2][0] + parts[2][1]
    near = over_child(call(add_kernel, struct(SYM + RANK + HALF), 0, core, *parts[1], after=(third,)))

    head_sib = swap(head, "rows", span_bits)
    tail_sib = swap(tail, "rows", span_bits)
    head_other = swap(head, "sub", 0)
    tail_other = swap(tail[:RANK], "sub", 0)
    p_sib_other = swap(head_sib[:SYM], "sub", 0)
    inverted, product = call(
        invert_kernel, [struct(RANK, RANK), struct(RANK, 2 * HALF + QUARTER)], INVERT_FLOPS,
        core, head, head_sib, head_other, p_sib_other, tail, scratch=((RANK, RANK),),
    )
    z0, crossed, lost = call(
        first_kernel, [struct(2 * RANK + HALF), struct(SYM + RANK + HALF), struct(last)], FIRST_FLOPS,
        core, inverted, product, head, head_sib, head_other, tail, tail_other, tail_sib,
    )
    p_own = call(subtract_kernel, struct(SYM), 0, core, near[:SYM], crossed[:SYM])
    r_own = call(subtract_kernel, struct(RANK + HALF), 0, core, near[SYM:], crossed[SYM:], after=(p_own,))
    third = over_child(
        call(add_kernel, struct(last), 0, core, third, swap(third, "rows", span_bits + 1), after=(r_own,))
    )
    crossed = call(keep_kernel, struct(last), THIRD_FLOPS, core, lost, after=(r_own,))
    third = third - (crossed + swap(crossed, "rows", span_bits + 1))
    third = third + swap(third, "rows", span_bits)

    p_own = p_own + swap(p_own, "rows", span_bits)
    r_own = r_own + swap(r_own, "rows", span_bits)
    p_sib = swap(p_own, "rows", span_bits + 1)
    r_sib = swap(r_own, "rows", span_bits + 1)
    p_own_other = swap(p_own, "sub", 0)
    r_own_other = swap(r_own[:RANK], "sub", 0)
    p_sib_other = swap(p_sib, "sub", 0)
    width = HALF + QUARTER
    inverted, product, turned = call(
        invert_second_kernel, [struct(RANK, RANK), struct(RANK, width), struct(2 * RANK, RANK)], INVERT_SECOND,
        core, p_own, p_sib, p_own_other, p_sib_other, r_own, r_own_other, scratch=((RANK, RANK),),
    )
    cross_sib = call(keep_kernel, struct(RANK), 0, core, r_sib[:RANK], after=(inverted,))
    z1, z_sib, crossed = call(
        middle_kernel, [struct(RANK + HALF), struct(RANK + HALF), struct(last)], MIDDLE_FLOPS,
        core, inverted, product, turned, r_own, r_sib,
    )
    crossed = call(cross_kernel, struct(last), CROSS_FLOPS, core, cross_sib, swap(cross_sib, "sub", 0), z_sib, crossed)

    own = third - crossed
    sib = swap(own, "rows", span_bits + 2)
    solved = swap(call(join_kernel, struct(3 * RANK + 2 * HALF), 0, core, z1, z0, after=(own,)), "sub", 0)
    z1_other, z0_other = solved[: RANK + HALF], solved[RANK + HALF :]
    part = jax.ShapeDtypeStruct((rhs.shape[0], RANK), jnp.bfloat16)
    high, low, current = call(
        reduced_kernel, [part, part, struct(rhs.shape[0], RHS)], 6 * rhs.shape[0] * 2 * RANK * (RANK + RHS),
        core, z1, z1_other, z0, z0_other, solved_gens, rhs,
    )
    sib = call(keep_kernel, struct(last), 0, core, sib, after=(high,))
    own_other, sib_other = swap(own, "sub", 0), swap(sib, "sub", 0)
    rows = rhs.shape[0]
    small = (own, own_other, sib, sib_other, high, low, current)
    return pl.pallas_call(
        final_kernel,
        in_specs=[SMEM] + [VMEM] * len(small),
        out_specs=HBM,
        out_shape=struct(rows, RHS),
        scratch_shapes=[
            pltpu.VMEM((RANK, RANK), jnp.float32),
            pltpu.VMEM((RANK, RHS), jnp.float32),
            pltpu.VMEM((rows, RHS), jnp.float32),
            pltpu.SemaphoreType.DMA((2,)),
        ],
        compiler_params=pltpu.CompilerParams(vmem_limit_bytes=VMEM_LIMIT),
        cost_estimate=cost(6 * rows * RANK * RHS + 6 * 9 * RANK**3, 3 * rows * RANK),
    )(core, *small)


def solution(mesh):
    placed = (
        P(("rows", "sub"), None),
        P(None, ("rows", "sub"), None),
        P(None, ("rows", "sub"), None),
    )
    return jax.shard_map(
        on_device, mesh=mesh, in_specs=placed, out_specs=P(("rows", "sub"), None), check_vma=False
    )
```
